32 devices in a mesh: dp: 2 (over x), context: 4 (over z), experts: 4 (over y, core).
Axes of the slice: x: 2, y: 2, z: 4, core: 2. Of those that a mesh axis runs over, the one named last changes fastest.
Arguments:
- tokens: bfloat16 [2, 4, 2, 4, 384, 768], P('dp', 'experts', None, 'context'), may hold values from -6 to 6
- cotangent: bfloat16 [2, 4, 2, 4, 384, 768], P('dp', 'experts', None, 'context'), may hold values from -6 to 6
- gates: float32 [2, 4, 2, 4, 384, 2], P('dp', 'experts', None, 'context'), may hold values from 0.3 to 1
- routes: int32 [2, 4, 2, 4, 384, 2], P('dp', 'experts', None, 'context'), may hold values from 0 to 7, all different within a row; in each aligned block of 384 rows (0 to 383, 384 to 767, ..., all dimensions but the last counted through in order) at most 128 rows name the same one
- qkv_weight: bfloat16 [768, 2304], P(None, ('context', 'experts')), may hold values from -0.21875 to 0.21875
- out_weight: bfloat16 [768, 768], P(('context', 'experts')), may hold values from -0.875 to 0.875
- shared_gate: bfloat16 [768, 2048], P(None, ('context', 'experts')), may hold values from -0.21875 to 0.21875
- shared_up: bfloat16 [768, 2048], P(None, ('context', 'experts')), may hold values from -0.21875 to 0.21875
- shared_down: bfloat16 [2048, 768], P(('context', 'experts')), may hold values from -0.1875 to 0.1875
- gains: bfloat16 [2, 768], P(None, ('context', 'experts')), may hold values from 0.5 to 1.5
- expert_gate: bfloat16 [8, 768, 2048], P('experts', None, ('dp', 'context')), may hold values from -0.21875 to 0.21875
- expert_up: bfloat16 [8, 768, 2048], P('experts', None, ('dp', 'context')), may hold values from -0.21875 to 0.21875
- expert_down: bfloat16 [8, 2048, 768], P('experts', ('dp', 'context')), may hold values from -0.1875 to 0.1875
Outputs:
- mixed: bfloat16 [2, 4, 2, 4, 384, 768], P('dp', 'experts', None, 'context')
- input_grad: bfloat16 [2, 4, 2, 4, 384, 768], P('dp', 'experts', None, 'context')
- grad_qkv: float32 [768, 2304], P(None, ('context', 'experts'))
- grad_out: float32 [768, 768], P(('context', 'experts'))
- grad_shared_gate: float32 [768, 2048], P(None, ('context', 'experts'))
- grad_shared_up: float32 [768, 2048], P(None, ('context', 'experts'))
- grad_shared_down: float32 [2048, 768], P(('context', 'experts'))
- grad_gains: float32 [2, 768], P(None, ('context', 'experts'))
- grad_expert_gate: float32 [8, 768, 2048], P('experts', None, ('dp', 'context'))
- grad_expert_up: float32 [8, 768, 2048], P('experts', None, ('dp', 'context'))
- grad_expert_down: float32 [8, 2048, 768], P('experts', ('dp', 'context'))
The draws below stay inside these ranges and needn't reach their ends.
Inputs may be any that keep to these rules, and one draw needn't show every extreme that they name: `routes`: in each aligned block of 384 rows (one block of one group and micro-batch) no expert is named more than 128 times, a bound that some block reaches; a row's 2 experts differ.
All inputs are finite; a program needn't handle non-finite values.
Results may differ from the reference program's by a relative error of at most 0.019.
Values may be sent and summed in bfloat16 or wider, within the bound.
A program may use at most 384 MiB of HBM per device.

```python
import math
from functools import partial
import jax
import jax.numpy as jnp
import numpy as np
from jax import lax

D = 768
H = 12
HD = 64
FF = 2048
TOP = 2
PB = 128
CONT = 256
MICRO = 2
EXPERTS = 8
ROWS = 384
PROMPT = 512
CAP = 128
N_DP = 2
N_CONTEXT = 4
N_EXPERTS = 4


def steps_of(stream_key, shape, split, low, top_value):
    def one(axis_at, shards_of):
        draws = jax.random.uniform(jax.random.fold_in(jax.random.fold_in(stream_key, 6), axis_at), (shards_of,), jnp.float32, low / len(split), top_value / len(split))
        return jnp.repeat(jnp.exp(draws), shape[axis_at] // shards_of).reshape((-1,) + (1,) * (len(shape) - axis_at - 1))

    factor_of = one(*split[0])
    for cut in split[1:]:
        factor_of = factor_of * one(*cut)
    return factor_of


def assign_block(rng, own, number, rows, amount, top, limit, skew):
    order = jax.random.permutation(rng, amount)
    heavy_load, usual = shares(amount, rows * top, limit, skew, True), shares(amount, rows * top, limit, skew, False)
    places = jnp.arange(amount)

    def named(lengths, offset_by):
        used = int((lengths > 0).sum())
        fixed = max(1, used // 4)
        moved = fixed + (places - fixed + offset_by * (used - fixed)) % max(1, amount - fixed)
        return jnp.zeros((amount,), jnp.int32).at[order[jnp.where(places < fixed, places, moved)]].set(jnp.asarray(lengths, jnp.int32))

    lengths = jnp.where(number % 4 == 0, named(heavy_load, number // 4), named(usual, number - number // 4 - 1))
    mixed = jax.random.permutation(jax.random.fold_in(own, 3), amount)
    donor, sink = mixed[0:amount // 2 * 2:2], mixed[1:amount // 2 * 2:2]
    room = jnp.minimum(lengths[donor] - 1, limit - lengths[sink]) // 2
    room = jnp.where((donor == order[0]) | (sink == order[0]) | (lengths[sink] == 0), 0, jnp.maximum(room, 0))
    moved = jax.random.randint(jax.random.fold_in(own, 4), (amount // 2,), 0, 1 << 20) % (room + 1)
    lengths = lengths.at[donor].add(-moved).at[sink].add(moved)
    members = jnp.searchsorted(jnp.cumsum(lengths), jnp.arange(rows * top), side="right").astype(jnp.int32)
    table = members.reshape(top, rows).T
    table = table[jax.random.permutation(jax.random.fold_in(own, 1), rows)]
    offset_by = jax.random.randint(jax.random.fold_in(own, 2), (rows, 1), 0, top)
    return jnp.take_along_axis(table, (jnp.arange(top)[None, :] + offset_by) % top, axis=1)


def shares(number_of, total, reach, skew, full):
    portions = [(1 << 20) // math.isqrt(grade ** skew) + 1 for grade in range(1, number_of + 1)]
    largest = reach if full else min(reach, max(-(-total // number_of), total * portions[0] // sum(portions)))
    least = 1 if total - largest >= number_of - 1 else 0
    counts, surplus = [largest] + [least] * (number_of - 1), total - largest - least * (number_of - 1)
    while surplus > 0:
        free = [i for i in range(1, number_of) if counts[i] < largest] or [i for i in range(1, number_of) if counts[i] < reach]
        pool, remaining = sum([portions[i] for i in free]), surplus
        for i in free:
            addition = min(reach - counts[i], max(1, remaining * portions[i] // pool), surplus)
            counts[i] = counts[i] + addition
            surplus = surplus - addition
    return np.array(counts)


def scatter_about(own_key, dims, width, bound, split=(), held_as=jnp.bfloat16):
    loudness = steps_of(own_key, dims, split, -0.22, 0.18) if split else 1.0
    result = jax.random.normal(own_key, dims, jnp.float32) * width * loudness
    return jnp.minimum(jnp.maximum(result, -bound), bound).astype(held_as)


def setup_inputs(seed: int = 0) -> dict:
    key_of = jax.random.split(jax.random.key(seed), 14)
    tokens = scatter_about(key_of[0], (N_DP, N_EXPERTS, MICRO, N_CONTEXT, ROWS, D), 1.0, 6.0, ((0, 2), (1, 4), (3, 4)))
    cotangent = scatter_about(key_of[1], (N_DP, N_EXPERTS, MICRO, N_CONTEXT, ROWS, D), 1.0, 6.0, ((0, 2), (1, 4), (3, 4)))
    gates = jnp.clip(0.3 + 0.7 * jax.random.uniform(key_of[2], (N_DP, N_EXPERTS, MICRO, N_CONTEXT, ROWS, TOP), jnp.float32) ** steps_of(key_of[2], (N_DP, N_EXPERTS, MICRO, N_CONTEXT, ROWS, TOP), ((0, 2), (1, 4), (3, 4)), -0.2, 0.2), 0.3, 1.0)
    routes_keys = jax.random.split(jax.random.fold_in(key_of[3], 1), N_DP * N_EXPERTS * MICRO * N_CONTEXT * ROWS // ROWS)
    routes_turns = jax.random.permutation(jax.random.fold_in(key_of[3], 3), N_DP * N_EXPERTS * MICRO * N_CONTEXT * ROWS // ROWS)
    routes = jax.vmap(lambda own, number: assign_block(jax.random.fold_in(key_of[3], 2), own, number, ROWS, EXPERTS, TOP, CAP, 2))(routes_keys, routes_turns).reshape((N_DP, N_EXPERTS, MICRO, N_CONTEXT, ROWS, TOP))
    qkv_weight = scatter_about(key_of[4], (D, 3 * D), D ** -0.5, 0.21875, ((1, 16),))
    out_weight = scatter_about(key_of[5], (D, D), (D // 16) ** -0.5, 0.875, ((0, 16),))
    shared_gate = scatter_about(key_of[6], (D, FF), D ** -0.5, 0.21875, ((1, 16),))
    shared_up = scatter_about(key_of[7], (D, FF), D ** -0.5, 0.21875, ((1, 16),))
    shared_down = scatter_about(key_of[8], (FF, D), (FF // 2) ** -0.5, 0.1875, ((0, 16),))
    gains = jnp.clip(1.0 + 0.1 * jax.random.normal(key_of[9], (2, D), jnp.float32), 0.5, 1.5).astype(jnp.bfloat16)
    expert_gate = scatter_about(key_of[10], (EXPERTS, D, FF), D ** -0.5, 0.21875, ((0, 4), (2, 8)))
    expert_up = scatter_about(key_of[11], (EXPERTS, D, FF), D ** -0.5, 0.21875, ((0, 4), (2, 8)))
    expert_down = scatter_about(key_of[12], (EXPERTS, FF, D), (FF // 2) ** -0.5, 0.1875, ((0, 4), (1, 8)))
    return dict(tokens=tokens, cotangent=cotangent, gates=gates, routes=routes, qkv_weight=qkv_weight, out_weight=out_weight, shared_gate=shared_gate, shared_up=shared_up, shared_down=shared_down, gains=gains, expert_gate=expert_gate, expert_up=expert_up, expert_down=expert_down)


@jax.custom_vjp
def low(v):
    return lax.optimization_barrier(v.astype(jnp.bfloat16)).astype(jnp.float32)

@jax.custom_vjp
def low_back(v):
    return v

def low_keep(v):
    return (low(v), None)

def low_pass(kept, grad):
    return (grad,)

def back_keep(v):
    return (v, None)

def back_low(kept, grad):
    return (low(grad),)
low.defvjp(low_keep, low_pass)
low_back.defvjp(back_keep, back_low)
EPSILON = 1e-06
HIGHEST = lax.Precision.HIGHEST

def rms_norm(values, gain):
    root = lax.rsqrt(lax.optimization_barrier(jnp.mean(values * values, -1, keepdims=True)) + EPSILON)
    return values * root * gain

def rotate(values, positions, sign):
    half_size = HD // 2
    frequency = 10000.0 ** (-2.0 * jnp.arange(half_size, dtype=jnp.float32) / HD)
    angles = positions.astype(jnp.float32)[..., None] * frequency
    cosine = jnp.cos(angles)[..., None, :]
    sine_part = sign * jnp.sin(angles)[..., None, :]
    shaped = values.reshape(values.shape[:-1] + (H, HD))
    former = shaped[..., :half_size]
    latter = shaped[..., half_size:]
    turned = jnp.concatenate([former * cosine - latter * sine_part, latter * cosine + former * sine_part], -1)
    return turned.reshape(values.shape)

def slot_table(routes_block, expert_count):
    flat_routes = routes_block.reshape(-1)
    onehot = (flat_routes[:, None] == jnp.arange(expert_count, dtype=jnp.int32)[None, :]).astype(jnp.int32)
    before = jnp.cumsum(onehot, 0) - onehot
    return lax.optimization_barrier(jnp.sum(before * onehot, 1)).reshape(routes_block.shape)

def expert_apply(operands):
    inputs, weight_gate, weight_up, weight_down = operands
    gate_act = low_back(jnp.dot(inputs, weight_gate, precision=HIGHEST))
    up_act = low_back(jnp.dot(inputs, weight_up, precision=HIGHEST))
    hidden_act = low_back(low(jax.nn.silu(gate_act) * up_act))
    return low_back(low(jnp.dot(hidden_act, weight_down, precision=HIGHEST)))

def unit_forward(inputs, gate_unit, route_unit, qkv_weight, out_weight, shared_gate, shared_up, shared_down, gains, expert_gate, expert_up, expert_down):
    row_ids = jnp.arange(ROWS, dtype=jnp.int32)
    block_ids = jnp.arange(N_CONTEXT, dtype=jnp.int32)
    positions = jnp.where(row_ids[None, :] < PB, block_ids[:, None] * PB + row_ids[None, :], PROMPT + row_ids[None, :] - PB)
    normed_one = low(rms_norm(inputs, gains[0]))
    projected = jnp.dot(normed_one, qkv_weight, precision=HIGHEST)
    queries = low(rotate(low_back(projected[..., :D]), positions, 1.0))
    keys_all = low(rotate(low_back(projected[..., D:2 * D]), positions, 1.0))
    values_all = low(low_back(projected[..., 2 * D:]))
    prompt_keys = keys_all[:, :PB].reshape(PROMPT, D)
    prompt_values = values_all[:, :PB].reshape(PROMPT, D)
    key_positions = jnp.arange(PROMPT + CONT, dtype=jnp.int32)

    def attend(operands):
        query_block, own_keys, own_values, query_positions = operands
        key_heads = jnp.concatenate([prompt_keys, own_keys], 0).reshape(PROMPT + CONT, H, HD)
        value_heads = jnp.concatenate([prompt_values, own_values], 0).reshape(PROMPT + CONT, H, HD)
        scores = jnp.einsum('qhd,khd->hqk', query_block.reshape(ROWS, H, HD), key_heads, precision=HIGHEST) * HD ** (-0.5)
        scores = low_back(scores)
        scores = jnp.where(key_positions[None, None, :] <= query_positions[None, :, None], scores, -1000000000.0)
        highest = lax.optimization_barrier(jnp.max(scores, -1, keepdims=True))
        weights = jnp.exp(scores - highest)
        probs = low(weights / lax.optimization_barrier(jnp.sum(weights, -1, keepdims=True)))
        mixed_heads = jnp.einsum('hqk,khd->qhd', probs, value_heads, precision=HIGHEST).reshape(ROWS, D)
        return low_back(low(mixed_heads))
    attended = lax.map(jax.checkpoint(attend), (queries, keys_all[:, PB:], values_all[:, PB:], positions))
    hidden = inputs + low_back(jnp.dot(attended, out_weight, precision=HIGHEST))
    normed_two = low(rms_norm(hidden, gains[1]))
    side_gate = low_back(jnp.dot(normed_two, shared_gate, precision=HIGHEST))
    side_up = low_back(jnp.dot(normed_two, shared_up, precision=HIGHEST))
    side_act = low_back(low(jax.nn.silu(side_gate) * side_up))
    side = low_back(jnp.dot(side_act, shared_down, precision=HIGHEST))
    slots = jax.vmap(partial(slot_table, expert_count=EXPERTS))(route_unit)
    block_base = jnp.arange(N_CONTEXT, dtype=jnp.int32)[:, None, None] * CAP
    destination = route_unit * (N_CONTEXT * CAP) + block_base + slots
    flat_normed = normed_two.reshape(N_CONTEXT * ROWS, D)
    buffer = jnp.zeros((EXPERTS * N_CONTEXT * CAP, D), jnp.float32)
    for slot_index in range(TOP):
        buffer = buffer.at[destination[..., slot_index].reshape(-1)].set(low_back(flat_normed))
    expert_outs = lax.map(jax.checkpoint(expert_apply), (buffer.reshape(EXPERTS, N_CONTEXT * CAP, D), expert_gate, expert_up, expert_down)).reshape(-1, D)
    routed = jnp.zeros_like(flat_normed)
    for slot_index in range(TOP):
        picked = expert_outs[destination[..., slot_index].reshape(-1)]
        routed = routed + gate_unit[..., slot_index].reshape(-1)[:, None] * picked
    return hidden + routed.reshape(N_CONTEXT, ROWS, D) + side

def reference(tokens, cotangent, gates, routes, qkv_weight, out_weight, shared_gate, shared_up, shared_down, gains, expert_gate, expert_up, expert_down):
    units = N_DP * N_EXPERTS * MICRO
    inputs_all = tokens.astype(jnp.float32).reshape(units, N_CONTEXT, ROWS, D)
    cot_all = cotangent.astype(jnp.float32).reshape(units, N_CONTEXT, ROWS, D)
    gate_all = gates.astype(jnp.float32).reshape(units, N_CONTEXT, ROWS, TOP)
    route_all = routes.reshape(units, N_CONTEXT, ROWS, TOP)
    weights = tuple((item.astype(jnp.float32) for item in (qkv_weight, out_weight, shared_gate, shared_up, shared_down, gains, expert_gate, expert_up, expert_down)))

    def step(totals, operands):
        inputs, cot_unit, gate_unit, route_unit = operands

        def forward(inputs_now, *weights_now):
            return unit_forward(inputs_now, gate_unit, route_unit, *weights_now)
        output, pullback = jax.vjp(forward, inputs, *weights)
        grads = pullback(cot_unit)
        totals = tuple((total + grad for total, grad in zip(totals, grads[1:])))
        return (totals, (output.astype(jnp.bfloat16), grads[0].astype(jnp.bfloat16)))
    zero_filled = tuple((jnp.zeros(item.shape, jnp.float32) for item in weights))
    totals, (outputs, input_grads) = lax.scan(step, zero_filled, (inputs_all, cot_all, gate_all, route_all))
    grad_qkv, grad_out, grad_shared_gate, grad_shared_up, grad_shared_down, grad_gains, grad_expert_gate, grad_expert_up, grad_expert_down = totals
    return (outputs.reshape(tokens.shape), input_grads.reshape(tokens.shape), grad_qkv, grad_out, grad_shared_gate, grad_shared_up, grad_shared_down, grad_gains, grad_expert_gate, grad_expert_up, grad_expert_down)
```

```python
import functools

import jax
import jax.numpy as jnp
import numpy as np
from jax import lax
from jax.experimental import pallas as pl
from jax.experimental.pallas import tpu as pltpu
from jax.sharding import PartitionSpec as P

DP, CONTEXT, EXPERTS = "dp", "context", "experts"

H = 12
HD = 64
PB = 128
CONT = 256


EPSILON = 1e-06


def mdot(former, latter):
    return jnp.dot(former, latter, preferred_element_type=jnp.float32)


def tdot(former, latter):
    return lax.dot_general(
        former, latter, (((0,), (0,)), ((), ())), preferred_element_type=jnp.float32
    )


def ndot(former, latter):
    return lax.dot_general(
        former, latter, (((1,), (1,)), ((), ())), preferred_element_type=jnp.float32
    )


def rotate(values, cosine, sine_part):
    half_size = HD // 2
    shaped = values.reshape(values.shape[0], H, HD)
    former = shaped[..., :half_size]
    latter = shaped[..., half_size:]
    turned = jnp.concatenate(
        [former * cosine - latter * sine_part, latter * cosine + former * sine_part], -1
    )
    return turned.reshape(values.shape)


def slot_table(routes_block, expert_count):
    flat_routes = routes_block.reshape(-1)
    onehot = (flat_routes[:, None] == jnp.arange(expert_count, dtype=jnp.int32)[None, :]).astype(
        jnp.int32
    )
    before = jnp.cumsum(onehot, 0) - onehot
    return jnp.sum(before * onehot, 1).reshape(routes_block.shape)


def silu_parts(values):
    sigma = jax.nn.sigmoid(values)
    return (values * sigma, sigma * (1.0 + values * (1.0 - sigma)))


MESH = pl.DeviceIdType.MESH
MIB = 1024 * 1024
BF = jnp.bfloat16
F32 = jnp.float32


def remote(source, target, send_sem, recv_sem, **device):
    return pltpu.make_async_remote_copy(
        src_ref=source,
        dst_ref=target,
        send_sem=send_sem,
        recv_sem=recv_sem,
        device_id=device,
        device_id_type=MESH,
    )


def arrived(slot, recv_sem):
    remote(slot, slot, recv_sem, recv_sem, context=0).wait_recv()


def either(first, second):
    return jnp.logical_and(first, second)


class Place:
    def __init__(self, sizes):
        self.depth, self.high_count = sizes
        self.owners = self.high_count * 2
        self.x = lax.axis_index(DP)
        self.z = lax.axis_index(CONTEXT)
        self.e = lax.axis_index(EXPERTS)
        self.high = self.e // 2
        self.low = self.e % 2

    def shard(self, z):
        return self.x * self.depth + z

    def other_shard(self, z):
        return (1 - self.x) * self.depth + z

    def peer_high(self, step):
        return lax.rem(self.high + step, self.high_count)

    def peer_owner(self, step):
        return lax.rem(self.e + step, self.owners)

    def on_line(self, z):
        return (z >= 0) & (z < self.depth)

    def greet(self):
        barrier = pltpu.get_barrier_semaphore()

        def signal(**device):
            pl.semaphore_signal(barrier, inc=1, device_id=device, device_id_type=MESH)

        signal(dp=1 - self.x)
        for step in range(1, self.owners):
            signal(experts=self.peer_owner(step))
        pl.when(self.z > 0)(lambda: signal(context=self.z - 1))
        pl.when(self.z < self.depth - 1)(lambda: signal(context=self.z + 1))
        count = 1 + self.owners - 1
        count += jnp.where(self.z > 0, 1, 0) + jnp.where(self.z < self.depth - 1, 1, 0)
        pl.semaphore_wait(barrier, count)


class Line:
    def __init__(self, place, own, slot, send_sem, recv_sem):
        self.place, self.own, self.slot = place, own, slot
        self.send_sem, self.recv_sem = send_sem, recv_sem

    def _copy(self, direction, step):
        place = self.place
        z = place.z - direction * step
        source = self.own if step == 0 else self.slot(z)
        return remote(
            source,
            self.slot(z),
            self.send_sem.at[(direction + 1) // 2, step],
            self.recv_sem.at[z],
            context=place.z + direction,
        )

    def _valid(self, direction, step):
        place = self.place
        return place.on_line(place.z - direction * step) & place.on_line(place.z + direction)

    def send(self, direction, step):
        if step < self.place.depth - 1:
            pl.when(self._valid(direction, step))(lambda: self._copy(direction, step).start())

    def start(self):
        self.send(1, 0)
        self.send(-1, 0)

    def hop(self, step, then=None):
        for direction in (1, -1):
            z = self.place.z - direction * (step + 1)

            def body(direction=direction, z=z):
                arrived(self.slot(z), self.recv_sem.at[z])
                self.send(direction, step + 1)
                if then is not None:
                    then(z)

            pl.when(self.place.on_line(z))(body)

    def drain(self):
        for direction in (1, -1):
            for step in range(self.place.depth - 1):
                pl.when(self._valid(direction, step))(
                    lambda d=direction, s=step: self._copy(d, s).wait_send()
                )


class DenseGather:
    def __init__(self, place, own, slot, sems):
        self.place, self.own, self.slot_of = place, own, slot
        zs, zr, self.h_send, self.h_recv, self.l_send, self.l_recv = sems
        self.line = Line(place, own, lambda z: self.slot(z, place.high, place.low), zs, zr)

    @staticmethod
    def semaphores(count, depth, high_count):
        dma = pltpu.SemaphoreType.DMA
        cross = dma((count, high_count, depth))
        return [dma((count, 2, depth)), dma((count, depth)), cross, cross, cross, cross]

    def slot(self, z, high, low):
        return self.slot_of((z * self.place.high_count + high) * 2 + low)

    def _to_high(self, z, step, own):
        place = self.place
        target = self.slot(z, place.high, place.low)
        return remote(
            self.own if own else target,
            target,
            self.h_send.at[step, z],
            self.h_recv.at[place.high, z],
            experts=place.peer_high(step) * 2 + place.low,
        )

    def _to_low(self, z, high, own):
        place = self.place
        target = self.slot(z, high, place.low)
        return remote(
            self.own if own else target,
            target,
            self.l_send.at[high, z],
            self.l_recv.at[high, z],
            experts=place.e + 1 - 2 * place.low,
        )

    def _spread(self, z, own=False):
        for step in range(1, self.place.high_count):
            self._to_high(z, step, own).start()
        self._to_low(z, self.place.high, own).start()

    def start(self):
        self.line.start()
        self._spread(self.place.z, True)

    def hop(self, step):
        self.line.hop(step, self._spread)

    def cross(self, z):
        place = self.place
        for step in range(1, place.high_count):
            high = place.peer_high(step)
            arrived(self.slot(z, high, place.low), self.h_recv.at[high, z])
            self._to_low(z, high, False).start()

    def finish(self):
        place = self.place
        for z in range(place.depth):
            for high in range(place.high_count):
                arrived(self.slot(z, high, 1 - place.low), self.l_recv.at[high, z])

    def drain(self):
        place = self.place
        self.line.drain()
        for z in range(place.depth):
            for step in range(1, place.high_count):
                self._to_high(z, step, False).wait_send()
            for high in range(place.high_count):
                self._to_low(z, high, False).wait_send()


def expert_slab(ref, kind, local, shard, width):
    start = pl.multiple_of(shard * width, 128)
    if kind == 2:
        return ref.at[local, pl.ds(start, width)]
    return ref.at[local, :, pl.ds(start, width)]


class ExpertGather:
    def __init__(self, place, own, out, sems):
        self.place, self.own, self.out = place, own, out
        self.z_send, self.z_recv, self.x_send, self.x_recv = sems
        self.local_count, self.width = own[0].shape[0], own[0].shape[2]

    @staticmethod
    def semaphores(depth, local_count):
        dma = pltpu.SemaphoreType.DMA
        return [
            dma((local_count, 3, 2, depth)),
            dma((local_count, 3, depth)),
            dma((local_count, 3, depth)),
            dma((local_count, 3, depth)),
        ]

    def slot(self, local, kind, shard):
        return expert_slab(self.out[kind], kind, local, shard, self.width)

    def _line(self, local, kind):
        return Line(
            self.place,
            self.own[kind].at[local],
            lambda z: self.slot(local, kind, self.place.shard(z)),
            self.z_send.at[local, kind],
            self.z_recv.at[local, kind],
        )

    def _across(self, local, kind, z, own=False):
        target = self.slot(local, kind, self.place.shard(z))
        return remote(
            self.own[kind].at[local] if own else target,
            target,
            self.x_send.at[local, kind, z],
            self.x_recv.at[local, kind, z],
            dp=1 - self.place.x,
        )

    def start_x(self):
        for local in range(self.local_count):
            for kind in range(3):
                self._across(local, kind, self.place.z, True).start()

    def start_z(self):
        for local in range(self.local_count):
            for kind in range(3):
                self._line(local, kind).start()

    def hop(self, local, step):
        for kind in range(3):
            self._line(local, kind).hop(
                step, lambda z, kind=kind: self._across(local, kind, z).start()
            )

    def wait_x(self, local, z):
        for kind in range(3):
            arrived(
                self.slot(local, kind, self.place.other_shard(z)), self.x_recv.at[local, kind, z]
            )

    def drain(self):
        for local in range(self.local_count):
            for kind in range(3):
                self._line(local, kind).drain()
                for z in range(self.place.depth):
                    self._across(local, kind, z).wait_send()


def rope(values, cosine, sine_part):
    lane = lax.broadcasted_iota(jnp.int32, cosine.shape, 1)
    first = lax.rem(lane, HD) < HD // 2
    turned = []
    for start in range(0, values.shape[1], 2 * HD):
        part = values[:, start : start + 2 * HD]
        partner = jnp.where(
            first, pltpu.roll(part, 2 * HD - HD // 2, 1), pltpu.roll(part, HD // 2, 1)
        )
        turned.append(part * cosine + partner * sine_part)
    return jnp.concatenate(turned, 1)


def norm_rows(values, gain):
    root = lax.rsqrt(jnp.mean(values * values, -1, keepdims=True) + EPSILON)
    return (values * root * gain).astype(BF)


def tiles(total, size, body):
    def run(i, carry):
        body(pl.ds(pl.multiple_of(i * size, size), size))
        return carry

    lax.fori_loop(0, total // size, run, 0)


def one_hots(routes, gates, me, local_count, total):
    rows = routes.shape[1]
    capacity = rows * 8 // (3 * total)
    first, second = routes[0:1, :], routes[1:2, :]
    ids = lax.rem(
        lax.broadcasted_iota(jnp.int32, (total, rows), 0) + me * local_count, total
    )
    named = (first == ids) | (second == ids)
    earlier = (
        lax.broadcasted_iota(jnp.int32, (rows, rows), 0)
        < lax.broadcasted_iota(jnp.int32, (rows, rows), 1)
    ).astype(F32).astype(BF)
    counts = mdot(named.astype(F32).astype(BF), earlier).astype(jnp.int32)
    places = jnp.where(named, counts, -1)
    weights = jnp.where(first == ids, gates[0:1, :], 0.0) + jnp.where(
        second == ids, gates[1:2, :], 0.0
    )
    slot = lax.broadcasted_iota(jnp.int32, (capacity, rows), 0)
    for i in range(total):
        yield i, slot == places[i : i + 1, :], weights[i : i + 1, :]


def ffn_chunk(x, g, weights, saved, sums, grads, tile):
    gate_w, up_w, down_w = weights
    act_s, d_gate_s, d_up_s = saved
    out_sum, in_sum = sums

    def forward(here):
        x_rows, g_rows = x[here, :], g[here, :]
        gate = mdot(x_rows, gate_w[...])
        up = mdot(x_rows, up_w[...])
        d_act = ndot(g_rows, down_w[...]).astype(BF).astype(F32)
        sigma = jax.nn.sigmoid(gate)
        silu = gate * sigma
        act = (silu * up).astype(BF)
        d_gate = (d_act * up * (sigma * (1.0 + gate * (1.0 - sigma)))).astype(BF)
        d_up = (d_act * silu).astype(BF)
        act_s[here, :] = act
        d_gate_s[here, :] = d_gate
        d_up_s[here, :] = d_up
        out_sum[here, :] += mdot(act, down_w[...])
        in_sum[here, :] += ndot(d_gate, gate_w[...]) + ndot(d_up, up_w[...])

    rows = x.shape[0]
    tiles(rows, tile, forward)
    used = pl.ds(0, rows)

    def weight_grads(here):
        grads[0][here, :] = tdot(x[:, here], d_gate_s[used, :]).astype(BF)
        grads[1][here, :] = tdot(x[:, here], d_up_s[used, :]).astype(BF)
        grads[2][:, here] = tdot(act_s[used, :], g[:, here]).astype(BF)

    tiles(x.shape[1], 256, weight_grads)


def forward_kernel(sizes, *refs):
    place = Place(sizes)
    depth, high_count = sizes
    owners = place.owners
    (
        tokens, cot, gates, routes, cosine, sine_part,
        qkv_in, out_in, gain_in, sg_in, su_in, sd_in, eg_in, eu_in, ed_in,
        qkv_o, out_o, gain_o, sg_o, su_o, sd_o, eg_o, eu_o, ed_o,
        n1_o, k_o, v_o, q_o, att_o, hid_o, lse_o, side_o, dn2_o,
        gsg_o, gsu_o, gsd_o, geg_o, geu_o, ged_o, outs_o, dins_o,
        xk, wq, wo, gain_land, gain_v, g_all, n2, in_s, do_s, send_in, send_do,
        wg, wu, wd, act_s, dg_s, du_s, stage_g, stage_u, stage_d,
        *sems,
    ) = refs
    dense_sems, sems = sems[:6], sems[6:]
    expert_sems, sems = sems[:4], sems[4:]
    (
        line_send, line_recv, load_sem, ai_send, ai_recv, ad_send, ad_recv,
        chunk_sem, store_sem, out_sem,
    ) = sems
    micro_count, rows, features = tokens.shape
    prompt = depth * PB
    length = prompt + CONT
    local_count, _, width = eg_in.shape
    total = owners * local_count
    capacity = rows * 8 // (3 * total)
    slots = in_s.shape[1]
    me = place.e

    def dense(i, own, slot):
        return DenseGather(place, own, slot, [s.at[i] for s in dense_sems])

    def rows_of(ref, count):
        return lambda s: ref.at[pl.ds(pl.multiple_of(s * count, 16), count)]

    def columns_of(ref, count):
        return lambda s: ref.at[:, pl.ds(pl.multiple_of(s * count, 128), count)]

    early = [
        dense(0, qkv_in, rows_of(wq, qkv_in.shape[0])),
        dense(1, out_in, rows_of(wo, out_in.shape[0])),
        dense(2, gain_in, rows_of(gain_land, gain_in.shape[0])),
    ]
    late = [
        dense(3, sg_in, columns_of(sg_o, sg_in.shape[1])),
        dense(4, su_in, columns_of(su_o, su_in.shape[1])),
        dense(5, sd_in, rows_of(sd_o, sd_in.shape[0])),
    ]
    experts = ExpertGather(place, (eg_in, eu_in, ed_in), (eg_o, eu_o, ed_o), expert_sems)
    own_prompt = pl.ds(pl.multiple_of(place.z * PB, PB), PB)
    prompts = Line(
        place,
        tokens.at[:, pl.ds(0, PB)],
        lambda z: xk.at[:, pl.ds(pl.multiple_of(z * PB, PB), PB)],
        line_send,
        line_recv,
    )
    own_at = (place.z * high_count + place.high) * 2 + place.low
    loads = [
        (tokens.at[:, pl.ds(0, PB)], xk.at[:, own_prompt]),
        (tokens.at[:, pl.ds(PB, CONT)], xk.at[:, pl.ds(prompt, CONT)]),
    ]
    loads += [(cot.at[m], g_all.at[pl.ds(m * rows, rows)]) for m in range(micro_count)]
    loads += [(d.own, d.slot_of(own_at)) for d in early]
    bounce = [
        (sg_in, wg.at[0, :, pl.ds(0, sg_in.shape[1])], late[0].slot_of(own_at)),
        (su_in, wu.at[0, :, pl.ds(0, su_in.shape[1])], late[1].slot_of(own_at)),
        (sd_in, wd.at[0, pl.ds(0, sd_in.shape[0])], late[2].slot_of(own_at)),
    ]
    loads += [(source, middle) for source, middle, _ in bounce]
    load_copies = [
        pltpu.make_async_copy(source, target, load_sem.at[i])
        for i, (source, target) in enumerate(loads)
    ]
    bounce_copies = [
        pltpu.make_async_copy(middle, target, load_sem.at[i])
        for i, (_, middle, target) in enumerate(bounce)
    ]
    for copy in load_copies:
        copy.start()
    place.greet()
    prompts.start()
    for d in early:
        d.start()
    experts.start_x()
    for copy in load_copies:
        copy.wait()
    for copy in bounce_copies:
        copy.start()
    stores = []

    def store(source, target):
        copy = pltpu.make_async_copy(source, target, out_sem.at[len(stores)])
        copy.start()
        stores.append(copy)

    def slot_rows(m, sender):
        return pl.ds(pl.multiple_of((m * owners + sender) * capacity, 16), capacity)

    def exchange(buffer, land, send_sem, recv_sem, m, step):
        return remote(
            buffer.at[step - 1, m],
            land.at[:, slot_rows(m, me)],
            send_sem.at[step - 1, m],
            recv_sem.at[step - 1, m],
            experts=place.peer_owner(step),
        )

    def exchanged(land, recv_sem, m, step):
        sender = lax.rem(me - step + owners, owners)
        arrived(land.at[:, slot_rows(m, sender)], recv_sem.at[step - 1, m])

    def put(buffer, land, m, i, value):
        if i < local_count:
            land[i, slot_rows(m, me), :] = value
        else:
            buffer[i // local_count - 1, m, i % local_count] = value

    for m in range(micro_count):
        g_rows = g_all[pl.ds(m * rows, rows), :]
        for i, hit, weight in one_hots(routes.at[m], gates.at[m], me, local_count, total):
            gate = jnp.sum(jnp.where(hit, weight, 0.0), -1, keepdims=True)
            value = mdot(hit.astype(F32).astype(BF), g_rows)
            put(send_do, do_s, m, i, (gate * value).astype(BF))
    prompts.hop(0)
    for step in range(depth - 1):
        for d in early:
            d.hop(step)
        if step + 1 < depth - 1:
            prompts.hop(step + 1)
    for copy in bounce_copies:
        copy.wait()
    for d in late:
        d.start()
    experts.start_z()
    for z in range(depth):
        for d in early:
            d.cross(z)
    for d in early:
        d.finish()
    for m in range(micro_count):
        for step in range(1, owners):
            exchange(send_do, do_s, ad_send, ad_recv, m, step).start()
    store(wq, qkv_o)
    store(wo, out_o)
    shards = depth * owners
    gain_rows = gain_in.shape[0]
    gain_sum = jnp.zeros((8, features), F32)
    for s in range(shards):
        gain_sum += gain_land[pl.ds(s * gain_rows, gain_rows), :].astype(F32)[:8]
    gain_v[...] = gain_sum
    store(gain_v, gain_o)

    def own_rows(i):
        start = place.z * PB if i == 0 else prompt + (i - 1) * PB
        return start, pl.ds(start if i else pl.multiple_of(start, PB), PB)

    def front(n1, k, v, q, att, hid, lse):
        lse[...] = jnp.zeros_like(lse)
        for m in range(micro_count):

            def project(here):
                normed = norm_rows(xk[m, here, :].astype(F32), gain_v[0:1, :])
                n1[m, here, :] = normed
                key = ndot(normed, wq[pl.ds(features, features), :])
                k[m, here, :] = rope(key, cosine[here, :], sine_part[here, :]).astype(BF)
                v[m, here, :] = ndot(normed, wq[pl.ds(2 * features, features), :]).astype(BF)

            tiles(length, 256, project)
            for i in range(rows // PB):
                _, here = own_rows(i)
                query = ndot(n1[m, here, :], wq[pl.ds(0, features), :])
                query = rope(query, cosine[here, :], sine_part[here, :]).astype(BF)
                q[m, pl.ds(i * PB, PB), :] = query * jnp.asarray(HD**-0.5, BF)
            for d in late:
                d.hop(m)
        store(n1, n1_o)
        store(k, k_o)
        store(v, v_o)
        store(q, q_o)
        lane = lax.broadcasted_iota(jnp.int32, (PB, 2 * HD), 1)
        column = lax.broadcasted_iota(jnp.int32, (PB, length), 1)
        row = lax.broadcasted_iota(jnp.int32, (PB, length), 0)
        for m in range(micro_count):

            def pair(index, carry):
                lanes = pl.ds(pl.multiple_of(index * 2 * HD, 2 * HD), 2 * HD)
                keys, values = k[m, :, lanes], v[m, :, lanes]
                for i in range(rows // PB):
                    here = pl.ds(i * PB, PB)
                    query = q[m, here, lanes]
                    allowed = column <= row + own_rows(i)[0]
                    parts = []
                    logs = lse[m, here, :]
                    for sub in range(2):
                        only = jnp.where(lane // HD == sub, query, jnp.zeros_like(query))
                        scores = jnp.where(allowed, ndot(only, keys), -1000000000.0)
                        highest = jnp.max(scores, -1, keepdims=True)
                        weights = jnp.exp(scores - highest)
                        sums = jnp.sum(weights, -1, keepdims=True)
                        parts.append(mdot((weights * (1.0 / sums)).astype(BF), values))
                        logs = jnp.where(lane == 2 * index + sub, highest + jnp.log(sums), logs)
                    lse[m, here, :] = logs
                    att[m, here, lanes] = jnp.where(lane < HD, parts[0], parts[1]).astype(BF)
                return carry

            lax.fori_loop(0, features // (2 * HD), pair, 0)
            for i in range(rows // PB):
                here = pl.ds(i * PB, PB)
                hidden = xk[m, own_rows(i)[1], :].astype(F32) + mdot(att[m, here, :], wo[...])
                hid[m, here, :] = hidden
                n2[pl.ds(m * rows + i * PB, PB), :] = norm_rows(hidden, gain_v[1:2, :])
            normed = n2[pl.ds(m * rows, rows), :]
            for i, hit, _ in one_hots(routes.at[m], gates.at[m], me, local_count, total):
                value = mdot(hit.astype(F32).astype(BF), normed)
                put(send_in, in_s, m, i, value.astype(BF))
            for step in range(1, owners):
                exchange(send_in, in_s, ai_send, ai_recv, m, step).start()
            if m == 0:
                for step in range(micro_count, depth - 1):
                    for d in late:
                        d.hop(step)
        store(att, att_o)
        store(hid, hid_o)
        store(lse, lse_o)
        for z in range(depth):
            for d in late:
                d.cross(z)
        for d in late:
            d.finish()
        for copy in stores:
            copy.wait()

    pl.run_scoped(
        front,
        pltpu.VMEM((micro_count, length, features), BF),
        pltpu.VMEM((micro_count, length, features), BF),
        pltpu.VMEM((micro_count, length, features), BF),
        pltpu.VMEM((micro_count, rows, features), BF),
        pltpu.VMEM((micro_count, rows, features), BF),
        pltpu.VMEM((micro_count, rows, features), F32),
        pltpu.VMEM((micro_count, rows, 2 * HD), F32),
    )
    saved = (act_s, dg_s, du_s)
    staged = (stage_g, stage_u, stage_d)

    def chunk_loads(sources, slot):
        return [
            pltpu.make_async_copy(source, buffer.at[slot], chunk_sem.at[slot, kind])
            for kind, (source, buffer) in enumerate(zip(sources, (wg, wu, wd)))
        ]

    def chunk_stores(targets, slot):
        return [
            pltpu.make_async_copy(buffer.at[slot], target, store_sem.at[slot, kind])
            for kind, (target, buffer) in enumerate(zip(targets, staged))
        ]

    def shared(out_sum, in_sum):
        out_sum[...] = jnp.zeros_like(out_sum)
        in_sum[...] = jnp.zeros_like(in_sum)
        count = sg_o.shape[1] // width

        def part(refs, c):
            here = pl.ds(pl.multiple_of(c * width, 128), width)
            return [refs[0].at[:, here], refs[1].at[:, here], refs[2].at[here]]

        for copy in chunk_loads(part((sg_o, su_o, sd_o), 0), 0):
            copy.start()

        def run(c, carry):
            slot = lax.rem(c, 2)

            def prefetch():
                for copy in chunk_loads(part((sg_o, su_o, sd_o), c + 1), 1 - slot):
                    copy.start()

            pl.when(c + 1 < count)(prefetch)
            for copy in chunk_loads(part((sg_o, su_o, sd_o), c), slot):
                copy.wait()
            targets = part((gsg_o, gsu_o, gsd_o), c)

            def previous():
                for copy in chunk_stores(targets, slot):
                    copy.wait()

            pl.when(c >= 2)(previous)
            ffn_chunk(
                n2,
                g_all,
                (wg.at[slot], wu.at[slot], wd.at[slot]),
                saved,
                (out_sum, in_sum),
                [buffer.at[slot] for buffer in staged],
                384,
            )
            for copy in chunk_stores(targets, slot):
                copy.start()
            for local in range(local_count):
                pl.when(c == count // 2 + local)(lambda local=local: experts.hop(local, 0))
            return carry

        lax.fori_loop(0, count, run, 0)
        for slot in range(2):
            for copy in chunk_stores(part((gsg_o, gsu_o, gsd_o), slot), slot):
                copy.wait()
        ends = [
            pltpu.make_async_copy(out_sum, side_o, out_sem.at[0]),
            pltpu.make_async_copy(in_sum, dn2_o, out_sem.at[1]),
        ]
        for copy in ends:
            copy.start()
        for copy in ends:
            copy.wait()

    pl.run_scoped(
        shared,
        pltpu.VMEM((micro_count * rows, features), F32),
        pltpu.VMEM((micro_count * rows, features), F32),
    )
    for m in range(micro_count):
        for step in range(1, owners):
            exchanged(in_s, ai_recv, m, step)
            exchanged(do_s, ad_recv, m, step)

    def routed(out_sum, in_sum):
        out_sum[...] = jnp.zeros_like(out_sum)
        in_sum[...] = jnp.zeros_like(in_sum)

        def item(w, carry):
            after = jnp.maximum(w - 2, 0)
            step, kind = after // 4, lax.rem(after, 4)
            side = lax.rem(kind, 2)
            z = jnp.where(w < 2, place.z, place.z + (2 * side - 1) * (1 + step))
            crossed = jnp.where(w < 2, w, kind // 2)
            valid = place.on_line(z)
            shard = jnp.where(crossed == 1, place.other_shard(z), place.shard(z))

            def load(local):
                sources = [
                    expert_slab(ref, kind, local, shard, width)
                    for kind, ref in enumerate((eg_o, eu_o, ed_o))
                ]
                return chunk_loads(sources, local)

            def begin():
                def own():
                    for local in range(local_count):
                        mine = [ref.at[local] for ref in (eg_in, eu_in, ed_in)]
                        for copy in chunk_loads(mine, local):
                            copy.start()

                def landed():
                    def wait_x():
                        for local in range(local_count):
                            experts.wait_x(local, z)

                    pl.when(crossed == 1)(wait_x)
                    for local in range(local_count):
                        for copy in load(local):
                            copy.start()

                pl.when(w == 0)(own)
                pl.when(w > 0)(landed)

            pl.when(valid)(begin)

            def one(local, carry):
                targets = [
                    expert_slab(ref, kind, local, shard, width)
                    for kind, ref in enumerate((geg_o, geu_o, ged_o))
                ]

                def compute():
                    for copy in load(local):
                        copy.wait()

                    def previous():
                        for copy in chunk_stores(targets, local):
                            copy.wait()

                    pl.when(w > 0)(previous)
                    ffn_chunk(
                        in_s.at[local],
                        do_s.at[local],
                        (wg.at[local], wu.at[local], wd.at[local]),
                        saved,
                        (out_sum.at[local], in_sum.at[local]),
                        [buffer.at[local] for buffer in staged],
                        512,
                    )
                    for copy in chunk_stores(targets, local):
                        copy.start()

                pl.when(valid)(compute)
                for later in range(1, depth - 1):
                    at = 0 if later == 1 else 2 + 4 * (later - 2)
                    pl.when(w == at)(lambda later=later: experts.hop(local, later))
                return carry

            lax.fori_loop(0, local_count, one, 0)
            return carry

        lax.fori_loop(0, 2 + 4 * (depth - 1), item, 0)
        for local in range(local_count):
            targets = [
                expert_slab(ref, kind, local, 0, width)
                for kind, ref in enumerate((geg_o, geu_o, ged_o))
            ]
            for copy in chunk_stores(targets, local):
                copy.wait()

            def finish(here, local=local):
                in_s[local, here, :] = out_sum[local, here, :].astype(BF)
                do_s[local, here, :] = in_sum[local, here, :].astype(BF)

            tiles(slots, 256, finish)

    pl.run_scoped(
        routed,
        pltpu.VMEM((local_count, slots, features), F32),
        pltpu.VMEM((local_count, slots, features), F32),
    )
    ends = [
        pltpu.make_async_copy(in_s, outs_o, out_sem.at[0]),
        pltpu.make_async_copy(do_s, dins_o, out_sem.at[1]),
    ]
    for copy in ends:
        copy.start()
    for copy in ends:
        copy.wait()
    prompts.drain()
    for d in early + late:
        d.drain()
    experts.drain()
    for m in range(micro_count):
        for step in range(1, owners):
            exchange(send_do, do_s, ad_send, ad_recv, m, step).wait_send()
            exchange(send_in, in_s, ai_send, ai_recv, m, step).wait_send()


def rope_tables(prompt):
    positions = np.arange(prompt + CONT, dtype=np.float64)
    frequency = 10000.0 ** (-2.0 * np.arange(HD // 2) / HD)
    angles = positions[:, None] * frequency
    cosine, sine_part = np.cos(angles), np.sin(angles)
    return (
        np.concatenate([cosine] * 4, 1).astype(np.float32),
        np.concatenate([-sine_part, sine_part] * 2, 1).astype(np.float32),
    )


def run_forward(sizes, tokens, cot, gates, routes, dense, experts):
    depth, high_count = sizes
    micro_count, rows, features = tokens.shape
    owners = high_count * 2
    line = depth * owners
    prompt = depth * PB
    length = prompt + CONT
    local_count, _, width = experts[0].shape
    hidden_units = dense[3].shape[1] * line
    capacity = rows * 8 // (3 * owners * local_count)
    slots = micro_count * owners * capacity
    cosine, sine_part = rope_tables(prompt)
    hbm, vmem = pl.BlockSpec(memory_space=pltpu.HBM), pl.BlockSpec(memory_space=pltpu.VMEM)

    def shape(dtype, *dims):
        return jax.ShapeDtypeStruct(dims, dtype)

    token_rows = micro_count * rows
    wide, tall = (features, hidden_units), (hidden_units, features)
    out_shape = [
        shape(BF, dense[0].shape[0] * line, features),
        shape(BF, dense[1].shape[0] * line, features),
        shape(F32, 8, features),
        shape(BF, *wide), shape(BF, *wide), shape(BF, *tall),
        shape(BF, local_count, *wide), shape(BF, local_count, *wide), shape(BF, local_count, *tall),
        shape(BF, micro_count, length, features),
        shape(BF, micro_count, length, features),
        shape(BF, micro_count, length, features),
        shape(BF, micro_count, rows, features),
        shape(BF, micro_count, rows, features),
        shape(F32, micro_count, rows, features),
        shape(F32, micro_count, rows, 2 * HD),
        shape(F32, token_rows, features),
        shape(F32, token_rows, features),
        shape(BF, *wide), shape(BF, *wide), shape(BF, *tall),
        shape(BF, local_count, *wide), shape(BF, local_count, *wide), shape(BF, local_count, *tall),
        shape(BF, local_count, slots, features),
        shape(BF, local_count, slots, features),
    ]
    dma = pltpu.SemaphoreType.DMA
    buffers = max(2, local_count)
    send = pltpu.VMEM((owners - 1, micro_count, local_count, capacity, features), BF)
    scratch = [
        pltpu.VMEM((micro_count, length, features), BF),
        pltpu.VMEM(out_shape[0].shape, BF),
        pltpu.VMEM(out_shape[1].shape, BF),
        pltpu.VMEM((dense[2].shape[0] * line, features), BF),
        pltpu.VMEM((8, features), F32),
        pltpu.VMEM((token_rows, features), BF),
        pltpu.VMEM((token_rows, features), BF),
        pltpu.VMEM((local_count, slots, features), BF),
        pltpu.VMEM((local_count, slots, features), BF),
        send,
        send,
        pltpu.VMEM((buffers, features, width), BF),
        pltpu.VMEM((buffers, features, width), BF),
        pltpu.VMEM((buffers, width, features), BF),
        pltpu.VMEM((max(slots, token_rows), width), BF),
        pltpu.VMEM((max(slots, token_rows), width), BF),
        pltpu.VMEM((max(slots, token_rows), width), BF),
        pltpu.VMEM((buffers, features, width), BF),
        pltpu.VMEM((buffers, features, width), BF),
        pltpu.VMEM((buffers, width, features), BF),
    ]
    scratch += DenseGather.semaphores(len(dense), depth, high_count)
    scratch += ExpertGather.semaphores(depth, local_count)
    scratch += [
        dma((2, depth)),
        dma((depth,)),
        dma((10 + micro_count,)),
        dma((owners - 1, micro_count)),
        dma((owners - 1, micro_count)),
        dma((owners - 1, micro_count)),
        dma((owners - 1, micro_count)),
        dma((buffers, 3)),
        dma((buffers, 3)),
        dma((12,)),
    ]
    return pl.pallas_call(
        functools.partial(forward_kernel, sizes),
        out_shape=out_shape,
        in_specs=[hbm] * 2 + [vmem] * 4 + [hbm] * 9,
        out_specs=[hbm] * len(out_shape),
        scratch_shapes=scratch,
        compiler_params=pltpu.CompilerParams(
            collective_id=0, has_side_effects=True, vmem_limit_bytes=60 * MIB
        ),
        name="gather_and_forward",
    )(tokens, cot, gates, routes, cosine, sine_part, *dense, *experts)


class PlaceS:
    def __init__(self, sizes):
        self.depth, self.high_count = sizes
        self.x = lax.axis_index(DP)
        self.z = lax.axis_index(CONTEXT)
        self.e = lax.axis_index(EXPERTS)
        self.high = self.e // 2
        self.low = self.e % 2

    def shard(self, z):
        return self.x * self.depth + z

    def other_shard(self, z):
        return (1 - self.x) * self.depth + z

    def peer_high(self, step):
        return lax.rem(self.high + step, self.high_count)

    def greet(self, everyone=False):
        barrier = pltpu.get_barrier_semaphore()

        def signal(**device):
            pl.semaphore_signal(barrier, inc=1, device_id=device, device_id_type=MESH)

        signal(dp=1 - self.x)
        signal(experts=self.e + 1 - 2 * self.low)
        count = 2
        for step in range(1, self.high_count):
            signal(experts=self.peer_high(step) * 2 + self.low)
            count += 1
            if everyone:
                signal(experts=self.peer_high(step) * 2 + 1 - self.low)
                count += 1
        if everyone:
            for step in range(1, self.depth):
                signal(context=lax.rem(self.z + step, self.depth))
                count += 1
            pl.semaphore_wait(barrier, count)
        else:
            pl.when(self.z > 0)(lambda: signal(context=self.z - 1))
            pl.when(self.z < self.depth - 1)(lambda: signal(context=self.z + 1))
            count += jnp.where(self.z > 0, 1, 0) + jnp.where(self.z < self.depth - 1, 1, 0)
            pl.semaphore_wait(barrier, count)


def slab(ref, index, rows):
    return ref.at[pl.ds(pl.multiple_of(index * rows, 16), rows)]


def add_into(target, sources, rows):
    total = target.shape[0]

    def body(i, carry):
        here = pl.ds(pl.multiple_of(i * rows, rows), rows)
        value = target[here, :].astype(jnp.float32)
        for source in sources:
            value = value + source[here, :].astype(jnp.float32)
        target[here, :] = value.astype(target.dtype)
        return carry

    lax.fori_loop(0, total // rows, body, 0)


class ScatterAll:
    def __init__(self, place, dense, expert, dense_outs, expert_outs, gain, gain_out, buffers, sems):
        self.place = place
        self.dense, self.expert = dense, expert
        self.dense_outs, self.expert_outs = dense_outs, expert_outs
        self.gain, self.gain_out = gain, gain_out
        count = len(dense)
        self.count = count
        self.dlow = buffers[:count]
        self.dhigh = buffers[count : 2 * count]
        self.dline = buffers[2 * count : 3 * count]
        self.dcross = buffers[3 * count : 4 * count]
        rest = buffers[4 * count :]
        self.dense_own, self.ecross, self.eline, self.eown = rest[0], rest[1:4], rest[4:7], rest[7:10]
        self.gmine, self.glow, self.ghigh, self.gline, self.gcross = rest[10:15]
        (
            self.sl_send,
            self.sl_recv,
            self.sh_send,
            self.sh_recv,
            self.sz_send,
            self.sz_recv,
            self.sx_send,
            self.sx_recv,
            self.ez_send,
            self.ez_recv,
            self.ex_send,
            self.ex_recv,
            self.own_sem,
            self.eown_sem,
            self.out_sem,
            self.eout_sem,
            self.g_send,
            self.g_recv,
        ) = sems
        self.local_count = self.ecross[0].shape[1]
        self.pieces = [(a, e) for e in range(self.local_count) for a in range(3)]
        self.width = self.ecross[0].shape[3]

    @staticmethod
    def scratch(sizes, rows, features, local_count, width):
        depth, high_count = sizes
        bf = jnp.bfloat16
        buffers = [pltpu.VMEM((depth, high_count, r, features), bf) for r in rows]
        buffers += [pltpu.VMEM((high_count - 1, depth, r, features), bf) for r in rows]
        buffers += [pltpu.VMEM((depth + 1, r, features), bf) for r in rows]
        buffers += [pltpu.VMEM((r, features), bf) for r in rows]
        buffers += [pltpu.VMEM((depth, high_count, max(rows), features), bf)]
        for lead in (depth, depth + 1, None):
            for a in range(3):
                shape = (local_count,) + ((features, width) if a < 2 else (width, features))
                buffers.append(pltpu.VMEM(shape if lead is None else (lead,) + shape, bf))
        gain = (8, features)
        buffers += [
            pltpu.VMEM(gain, jnp.float32),
            pltpu.VMEM(gain, jnp.float32),
            pltpu.VMEM((high_count - 1,) + gain, jnp.float32),
            pltpu.VMEM((depth - 1,) + gain, jnp.float32),
            pltpu.VMEM(gain, jnp.float32),
        ]
        dma = pltpu.SemaphoreType.DMA
        count, pieces = len(rows), 3 * local_count
        sems = [
            dma((count,)),
            dma((count,)),
            dma((count, high_count)),
            dma((count, high_count)),
            dma((count, depth)),
            dma((count, depth + 1)),
            dma((count,)),
            dma((count,)),
            dma((pieces, depth)),
            dma((pieces, depth + 1)),
            dma((pieces, depth)),
            dma((pieces, depth)),
            dma((1,)),
            dma((pieces,)),
            dma((count,)),
            dma((pieces,)),
            dma((3 + depth + high_count,)),
            dma((3 + depth + high_count,)),
        ]
        return buffers, sems

    def _x_copy(self, p, z):
        a, local = self.pieces[p]
        return remote(
            expert_slab(self.expert[a], a, local, self.place.other_shard(z), self.width),
            self.ecross[a].at[z, local],
            self.ex_send.at[p, z],
            self.ex_recv.at[p, z],
            dp=1 - self.place.x,
        )

    def _order(self, do):
        place = self.place
        for step in range(place.depth - 1, 0, -1):
            for direction in (1, -1):
                z = place.z + direction * step
                pl.when((z >= 0) & (z < place.depth))(
                    lambda z=z, d=direction, s=step: do(z, d, s)
                )
        do(place.z, 0, 0)

    def expert_start(self):
        def start(z, direction, step):
            for p in range(len(self.pieces)):
                self._x_copy(p, z).start()

        self._order(start)

    def _own_load(self, p, z):
        a, local = self.pieces[p]
        return pltpu.make_async_copy(
            expert_slab(self.expert[a], a, local, self.place.shard(z), self.width),
            self.eown[a].at[local],
            self.eown_sem.at[p],
        )

    def _line_copy(self, p, z, direction):
        a, local = self.pieces[p]
        place = self.place
        if direction > 0:
            slot = z
        else:
            slot = jnp.where(z == place.z - 1, place.depth, z)
        return remote(
            self.ecross[a].at[z, local],
            self.eline[a].at[slot, local],
            self.ez_send.at[p, z],
            self.ez_recv.at[p, slot],
            context=place.z + direction,
        )

    def _line_wait(self, p, slot):
        a, local = self.pieces[p]
        here = self.eline[a].at[slot, local]
        remote(here, here, self.ez_send.at[p, 0], self.ez_recv.at[p, slot], context=0).wait_recv()

    def expert_loads(self, z):
        for p in range(len(self.pieces)):
            self._own_load(p, z).start()

    def expert_piece(self, p, z, direction):
        a, local = self.pieces[p]
        place = self.place
        rows = 64
        self._x_copy(p, z).wait_recv()
        self._own_load(p, z).wait()
        target, own = self.ecross[a].at[z, local], self.eown[a].at[local]
        if direction:
            upstream = place.z > 0 if direction > 0 else place.z < place.depth - 1

            def with_line():
                self._line_wait(p, z)
                add_into(target, [own, self.eline[a].at[z, local]], rows)

            pl.when(upstream)(with_line)
            pl.when(jnp.logical_not(upstream))(lambda: add_into(target, [own], rows))
            self._line_copy(p, z, direction).start()
        else:
            left, right = place.z > 0, place.z < place.depth - 1

            def both():
                self._line_wait(p, z)
                self._line_wait(p, place.depth)
                add_into(
                    target, [own, self.eline[a].at[z, local], self.eline[a].at[place.depth, local]], rows
                )

            def one(slot):
                self._line_wait(p, slot)
                add_into(target, [own, self.eline[a].at[slot, local]], rows)

            pl.when(left & right)(both)
            pl.when(left & jnp.logical_not(right))(lambda: one(z))
            pl.when(jnp.logical_not(left) & right)(lambda: one(place.depth))
            pltpu.make_async_copy(
                target, self.expert_outs[a].at[local], self.eout_sem.at[p]
            ).start()

    def expert_all(self):
        def run(z, direction, step):
            self.expert_loads(z)
            for p in range(len(self.pieces)):
                self.expert_piece(p, z, direction)

        self._order(run)

    def expert_drain(self):
        def drain(z, direction, step):
            for p, (a, local) in enumerate(self.pieces):
                self._x_copy(p, z).wait_send()
                if direction:
                    self._line_copy(p, z, direction).wait_send()
                else:
                    pltpu.make_async_copy(
                        self.ecross[a].at[z, local], self.expert_outs[a].at[local], self.eout_sem.at[p]
                    ).wait()

        self._order(drain)

    def _low_copy(self, a):
        place = self.place
        return remote(
            self.dense[a].at[:, :, 1 - place.low],
            self.dlow[a],
            self.sl_send.at[a],
            self.sl_recv.at[a],
            experts=place.e + 1 - 2 * place.low,
        )

    def dense_start(self, a):
        self._low_copy(a).start()

    def _high_copy(self, a, step):
        place = self.place
        peer = place.peer_high(step)
        return remote(
            self.dlow[a].at[:, peer],
            self.dhigh[a].at[step - 1],
            self.sh_send.at[a, step],
            self.sh_recv.at[a, step],
            experts=peer * 2 + place.low,
        )

    def dense_low(self, a):
        place = self.place
        rows = self.dlow[a].shape[2]
        own = self.dense_own.at[:, :, pl.ds(0, rows)]
        copy = pltpu.make_async_copy(self.dense[a].at[:, :, place.low], own, self.own_sem.at[0])
        copy.start()
        self._low_copy(a).wait_recv()
        copy.wait()
        for z in range(place.depth):
            for high in range(place.high_count):
                add_into(self.dlow[a].at[z, high], [self.dense_own.at[z, high, pl.ds(0, rows)]], 16)
        for step in range(1, place.high_count):
            self._high_copy(a, step).start()

    def dense_high(self, a):
        place = self.place
        for step in range(1, place.high_count):
            self._high_copy(a, step).wait_recv()
        for z in range(place.depth):
            add_into(
                self.dlow[a].at[z, place.high],
                [self.dhigh[a].at[step - 1, z] for step in range(1, place.high_count)],
                16,
            )

    def _dline_copy(self, a, z, direction):
        place = self.place
        if direction > 0:
            slot = z
        else:
            slot = jnp.where(z == place.z - 1, place.depth, z)
        return remote(
            self.dlow[a].at[z, place.high],
            self.dline[a].at[slot],
            self.sz_send.at[a, z],
            self.sz_recv.at[a, slot],
            context=place.z + direction,
        )

    def _dline_wait(self, a, slot):
        here = self.dline[a].at[slot]
        remote(here, here, self.sz_send.at[a, 0], self.sz_recv.at[a, slot], context=0).wait_recv()

    def _dcross_copy(self, a):
        place = self.place
        return remote(
            self.dlow[a].at[place.z, place.high],
            self.dcross[a],
            self.sx_send.at[a],
            self.sx_recv.at[a],
            dp=1 - place.x,
        )

    def dense_line(self, which):
        place = self.place

        def run(z, direction, step):
            for a in which:
                target = self.dlow[a].at[z, place.high]
                if direction:
                    upstream = place.z > 0 if direction > 0 else place.z < place.depth - 1

                    def with_line(a=a, target=target):
                        self._dline_wait(a, z)
                        add_into(target, [self.dline[a].at[z]], 16)

                    pl.when(upstream)(with_line)
                    self._dline_copy(a, z, direction).start()
                else:

                    def one(slot, a=a, target=target):
                        self._dline_wait(a, slot)
                        add_into(target, [self.dline[a].at[slot]], 16)

                    pl.when(place.z > 0)(lambda one=one: one(place.z))
                    pl.when(place.z < place.depth - 1)(lambda one=one: one(place.depth))
                    self._dcross_copy(a).start()

        self._order(run)

    def dense_finish(self, a):
        place = self.place
        cross = self._dcross_copy(a)
        cross.wait_recv()
        add_into(self.dcross[a], [self.dlow[a].at[place.z, place.high]], 16)
        pltpu.make_async_copy(self.dcross[a], self.dense_outs[a], self.out_sem.at[a]).start()

    def dense_drain(self, a):
        place = self.place
        self._low_copy(a).wait_send()
        for step in range(1, place.high_count):
            self._high_copy(a, step).wait_send()

        def drain(z, direction, step):
            if direction:
                self._dline_copy(a, z, direction).wait_send()

        self._order(drain)
        self._dcross_copy(a).wait_send()
        pltpu.make_async_copy(self.dcross[a], self.dense_outs[a], self.out_sem.at[a]).wait()

    def gains_all(self):
        place = self.place
        depth, high_count = place.depth, place.high_count

        def stage(first, targets, slots):
            copies = [
                remote(self.gmine, slot, self.g_send.at[first + i], self.g_recv.at[first + i], **target)
                for i, (target, slot) in enumerate(zip(targets, slots))
            ]
            for copy in copies:
                copy.start()
            for copy in copies:
                copy.wait()
            self.gmine[...] = sum((slot[...] for slot in slots), self.gmine[...])

        stage(0, [dict(experts=place.e + 1 - 2 * place.low)], [self.glow])
        stage(
            1,
            [dict(experts=place.peer_high(s) * 2 + place.low) for s in range(1, high_count)],
            [self.ghigh.at[s - 1] for s in range(1, high_count)],
        )
        stage(
            high_count,
            [dict(context=lax.rem(place.z + s, depth)) for s in range(1, depth)],
            [self.gline.at[s - 1] for s in range(1, depth)],
        )
        stage(high_count + depth - 1, [dict(dp=1 - place.x)], [self.gcross])
        self.gain_out[...] = self.gmine[...]


def scatter_kernel(sizes, count, *refs):
    place = PlaceS(sizes)
    dense, refs = refs[:count], refs[count:]
    expert, refs = refs[:3], refs[3:]
    gain, refs = refs[0], refs[1:]
    dense_outs, refs = refs[:count], refs[count:]
    expert_outs, refs = refs[:3], refs[3:]
    gain_out, refs = refs[0], refs[1:]
    buffers, sems = refs[: 4 * count + 15], refs[4 * count + 15 :]
    work = ScatterAll(
        place, dense, expert, dense_outs, expert_outs, gain, gain_out, buffers, sems
    )
    place.greet(everyone=True)
    for a in range(count):
        work.dense_start(a)
    work.expert_start()
    work.gmine[...] = gain[...]
    for a in range(count):
        work.dense_low(a)
    for a in range(count):
        work.dense_high(a)
    work.dense_line(list(range(count)))
    work.expert_all()
    work.gains_all()
    for a in range(count):
        work.dense_finish(a)
    for a in range(count):
        work.dense_drain(a)
    work.expert_drain()


def scatter_gradients(sizes, dense, experts, gain):
    depth, high_count = sizes
    hbm = pl.BlockSpec(memory_space=pltpu.HBM)
    vmem = pl.BlockSpec(memory_space=pltpu.VMEM)
    count = len(dense)
    rows = [a.shape[3] for a in dense]
    features = gain.shape[1]
    local_count = experts[0].shape[0]
    width = experts[2].shape[1] // (2 * depth)
    shapes = [jax.ShapeDtypeStruct(a.shape[3:], a.dtype) for a in dense]
    shapes += [
        jax.ShapeDtypeStruct(
            (local_count,) + ((features, width) if a < 2 else (width, features)), experts[a].dtype
        )
        for a in range(3)
    ]
    shapes += [jax.ShapeDtypeStruct(gain.shape, gain.dtype)]
    buffers, sems = ScatterAll.scratch(sizes, rows, features, local_count, width)
    outs = pl.pallas_call(
        functools.partial(scatter_kernel, sizes, count),
        out_shape=shapes,
        in_specs=[hbm] * (count + 3) + [vmem],
        out_specs=[hbm] * (count + 3) + [vmem],
        scratch_shapes=buffers + sems,
        compiler_params=pltpu.CompilerParams(
            collective_id=1, has_side_effects=True, vmem_limit_bytes=60 * MIB
        ),
        name="scatter_gradients",
    )(*dense, *experts, gain)
    return outs[:count], outs[count : count + 3], outs[count + 3]


def on_device_plain(
    tokens,
    cotangent,
    gates,
    routes,
    qkv_weight,
    out_weight,
    shared_gate,
    shared_up,
    shared_down,
    gains,
    expert_gate,
    expert_up,
    expert_down,
):
    micro_count = tokens.shape[2]
    row_count = tokens.shape[4]
    feature_count = tokens.shape[5]
    owners = lax.axis_size(EXPERTS)
    local_experts = expert_gate.shape[0]
    total_experts = owners * local_experts
    capacity = row_count * 8 // (3 * total_experts)
    blocks = lax.axis_size(CONTEXT)
    prompt = blocks * PB
    scaling = HD ** (-0.5)
    w_qkv, w_out, w_sgate, w_sup, w_sdown, w_gains = (
        lax.all_gather(qkv_weight, (CONTEXT, EXPERTS), axis=1, tiled=True),
        lax.all_gather(out_weight, (CONTEXT, EXPERTS), axis=0, tiled=True),
        lax.all_gather(shared_gate, (CONTEXT, EXPERTS), axis=1, tiled=True),
        lax.all_gather(shared_up, (CONTEXT, EXPERTS), axis=1, tiled=True),
        lax.all_gather(shared_down, (CONTEXT, EXPERTS), axis=0, tiled=True),
        lax.all_gather(gains, (CONTEXT, EXPERTS), axis=1, tiled=True),
    )
    e_gate, expert_up_weight, e_down = (
        lax.all_gather(expert_gate, (DP, CONTEXT), axis=2, tiled=True),
        lax.all_gather(expert_up, (DP, CONTEXT), axis=2, tiled=True),
        lax.all_gather(expert_down, (DP, CONTEXT), axis=1, tiled=True),
    )
    gain_one = w_gains[0].astype(jnp.float32)
    gain_two = w_gains[1].astype(jnp.float32)
    here_index = lax.axis_index(CONTEXT)
    row_ids = jnp.arange(row_count, dtype=jnp.int32)
    query_pos = jnp.where(row_ids < PB, here_index * PB + row_ids, prompt + row_ids - PB)
    key_pos = jnp.arange(prompt + CONT, dtype=jnp.int32)
    allowed = key_pos[None, None, :] <= query_pos[None, :, None]
    half_size = HD // 2
    frequency = 10000.0 ** (-2.0 * jnp.arange(half_size, dtype=jnp.float32) / HD)
    angles = query_pos.astype(jnp.float32)[:, None] * frequency
    cosine = jnp.cos(angles)[:, None, :]
    sine_part = jnp.sin(angles)[:, None, :]
    kept_list = []
    mixed_list = []
    for step_index in range(micro_count):
        inputs = tokens[0, 0, step_index, 0].astype(jnp.float32)
        root_one = lax.rsqrt(jnp.mean(inputs * inputs, -1, keepdims=True) + EPSILON)
        normed_one = (inputs * root_one * gain_one).astype(jnp.bfloat16)
        projected = mdot(normed_one, w_qkv)
        query = rotate(projected[:, :feature_count], cosine, sine_part).astype(jnp.bfloat16)
        key_rows = rotate(
            projected[:, feature_count : 2 * feature_count], cosine, sine_part
        ).astype(jnp.bfloat16)
        value_rows = projected[:, 2 * feature_count :].astype(jnp.bfloat16)
        prompt_key, prompt_value = (
            lax.all_gather(key_rows[:PB], CONTEXT, axis=0, tiled=True),
            lax.all_gather(value_rows[:PB], CONTEXT, axis=0, tiled=True),
        )
        key_heads = jnp.concatenate([prompt_key, key_rows[PB:]], 0).reshape(prompt + CONT, H, HD)
        value_heads = jnp.concatenate([prompt_value, value_rows[PB:]], 0).reshape(
            prompt + CONT, H, HD
        )
        query_heads = query.reshape(row_count, H, HD)
        scores = (
            jnp.einsum("qhd,khd->hqk", query_heads, key_heads, preferred_element_type=jnp.float32)
            * scaling
        )
        scores = jnp.where(allowed, scores, -1000000000.0)
        highest = jnp.max(scores, -1, keepdims=True)
        weights = jnp.exp(scores - highest)
        total = jnp.sum(weights, -1, keepdims=True)
        log_total = highest + jnp.log(total)
        probs = (weights / total).astype(jnp.bfloat16)
        attended = (
            jnp.einsum("hqk,khd->qhd", probs, value_heads, preferred_element_type=jnp.float32)
            .reshape(row_count, feature_count)
            .astype(jnp.bfloat16)
        )
        hidden = inputs + mdot(attended, w_out)
        root_two = lax.rsqrt(jnp.mean(hidden * hidden, -1, keepdims=True) + EPSILON)
        normed_two = (hidden * root_two * gain_two).astype(jnp.bfloat16)
        side_gate = mdot(normed_two, w_sgate)
        side_up = mdot(normed_two, w_sup)
        side_act = (jax.nn.silu(side_gate) * side_up).astype(jnp.bfloat16)
        side = mdot(side_act, w_sdown)
        route_rows = routes[0, 0, step_index, 0]
        slots = slot_table(route_rows, total_experts)
        flat_dest = (route_rows * capacity + slots).reshape(-1)
        source = (
            jnp.full((total_experts * capacity,), 2 * row_count, jnp.int32)
            .at[flat_dest]
            .set(jnp.arange(2 * row_count, dtype=jnp.int32))
        )
        padded = jnp.concatenate([normed_two, jnp.zeros((1, feature_count), jnp.bfloat16)], 0)
        send = padded[source // 2].reshape(total_experts, capacity, feature_count)
        received = lax.all_to_all(send, EXPERTS, split_axis=0, concat_axis=0, tiled=True)
        count = received.shape[1]
        expert_grouped = received.reshape(owners, local_experts, count, feature_count)
        expert_gate_act = jnp.einsum(
            "send,edf->senf", expert_grouped, e_gate, preferred_element_type=jnp.float32
        )
        expert_up_act = jnp.einsum(
            "send,edf->senf", expert_grouped, expert_up_weight, preferred_element_type=jnp.float32
        )
        expert_hidden_act = (jax.nn.silu(expert_gate_act) * expert_up_act).astype(jnp.bfloat16)
        result = jnp.einsum(
            "senf,efd->send", expert_hidden_act, e_down, preferred_element_type=jnp.float32
        ).astype(jnp.bfloat16)
        expert_out = result.reshape(owners * local_experts, count, feature_count)
        expert_in = received
        returned = lax.all_to_all(
            expert_out, EXPERTS, split_axis=0, concat_axis=0, tiled=True
        ).reshape(-1, feature_count)
        gate_rows = gates[0, 0, step_index, 0]
        picked = returned[flat_dest].reshape(row_count, 2, feature_count).astype(jnp.float32)
        routed = jnp.sum(gate_rows[:, :, None] * picked, 1)
        mixed_list.append((hidden + routed + side).astype(jnp.bfloat16))
        cached = (prompt_key, prompt_value)
        kept_list.append(
            (
                inputs,
                root_one,
                normed_one,
                query,
                key_rows,
                value_rows,
                cached,
                log_total,
                attended,
                hidden,
                root_two,
                normed_two,
                side_gate,
                side_up,
                side_act,
                flat_dest,
                source,
                expert_in,
                gate_rows,
            )
        )
    acc_qkv = jnp.zeros(w_qkv.shape, jnp.float32)
    acc_out = jnp.zeros(w_out.shape, jnp.float32)
    acc_sgate = jnp.zeros(w_sgate.shape, jnp.float32)
    acc_sup = jnp.zeros(w_sup.shape, jnp.float32)
    acc_sdown = jnp.zeros(w_sdown.shape, jnp.float32)
    acc_gain_one = jnp.zeros((feature_count,), jnp.float32)
    acc_gain_two = jnp.zeros((feature_count,), jnp.float32)
    local_egate = jnp.zeros(e_gate.shape, jnp.float32)
    local_expert_up_weight = jnp.zeros(expert_up_weight.shape, jnp.float32)
    local_edown = jnp.zeros(e_down.shape, jnp.float32)
    input_list = []
    for step_index in range(micro_count):
        (
            inputs,
            root_one,
            normed_one,
            query,
            key_rows,
            value_rows,
            cached,
            log_total,
            attended,
            hidden,
            root_two,
            normed_two,
            side_gate,
            side_up,
            side_act,
            flat_dest,
            source,
            expert_in,
            gate_rows,
        ) = kept_list[step_index]
        grad_rows = cotangent[0, 0, step_index, 0].astype(jnp.float32)
        grad_low = grad_rows.astype(jnp.bfloat16)
        acc_sdown = acc_sdown + tdot(side_act, grad_low)
        d_side_act = ndot(grad_low, w_sdown).astype(jnp.bfloat16).astype(jnp.float32)
        silu_side, slope_side = silu_parts(side_gate)
        d_side_gate = (d_side_act * side_up * slope_side).astype(jnp.bfloat16)
        d_side_up = (d_side_act * silu_side).astype(jnp.bfloat16)
        acc_sgate = acc_sgate + tdot(normed_two, d_side_gate)
        acc_sup = acc_sup + tdot(normed_two, d_side_up)
        d_normed_two = ndot(d_side_gate, w_sgate) + ndot(d_side_up, w_sup)
        d_pairs = (
            (gate_rows[:, :, None] * grad_rows[:, None, :])
            .astype(jnp.bfloat16)
            .reshape(2 * row_count, feature_count)
        )
        padded_grad = jnp.concatenate([d_pairs, jnp.zeros((1, feature_count), jnp.bfloat16)], 0)
        grad_send = padded_grad[source].reshape(total_experts, capacity, feature_count)
        grad_in = lax.all_to_all(grad_send, EXPERTS, split_axis=0, concat_axis=0, tiled=True)
        grouped_grad = grad_in.reshape(owners, local_experts, capacity, feature_count)
        grouped = expert_in.reshape(owners, local_experts, capacity, feature_count)
        gate_act = jnp.einsum("send,edf->senf", grouped, e_gate, preferred_element_type=jnp.float32)
        up_act = jnp.einsum(
            "send,edf->senf", grouped, expert_up_weight, preferred_element_type=jnp.float32
        )
        silu_gate, slope_gate = silu_parts(gate_act)
        hidden_act = (silu_gate * up_act).astype(jnp.bfloat16)
        d_hidden_act = (
            jnp.einsum("send,efd->senf", grouped_grad, e_down, preferred_element_type=jnp.float32)
            .astype(jnp.bfloat16)
            .astype(jnp.float32)
        )
        d_gate_act = (d_hidden_act * up_act * slope_gate).astype(jnp.bfloat16)
        d_up_act = (d_hidden_act * silu_gate).astype(jnp.bfloat16)
        step_edown = jnp.einsum(
            "senf,send->efd", hidden_act, grouped_grad, preferred_element_type=jnp.float32
        )
        step_egate = jnp.einsum(
            "send,senf->edf", grouped, d_gate_act, preferred_element_type=jnp.float32
        )
        stepwise_expert_up = jnp.einsum(
            "send,senf->edf", grouped, d_up_act, preferred_element_type=jnp.float32
        )
        local_egate = local_egate + step_egate
        local_expert_up_weight = local_expert_up_weight + stepwise_expert_up
        local_edown = local_edown + step_edown
        d_expert_in = jnp.einsum(
            "senf,edf->send", d_gate_act, e_gate, preferred_element_type=jnp.float32
        ) + jnp.einsum(
            "senf,edf->send", d_up_act, expert_up_weight, preferred_element_type=jnp.float32
        )
        d_expert_in = d_expert_in.astype(jnp.bfloat16).reshape(
            total_experts, capacity, feature_count
        )
        back = lax.all_to_all(
            d_expert_in, EXPERTS, split_axis=0, concat_axis=0, tiled=True
        ).reshape(-1, feature_count)
        d_normed_two = d_normed_two + jnp.sum(
            back[flat_dest].reshape(row_count, 2, feature_count).astype(jnp.float32), 1
        )
        scaled_two = gain_two * d_normed_two
        d_hidden = (
            grad_rows
            + root_two * scaled_two
            - hidden * root_two**3 * jnp.mean(hidden * scaled_two, -1, keepdims=True)
        )
        acc_gain_two = acc_gain_two + jnp.sum(d_normed_two * hidden * root_two, 0)
        d_attn = d_hidden.astype(jnp.bfloat16)
        acc_out = acc_out + tdot(attended, d_attn)
        d_attended = ndot(d_attn, w_out).astype(jnp.bfloat16)
        prompt_key, prompt_value = cached
        key_heads = jnp.concatenate([prompt_key, key_rows[PB:]], 0).reshape(prompt + CONT, H, HD)
        value_heads = jnp.concatenate([prompt_value, value_rows[PB:]], 0).reshape(
            prompt + CONT, H, HD
        )
        query_heads = query.reshape(row_count, H, HD)
        scores = (
            jnp.einsum("qhd,khd->hqk", query_heads, key_heads, preferred_element_type=jnp.float32)
            * scaling
        )
        scores = jnp.where(allowed, scores, -1000000000.0)
        probs = jnp.exp(scores - log_total)
        d_heads = d_attended.reshape(row_count, H, HD)
        d_probs = jnp.einsum(
            "qhd,khd->hqk", d_heads, value_heads, preferred_element_type=jnp.float32
        )
        centre = jnp.sum(probs * d_probs, -1, keepdims=True)
        d_scores = (probs * (d_probs - centre)).astype(jnp.bfloat16)
        d_query = (
            jnp.einsum(
                "hqk,khd->qhd", d_scores, key_heads, preferred_element_type=jnp.float32
            ).reshape(row_count, feature_count)
            * scaling
        )
        d_keys = (
            jnp.einsum(
                "hqk,qhd->khd", d_scores, query_heads, preferred_element_type=jnp.float32
            ).reshape(prompt + CONT, feature_count)
            * scaling
        )
        d_values = jnp.einsum(
            "hqk,qhd->khd", probs.astype(jnp.bfloat16), d_heads, preferred_element_type=jnp.float32
        ).reshape(prompt + CONT, feature_count)
        own_dkey, own_dvalue = (
            lax.psum_scatter(
                d_keys[:prompt].astype(jnp.bfloat16), CONTEXT, scatter_dimension=0, tiled=True
            ).astype(jnp.float32),
            lax.psum_scatter(
                d_values[:prompt].astype(jnp.bfloat16), CONTEXT, scatter_dimension=0, tiled=True
            ).astype(jnp.float32),
        )
        d_key_rows = jnp.concatenate([own_dkey, d_keys[prompt:]], 0)
        d_value_rows = jnp.concatenate([own_dvalue, d_values[prompt:]], 0)
        d_projected = jnp.concatenate(
            [
                rotate(d_query, cosine, -sine_part).astype(jnp.bfloat16),
                rotate(d_key_rows, cosine, -sine_part).astype(jnp.bfloat16),
                d_value_rows.astype(jnp.bfloat16),
            ],
            1,
        )
        acc_qkv = acc_qkv + tdot(normed_one, d_projected)
        d_normed_one = ndot(d_projected, w_qkv)
        scaled_one = gain_one * d_normed_one
        d_inputs = (
            d_hidden
            + root_one * scaled_one
            - inputs * root_one**3 * jnp.mean(inputs * scaled_one, -1, keepdims=True)
        )
        acc_gain_one = acc_gain_one + jnp.sum(d_normed_one * inputs * root_one, 0)
        input_list.append(d_inputs.astype(jnp.bfloat16))
    sharded_expert_gate, sharded_expert_up, sharded_expert_down = (
        lax.psum_scatter(
            local_egate.astype(jnp.bfloat16), (DP, CONTEXT), scatter_dimension=2, tiled=True
        ).astype(jnp.float32),
        lax.psum_scatter(
            local_expert_up_weight.astype(jnp.bfloat16),
            (DP, CONTEXT),
            scatter_dimension=2,
            tiled=True,
        ).astype(jnp.float32),
        lax.psum_scatter(
            local_edown.astype(jnp.bfloat16), (DP, CONTEXT), scatter_dimension=1, tiled=True
        ).astype(jnp.float32),
    )
    acc_gains = jnp.stack([acc_gain_one, acc_gain_two], 0)
    dense_shards = (
        lax.psum_scatter(acc_qkv, (CONTEXT, EXPERTS), scatter_dimension=1, tiled=True),
        lax.psum_scatter(acc_out, (CONTEXT, EXPERTS), scatter_dimension=0, tiled=True),
        lax.psum_scatter(acc_sgate, (CONTEXT, EXPERTS), scatter_dimension=1, tiled=True),
        lax.psum_scatter(acc_sup, (CONTEXT, EXPERTS), scatter_dimension=1, tiled=True),
        lax.psum_scatter(acc_sdown, (CONTEXT, EXPERTS), scatter_dimension=0, tiled=True),
        lax.psum_scatter(acc_gains, (CONTEXT, EXPERTS), scatter_dimension=1, tiled=True),
    )
    grad_qkv, grad_out, grad_sgate, grad_sup, grad_sdown, grad_gains = (
        lax.psum(dense_shards[0].astype(jnp.bfloat16), DP).astype(jnp.float32),
        lax.psum(dense_shards[1].astype(jnp.bfloat16), DP).astype(jnp.float32),
        lax.psum(dense_shards[2].astype(jnp.bfloat16), DP).astype(jnp.float32),
        lax.psum(dense_shards[3].astype(jnp.bfloat16), DP).astype(jnp.float32),
        lax.psum(dense_shards[4].astype(jnp.bfloat16), DP).astype(jnp.float32),
        lax.psum(dense_shards[5].astype(jnp.bfloat16), DP).astype(jnp.float32),
    )
    mixed = jnp.stack(mixed_list, 0).reshape(tokens.shape)
    input_grad = jnp.stack(input_list, 0).reshape(tokens.shape)
    return (
        mixed,
        input_grad,
        grad_qkv,
        grad_out,
        grad_sgate,
        grad_sup,
        grad_sdown,
        grad_gains,
        sharded_expert_gate,
        sharded_expert_up,
        sharded_expert_down,
    )


def on_device(
    tokens,
    cotangent,
    gates,
    routes,
    qkv_weight,
    out_weight,
    shared_gate,
    shared_up,
    shared_down,
    gains,
    expert_gate,
    expert_up,
    expert_down,
):
    micro_count = tokens.shape[2]
    row_count = tokens.shape[4]
    feature_count = tokens.shape[5]
    owners = lax.axis_size(EXPERTS)
    local_experts = expert_gate.shape[0]
    total_experts = owners * local_experts
    capacity = row_count * 8 // (3 * total_experts)
    blocks = lax.axis_size(CONTEXT)
    prompt = blocks * PB
    scaling = HD ** (-0.5)
    sizes = (blocks, owners // 2)
    own_at = lax.axis_index(CONTEXT) * owners + lax.axis_index(EXPERTS)
    gain_width = gains.shape[1]
    gain_rows = lax.dynamic_update_slice(
        jnp.zeros((16, feature_count), jnp.bfloat16), gains, (0, own_at * gain_width)
    )
    (
        w_qkv, w_out, w_gains, _, _, _, _, _, _,
        n1_all, k_all, v_all, q_all, att_all, hid_all, lse_all, side_all, dn2_all,
        gsg, gsu, gsd, geg, geu, ged, outs, dins,
    ) = run_forward(
        sizes,
        tokens[0, 0, :, 0],
        cotangent[0, 0, :, 0],
        gates[0, 0, :, 0].transpose(0, 2, 1),
        routes[0, 0, :, 0].transpose(0, 2, 1),
        (qkv_weight.T, out_weight, gain_rows, shared_gate, shared_up, shared_down),
        (expert_gate, expert_up, expert_down),
    )
    gain_one, gain_two = w_gains[0], w_gains[1]
    here_index = lax.axis_index(CONTEXT)
    row_ids = jnp.arange(row_count, dtype=jnp.int32)
    query_pos = jnp.where(row_ids < PB, here_index * PB + row_ids, prompt + row_ids - PB)
    key_pos = jnp.arange(prompt + CONT, dtype=jnp.int32)
    allowed = key_pos[None, None, :] <= query_pos[None, :, None]
    half_size = HD // 2
    frequency = 10000.0 ** (-2.0 * jnp.arange(half_size, dtype=jnp.float32) / HD)
    angles = query_pos.astype(jnp.float32)[:, None] * frequency
    cosine = jnp.cos(angles)[:, None, :]
    sine_part = jnp.sin(angles)[:, None, :]
    acc_qkv = jnp.zeros(w_qkv.shape, jnp.float32)
    acc_out = jnp.zeros(w_out.shape, jnp.float32)
    acc_gain_one = jnp.zeros((feature_count,), jnp.float32)
    acc_gain_two = jnp.zeros((feature_count,), jnp.float32)
    mixed_list = []
    input_list = []
    for step_index in range(micro_count):
        inputs = tokens[0, 0, step_index, 0].astype(jnp.float32)
        root_one = lax.rsqrt(jnp.mean(inputs * inputs, -1, keepdims=True) + EPSILON)
        hidden = hid_all[step_index]
        root_two = lax.rsqrt(jnp.mean(hidden * hidden, -1, keepdims=True) + EPSILON)
        grad_rows = cotangent[0, 0, step_index, 0].astype(jnp.float32)
        rows_here = slice(step_index * row_count, (step_index + 1) * row_count)
        side, d_normed_two = side_all[rows_here], dn2_all[rows_here]
        route_rows = routes[0, 0, step_index, 0]
        slots = slot_table(route_rows, total_experts)
        flat_dest = (route_rows * capacity + slots).reshape(-1)
        gate_rows = gates[0, 0, step_index, 0]

        def come_back(item):
            item = item.reshape(local_experts, micro_count, owners, capacity, feature_count)
            item = item[:, step_index].transpose(1, 0, 2, 3)
            item = item.reshape(total_experts, capacity, feature_count)
            return lax.all_to_all(item, EXPERTS, split_axis=0, concat_axis=0, tiled=True).reshape(-1, feature_count)

        returned, back = come_back(outs), come_back(dins)
        picked = returned[flat_dest].reshape(row_count, 2, feature_count).astype(jnp.float32)
        routed = jnp.sum(gate_rows[:, :, None] * picked, 1)
        mixed_list.append((hidden + routed + side).astype(jnp.bfloat16))
        d_normed_two = d_normed_two + jnp.sum(
            back[flat_dest].reshape(row_count, 2, feature_count).astype(jnp.float32), 1
        )
        query, key_rows, value_rows = q_all[step_index], k_all[step_index], v_all[step_index]
        attended = att_all[step_index]
        log_total = lse_all[step_index][:, :H].T[:, :, None]
        normed_one = jnp.concatenate(
            [
                lax.dynamic_slice(n1_all[step_index], (here_index * PB, 0), (PB, feature_count)),
                n1_all[step_index][prompt:],
            ],
            0,
        )
        scaled_two = gain_two * d_normed_two
        d_hidden = (
            grad_rows
            + root_two * scaled_two
            - hidden * root_two**3 * jnp.mean(hidden * scaled_two, -1, keepdims=True)
        )
        acc_gain_two = acc_gain_two + jnp.sum(d_normed_two * hidden * root_two, 0)
        d_attn = d_hidden.astype(jnp.bfloat16)
        acc_out = acc_out + tdot(attended, d_attn)
        d_attended = ndot(d_attn, w_out).astype(jnp.bfloat16)
        key_heads = key_rows.reshape(prompt + CONT, H, HD)
        value_heads = value_rows.reshape(prompt + CONT, H, HD)
        query_heads = query.reshape(row_count, H, HD)
        scores = (
            jnp.einsum("qhd,khd->hqk", query_heads, key_heads, preferred_element_type=jnp.float32)
        )
        scores = jnp.where(allowed, scores, -1000000000.0)
        probs = jnp.exp(scores - log_total)
        d_heads = d_attended.reshape(row_count, H, HD)
        d_probs = jnp.einsum(
            "qhd,khd->hqk", d_heads, value_heads, preferred_element_type=jnp.float32
        )
        centre = jnp.sum(probs * d_probs, -1, keepdims=True)
        d_scores = (probs * (d_probs - centre)).astype(jnp.bfloat16)
        d_query = (
            jnp.einsum(
                "hqk,khd->qhd", d_scores, key_heads, preferred_element_type=jnp.float32
            ).reshape(row_count, feature_count)
            * scaling
        )
        d_keys = (
            jnp.einsum(
                "hqk,qhd->khd", d_scores, query_heads, preferred_element_type=jnp.float32
            ).reshape(prompt + CONT, feature_count)
        )
        d_values = jnp.einsum(
            "hqk,qhd->khd", probs.astype(jnp.bfloat16), d_heads, preferred_element_type=jnp.float32
        ).reshape(prompt + CONT, feature_count)
        own_dkey, own_dvalue = (
            lax.psum_scatter(
                d_keys[:prompt].astype(jnp.bfloat16), CONTEXT, scatter_dimension=0, tiled=True
            ).astype(jnp.float32),
            lax.psum_scatter(
                d_values[:prompt].astype(jnp.bfloat16), CONTEXT, scatter_dimension=0, tiled=True
            ).astype(jnp.float32),
        )
        d_key_rows = jnp.concatenate([own_dkey, d_keys[prompt:]], 0)
        d_value_rows = jnp.concatenate([own_dvalue, d_values[prompt:]], 0)
        d_projected = jnp.concatenate(
            [
                rotate(d_query, cosine, -sine_part).astype(jnp.bfloat16),
                rotate(d_key_rows, cosine, -sine_part).astype(jnp.bfloat16),
                d_value_rows.astype(jnp.bfloat16),
            ],
            1,
        )
        acc_qkv = acc_qkv + tdot(d_projected, normed_one)
        d_normed_one = mdot(d_projected, w_qkv)
        scaled_one = gain_one * d_normed_one
        d_inputs = (
            d_hidden
            + root_one * scaled_one
            - inputs * root_one**3 * jnp.mean(inputs * scaled_one, -1, keepdims=True)
        )
        acc_gain_one = acc_gain_one + jnp.sum(d_normed_one * inputs * root_one, 0)
        input_list.append(d_inputs.astype(jnp.bfloat16))
    acc_gains = jnp.concatenate(
        [acc_gain_one[None], acc_gain_two[None], jnp.zeros((6, feature_count), jnp.float32)], 0
    )
    dense_sums, expert_sums, gain_sum = scatter_gradients(
        sizes,
        tuple(
            item.astype(jnp.bfloat16).reshape(blocks, owners // 2, 2, -1, feature_count)
            for item in (acc_qkv, acc_out, gsg.T, gsu.T, gsd)
        ),
        (geg, geu, ged),
        acc_gains,
    )
    grad_qkv, grad_out, grad_sgate, grad_sup, grad_sdown = (
        item.astype(jnp.float32) for item in dense_sums
    )
    grad_qkv, grad_sgate, grad_sup = grad_qkv.T, grad_sgate.T, grad_sup.T
    grad_gains = lax.dynamic_slice(gain_sum, (0, own_at * gain_width), (2, gain_width))
    sharded_expert_gate, sharded_expert_up, sharded_expert_down = (
        item.astype(jnp.float32) for item in expert_sums
    )
    mixed = jnp.stack(mixed_list, 0).reshape(tokens.shape)
    input_grad = jnp.stack(input_list, 0).reshape(tokens.shape)
    return (
        mixed,
        input_grad,
        grad_qkv,
        grad_out,
        grad_sgate,
        grad_sup,
        grad_sdown,
        grad_gains,
        sharded_expert_gate,
        sharded_expert_up,
        sharded_expert_down,
    )


def kernels_fit(mesh_shape, arrays):
    qkv_weight, out_weight, shared_gate, _, shared_down = arrays[4:9]
    rows = (qkv_weight.shape[1], out_weight.shape[0], shared_gate.shape[1], shared_down.shape[0])
    return (
        mesh_shape[DP] == 2
        and mesh_shape[EXPERTS] % 2 == 0
        and all(count % 16 == 0 for count in rows)
        and arrays[10].shape[2] % 128 == 0
    )


def solution(mesh):
    def device_program(*arrays):
        return (on_device if kernels_fit(mesh.shape, arrays) else on_device_plain)(*arrays)

    return jax.shard_map(
        device_program,
        mesh=mesh,
        in_specs=(
            P(DP, EXPERTS, None, CONTEXT, None, None),
            P(DP, EXPERTS, None, CONTEXT, None, None),
            P(DP, EXPERTS, None, CONTEXT, None, None),
            P(DP, EXPERTS, None, CONTEXT, None, None),
            P(None, (CONTEXT, EXPERTS)),
            P((CONTEXT, EXPERTS), None),
            P(None, (CONTEXT, EXPERTS)),
            P(None, (CONTEXT, EXPERTS)),
            P((CONTEXT, EXPERTS), None),
            P(None, (CONTEXT, EXPERTS)),
            P(EXPERTS, None, (DP, CONTEXT)),
            P(EXPERTS, None, (DP, CONTEXT)),
            P(EXPERTS, (DP, CONTEXT), None),
        ),
        out_specs=(
            P(DP, EXPERTS, None, CONTEXT, None, None),
            P(DP, EXPERTS, None, CONTEXT, None, None),
            P(None, (CONTEXT, EXPERTS)),
            P((CONTEXT, EXPERTS), None),
            P(None, (CONTEXT, EXPERTS)),
            P(None, (CONTEXT, EXPERTS)),
            P((CONTEXT, EXPERTS), None),
            P(None, (CONTEXT, EXPERTS)),
            P(EXPERTS, None, (DP, CONTEXT)),
            P(EXPERTS, None, (DP, CONTEXT)),
            P(EXPERTS, (DP, CONTEXT), None),
        ),
        check_vma=False,
    )
```

```python
import functools

import jax
import jax.numpy as jnp
import numpy as np
from jax import lax
from jax.experimental import pallas as pl
from jax.experimental.pallas import tpu as pltpu
from jax.sharding import PartitionSpec as P

DP, CONTEXT, EXPERTS = "dp", "context", "experts"

H = 12
HD = 64
PB = 128
CONT = 256


EPSILON = 1e-06


def mdot(former, latter):
    return jnp.dot(former, latter, preferred_element_type=jnp.float32)


def tdot(former, latter):
    return lax.dot_general(
        former, latter, (((0,), (0,)), ((), ())), preferred_element_type=jnp.float32
    )


def ndot(former, latter):
    return lax.dot_general(
        former, latter, (((1,), (1,)), ((), ())), preferred_element_type=jnp.float32
    )


def rotate(values, cosine, sine_part):
    half_size = HD // 2
    shaped = values.reshape(values.shape[0], H, HD)
    former = shaped[..., :half_size]
    latter = shaped[..., half_size:]
    turned = jnp.concatenate(
        [former * cosine - latter * sine_part, latter * cosine + former * sine_part], -1
    )
    return turned.reshape(values.shape)


def slot_table(routes_block, expert_count):
    flat_routes = routes_block.reshape(-1)
    onehot = (flat_routes[:, None] == jnp.arange(expert_count, dtype=jnp.int32)[None, :]).astype(
        jnp.int32
    )
    before = jnp.cumsum(onehot, 0) - onehot
    return jnp.sum(before * onehot, 1).reshape(routes_block.shape)


def silu_parts(values):
    sigma = jax.nn.sigmoid(values)
    return (values * sigma, sigma * (1.0 + values * (1.0 - sigma)))


MESH = pl.DeviceIdType.MESH
MIB = 1024 * 1024
BF = jnp.bfloat16
F32 = jnp.float32


def remote(source, target, send_sem, recv_sem, **device):
    return pltpu.make_async_remote_copy(
        src_ref=source,
        dst_ref=target,
        send_sem=send_sem,
        recv_sem=recv_sem,
        device_id=device,
        device_id_type=MESH,
    )


def arrived(slot, recv_sem):
    remote(slot, slot, recv_sem, recv_sem, context=0).wait_recv()


def either(first, second):
    return jnp.logical_and(first, second)


class Place:
    def __init__(self, sizes):
        self.depth, self.high_count = sizes
        self.owners = self.high_count * 2
        self.x = lax.axis_index(DP)
        self.z = lax.axis_index(CONTEXT)
        self.e = lax.axis_index(EXPERTS)
        self.high = self.e // 2
        self.low = self.e % 2

    def shard(self, z):
        return self.x * self.depth + z

    def other_shard(self, z):
        return (1 - self.x) * self.depth + z

    def peer_high(self, step):
        return lax.rem(self.high + step, self.high_count)

    def peer_owner(self, step):
        return lax.rem(self.e + step, self.owners)

    def on_line(self, z):
        return (z >= 0) & (z < self.depth)

    def greet(self):
        barrier = pltpu.get_barrier_semaphore()

        def signal(**device):
            pl.semaphore_signal(barrier, inc=1, device_id=device, device_id_type=MESH)

        signal(dp=1 - self.x)
        for step in range(1, self.owners):
            signal(experts=self.peer_owner(step))
        for step in range(1, self.depth):
            signal(context=lax.rem(self.z + step, self.depth))
        count = self.owners + self.depth - 1
        pl.semaphore_wait(barrier, count)


class Line:
    def __init__(self, place, own, slot, send_sem, recv_sem):
        self.place, self.own, self.slot = place, own, slot
        self.send_sem, self.recv_sem = send_sem, recv_sem

    def _copy(self, direction, step):
        place = self.place
        z = place.z - direction * step
        source = self.own if step == 0 else self.slot(z)
        return remote(
            source,
            self.slot(z),
            self.send_sem.at[(direction + 1) // 2, step],
            self.recv_sem.at[z],
            context=place.z + direction,
        )

    def _valid(self, direction, step):
        place = self.place
        return place.on_line(place.z - direction * step) & place.on_line(place.z + direction)

    def send(self, direction, step):
        if step < self.place.depth - 1:
            pl.when(self._valid(direction, step))(lambda: self._copy(direction, step).start())

    def start(self):
        self.send(1, 0)
        self.send(-1, 0)

    def hop(self, step, then=None):
        for direction in (1, -1):
            z = self.place.z - direction * (step + 1)

            def body(direction=direction, z=z):
                arrived(self.slot(z), self.recv_sem.at[z])
                self.send(direction, step + 1)
                if then is not None:
                    then(z)

            pl.when(self.place.on_line(z))(body)

    def drain(self):
        for direction in (1, -1):
            for step in range(self.place.depth - 1):
                pl.when(self._valid(direction, step))(
                    lambda d=direction, s=step: self._copy(d, s).wait_send()
                )


class DenseGather:
    def __init__(self, place, own, slot, sems):
        self.place, self.own, self.slot_of = place, own, slot
        zs, zr, self.h_send, self.h_recv, self.l_send, self.l_recv = sems
        self.line = Line(place, own, lambda z: self.slot(z, place.high, place.low), zs, zr)

    @staticmethod
    def semaphores(count, depth, high_count):
        dma = pltpu.SemaphoreType.DMA
        cross = dma((count, high_count, depth))
        return [dma((count, 2, depth)), dma((count, depth)), cross, cross, cross, cross]

    def slot(self, z, high, low):
        return self.slot_of((z * self.place.high_count + high) * 2 + low)

    def _to_high(self, z, step, own):
        place = self.place
        target = self.slot(z, place.high, place.low)
        return remote(
            self.own if own else target,
            target,
            self.h_send.at[step, z],
            self.h_recv.at[place.high, z],
            experts=place.peer_high(step) * 2 + place.low,
        )

    def _to_low(self, z, high, own):
        place = self.place
        target = self.slot(z, high, place.low)
        return remote(
            self.own if own else target,
            target,
            self.l_send.at[high, z],
            self.l_recv.at[high, z],
            experts=place.e + 1 - 2 * place.low,
        )

    def _spread(self, z, own=False):
        for step in range(1, self.place.high_count):
            self._to_high(z, step, own).start()
        self._to_low(z, self.place.high, own).start()

    def start(self):
        self.line.start()
        self._spread(self.place.z, True)

    def hop(self, step):
        self.line.hop(step, self._spread)

    def cross(self, z):
        place = self.place
        for step in range(1, place.high_count):
            high = place.peer_high(step)
            arrived(self.slot(z, high, place.low), self.h_recv.at[high, z])
            self._to_low(z, high, False).start()

    def finish(self):
        place = self.place
        for z in range(place.depth):
            for high in range(place.high_count):
                arrived(self.slot(z, high, 1 - place.low), self.l_recv.at[high, z])

    def drain(self):
        place = self.place
        self.line.drain()
        for z in range(place.depth):
            for step in range(1, place.high_count):
                self._to_high(z, step, False).wait_send()
            for high in range(place.high_count):
                self._to_low(z, high, False).wait_send()


def expert_slab(ref, kind, local, shard, width):
    start = pl.multiple_of(shard * width, 128)
    if kind == 2:
        return ref.at[local, pl.ds(start, width)]
    return ref.at[local, :, pl.ds(start, width)]


class ExpertGather:
    def __init__(self, place, own, out, sems):
        self.place, self.own, self.out = place, own, out
        self.z_send, self.z_recv, self.x_send, self.x_recv = sems
        self.local_count, self.width = own[0].shape[0], own[0].shape[2]

    @staticmethod
    def semaphores(depth, local_count):
        dma = pltpu.SemaphoreType.DMA
        return [
            dma((local_count, 3, 2, depth)),
            dma((local_count, 3, depth)),
            dma((local_count, 3, depth)),
            dma((local_count, 3, depth)),
        ]

    def slot(self, local, kind, shard):
        return expert_slab(self.out[kind], kind, local, shard, self.width)

    def _line(self, local, kind):
        return Line(
            self.place,
            self.own[kind].at[local],
            lambda z: self.slot(local, kind, self.place.shard(z)),
            self.z_send.at[local, kind],
            self.z_recv.at[local, kind],
        )

    def _across(self, local, kind, z, own=False):
        target = self.slot(local, kind, self.place.shard(z))
        return remote(
            self.own[kind].at[local] if own else target,
            target,
            self.x_send.at[local, kind, z],
            self.x_recv.at[local, kind, z],
            dp=1 - self.place.x,
        )

    def start_x(self):
        for local in range(self.local_count):
            for kind in range(3):
                self._across(local, kind, self.place.z, True).start()

    def start_z(self):
        for local in range(self.local_count):
            for kind in range(3):
                self._line(local, kind).start()

    def hop(self, local, step):
        for kind in range(3):
            self._line(local, kind).hop(
                step, lambda z, kind=kind: self._across(local, kind, z).start()
            )

    def wait_x(self, local, z):
        for kind in range(3):
            arrived(
                self.slot(local, kind, self.place.other_shard(z)), self.x_recv.at[local, kind, z]
            )

    def drain(self):
        for local in range(self.local_count):
            for kind in range(3):
                self._line(local, kind).drain()
                for z in range(self.place.depth):
                    self._across(local, kind, z).wait_send()


def rope(values, cosine, sine_part):
    lane = lax.broadcasted_iota(jnp.int32, cosine.shape, 1)
    first = lax.rem(lane, HD) < HD // 2
    turned = []
    for start in range(0, values.shape[1], 2 * HD):
        part = values[:, start : start + 2 * HD]
        partner = jnp.where(
            first, pltpu.roll(part, 2 * HD - HD // 2, 1), pltpu.roll(part, HD // 2, 1)
        )
        turned.append(part * cosine + partner * sine_part)
    return jnp.concatenate(turned, 1)


def norm_rows(values, gain):
    root = lax.rsqrt(jnp.mean(values * values, -1, keepdims=True) + EPSILON)
    return (values * root * gain).astype(BF)


def tiles(total, size, body):
    def run(i, carry):
        body(pl.ds(pl.multiple_of(i * size, size), size))
        return carry

    lax.fori_loop(0, total // size, run, 0)


def one_hots(routes, gates, me, local_count, total):
    rows = routes.shape[1]
    capacity = rows * 8 // (3 * total)
    first, second = routes[0:1, :], routes[1:2, :]
    ids = lax.rem(
        lax.broadcasted_iota(jnp.int32, (total, rows), 0) + me * local_count, total
    )
    named = (first == ids) | (second == ids)
    earlier = (
        lax.broadcasted_iota(jnp.int32, (rows, rows), 0)
        < lax.broadcasted_iota(jnp.int32, (rows, rows), 1)
    ).astype(F32).astype(BF)
    counts = mdot(named.astype(F32).astype(BF), earlier).astype(jnp.int32)
    places = jnp.where(named, counts, -1)
    weights = jnp.where(first == ids, gates[0:1, :], 0.0) + jnp.where(
        second == ids, gates[1:2, :], 0.0
    )
    slot = lax.broadcasted_iota(jnp.int32, (capacity, rows), 0)
    for i in range(total):
        yield i, slot == places[i : i + 1, :], weights[i : i + 1, :]


def ffn_chunk(x, g, weights, saved, sums, grads, tile):
    gate_w, up_w, down_w = weights
    act_s, d_gate_s, d_up_s = saved
    out_sum, in_sum = sums

    def forward(here):
        x_rows, g_rows = x[here, :], g[here, :]
        gate = mdot(x_rows, gate_w[...])
        up = mdot(x_rows, up_w[...])
        d_act = ndot(g_rows, down_w[...]).astype(BF).astype(F32)
        sigma = jax.nn.sigmoid(gate)
        silu = gate * sigma
        act = (silu * up).astype(BF)
        d_gate = (d_act * up * (sigma * (1.0 + gate * (1.0 - sigma)))).astype(BF)
        d_up = (d_act * silu).astype(BF)
        act_s[here, :] = act
        d_gate_s[here, :] = d_gate
        d_up_s[here, :] = d_up
        out_sum[here, :] += mdot(act, down_w[...])
        in_sum[here, :] += ndot(d_gate, gate_w[...]) + ndot(d_up, up_w[...])

    rows = x.shape[0]
    tiles(rows, tile, forward)
    used = pl.ds(0, rows)

    def weight_grads(here):
        grads[0][here, :] = tdot(x[:, here], d_gate_s[used, :]).astype(BF)
        grads[1][here, :] = tdot(x[:, here], d_up_s[used, :]).astype(BF)
        grads[2][:, here] = tdot(act_s[used, :], g[:, here]).astype(BF)

    tiles(x.shape[1], 256, weight_grads)


def forward_kernel(sizes, *refs):
    place = Place(sizes)
    depth, high_count = sizes
    owners = place.owners
    (
        tokens, cot, gates, routes, cosine, sine_part,
        qkv_in, out_in, gain_in, sg_in, su_in, sd_in, eg_in, eu_in, ed_in,
        qkv_o, out_o, gain_o, sg_o, su_o, sd_o, eg_o, eu_o, ed_o,
        n1_o, k_o, v_o, q_o, att_o, hid_o, lse_o, side_o, dn2_o,
        gsg_o, gsu_o, gsd_o, geg_o, geu_o, ged_o, outs_o, dins_o,
        xk, wq, wo, gain_land, gain_v, g_all, n2, in_s, do_s, send_in, send_do,
        wg, wu, wd, act_s, dg_s, du_s, stage_g, stage_u, stage_d,
        *sems,
    ) = refs
    dense_sems, sems = sems[:6], sems[6:]
    expert_sems, sems = sems[:4], sems[4:]
    (
        line_send, line_recv, load_sem, ai_send, ai_recv, ad_send, ad_recv,
        chunk_sem, store_sem, out_sem,
    ) = sems
    micro_count, rows, features = tokens.shape
    prompt = depth * PB
    length = prompt + CONT
    local_count, _, width = eg_in.shape
    total = owners * local_count
    capacity = rows * 8 // (3 * total)
    slots = in_s.shape[1]
    me = place.e

    def dense(i, own, slot):
        return DenseGather(place, own, slot, [s.at[i] for s in dense_sems])

    def rows_of(ref, count):
        return lambda s: ref.at[pl.ds(pl.multiple_of(s * count, 16), count)]

    def columns_of(ref, count):
        return lambda s: ref.at[:, pl.ds(pl.multiple_of(s * count, 128), count)]

    early = [
        dense(0, qkv_in, rows_of(wq, qkv_in.shape[0])),
        dense(1, out_in, rows_of(wo, out_in.shape[0])),
        dense(2, gain_in, rows_of(gain_land, gain_in.shape[0])),
    ]
    late = [
        dense(3, sg_in, columns_of(sg_o, sg_in.shape[1])),
        dense(4, su_in, columns_of(su_o, su_in.shape[1])),
        dense(5, sd_in, rows_of(sd_o, sd_in.shape[0])),
    ]
    experts = ExpertGather(place, (eg_in, eu_in, ed_in), (eg_o, eu_o, ed_o), expert_sems)
    own_prompt = pl.ds(pl.multiple_of(place.z * PB, PB), PB)
    prompts = Line(
        place,
        tokens.at[:, pl.ds(0, PB)],
        lambda z: xk.at[:, pl.ds(pl.multiple_of(z * PB, PB), PB)],
        line_send,
        line_recv,
    )
    own_at = (place.z * high_count + place.high) * 2 + place.low
    loads = [
        (tokens.at[:, pl.ds(0, PB)], xk.at[:, own_prompt]),
        (tokens.at[:, pl.ds(PB, CONT)], xk.at[:, pl.ds(prompt, CONT)]),
    ]
    loads += [(cot.at[m], g_all.at[pl.ds(m * rows, rows)]) for m in range(micro_count)]
    loads += [(d.own, d.slot_of(own_at)) for d in early]
    bounce = [
        (sg_in, wg.at[0, :, pl.ds(0, sg_in.shape[1])], late[0].slot_of(own_at)),
        (su_in, wu.at[0, :, pl.ds(0, su_in.shape[1])], late[1].slot_of(own_at)),
        (sd_in, wd.at[0, pl.ds(0, sd_in.shape[0])], late[2].slot_of(own_at)),
    ]
    loads += [(source, middle) for source, middle, _ in bounce]
    load_copies = [
        pltpu.make_async_copy(source, target, load_sem.at[i])
        for i, (source, target) in enumerate(loads)
    ]
    bounce_copies = [
        pltpu.make_async_copy(middle, target, load_sem.at[i])
        for i, (_, middle, target) in enumerate(bounce)
    ]
    for copy in load_copies:
        copy.start()
    place.greet()
    prompts.start()
    for d in early:
        d.start()
    experts.start_x()
    for copy in load_copies:
        copy.wait()
    for copy in bounce_copies:
        copy.start()
    stores = []

    def store(source, target):
        copy = pltpu.make_async_copy(source, target, out_sem.at[len(stores)])
        copy.start()
        stores.append(copy)

    def slot_rows(m, sender):
        return pl.ds(pl.multiple_of((m * owners + sender) * capacity, 16), capacity)

    def exchange(buffer, land, send_sem, recv_sem, m, step):
        return remote(
            buffer.at[step - 1, m],
            land.at[:, slot_rows(m, me)],
            send_sem.at[step - 1, m],
            recv_sem.at[step - 1, m],
            experts=place.peer_owner(step),
        )

    def exchanged(land, recv_sem, m, step):
        sender = lax.rem(me - step + owners, owners)
        arrived(land.at[:, slot_rows(m, sender)], recv_sem.at[step - 1, m])

    def put(buffer, land, m, i, value):
        if i < local_count:
            land[i, slot_rows(m, me), :] = value
        else:
            buffer[i // local_count - 1, m, i % local_count] = value

    for m in range(micro_count):
        g_rows = g_all[pl.ds(m * rows, rows), :]
        for i, hit, weight in one_hots(routes.at[m], gates.at[m], me, local_count, total):
            gate = jnp.sum(jnp.where(hit, weight, 0.0), -1, keepdims=True)
            value = mdot(hit.astype(F32).astype(BF), g_rows)
            put(send_do, do_s, m, i, (gate * value).astype(BF))
    prompts.hop(0)
    for step in range(depth - 1):
        for d in early:
            d.hop(step)
        if step + 1 < depth - 1:
            prompts.hop(step + 1)
    for copy in bounce_copies:
        copy.wait()
    for d in late:
        d.start()
    experts.start_z()
    for z in range(depth):
        for d in early:
            d.cross(z)
    for d in early:
        d.finish()
    for m in range(micro_count):
        for step in range(1, owners):
            exchange(send_do, do_s, ad_send, ad_recv, m, step).start()
    store(wq, qkv_o)
    store(wo, out_o)
    shards = depth * owners
    gain_rows = gain_in.shape[0]
    gain_sum = jnp.zeros((8, features), F32)
    for s in range(shards):
        gain_sum += gain_land[pl.ds(s * gain_rows, gain_rows), :].astype(F32)[:8]
    gain_v[...] = gain_sum
    store(gain_v, gain_o)

    def own_rows(i):
        start = place.z * PB if i == 0 else prompt + (i - 1) * PB
        return start, pl.ds(start if i else pl.multiple_of(start, PB), PB)

    def front(n1, k, v, q, att, hid, lse):
        lse[...] = jnp.zeros_like(lse)
        for m in range(micro_count):

            def project(here):
                normed = norm_rows(xk[m, here, :].astype(F32), gain_v[0:1, :])
                n1[m, here, :] = normed
                key = ndot(normed, wq[pl.ds(features, features), :])
                k[m, here, :] = rope(key, cosine[here, :], sine_part[here, :]).astype(BF)
                v[m, here, :] = ndot(normed, wq[pl.ds(2 * features, features), :]).astype(BF)

            tiles(length, 256, project)
            for i in range(rows // PB):
                _, here = own_rows(i)
                query = ndot(n1[m, here, :], wq[pl.ds(0, features), :])
                query = rope(query, cosine[here, :], sine_part[here, :]).astype(BF)
                q[m, pl.ds(i * PB, PB), :] = query * jnp.asarray(HD**-0.5, BF)
            for d in late:
                d.hop(m)
        store(n1, n1_o)
        store(k, k_o)
        store(v, v_o)
        store(q, q_o)
        lane = lax.broadcasted_iota(jnp.int32, (PB, 2 * HD), 1)
        column = lax.broadcasted_iota(jnp.int32, (PB, length), 1)
        row = lax.broadcasted_iota(jnp.int32, (PB, length), 0)
        for m in range(micro_count):

            def pair(index, carry):
                lanes = pl.ds(pl.multiple_of(index * 2 * HD, 2 * HD), 2 * HD)
                keys, values = k[m, :, lanes], v[m, :, lanes]
                for i in range(rows // PB):
                    here = pl.ds(i * PB, PB)
                    query = q[m, here, lanes]
                    allowed = column <= row + own_rows(i)[0]
                    parts = []
                    logs = lse[m, here, :]
                    for sub in range(2):
                        only = jnp.where(lane // HD == sub, query, jnp.zeros_like(query))
                        scores = jnp.where(allowed, ndot(only, keys), -1000000000.0)
                        highest = jnp.max(scores, -1, keepdims=True)
                        weights = jnp.exp(scores - highest)
                        sums = jnp.sum(weights, -1, keepdims=True)
                        parts.append(mdot((weights * (1.0 / sums)).astype(BF), values))
                        logs = jnp.where(lane == 2 * index + sub, highest + jnp.log(sums), logs)
                    lse[m, here, :] = logs
                    att[m, here, lanes] = jnp.where(lane < HD, parts[0], parts[1]).astype(BF)
                return carry

            lax.fori_loop(0, features // (2 * HD), pair, 0)
            for i in range(rows // PB):
                here = pl.ds(i * PB, PB)
                hidden = xk[m, own_rows(i)[1], :].astype(F32) + mdot(att[m, here, :], wo[...])
                hid[m, here, :] = hidden
                n2[pl.ds(m * rows + i * PB, PB), :] = norm_rows(hidden, gain_v[1:2, :])
            normed = n2[pl.ds(m * rows, rows), :]
            for i, hit, _ in one_hots(routes.at[m], gates.at[m], me, local_count, total):
                value = mdot(hit.astype(F32).astype(BF), normed)
                put(send_in, in_s, m, i, value.astype(BF))
            for step in range(1, owners):
                exchange(send_in, in_s, ai_send, ai_recv, m, step).start()
            if m == 0:
                for step in range(micro_count, depth - 1):
                    for d in late:
                        d.hop(step)
        store(att, att_o)
        store(hid, hid_o)
        store(lse, lse_o)
        for z in range(depth):
            for d in late:
                d.cross(z)
        for d in late:
            d.finish()
        for copy in stores:
            copy.wait()

    pl.run_scoped(
        front,
        pltpu.VMEM((micro_count, length, features), BF),
        pltpu.VMEM((micro_count, length, features), BF),
        pltpu.VMEM((micro_count, length, features), BF),
        pltpu.VMEM((micro_count, rows, features), BF),
        pltpu.VMEM((micro_count, rows, features), BF),
        pltpu.VMEM((micro_count, rows, features), F32),
        pltpu.VMEM((micro_count, rows, 2 * HD), F32),
    )
    saved = (act_s, dg_s, du_s)
    staged = (stage_g, stage_u, stage_d)

    def chunk_loads(sources, slot):
        return [
            pltpu.make_async_copy(source, buffer.at[slot], chunk_sem.at[slot, kind])
            for kind, (source, buffer) in enumerate(zip(sources, (wg, wu, wd)))
        ]

    def chunk_stores(targets, slot):
        return [
            pltpu.make_async_copy(buffer.at[slot], target, store_sem.at[slot, kind])
            for kind, (target, buffer) in enumerate(zip(targets, staged))
        ]

    def shared(out_sum, in_sum):
        out_sum[...] = jnp.zeros_like(out_sum)
        in_sum[...] = jnp.zeros_like(in_sum)
        count = sg_o.shape[1] // width

        def part(refs, c):
            here = pl.ds(pl.multiple_of(c * width, 128), width)
            return [refs[0].at[:, here], refs[1].at[:, here], refs[2].at[here]]

        for copy in chunk_loads(part((sg_o, su_o, sd_o), 0), 0):
            copy.start()

        def run(c, carry):
            slot = lax.rem(c, 2)

            def prefetch():
                for copy in chunk_loads(part((sg_o, su_o, sd_o), c + 1), 1 - slot):
                    copy.start()

            pl.when(c + 1 < count)(prefetch)
            for copy in chunk_loads(part((sg_o, su_o, sd_o), c), slot):
                copy.wait()
            targets = part((gsg_o, gsu_o, gsd_o), c)

            def previous():
                for copy in chunk_stores(targets, slot):
                    copy.wait()

            pl.when(c >= 2)(previous)
            ffn_chunk(
                n2,
                g_all,
                (wg.at[slot], wu.at[slot], wd.at[slot]),
                saved,
                (out_sum, in_sum),
                [buffer.at[slot] for buffer in staged],
                384,
            )
            for copy in chunk_stores(targets, slot):
                copy.start()
            for local in range(local_count):
                pl.when(c == count // 2 + local)(lambda local=local: experts.hop(local, 0))
            return carry

        lax.fori_loop(0, count, run, 0)
        for slot in range(2):
            for copy in chunk_stores(part((gsg_o, gsu_o, gsd_o), slot), slot):
                copy.wait()
        ends = [
            pltpu.make_async_copy(out_sum, side_o, out_sem.at[0]),
            pltpu.make_async_copy(in_sum, dn2_o, out_sem.at[1]),
        ]
        for copy in ends:
            copy.start()
        for copy in ends:
            copy.wait()

    pl.run_scoped(
        shared,
        pltpu.VMEM((micro_count * rows, features), F32),
        pltpu.VMEM((micro_count * rows, features), F32),
    )
    for m in range(micro_count):
        for step in range(1, owners):
            exchanged(in_s, ai_recv, m, step)
            exchanged(do_s, ad_recv, m, step)

    def routed(out_sum, in_sum):
        out_sum[...] = jnp.zeros_like(out_sum)
        in_sum[...] = jnp.zeros_like(in_sum)

        def item(w, carry):
            after = jnp.maximum(w - 2, 0)
            step, kind = after // 4, lax.rem(after, 4)
            side = lax.rem(kind, 2)
            z = jnp.where(w < 2, place.z, place.z + (2 * side - 1) * (1 + step))
            crossed = jnp.where(w < 2, w, kind // 2)
            valid = place.on_line(z)
            shard = jnp.where(crossed == 1, place.other_shard(z), place.shard(z))

            def load(local):
                sources = [
                    expert_slab(ref, kind, local, shard, width)
                    for kind, ref in enumerate((eg_o, eu_o, ed_o))
                ]
                return chunk_loads(sources, local)

            def begin():
                def own():
                    for local in range(local_count):
                        mine = [ref.at[local] for ref in (eg_in, eu_in, ed_in)]
                        for copy in chunk_loads(mine, local):
                            copy.start()

                def landed():
                    def wait_x():
                        for local in range(local_count):
                            experts.wait_x(local, z)

                    pl.when(crossed == 1)(wait_x)
                    for local in range(local_count):
                        for copy in load(local):
                            copy.start()

                pl.when(w == 0)(own)
                pl.when(w > 0)(landed)

            pl.when(valid)(begin)

            def one(local, carry):
                targets = [
                    expert_slab(ref, kind, local, shard, width)
                    for kind, ref in enumerate((geg_o, geu_o, ged_o))
                ]

                def compute():
                    for copy in load(local):
                        copy.wait()

                    def previous():
                        for copy in chunk_stores(targets, local):
                            copy.wait()

                    pl.when(w > 0)(previous)
                    ffn_chunk(
                        in_s.at[local],
                        do_s.at[local],
                        (wg.at[local], wu.at[local], wd.at[local]),
                        saved,
                        (out_sum.at[local], in_sum.at[local]),
                        [buffer.at[local] for buffer in staged],
                        512,
                    )
                    for copy in chunk_stores(targets, local):
                        copy.start()

                pl.when(valid)(compute)
                for later in range(1, depth - 1):
                    at = 0 if later == 1 else 2 + 4 * (later - 2)
                    pl.when(w == at)(lambda later=later: experts.hop(local, later))
                return carry

            lax.fori_loop(0, local_count, one, 0)
            return carry

        lax.fori_loop(0, 2 + 4 * (depth - 1), item, 0)
        for local in range(local_count):
            targets = [
                expert_slab(ref, kind, local, 0, width)
                for kind, ref in enumerate((geg_o, geu_o, ged_o))
            ]
            for copy in chunk_stores(targets, local):
                copy.wait()

            def finish(here, local=local):
                in_s[local, here, :] = out_sum[local, here, :].astype(BF)
                do_s[local, here, :] = in_sum[local, here, :].astype(BF)

            tiles(slots, 256, finish)

    pl.run_scoped(
        routed,
        pltpu.VMEM((local_count, slots, features), F32),
        pltpu.VMEM((local_count, slots, features), F32),
    )
    ends = [
        pltpu.make_async_copy(in_s, outs_o, out_sem.at[0]),
        pltpu.make_async_copy(do_s, dins_o, out_sem.at[1]),
    ]
    for copy in ends:
        copy.start()
    for copy in ends:
        copy.wait()
    prompts.drain()
    for d in early + late:
        d.drain()
    experts.drain()
    for m in range(micro_count):
        for step in range(1, owners):
            exchange(send_do, do_s, ad_send, ad_recv, m, step).wait_send()
            exchange(send_in, in_s, ai_send, ai_recv, m, step).wait_send()


def rope_tables(prompt):
    positions = np.arange(prompt + CONT, dtype=np.float64)
    frequency = 10000.0 ** (-2.0 * np.arange(HD // 2) / HD)
    angles = positions[:, None] * frequency
    cosine, sine_part = np.cos(angles), np.sin(angles)
    return (
        np.concatenate([cosine] * 4, 1).astype(np.float32),
        np.concatenate([-sine_part, sine_part] * 2, 1).astype(np.float32),
    )


def run_forward(sizes, tokens, cot, gates, routes, dense, experts):
    depth, high_count = sizes
    micro_count, rows, features = tokens.shape
    owners = high_count * 2
    line = depth * owners
    prompt = depth * PB
    length = prompt + CONT
    local_count, _, width = experts[0].shape
    hidden_units = dense[3].shape[1] * line
    capacity = rows * 8 // (3 * owners * local_count)
    slots = micro_count * owners * capacity
    cosine, sine_part = rope_tables(prompt)
    hbm, vmem = pl.BlockSpec(memory_space=pltpu.HBM), pl.BlockSpec(memory_space=pltpu.VMEM)

    def shape(dtype, *dims):
        return jax.ShapeDtypeStruct(dims, dtype)

    token_rows = micro_count * rows
    wide, tall = (features, hidden_units), (hidden_units, features)
    out_shape = [
        shape(BF, dense[0].shape[0] * line, features),
        shape(BF, dense[1].shape[0] * line, features),
        shape(F32, 8, features),
        shape(BF, *wide), shape(BF, *wide), shape(BF, *tall),
        shape(BF, local_count, *wide), shape(BF, local_count, *wide), shape(BF, local_count, *tall),
        shape(BF, micro_count, length, features),
        shape(BF, micro_count, length, features),
        shape(BF, micro_count, length, features),
        shape(BF, micro_count, rows, features),
        shape(BF, micro_count, rows, features),
        shape(F32, micro_count, rows, features),
        shape(F32, micro_count, rows, 2 * HD),
        shape(F32, token_rows, features),
        shape(F32, token_rows, features),
        shape(BF, *wide), shape(BF, *wide), shape(BF, *tall),
        shape(BF, local_count, *wide), shape(BF, local_count, *wide), shape(BF, local_count, *tall),
        shape(BF, local_count, slots, features),
        shape(BF, local_count, slots, features),
    ]
    dma = pltpu.SemaphoreType.DMA
    buffers = max(2, local_count)
    send = pltpu.VMEM((owners - 1, micro_count, local_count, capacity, features), BF)
    scratch = [
        pltpu.VMEM((micro_count, length, features), BF),
        pltpu.VMEM(out_shape[0].shape, BF),
        pltpu.VMEM(out_shape[1].shape, BF),
        pltpu.VMEM((dense[2].shape[0] * line, features), BF),
        pltpu.VMEM((8, features), F32),
        pltpu.VMEM((token_rows, features), BF),
        pltpu.VMEM((token_rows, features), BF),
        pltpu.VMEM((local_count, slots, features), BF),
        pltpu.VMEM((local_count, slots, features), BF),
        send,
        send,
        pltpu.VMEM((buffers, features, width), BF),
        pltpu.VMEM((buffers, features, width), BF),
        pltpu.VMEM((buffers, width, features), BF),
        pltpu.VMEM((max(slots, token_rows), width), BF),
        pltpu.VMEM((max(slots, token_rows), width), BF),
        pltpu.VMEM((max(slots, token_rows), width), BF),
        pltpu.VMEM((buffers, features, width), BF),
        pltpu.VMEM((buffers, features, width), BF),
        pltpu.VMEM((buffers, width, features), BF),
    ]
    scratch += DenseGather.semaphores(len(dense), depth, high_count)
    scratch += ExpertGather.semaphores(depth, local_count)
    scratch += [
        dma((2, depth)),
        dma((depth,)),
        dma((10 + micro_count,)),
        dma((owners - 1, micro_count)),
        dma((owners - 1, micro_count)),
        dma((owners - 1, micro_count)),
        dma((owners - 1, micro_count)),
        dma((buffers, 3)),
        dma((buffers, 3)),
        dma((12,)),
    ]
    return pl.pallas_call(
        functools.partial(forward_kernel, sizes),
        out_shape=out_shape,
        in_specs=[hbm] * 2 + [vmem] * 4 + [hbm] * 9,
        out_specs=[hbm] * len(out_shape),
        scratch_shapes=scratch,
        compiler_params=pltpu.CompilerParams(
            collective_id=0, has_side_effects=True, vmem_limit_bytes=60 * MIB
        ),
        name="gather_and_forward",
    )(tokens, cot, gates, routes, cosine, sine_part, *dense, *experts)


def add_into(target, sources, step):
    def body(here):
        value = target[here, :].astype(F32)
        for source in sources:
            value = value + source[here, :].astype(F32)
        target[here, :] = value.astype(target.dtype)

    tiles(target.shape[0], step, body)


class LineSum:
    def __init__(self, place, part, land, send_sem, recv_sem):
        self.place, self.part, self.land = place, part, land
        self.send_sem, self.recv_sem = send_sem, recv_sem

    def copy(self, z, direction):
        place = self.place
        slot = z if direction > 0 else jnp.where(z == place.z - 1, place.depth, z)
        return remote(
            self.part(z),
            self.land(slot),
            self.send_sem.at[z],
            self.recv_sem.at[slot],
            context=place.z + direction,
        )

    def upstream(self, direction):
        return self.place.z > 0 if direction > 0 else self.place.z < self.place.depth - 1

    def arrive(self, slot):
        arrived(self.land(slot), self.recv_sem.at[slot])

    def at(self, direction, step, body):
        z = self.place.z + direction * step
        pl.when(self.place.on_line(z))(lambda: body(z))

    def pass_on(self, direction, step, add):
        def body(z):
            def more():
                self.arrive(z)
                add(self.part(z), self.land(z))

            pl.when(self.upstream(direction))(more)
            self.copy(z, direction).start()

        self.at(direction, step, body)

    def end(self, add):
        for direction, slot in ((1, self.place.z), (-1, self.place.depth)):

            def body(slot=slot):
                self.arrive(slot)
                add(self.part(self.place.z), self.land(slot))

            pl.when(self.upstream(direction))(body)

    def drain(self):
        for step in range(1, self.place.depth):
            for direction in (1, -1):
                self.at(direction, step, lambda z, d=direction: self.copy(z, d).wait_send())


class DenseScatter:
    def __init__(self, place, source, low, high, line, cross, spare, out, sems):
        self.place, self.source, self.spare, self.out = place, source, spare, out
        self.low, self.high, self.cross = low, high, cross
        (
            self.l_send, self.l_recv, self.h_send, self.h_recv, z_send, z_recv,
            self.x_send, self.x_recv, self.own_sem,
        ) = sems
        self.step = min(64, low.shape[2]) if low.shape[2] % 64 == 0 else 16
        self.line = LineSum(
            place, lambda z: low.at[z, place.high], lambda slot: line.at[slot], z_send, z_recv
        )

    @staticmethod
    def semaphores(count, depth, high_count):
        dma = pltpu.SemaphoreType.DMA
        cross = dma((count, depth, high_count))
        return [
            cross, cross, dma((count, high_count)), dma((count, high_count)),
            dma((count, depth + 1)), dma((count, depth + 1)),
            dma((count,)), dma((count,)), dma((count, 2)),
        ]

    def _index(self, z, high, low):
        return (z * self.place.high_count + high) * 2 + low

    def _to_low(self, z, high):
        place = self.place
        return remote(
            self.source(self._index(z, high, 1 - place.low)),
            self.low.at[z, high],
            self.l_send.at[z, high],
            self.l_recv.at[z, high],
            experts=place.e + 1 - 2 * place.low,
        )

    def _each(self, body):
        for z in range(self.place.depth):
            for high in range(self.place.high_count):
                body(z, high)

    def start(self):
        self._each(lambda z, high: self._to_low(z, high).start())

    def add_low(self):
        place = self.place
        places = [(z, high) for z in range(place.depth) for high in range(place.high_count)]

        def load(i):
            z, high = places[i]
            return pltpu.make_async_copy(
                self.source(self._index(z, high, place.low)),
                self.spare.at[i % 2],
                self.own_sem.at[i % 2],
            )

        if self.spare is not None:
            load(0).start()
        for i, (z, high) in enumerate(places):
            self._to_low(z, high).wait_recv()
            if self.spare is None:
                own = self.source(self._index(z, high, place.low))
            else:
                if i + 1 < len(places):
                    load(i + 1).start()
                load(i).wait()
                own = self.spare.at[i % 2]
            add_into(self.low.at[z, high], [own], self.step)
        for step in range(1, place.high_count):
            self._to_high(step).start()

    def _to_high(self, step):
        place = self.place
        peer = place.peer_high(step)
        return remote(
            self.low.at[:, peer],
            self.high.at[step - 1],
            self.h_send.at[step],
            self.h_recv.at[step],
            experts=peer * 2 + place.low,
        )

    def add_high(self):
        place = self.place
        for step in range(1, place.high_count):
            self._to_high(step).wait_recv()
        for z in range(place.depth):
            add_into(
                self.low.at[z, place.high],
                [self.high.at[step - 1, z] for step in range(1, place.high_count)],
                self.step,
            )

    def _add(self, target, more):
        add_into(target, [more], self.step)

    def pass_on(self, direction, step):
        self.line.pass_on(direction, step, self._add)

    def _across(self):
        place = self.place
        return remote(
            self.low.at[place.z, place.high], self.cross, self.x_send, self.x_recv, dp=1 - place.x
        )

    def end(self):
        self.line.end(self._add)
        self._across().start()

    def _store(self):
        return pltpu.make_async_copy(self.cross, self.out, self.own_sem.at[0])

    def finish(self):
        self._across().wait_recv()
        self._add(self.cross, self.low.at[self.place.z, self.place.high])
        self._store().start()

    def drain(self):
        self._each(lambda z, high: self._to_low(z, high).wait_send())
        for step in range(1, self.place.high_count):
            self._to_high(step).wait_send()
        self.line.drain()
        self._across().wait_send()
        self._store().wait()


class ExpertScatter:
    def __init__(self, place, sums, cross, land, own, more, outs, sems):
        self.place, self.sums, self.cross, self.land = place, sums, cross, land
        self.own, self.more, self.outs = own, more, outs
        self.x_send, self.x_recv, self.z_send, self.z_recv, self.load_sem, self.out_sem = sems
        self.local_count, self.width = cross[0].shape[1], cross[0].shape[3]

    @staticmethod
    def semaphores(depth, local_count):
        dma = pltpu.SemaphoreType.DMA
        return [
            dma((local_count, 3, depth)),
            dma((local_count, 3, depth)),
            dma((local_count, 3, depth + 1)),
            dma((local_count, 3, depth + 1)),
            dma((3, 3)),
            dma((local_count, 3)),
        ]

    def _line(self, local, kind):
        return LineSum(
            self.place,
            lambda z: self.cross[kind].at[z, local],
            lambda slot: self.land[kind].at[slot, local],
            self.z_send.at[local, kind],
            self.z_recv.at[local, kind],
        )

    def _across(self, local, kind, z):
        return remote(
            expert_slab(self.sums[kind], kind, local, self.place.other_shard(z), self.width),
            self.cross[kind].at[z, local],
            self.x_send.at[local, kind, z],
            self.x_recv.at[local, kind, z],
            dp=1 - self.place.x,
        )

    def _order(self, body):
        place = self.place
        for step in range(place.depth - 1, 0, -1):
            for direction in (1, -1):
                z = place.z + direction * step
                pl.when(place.on_line(z))(lambda z=z: body(z))
        body(place.z)

    def start(self):
        def body(z):
            for local in range(self.local_count):
                for kind in range(3):
                    self._across(local, kind, z).start()

        self._order(body)

    def _own_load(self, local, kind, z):
        return pltpu.make_async_copy(
            expert_slab(self.sums[kind], kind, local, self.place.shard(z), self.width),
            self.own[kind],
            self.load_sem.at[0, kind],
        )

    def _more_load(self, local, kind, slot, which):
        return pltpu.make_async_copy(
            self.land[kind].at[slot, local], self.more[kind].at[which], self.load_sem.at[1 + which, kind]
        )

    def pass_on(self, direction, step, local):
        def body(z):
            line = self._line(local, 0)
            for kind in range(3):
                self._own_load(local, kind, z).start()
            for kind in range(3):
                line = self._line(local, kind)
                target = self.cross[kind].at[z, local]

                def come(line=line, kind=kind):
                    line.arrive(z)
                    self._more_load(local, kind, z, 0).start()

                pl.when(line.upstream(direction))(come)
                self._across(local, kind, z).wait_recv()
                self._own_load(local, kind, z).wait()

                def both(target=target, kind=kind):
                    self._more_load(local, kind, z, 0).wait()
                    add_into(target, [self.own[kind], self.more[kind].at[0]], 64)

                def single(target=target, kind=kind):
                    add_into(target, [self.own[kind]], 64)

                pl.when(line.upstream(direction))(both)
                pl.when(jnp.logical_not(line.upstream(direction)))(single)
                line.copy(z, direction).start()

        self._line(local, 0).at(direction, step, body)

    def end(self, local):
        place = self.place
        z = place.z
        for kind in range(3):
            self._own_load(local, kind, z).start()
        for kind in range(3):
            line = self._line(local, kind)
            target = self.cross[kind].at[z, local]
            for which, (direction, slot) in enumerate(((1, z), (-1, place.depth))):

                def come(slot=slot, which=which, line=line, kind=kind):
                    line.arrive(slot)
                    self._more_load(local, kind, slot, which).start()

                pl.when(line.upstream(direction))(come)
            self._across(local, kind, z).wait_recv()
            self._own_load(local, kind, z).wait()
            add_into(target, [self.own[kind]], 64)
            for which, (direction, slot) in enumerate(((1, z), (-1, place.depth))):

                def more(slot=slot, which=which, kind=kind, target=target):
                    self._more_load(local, kind, slot, which).wait()
                    add_into(target, [self.more[kind].at[which]], 64)

                pl.when(line.upstream(direction))(more)
            self._store(local, kind).start()

    def _store(self, local, kind):
        return pltpu.make_async_copy(
            self.cross[kind].at[self.place.z, local],
            self.outs[kind].at[local],
            self.out_sem.at[local, kind],
        )

    def drain(self):
        for local in range(self.local_count):
            for kind in range(3):
                for z in range(self.place.depth):
                    self._across(local, kind, z).wait_send()
                self._line(local, kind).drain()
                self._store(local, kind).wait()


def backward_kernel(sizes, *refs):
    place = Place(sizes)
    depth, high_count = sizes
    owners = place.owners
    (
        tokens, cot, gates, routes, gate_rows, cosine, sine_part,
        qkv_w, out_w, gain_v, n1_i, k_i, v_i, q_i, att_i, hid_i, lse_i, side_i, dn2_i,
        gsg, gsu, gsd, geg, geu, ged, outs_i, dins_i,
        mixed_o, input_o, gqkv_o, gout_o, gsg_o, gsu_o, gsd_o, geg_o, geu_o, ged_o, gain_o,
        eland_g, eland_u, eland_d, ret_in, ret_out, d_hidden_o, dn1_o,
        *rest,
    ) = refs
    count = 5
    low, rest = rest[:count], rest[count:]
    high, rest = rest[:count], rest[count:]
    line, rest = rest[:count], rest[count:]
    cross, rest = rest[:count], rest[count:]
    (
        spare_w, spare_t, ecross_g, ecross_u, ecross_d, eown_g, eown_u, eown_d,
        emore_g, emore_u, emore_d,
        d_att, dpq, dpk, dpv, g_qkv, g_out, part, part_land,
        gain_own, gain_low, gain_high, gain_line, gain_cross, out_rows,
        *sems,
    ) = rest
    dense_sems, sems = sems[:9], sems[9:]
    expert_sems, sems = sems[:6], sems[6:]
    (
        part_send, part_recv, ri_send, ri_recv, ro_send, ro_recv,
        gain_send, gain_recv, load_sem, wq_sem, out_sem,
    ) = sems
    micro_count, rows, features = tokens.shape
    prompt = depth * PB
    length = prompt + CONT
    local_count, slots = outs_i.shape[0], outs_i.shape[1]
    total = owners * local_count
    capacity = rows * 8 // (3 * total)
    me = place.e

    def rows_of(ref, size):
        return lambda s: ref.at[pl.ds(pl.multiple_of(s * size, 16), size)]

    def columns_of(ref, size):
        return lambda s: ref.at[:, pl.ds(pl.multiple_of(s * size, 128), size)]

    sources = [
        columns_of(gsg, gsg_o.shape[1]),
        columns_of(gsu, gsu_o.shape[1]),
        rows_of(gsd, gsd_o.shape[0]),
        rows_of(g_qkv, gqkv_o.shape[0]),
        rows_of(g_out, gout_o.shape[0]),
    ]
    spares = [spare_w, spare_w, spare_t, None, None]
    dense = [
        DenseScatter(
            place, sources[i], low[i], high[i], line[i], cross[i], spares[i], out,
            [s.at[i] for s in dense_sems],
        )
        for i, out in enumerate((gsg_o, gsu_o, gsd_o, gqkv_o, gout_o))
    ]
    early, late = dense[:3], dense[3:]
    experts = ExpertScatter(
        place,
        (geg, geu, ged),
        (ecross_g, ecross_u, ecross_d),
        (eland_g, eland_u, eland_d),
        (eown_g, eown_u, eown_d),
        (emore_g, emore_u, emore_d),
        (geg_o, geu_o, ged_o),
        expert_sems,
    )
    prompts = [
        LineSum(
            place,
            lambda z, m=m: part.at[m, z],
            lambda slot, m=m: part_land.at[m, slot],
            part_send.at[m],
            part_recv.at[m],
        )
        for m in range(micro_count)
    ]

    def slot_rows(m, owner_of_rows):
        return pl.ds(pl.multiple_of((m * owners + owner_of_rows) * capacity, 16), capacity)

    def hand_back(source, land, send_sem, recv_sem, m, step):
        peer = place.peer_owner(step)
        return remote(
            source.at[:, slot_rows(m, peer)],
            land.at[m, owners - step],
            send_sem.at[step, m],
            recv_sem.at[owners - step, m],
            experts=peer,
        )

    returns = [(dins_i, ret_in, ri_send, ri_recv), (outs_i, ret_out, ro_send, ro_recv)]
    place.greet()
    for m in range(micro_count):
        for step in range(1, owners):
            hand_back(*returns[0], m, step).start()
    for d in early:
        d.start()
    experts.start()
    for m in range(micro_count):
        for step in range(1, owners):
            hand_back(*returns[1], m, step).start()

    def fetch(pairs):
        copies = [
            pltpu.make_async_copy(source, target, load_sem.at[i])
            for i, (source, target) in enumerate(pairs)
        ]
        for copy in copies:
            copy.start()
        for copy in copies:
            copy.wait()

    def fetch_returned(source, land, recv_sem, target, m):
        for step in range(1, owners):
            arrived(land.at[m, step], recv_sem.at[step, m])
        pairs = []
        for step in range(owners):
            for local in range(local_count):
                at = pl.ds((step * local_count + local) * capacity, capacity)
                if step == 0:
                    piece = source.at[local, slot_rows(m, me)]
                else:
                    piece = land.at[m, step, local]
                pairs.append((piece, target.at[at]))
        fetch(pairs)

    for d in early:
        d.add_low()
    gain_own[...] = jnp.zeros_like(gain_own)

    def after_experts(hidden, extra, back, first, second, g_rows, att, d_attn, wo):
        fetch([(out_w, wo)] + [(att_i.at[m], att.at[pl.ds(m * rows, rows)]) for m in range(micro_count)])
        for m in range(micro_count):
            fetch([(hid_i.at[m], hidden), (cot.at[m], g_rows), (dn2_i.at[pl.ds(m * rows, rows)], extra)])
            for i, hit, _ in one_hots(routes.at[m], gates.at[m], me, local_count, total):
                here = pl.ds(i * capacity, capacity)
                expert = lax.rem(me * local_count + i, total)
                hit_first = either(hit, routes[m, 0:1, :] == expert)
                hit_second = either(hit, routes[m, 1:2, :] == expert)
                first[here, :] = hit_first.astype(F32).astype(BF)
                second[here, :] = hit_second.astype(F32).astype(BF)
            fetch_returned(dins_i, ret_in, ri_recv, back, m)
            gain = gain_v[1:2, :]
            for i in range(rows // PB):
                here = pl.ds(i * PB, PB)
                both = first[:, here] + second[:, here]
                d_normed = extra[here, :] + tdot(both, back[...])
                values = hidden[here, :]
                root = lax.rsqrt(jnp.mean(values * values, -1, keepdims=True) + EPSILON)
                scaled = gain * d_normed
                d_values = (
                    g_rows[here, :].astype(F32)
                    + root * scaled
                    - values * (root * root * root) * jnp.mean(values * scaled, -1, keepdims=True)
                )
                gain_own[1:2, :] += jnp.sum(d_normed * values * root, 0, keepdims=True)
                there = pl.ds(m * rows + i * PB, PB)
                extra[here, :] = d_values
                low_part = d_values.astype(BF)
                d_attn[there, :] = low_part
                d_att[there, :] = ndot(low_part, wo[...]).astype(BF)
            fetch([(extra, d_hidden_o.at[m])])
            fetch([(side_i.at[pl.ds(m * rows, rows)], extra)])
            fetch_returned(outs_i, ret_out, ro_recv, back, m)
            for i in range(rows // PB):
                here = pl.ds(i * PB, PB)
                routed = gate_rows[m, here, 0:1] * tdot(first[:, here], back[...])
                routed += gate_rows[m, here, 1:2] * tdot(second[:, here], back[...])
                out_rows[here, :] = (hidden[here, :] + extra[here, :] + routed).astype(BF)
            fetch([(out_rows, mixed_o.at[m])])
            if m < local_count:
                experts.pass_on(1, depth - 1, m)
                experts.pass_on(-1, depth - 1, m)

        def out_grad(here):
            g_out[here, :] = tdot(att[:, here], d_attn[...]).astype(BF)

        tiles(features, 256, out_grad)

    pl.run_scoped(
        after_experts,
        pltpu.VMEM((rows, features), F32),
        pltpu.VMEM((rows, features), F32),
        pltpu.VMEM((total * capacity, features), BF),
        pltpu.VMEM((total * capacity, rows), BF),
        pltpu.VMEM((total * capacity, rows), BF),
        pltpu.VMEM((rows, features), BF),
        pltpu.VMEM((micro_count * rows, features), BF),
        pltpu.VMEM((micro_count * rows, features), BF),
        pltpu.VMEM((features, features), BF),
    )
    for local in range(micro_count, local_count):
        experts.pass_on(1, depth - 1, local)
        experts.pass_on(-1, depth - 1, local)
    for d in early:
        d.add_high()
    for step in range(depth - 1, 0, -1):
        for direction in (1, -1):
            for d in early:
                if step == depth - 1:
                    d.pass_on(direction, step)

    def own_rows(i):
        start = place.z * PB if i == 0 else prompt + (i - 1) * PB
        return start, pl.ds(start if i else pl.multiple_of(start, PB), PB)

    def attention(k, v, q, lse, ds_s, p_s, wq, dn1):
        load_wq = pltpu.make_async_copy(qkv_w, wq, wq_sem.at[0])
        load_wq.start()
        lane = lax.broadcasted_iota(jnp.int32, (PB, 2 * HD), 1)
        wide_lane = lax.broadcasted_iota(jnp.int32, (rows, 2 * HD), 1)
        column = lax.broadcasted_iota(jnp.int32, (PB, length), 1)
        row = lax.broadcasted_iota(jnp.int32, (PB, length), 0)
        for m in range(micro_count):
            fetch([(k_i.at[m], k), (v_i.at[m], v), (q_i.at[m], q), (lse_i.at[m], lse)])
            whole = pl.ds(m * rows, rows)

            def pair(index, carry):
                lanes = pl.ds(pl.multiple_of(index * 2 * HD, 2 * HD), 2 * HD)
                keys, values = k[:, lanes], v[:, lanes]
                for i in range(rows // PB):
                    here = pl.ds(i * PB, PB)
                    there = pl.ds(m * rows + i * PB, PB)
                    query, d_out, logs = q[here, lanes], d_att[there, lanes], lse[here, :]
                    start, table = own_rows(i)
                    allowed = column <= row + start
                    parts = []
                    for sub in range(2):
                        mine = lane // HD == sub
                        scores = ndot(jnp.where(mine, query, jnp.zeros_like(query)), keys)
                        log = jnp.sum(
                            jnp.where(lane == 2 * index + sub, logs, 0.0), -1, keepdims=True
                        )
                        probs = jnp.where(allowed, jnp.exp(scores - log), 0.0)
                        d_probs = ndot(jnp.where(mine, d_out, jnp.zeros_like(d_out)), values)
                        centre = jnp.sum(probs * d_probs, -1, keepdims=True)
                        d_scores = (probs * (d_probs - centre)).astype(BF)
                        ds_s[sub, here, :] = d_scores
                        p_s[sub, here, :] = probs.astype(BF)
                        parts.append(mdot(d_scores, keys))
                    d_query = jnp.where(lane < HD, parts[0], parts[1]) * HD**-0.5
                    d_query = rope(d_query, cosine[table, :], -sine_part[table, :])
                    dpq[there, lanes] = d_query.astype(BF)
                d_key = jnp.zeros((length, 2 * HD), F32)
                d_value = jnp.zeros((length, 2 * HD), F32)
                query, d_out = q[:, lanes], d_att[whole, lanes]
                for sub in range(2):
                    mine = wide_lane // HD == sub
                    d_key += tdot(ds_s[sub], jnp.where(mine, query, jnp.zeros_like(query)))
                    d_value += tdot(p_s[sub], jnp.where(mine, d_out, jnp.zeros_like(d_out)))
                keys_here = pl.ds(m * length, length)
                d_key = rope(d_key, cosine[...], -sine_part[...])
                dpk[keys_here, lanes] = d_key.astype(BF)
                dpv[keys_here, lanes] = d_value.astype(BF)
                return carry

            lax.fori_loop(0, features // (2 * HD), pair, 0)
            if m == 0:
                load_wq.wait()
            key_w, value_w = wq[pl.ds(features, features), :], wq[pl.ds(2 * features, features), :]
            for z in range(depth):
                here = pl.ds(m * length + z * PB, PB)
                part[m, z] = (mdot(dpk[here, :], key_w) + mdot(dpv[here, :], value_w)).astype(BF)
            for step in range(depth - 1, 0, -1):
                if step == depth - 1:
                    for direction in (1, -1):
                        prompts[m].pass_on(direction, step, lambda t, s: add_into(t, [s], 64))
            for i in range(rows // PB):
                _, table = own_rows(i)
                start = own_rows(i)[0] + m * length
                here = pl.ds(pl.multiple_of(start, PB), PB)
                there = pl.ds(m * rows + i * PB, PB)
                dn1[pl.ds(i * PB, PB), :] = (
                    mdot(dpq[there, :], wq[pl.ds(0, features), :])
                    + mdot(dpk[here, :], key_w)
                    + mdot(dpv[here, :], value_w)
                )
            fetch([(dn1, dn1_o.at[m])])
            for local in range(local_count):
                for direction in (1, -1):
                    if depth > 2 and m == 0:
                        experts.pass_on(direction, depth - 2, local)
            for step in range(depth - 2, 0, -1):
                for direction in (1, -1):
                    prompts[m].pass_on(direction, step, lambda t, s: add_into(t, [s], 64))
            if m == 0:
                for step in range(depth - 2, 0, -1):
                    for direction in (1, -1):
                        for d in early:
                            d.pass_on(direction, step)

    pl.run_scoped(
        attention,
        pltpu.VMEM((length, features), BF),
        pltpu.VMEM((length, features), BF),
        pltpu.VMEM((rows, features), BF),
        pltpu.VMEM((rows, 2 * HD), F32),
        pltpu.VMEM((2, rows, length), BF),
        pltpu.VMEM((2, rows, length), BF),
        pltpu.VMEM(qkv_w.shape, BF),
        pltpu.VMEM((rows, features), F32),
    )

    def weight_grads(n1, n1_own):
        pairs = []
        for m in range(micro_count):
            pairs.append((n1_i.at[m], n1.at[pl.ds(m * length, length)]))
            for i in range(rows // PB):
                _, here = own_rows(i)
                pairs.append((n1_i.at[m, here], n1_own.at[pl.ds(m * rows + i * PB, PB)]))
        fetch(pairs)

        def make(here):
            g_qkv[here, :] = tdot(dpq[:, here], n1_own[...]).astype(BF)

        def make_key(here):
            there = pl.ds(pl.multiple_of(here.start + features, 256), 256)
            g_qkv[there, :] = tdot(dpk[:, here], n1[...]).astype(BF)

        def make_value(here):
            there = pl.ds(pl.multiple_of(here.start + 2 * features, 256), 256)
            g_qkv[there, :] = tdot(dpv[:, here], n1[...]).astype(BF)

        tiles(features, 256, make)
        tiles(features, 256, make_key)
        tiles(features, 256, make_value)

    pl.run_scoped(
        weight_grads,
        pltpu.VMEM((micro_count * length, features), BF),
        pltpu.VMEM((micro_count * rows, features), BF),
    )
    for d in late:
        d.start()
    for local in range(local_count):
        for step in range(depth - 3, 0, -1):
            for direction in (1, -1):
                experts.pass_on(direction, step, local)
    for d in late:
        d.add_low()
    for d in early:
        d.end()

    def inputs(x_rows, d_hidden, dn1):
        for m in range(micro_count):
            fetch([(tokens.at[m], x_rows), (d_hidden_o.at[m], d_hidden), (dn1_o.at[m], dn1)])
            for direction, slot in ((1, place.z), (-1, depth)):

                def body(m=m, slot=slot):
                    prompts[m].arrive(slot)
                    dn1[pl.ds(0, PB), :] += part_land[m, slot].astype(F32)

                pl.when(prompts[m].upstream(direction))(body)
            gain = gain_v[0:1, :]
            for i in range(rows // PB):
                here = pl.ds(i * PB, PB)
                values, d_normed = x_rows[here, :].astype(F32), dn1[here, :]
                root = lax.rsqrt(jnp.mean(values * values, -1, keepdims=True) + EPSILON)
                scaled = gain * d_normed
                d_values = (
                    d_hidden[here, :]
                    + root * scaled
                    - values * (root * root * root) * jnp.mean(values * scaled, -1, keepdims=True)
                )
                gain_own[0:1, :] += jnp.sum(d_normed * values * root, 0, keepdims=True)
                out_rows[here, :] = d_values.astype(BF)
            fetch([(out_rows, input_o.at[m])])

    pl.run_scoped(
        inputs,
        pltpu.VMEM((rows, features), BF),
        pltpu.VMEM((rows, features), F32),
        pltpu.VMEM((rows, features), F32),
    )
    for d in late:
        d.add_high()
    for step in range(depth - 1, 0, -1):
        for direction in (1, -1):
            for d in late:
                d.pass_on(direction, step)

    def stage(first, targets, lands):
        copies = [
            remote(gain_own, land, gain_send.at[first + i], gain_recv.at[first + i], **target)
            for i, (target, land) in enumerate(zip(targets, lands))
        ]
        for copy in copies:
            copy.start()
        for copy in copies:
            copy.wait()
        total_gain = gain_own[...]
        for land in lands:
            total_gain = total_gain + land[...]
        gain_own[...] = total_gain

    stage(0, [dict(experts=place.e + 1 - 2 * place.low)], [gain_low])
    stage(
        1,
        [dict(experts=place.peer_high(s) * 2 + place.low) for s in range(1, high_count)],
        [gain_high.at[s - 1] for s in range(1, high_count)],
    )
    stage(
        high_count,
        [dict(context=lax.rem(place.z + s, depth)) for s in range(1, depth)],
        [gain_line.at[s - 1] for s in range(1, depth)],
    )
    stage(high_count + depth - 1, [dict(dp=1 - place.x)], [gain_cross])
    for local in range(local_count):
        experts.end(local)
    for d in late:
        d.end()
    for d in dense:
        d.finish()
    fetch([(gain_own, gain_o)])
    for d in dense:
        d.drain()
    experts.drain()
    for p in prompts:
        p.drain()
    for m in range(micro_count):
        for step in range(1, owners):
            for entry in returns:
                hand_back(*entry, m, step).wait_send()


def run_backward(sizes, tokens, cot, gates, routes, gate_rows, forward):
    depth, high_count = sizes
    micro_count, rows, features = tokens.shape
    owners = high_count * 2
    line = depth * owners
    prompt = depth * PB
    length = prompt + CONT
    cosine, sine_part = rope_tables(prompt)
    gsg, geg, outs = forward[12], forward[15], forward[18]
    local_count, slots, _ = outs.shape
    total = owners * local_count
    capacity = rows * 8 // (3 * total)
    part = gsg.shape[1] // line
    width = geg.shape[2] // (2 * depth)
    hbm, vmem = pl.BlockSpec(memory_space=pltpu.HBM), pl.BlockSpec(memory_space=pltpu.VMEM)
    shapes = [(features, part), (features, part), (part, features)]
    shapes += [(forward[0].shape[0] // line, features), (forward[1].shape[0] // line, features)]
    expert_shapes = [(features, width), (features, width), (width, features)]
    returned = (micro_count, owners, local_count, capacity, features)
    out_dims = [(micro_count, rows, features)] * 2
    out_dims += [shapes[3], shapes[4], shapes[0], shapes[1], shapes[2]]
    out_dims += [(local_count,) + s for s in expert_shapes]
    out_shape = [jax.ShapeDtypeStruct(dims, BF) for dims in out_dims]
    out_shape += [jax.ShapeDtypeStruct((8, features), F32)]
    out_shape += [jax.ShapeDtypeStruct((depth + 1, local_count) + s, BF) for s in expert_shapes]
    out_shape += [jax.ShapeDtypeStruct(returned, BF)] * 2
    out_shape += [jax.ShapeDtypeStruct((micro_count, rows, features), F32)] * 2
    scratch = [pltpu.VMEM((depth, high_count) + s, BF) for s in shapes]
    scratch += [pltpu.VMEM((high_count - 1, depth) + s, BF) for s in shapes]
    scratch += [pltpu.VMEM((depth + 1,) + s, BF) for s in shapes]
    scratch += [pltpu.VMEM(s, BF) for s in shapes]
    scratch += [pltpu.VMEM((2,) + shapes[0], BF), pltpu.VMEM((2,) + shapes[2], BF)]
    scratch += [pltpu.VMEM((depth, local_count) + s, BF) for s in expert_shapes]
    scratch += [pltpu.VMEM(s, BF) for s in expert_shapes]
    scratch += [pltpu.VMEM((2,) + s, BF) for s in expert_shapes]
    token_rows, key_rows = micro_count * rows, micro_count * length
    gain = (8, features)
    scratch += [
        pltpu.VMEM((token_rows, features), BF),
        pltpu.VMEM((token_rows, features), BF),
        pltpu.VMEM((key_rows, features), BF),
        pltpu.VMEM((key_rows, features), BF),
        pltpu.VMEM(forward[0].shape, BF),
        pltpu.VMEM(forward[1].shape, BF),
        pltpu.VMEM((micro_count, depth, PB, features), BF),
        pltpu.VMEM((micro_count, depth + 1, PB, features), BF),
        pltpu.VMEM(gain, F32),
        pltpu.VMEM(gain, F32),
        pltpu.VMEM((high_count - 1,) + gain, F32),
        pltpu.VMEM((depth - 1,) + gain, F32),
        pltpu.VMEM(gain, F32),
        pltpu.VMEM((rows, features), BF),
    ]
    dma = pltpu.SemaphoreType.DMA
    scratch += DenseScatter.semaphores(len(shapes), depth, high_count)
    scratch += ExpertScatter.semaphores(depth, local_count)
    stages = 1 + high_count + depth
    scratch += [
        dma((micro_count, depth + 1)),
        dma((micro_count, depth + 1)),
        dma((owners, micro_count)),
        dma((owners, micro_count)),
        dma((owners, micro_count)),
        dma((owners, micro_count)),
        dma((stages,)),
        dma((stages,)),
        dma((max(total, 2 + micro_count, 4 * micro_count + micro_count),)),
        dma((1,)),
        dma((1,)),
    ]
    return pl.pallas_call(
        functools.partial(backward_kernel, sizes),
        out_shape=out_shape,
        in_specs=[hbm] * 2 + [vmem] * 5 + [hbm] * 2 + [vmem] + [hbm] * 17,
        out_specs=[hbm] * len(out_shape),
        scratch_shapes=scratch,
        compiler_params=pltpu.CompilerParams(
            collective_id=1, has_side_effects=True, vmem_limit_bytes=60 * MIB
        ),
        name="backward_and_sum",
    )(tokens, cot, gates, routes, gate_rows, cosine, sine_part, *forward)


def on_device_plain(
    tokens,
    cotangent,
    gates,
    routes,
    qkv_weight,
    out_weight,
    shared_gate,
    shared_up,
    shared_down,
    gains,
    expert_gate,
    expert_up,
    expert_down,
):
    micro_count = tokens.shape[2]
    row_count = tokens.shape[4]
    feature_count = tokens.shape[5]
    owners = lax.axis_size(EXPERTS)
    local_experts = expert_gate.shape[0]
    total_experts = owners * local_experts
    capacity = row_count * 8 // (3 * total_experts)
    blocks = lax.axis_size(CONTEXT)
    prompt = blocks * PB
    scaling = HD ** (-0.5)
    w_qkv, w_out, w_sgate, w_sup, w_sdown, w_gains = (
        lax.all_gather(qkv_weight, (CONTEXT, EXPERTS), axis=1, tiled=True),
        lax.all_gather(out_weight, (CONTEXT, EXPERTS), axis=0, tiled=True),
        lax.all_gather(shared_gate, (CONTEXT, EXPERTS), axis=1, tiled=True),
        lax.all_gather(shared_up, (CONTEXT, EXPERTS), axis=1, tiled=True),
        lax.all_gather(shared_down, (CONTEXT, EXPERTS), axis=0, tiled=True),
        lax.all_gather(gains, (CONTEXT, EXPERTS), axis=1, tiled=True),
    )
    e_gate, expert_up_weight, e_down = (
        lax.all_gather(expert_gate, (DP, CONTEXT), axis=2, tiled=True),
        lax.all_gather(expert_up, (DP, CONTEXT), axis=2, tiled=True),
        lax.all_gather(expert_down, (DP, CONTEXT), axis=1, tiled=True),
    )
    gain_one = w_gains[0].astype(jnp.float32)
    gain_two = w_gains[1].astype(jnp.float32)
    here_index = lax.axis_index(CONTEXT)
    row_ids = jnp.arange(row_count, dtype=jnp.int32)
    query_pos = jnp.where(row_ids < PB, here_index * PB + row_ids, prompt + row_ids - PB)
    key_pos = jnp.arange(prompt + CONT, dtype=jnp.int32)
    allowed = key_pos[None, None, :] <= query_pos[None, :, None]
    half_size = HD // 2
    frequency = 10000.0 ** (-2.0 * jnp.arange(half_size, dtype=jnp.float32) / HD)
    angles = query_pos.astype(jnp.float32)[:, None] * frequency
    cosine = jnp.cos(angles)[:, None, :]
    sine_part = jnp.sin(angles)[:, None, :]
    kept_list = []
    mixed_list = []
    for step_index in range(micro_count):
        inputs = tokens[0, 0, step_index, 0].astype(jnp.float32)
        root_one = lax.rsqrt(jnp.mean(inputs * inputs, -1, keepdims=True) + EPSILON)
        normed_one = (inputs * root_one * gain_one).astype(jnp.bfloat16)
        projected = mdot(normed_one, w_qkv)
        query = rotate(projected[:, :feature_count], cosine, sine_part).astype(jnp.bfloat16)
        key_rows = rotate(
            projected[:, feature_count : 2 * feature_count], cosine, sine_part
        ).astype(jnp.bfloat16)
        value_rows = projected[:, 2 * feature_count :].astype(jnp.bfloat16)
        prompt_key, prompt_value = (
            lax.all_gather(key_rows[:PB], CONTEXT, axis=0, tiled=True),
            lax.all_gather(value_rows[:PB], CONTEXT, axis=0, tiled=True),
        )
        key_heads = jnp.concatenate([prompt_key, key_rows[PB:]], 0).reshape(prompt + CONT, H, HD)
        value_heads = jnp.concatenate([prompt_value, value_rows[PB:]], 0).reshape(
            prompt + CONT, H, HD
        )
        query_heads = query.reshape(row_count, H, HD)
        scores = (
            jnp.einsum("qhd,khd->hqk", query_heads, key_heads, preferred_element_type=jnp.float32)
            * scaling
        )
        scores = jnp.where(allowed, scores, -1000000000.0)
        highest = jnp.max(scores, -1, keepdims=True)
        weights = jnp.exp(scores - highest)
        total = jnp.sum(weights, -1, keepdims=True)
        log_total = highest + jnp.log(total)
        probs = (weights / total).astype(jnp.bfloat16)
        attended = (
            jnp.einsum("hqk,khd->qhd", probs, value_heads, preferred_element_type=jnp.float32)
            .reshape(row_count, feature_count)
            .astype(jnp.bfloat16)
        )
        hidden = inputs + mdot(attended, w_out)
        root_two = lax.rsqrt(jnp.mean(hidden * hidden, -1, keepdims=True) + EPSILON)
        normed_two = (hidden * root_two * gain_two).astype(jnp.bfloat16)
        side_gate = mdot(normed_two, w_sgate)
        side_up = mdot(normed_two, w_sup)
        side_act = (jax.nn.silu(side_gate) * side_up).astype(jnp.bfloat16)
        side = mdot(side_act, w_sdown)
        route_rows = routes[0, 0, step_index, 0]
        slots = slot_table(route_rows, total_experts)
        flat_dest = (route_rows * capacity + slots).reshape(-1)
        source = (
            jnp.full((total_experts * capacity,), 2 * row_count, jnp.int32)
            .at[flat_dest]
            .set(jnp.arange(2 * row_count, dtype=jnp.int32))
        )
        padded = jnp.concatenate([normed_two, jnp.zeros((1, feature_count), jnp.bfloat16)], 0)
        send = padded[source // 2].reshape(total_experts, capacity, feature_count)
        received = lax.all_to_all(send, EXPERTS, split_axis=0, concat_axis=0, tiled=True)
        count = received.shape[1]
        expert_grouped = received.reshape(owners, local_experts, count, feature_count)
        expert_gate_act = jnp.einsum(
            "send,edf->senf", expert_grouped, e_gate, preferred_element_type=jnp.float32
        )
        expert_up_act = jnp.einsum(
            "send,edf->senf", expert_grouped, expert_up_weight, preferred_element_type=jnp.float32
        )
        expert_hidden_act = (jax.nn.silu(expert_gate_act) * expert_up_act).astype(jnp.bfloat16)
        result = jnp.einsum(
            "senf,efd->send", expert_hidden_act, e_down, preferred_element_type=jnp.float32
        ).astype(jnp.bfloat16)
        expert_out = result.reshape(owners * local_experts, count, feature_count)
        expert_in = received
        returned = lax.all_to_all(
            expert_out, EXPERTS, split_axis=0, concat_axis=0, tiled=True
        ).reshape(-1, feature_count)
        gate_rows = gates[0, 0, step_index, 0]
        picked = returned[flat_dest].reshape(row_count, 2, feature_count).astype(jnp.float32)
        routed = jnp.sum(gate_rows[:, :, None] * picked, 1)
        mixed_list.append((hidden + routed + side).astype(jnp.bfloat16))
        cached = (prompt_key, prompt_value)
        kept_list.append(
            (
                inputs,
                root_one,
                normed_one,
                query,
                key_rows,
                value_rows,
                cached,
                log_total,
                attended,
                hidden,
                root_two,
                normed_two,
                side_gate,
                side_up,
                side_act,
                flat_dest,
                source,
                expert_in,
                gate_rows,
            )
        )
    acc_qkv = jnp.zeros(w_qkv.shape, jnp.float32)
    acc_out = jnp.zeros(w_out.shape, jnp.float32)
    acc_sgate = jnp.zeros(w_sgate.shape, jnp.float32)
    acc_sup = jnp.zeros(w_sup.shape, jnp.float32)
    acc_sdown = jnp.zeros(w_sdown.shape, jnp.float32)
    acc_gain_one = jnp.zeros((feature_count,), jnp.float32)
    acc_gain_two = jnp.zeros((feature_count,), jnp.float32)
    local_egate = jnp.zeros(e_gate.shape, jnp.float32)
    local_expert_up_weight = jnp.zeros(expert_up_weight.shape, jnp.float32)
    local_edown = jnp.zeros(e_down.shape, jnp.float32)
    input_list = []
    for step_index in range(micro_count):
        (
            inputs,
            root_one,
            normed_one,
            query,
            key_rows,
            value_rows,
            cached,
            log_total,
            attended,
            hidden,
            root_two,
            normed_two,
            side_gate,
            side_up,
            side_act,
            flat_dest,
            source,
            expert_in,
            gate_rows,
        ) = kept_list[step_index]
        grad_rows = cotangent[0, 0, step_index, 0].astype(jnp.float32)
        grad_low = grad_rows.astype(jnp.bfloat16)
        acc_sdown = acc_sdown + tdot(side_act, grad_low)
        d_side_act = ndot(grad_low, w_sdown).astype(jnp.bfloat16).astype(jnp.float32)
        silu_side, slope_side = silu_parts(side_gate)
        d_side_gate = (d_side_act * side_up * slope_side).astype(jnp.bfloat16)
        d_side_up = (d_side_act * silu_side).astype(jnp.bfloat16)
        acc_sgate = acc_sgate + tdot(normed_two, d_side_gate)
        acc_sup = acc_sup + tdot(normed_two, d_side_up)
        d_normed_two = ndot(d_side_gate, w_sgate) + ndot(d_side_up, w_sup)
        d_pairs = (
            (gate_rows[:, :, None] * grad_rows[:, None, :])
            .astype(jnp.bfloat16)
            .reshape(2 * row_count, feature_count)
        )
        padded_grad = jnp.concatenate([d_pairs, jnp.zeros((1, feature_count), jnp.bfloat16)], 0)
        grad_send = padded_grad[source].reshape(total_experts, capacity, feature_count)
        grad_in = lax.all_to_all(grad_send, EXPERTS, split_axis=0, concat_axis=0, tiled=True)
        grouped_grad = grad_in.reshape(owners, local_experts, capacity, feature_count)
        grouped = expert_in.reshape(owners, local_experts, capacity, feature_count)
        gate_act = jnp.einsum("send,edf->senf", grouped, e_gate, preferred_element_type=jnp.float32)
        up_act = jnp.einsum(
            "send,edf->senf", grouped, expert_up_weight, preferred_element_type=jnp.float32
        )
        silu_gate, slope_gate = silu_parts(gate_act)
        hidden_act = (silu_gate * up_act).astype(jnp.bfloat16)
        d_hidden_act = (
            jnp.einsum("send,efd->senf", grouped_grad, e_down, preferred_element_type=jnp.float32)
            .astype(jnp.bfloat16)
            .astype(jnp.float32)
        )
        d_gate_act = (d_hidden_act * up_act * slope_gate).astype(jnp.bfloat16)
        d_up_act = (d_hidden_act * silu_gate).astype(jnp.bfloat16)
        step_edown = jnp.einsum(
            "senf,send->efd", hidden_act, grouped_grad, preferred_element_type=jnp.float32
        )
        step_egate = jnp.einsum(
            "send,senf->edf", grouped, d_gate_act, preferred_element_type=jnp.float32
        )
        stepwise_expert_up = jnp.einsum(
            "send,senf->edf", grouped, d_up_act, preferred_element_type=jnp.float32
        )
        local_egate = local_egate + step_egate
        local_expert_up_weight = local_expert_up_weight + stepwise_expert_up
        local_edown = local_edown + step_edown
        d_expert_in = jnp.einsum(
            "senf,edf->send", d_gate_act, e_gate, preferred_element_type=jnp.float32
        ) + jnp.einsum(
            "senf,edf->send", d_up_act, expert_up_weight, preferred_element_type=jnp.float32
        )
        d_expert_in = d_expert_in.astype(jnp.bfloat16).reshape(
            total_experts, capacity, feature_count
        )
        back = lax.all_to_all(
            d_expert_in, EXPERTS, split_axis=0, concat_axis=0, tiled=True
        ).reshape(-1, feature_count)
        d_normed_two = d_normed_two + jnp.sum(
            back[flat_dest].reshape(row_count, 2, feature_count).astype(jnp.float32), 1
        )
        scaled_two = gain_two * d_normed_two
        d_hidden = (
            grad_rows
            + root_two * scaled_two
            - hidden * root_two**3 * jnp.mean(hidden * scaled_two, -1, keepdims=True)
        )
        acc_gain_two = acc_gain_two + jnp.sum(d_normed_two * hidden * root_two, 0)
        d_attn = d_hidden.astype(jnp.bfloat16)
        acc_out = acc_out + tdot(attended, d_attn)
        d_attended = ndot(d_attn, w_out).astype(jnp.bfloat16)
        prompt_key, prompt_value = cached
        key_heads = jnp.concatenate([prompt_key, key_rows[PB:]], 0).reshape(prompt + CONT, H, HD)
        value_heads = jnp.concatenate([prompt_value, value_rows[PB:]], 0).reshape(
            prompt + CONT, H, HD
        )
        query_heads = query.reshape(row_count, H, HD)
        scores = (
            jnp.einsum("qhd,khd->hqk", query_heads, key_heads, preferred_element_type=jnp.float32)
            * scaling
        )
        scores = jnp.where(allowed, scores, -1000000000.0)
        probs = jnp.exp(scores - log_total)
        d_heads = d_attended.reshape(row_count, H, HD)
        d_probs = jnp.einsum(
            "qhd,khd->hqk", d_heads, value_heads, preferred_element_type=jnp.float32
        )
        centre = jnp.sum(probs * d_probs, -1, keepdims=True)
        d_scores = (probs * (d_probs - centre)).astype(jnp.bfloat16)
        d_query = (
            jnp.einsum(
                "hqk,khd->qhd", d_scores, key_heads, preferred_element_type=jnp.float32
            ).reshape(row_count, feature_count)
            * scaling
        )
        d_keys = (
            jnp.einsum(
                "hqk,qhd->khd", d_scores, query_heads, preferred_element_type=jnp.float32
            ).reshape(prompt + CONT, feature_count)
            * scaling
        )
        d_values = jnp.einsum(
            "hqk,qhd->khd", probs.astype(jnp.bfloat16), d_heads, preferred_element_type=jnp.float32
        ).reshape(prompt + CONT, feature_count)
        own_dkey, own_dvalue = (
            lax.psum_scatter(
                d_keys[:prompt].astype(jnp.bfloat16), CONTEXT, scatter_dimension=0, tiled=True
            ).astype(jnp.float32),
            lax.psum_scatter(
                d_values[:prompt].astype(jnp.bfloat16), CONTEXT, scatter_dimension=0, tiled=True
            ).astype(jnp.float32),
        )
        d_key_rows = jnp.concatenate([own_dkey, d_keys[prompt:]], 0)
        d_value_rows = jnp.concatenate([own_dvalue, d_values[prompt:]], 0)
        d_projected = jnp.concatenate(
            [
                rotate(d_query, cosine, -sine_part).astype(jnp.bfloat16),
                rotate(d_key_rows, cosine, -sine_part).astype(jnp.bfloat16),
                d_value_rows.astype(jnp.bfloat16),
            ],
            1,
        )
        acc_qkv = acc_qkv + tdot(normed_one, d_projected)
        d_normed_one = ndot(d_projected, w_qkv)
        scaled_one = gain_one * d_normed_one
        d_inputs = (
            d_hidden
            + root_one * scaled_one
            - inputs * root_one**3 * jnp.mean(inputs * scaled_one, -1, keepdims=True)
        )
        acc_gain_one = acc_gain_one + jnp.sum(d_normed_one * inputs * root_one, 0)
        input_list.append(d_inputs.astype(jnp.bfloat16))
    sharded_expert_gate, sharded_expert_up, sharded_expert_down = (
        lax.psum_scatter(
            local_egate.astype(jnp.bfloat16), (DP, CONTEXT), scatter_dimension=2, tiled=True
        ).astype(jnp.float32),
        lax.psum_scatter(
            local_expert_up_weight.astype(jnp.bfloat16),
            (DP, CONTEXT),
            scatter_dimension=2,
            tiled=True,
        ).astype(jnp.float32),
        lax.psum_scatter(
            local_edown.astype(jnp.bfloat16), (DP, CONTEXT), scatter_dimension=1, tiled=True
        ).astype(jnp.float32),
    )
    acc_gains = jnp.stack([acc_gain_one, acc_gain_two], 0)
    dense_shards = (
        lax.psum_scatter(acc_qkv, (CONTEXT, EXPERTS), scatter_dimension=1, tiled=True),
        lax.psum_scatter(acc_out, (CONTEXT, EXPERTS), scatter_dimension=0, tiled=True),
        lax.psum_scatter(acc_sgate, (CONTEXT, EXPERTS), scatter_dimension=1, tiled=True),
        lax.psum_scatter(acc_sup, (CONTEXT, EXPERTS), scatter_dimension=1, tiled=True),
        lax.psum_scatter(acc_sdown, (CONTEXT, EXPERTS), scatter_dimension=0, tiled=True),
        lax.psum_scatter(acc_gains, (CONTEXT, EXPERTS), scatter_dimension=1, tiled=True),
    )
    grad_qkv, grad_out, grad_sgate, grad_sup, grad_sdown, grad_gains = (
        lax.psum(dense_shards[0].astype(jnp.bfloat16), DP).astype(jnp.float32),
        lax.psum(dense_shards[1].astype(jnp.bfloat16), DP).astype(jnp.float32),
        lax.psum(dense_shards[2].astype(jnp.bfloat16), DP).astype(jnp.float32),
        lax.psum(dense_shards[3].astype(jnp.bfloat16), DP).astype(jnp.float32),
        lax.psum(dense_shards[4].astype(jnp.bfloat16), DP).astype(jnp.float32),
        lax.psum(dense_shards[5].astype(jnp.bfloat16), DP).astype(jnp.float32),
    )
    mixed = jnp.stack(mixed_list, 0).reshape(tokens.shape)
    input_grad = jnp.stack(input_list, 0).reshape(tokens.shape)
    return (
        mixed,
        input_grad,
        grad_qkv,
        grad_out,
        grad_sgate,
        grad_sup,
        grad_sdown,
        grad_gains,
        sharded_expert_gate,
        sharded_expert_up,
        sharded_expert_down,
    )


def on_device(
    tokens,
    cotangent,
    gates,
    routes,
    qkv_weight,
    out_weight,
    shared_gate,
    shared_up,
    shared_down,
    gains,
    expert_gate,
    expert_up,
    expert_down,
):
    owners = lax.axis_size(EXPERTS)
    sizes = (lax.axis_size(CONTEXT), owners // 2)
    own_at = lax.axis_index(CONTEXT) * owners + lax.axis_index(EXPERTS)
    gain_width, features = gains.shape[1], tokens.shape[5]
    gain_rows = lax.dynamic_update_slice(
        jnp.zeros((16, features), jnp.bfloat16), gains, (0, own_at * gain_width)
    )
    rows, cot = tokens[0, 0, :, 0], cotangent[0, 0, :, 0]
    gate_rows, route_rows = gates[0, 0, :, 0], routes[0, 0, :, 0]
    gate_columns, route_columns = gate_rows.transpose(0, 2, 1), route_rows.transpose(0, 2, 1)
    forward = run_forward(
        sizes,
        rows,
        cot,
        gate_columns,
        route_columns,
        (qkv_weight.T, out_weight, gain_rows, shared_gate, shared_up, shared_down),
        (expert_gate, expert_up, expert_down),
    )
    (
        mixed, input_grad, grad_qkv, grad_out, grad_sgate, grad_sup, grad_sdown,
        grad_egate, grad_eup, grad_edown, gain_sum, *_,
    ) = run_backward(
        sizes, rows, cot, gate_columns, route_columns, gate_rows, forward[:3] + forward[9:]
    )
    return (
        mixed.reshape(tokens.shape),
        input_grad.reshape(tokens.shape),
        grad_qkv.T.astype(F32),
        grad_out.astype(F32),
        grad_sgate.astype(F32),
        grad_sup.astype(F32),
        grad_sdown.astype(F32),
        lax.dynamic_slice(gain_sum, (0, own_at * gain_width), (2, gain_width)),
        grad_egate.astype(F32),
        grad_eup.astype(F32),
        grad_edown.astype(F32),
    )


def kernels_fit(mesh_shape, arrays):
    qkv_weight, out_weight, shared_gate, _, shared_down = arrays[4:9]
    rows = (qkv_weight.shape[1], out_weight.shape[0], shared_gate.shape[1], shared_down.shape[0])
    return (
        mesh_shape[DP] == 2
        and mesh_shape[EXPERTS] % 2 == 0
        and all(count % 16 == 0 for count in rows)
        and shared_gate.shape[1] % 128 == 0
        and arrays[10].shape[2] % 128 == 0
    )


def solution(mesh):
    def device_program(*arrays):
        return (on_device if kernels_fit(mesh.shape, arrays) else on_device_plain)(*arrays)

    return jax.shard_map(
        device_program,
        mesh=mesh,
        in_specs=(
            P(DP, EXPERTS, None, CONTEXT, None, None),
            P(DP, EXPERTS, None, CONTEXT, None, None),
            P(DP, EXPERTS, None, CONTEXT, None, None),
            P(DP, EXPERTS, None, CONTEXT, None, None),
            P(None, (CONTEXT, EXPERTS)),
            P((CONTEXT, EXPERTS), None),
            P(None, (CONTEXT, EXPERTS)),
            P(None, (CONTEXT, EXPERTS)),
            P((CONTEXT, EXPERTS), None),
            P(None, (CONTEXT, EXPERTS)),
            P(EXPERTS, None, (DP, CONTEXT)),
            P(EXPERTS, None, (DP, CONTEXT)),
            P(EXPERTS, (DP, CONTEXT), None),
        ),
        out_specs=(
            P(DP, EXPERTS, None, CONTEXT, None, None),
            P(DP, EXPERTS, None, CONTEXT, None, None),
            P(None, (CONTEXT, EXPERTS)),
            P((CONTEXT, EXPERTS), None),
            P(None, (CONTEXT, EXPERTS)),
            P(None, (CONTEXT, EXPERTS)),
            P((CONTEXT, EXPERTS), None),
            P(None, (CONTEXT, EXPERTS)),
            P(EXPERTS, None, (DP, CONTEXT)),
            P(EXPERTS, None, (DP, CONTEXT)),
            P(EXPERTS, (DP, CONTEXT), None),
        ),
        check_vma=False,
    )
```

```python
import functools

import jax
import jax.numpy as jnp
import numpy as np
from jax import lax
from jax.experimental import pallas as pl
from jax.experimental.pallas import tpu as pltpu
from jax.sharding import PartitionSpec as P

DP, CONTEXT, EXPERTS = "dp", "context", "experts"

H = 12
HD = 64
PB = 128
CONT = 256


EPSILON = 1e-06


def mdot(former, latter):
    return jnp.dot(former, latter, preferred_element_type=jnp.float32)


def tdot(former, latter):
    return lax.dot_general(
        former, latter, (((0,), (0,)), ((), ())), preferred_element_type=jnp.float32
    )


def ndot(former, latter):
    return lax.dot_general(
        former, latter, (((1,), (1,)), ((), ())), preferred_element_type=jnp.float32
    )


def rotate(values, cosine, sine_part):
    half_size = HD // 2
    shaped = values.reshape(values.shape[0], H, HD)
    former = shaped[..., :half_size]
    latter = shaped[..., half_size:]
    turned = jnp.concatenate(
        [former * cosine - latter * sine_part, latter * cosine + former * sine_part], -1
    )
    return turned.reshape(values.shape)


def slot_table(routes_block, expert_count):
    flat_routes = routes_block.reshape(-1)
    onehot = (flat_routes[:, None] == jnp.arange(expert_count, dtype=jnp.int32)[None, :]).astype(
        jnp.int32
    )
    before = jnp.cumsum(onehot, 0) - onehot
    return jnp.sum(before * onehot, 1).reshape(routes_block.shape)


def silu_parts(values):
    sigma = jax.nn.sigmoid(values)
    return (values * sigma, sigma * (1.0 + values * (1.0 - sigma)))


MESH = pl.DeviceIdType.MESH
MIB = 1024 * 1024
BF = jnp.bfloat16
F32 = jnp.float32


def remote(source, target, send_sem, recv_sem, **device):
    return pltpu.make_async_remote_copy(
        src_ref=source,
        dst_ref=target,
        send_sem=send_sem,
        recv_sem=recv_sem,
        device_id=device,
        device_id_type=MESH,
    )


def arrived(slot, recv_sem):
    remote(slot, slot, recv_sem, recv_sem, context=0).wait_recv()


def either(first, second):
    return jnp.logical_and(first, second)


class Place:
    def __init__(self, sizes):
        self.depth, self.high_count = sizes
        self.owners = self.high_count * 2
        self.x = lax.axis_index(DP)
        self.z = lax.axis_index(CONTEXT)
        self.e = lax.axis_index(EXPERTS)
        self.high = self.e // 2
        self.low = self.e % 2

    def shard(self, z):
        return self.x * self.depth + z

    def other_shard(self, z):
        return (1 - self.x) * self.depth + z

    def peer_high(self, step):
        return lax.rem(self.high + step, self.high_count)

    def peer_owner(self, step):
        return lax.rem(self.e + step, self.owners)

    def on_line(self, z):
        return (z >= 0) & (z < self.depth)

    def greet(self):
        barrier = pltpu.get_barrier_semaphore()

        def signal(**device):
            pl.semaphore_signal(barrier, inc=1, device_id=device, device_id_type=MESH)

        signal(dp=1 - self.x)
        for step in range(1, self.owners):
            signal(experts=self.peer_owner(step))
        for step in range(1, self.depth):
            signal(context=lax.rem(self.z + step, self.depth))
        count = self.owners + self.depth - 1
        pl.semaphore_wait(barrier, count)


class Line:
    def __init__(self, place, own, slot, send_sem, recv_sem):
        self.place, self.own, self.slot = place, own, slot
        self.send_sem, self.recv_sem = send_sem, recv_sem

    def _copy(self, direction, step):
        place = self.place
        z = place.z - direction * step
        source = self.own if step == 0 else self.slot(z)
        return remote(
            source,
            self.slot(z),
            self.send_sem.at[(direction + 1) // 2, step],
            self.recv_sem.at[z],
            context=place.z + direction,
        )

    def _valid(self, direction, step):
        place = self.place
        return place.on_line(place.z - direction * step) & place.on_line(place.z + direction)

    def send(self, direction, step):
        if step < self.place.depth - 1:
            pl.when(self._valid(direction, step))(lambda: self._copy(direction, step).start())

    def start(self):
        self.send(1, 0)
        self.send(-1, 0)

    def hop(self, step, then=None):
        for direction in (1, -1):
            z = self.place.z - direction * (step + 1)

            def body(direction=direction, z=z):
                arrived(self.slot(z), self.recv_sem.at[z])
                self.send(direction, step + 1)
                if then is not None:
                    then(z)

            pl.when(self.place.on_line(z))(body)

    def drain(self):
        for direction in (1, -1):
            for step in range(self.place.depth - 1):
                pl.when(self._valid(direction, step))(
                    lambda d=direction, s=step: self._copy(d, s).wait_send()
                )


class DenseGather:
    def __init__(self, place, own, slot, sems):
        self.place, self.own, self.slot_of = place, own, slot
        zs, zr, self.h_send, self.h_recv, self.l_send, self.l_recv = sems
        self.line = Line(place, own, lambda z: self.slot(z, place.high, place.low), zs, zr)

    @staticmethod
    def semaphores(count, depth, high_count):
        dma = pltpu.SemaphoreType.DMA
        cross = dma((count, high_count, depth))
        return [dma((count, 2, depth)), dma((count, depth)), cross, cross, cross, cross]

    def slot(self, z, high, low):
        return self.slot_of((z * self.place.high_count + high) * 2 + low)

    def _to_high(self, z, step, own):
        place = self.place
        target = self.slot(z, place.high, place.low)
        return remote(
            self.own if own else target,
            target,
            self.h_send.at[step, z],
            self.h_recv.at[place.high, z],
            experts=place.peer_high(step) * 2 + place.low,
        )

    def _to_low(self, z, high, own):
        place = self.place
        target = self.slot(z, high, place.low)
        return remote(
            self.own if own else target,
            target,
            self.l_send.at[high, z],
            self.l_recv.at[high, z],
            experts=place.e + 1 - 2 * place.low,
        )

    def _spread(self, z, own=False):
        for step in range(1, self.place.high_count):
            self._to_high(z, step, own).start()
        self._to_low(z, self.place.high, own).start()

    def start(self):
        self.line.start()
        self._spread(self.place.z, True)

    def hop(self, step):
        self.line.hop(step, self._spread)

    def cross(self, z):
        place = self.place
        for step in range(1, place.high_count):
            high = place.peer_high(step)
            arrived(self.slot(z, high, place.low), self.h_recv.at[high, z])
            self._to_low(z, high, False).start()

    def finish(self, z):
        place = self.place
        for high in range(place.high_count):
            arrived(self.slot(z, high, 1 - place.low), self.l_recv.at[high, z])

    def drain(self):
        place = self.place
        self.line.drain()
        for z in range(place.depth):
            for step in range(1, place.high_count):
                self._to_high(z, step, False).wait_send()
            for high in range(place.high_count):
                self._to_low(z, high, False).wait_send()


def expert_slab(ref, kind, local, shard, width):
    start = pl.multiple_of(shard * width, 128)
    if kind == 2:
        return ref.at[local, pl.ds(start, width)]
    return ref.at[local, :, pl.ds(start, width)]


class ExpertGather:
    def __init__(self, place, own, out, sems):
        self.place, self.own, self.out = place, own, out
        self.z_send, self.z_recv, self.x_send, self.x_recv = sems
        self.local_count, self.width = own[0].shape[0], own[0].shape[2]

    @staticmethod
    def semaphores(depth, local_count):
        dma = pltpu.SemaphoreType.DMA
        return [
            dma((local_count, 3, 2, depth)),
            dma((local_count, 3, depth)),
            dma((local_count, 3, depth)),
            dma((local_count, 3, depth)),
        ]

    def slot(self, local, kind, shard):
        return expert_slab(self.out[kind], kind, local, shard, self.width)

    def _line(self, local, kind):
        return Line(
            self.place,
            self.own[kind].at[local],
            lambda z: self.slot(local, kind, self.place.shard(z)),
            self.z_send.at[local, kind],
            self.z_recv.at[local, kind],
        )

    def _across(self, local, kind, z, own=False):
        target = self.slot(local, kind, self.place.shard(z))
        return remote(
            self.own[kind].at[local] if own else target,
            target,
            self.x_send.at[local, kind, z],
            self.x_recv.at[local, kind, z],
            dp=1 - self.place.x,
        )

    def start_x(self):
        for local in range(self.local_count):
            for kind in range(3):
                self._across(local, kind, self.place.z, True).start()

    def start_z(self):
        for local in range(self.local_count):
            for kind in range(3):
                self._line(local, kind).start()

    def hop(self, local, step):
        for kind in range(3):
            self._line(local, kind).hop(
                step, lambda z, kind=kind: self._across(local, kind, z).start()
            )

    def wait_x(self, local, z):
        for kind in range(3):
            arrived(
                self.slot(local, kind, self.place.other_shard(z)), self.x_recv.at[local, kind, z]
            )

    def drain(self):
        for local in range(self.local_count):
            for kind in range(3):
                self._line(local, kind).drain()
                for z in range(self.place.depth):
                    self._across(local, kind, z).wait_send()


def rope(values, cosine, sine_part):
    lane = lax.broadcasted_iota(jnp.int32, cosine.shape, 1)
    first = lax.rem(lane, HD) < HD // 2
    turned = []
    for start in range(0, values.shape[1], 2 * HD):
        part = values[:, start : start + 2 * HD]
        partner = jnp.where(
            first, pltpu.roll(part, 2 * HD - HD // 2, 1), pltpu.roll(part, HD // 2, 1)
        )
        turned.append(part * cosine + partner * sine_part)
    return jnp.concatenate(turned, 1)


def norm_rows(values, gain):
    root = lax.rsqrt(jnp.mean(values * values, -1, keepdims=True) + EPSILON)
    return (values * root * gain).astype(BF)


def tiles(total, size, body):
    def run(i, carry):
        body(pl.ds(pl.multiple_of(i * size, size), size))
        return carry

    lax.fori_loop(0, total // size, run, 0)


def one_hots(routes, gates, me, local_count, total):
    rows = routes.shape[1]
    capacity = rows * 8 // (3 * total)
    first, second = routes[0:1, :], routes[1:2, :]
    ids = lax.rem(
        lax.broadcasted_iota(jnp.int32, (total, rows), 0) + me * local_count, total
    )
    named = (first == ids) | (second == ids)
    earlier = (
        lax.broadcasted_iota(jnp.int32, (rows, rows), 0)
        < lax.broadcasted_iota(jnp.int32, (rows, rows), 1)
    ).astype(F32).astype(BF)
    counts = mdot(named.astype(F32).astype(BF), earlier).astype(jnp.int32)
    places = jnp.where(named, counts, -1)
    weights = jnp.where(first == ids, gates[0:1, :], 0.0) + jnp.where(
        second == ids, gates[1:2, :], 0.0
    )
    slot = lax.broadcasted_iota(jnp.int32, (capacity, rows), 0)
    for i in range(total):
        yield i, slot == places[i : i + 1, :], weights[i : i + 1, :]


def ffn_chunk(x, g, weights, saved, sums, grads, tile):
    gate_w, up_w, down_w = weights
    act_s, d_gate_s, d_up_s = saved
    out_sum, in_sum = sums

    def forward(here):
        x_rows, g_rows = x[here, :], g[here, :]
        gate = mdot(x_rows, gate_w[...])
        up = mdot(x_rows, up_w[...])
        d_act = ndot(g_rows, down_w[...]).astype(BF).astype(F32)
        sigma = jax.nn.sigmoid(gate)
        silu = gate * sigma
        act = (silu * up).astype(BF)
        d_gate = (d_act * up * (sigma * (1.0 + gate * (1.0 - sigma)))).astype(BF)
        d_up = (d_act * silu).astype(BF)
        act_s[here, :] = act
        d_gate_s[here, :] = d_gate
        d_up_s[here, :] = d_up
        out_sum[here, :] += mdot(act, down_w[...])
        in_sum[here, :] += ndot(d_gate, gate_w[...]) + ndot(d_up, up_w[...])

    rows = x.shape[0]
    tiles(rows, tile, forward)
    used = pl.ds(0, rows)

    def weight_grads(here):
        grads[0][here, :] = tdot(x[:, here], d_gate_s[used, :]).astype(BF)
        grads[1][here, :] = tdot(x[:, here], d_up_s[used, :]).astype(BF)
        grads[2][:, here] = tdot(act_s[used, :], g[:, here]).astype(BF)

    tiles(x.shape[1], 256, weight_grads)


def forward_kernel(sizes, *refs):
    place = Place(sizes)
    depth, high_count = sizes
    owners = place.owners
    (
        tokens, cot, gates, routes, cosine, sine_part,
        qkv_in, out_in, gain_in, sg_in, su_in, sd_in, eg_in, eu_in, ed_in,
        qkv_o, out_o, gain_o, sg_o, su_o, sd_o, eg_o, eu_o, ed_o,
        n1_o, k_o, v_o, q_o, att_o, hid_o, lse_o, side_o, dn2_o,
        gsg_o, gsu_o, gsd_o, geg_o, geu_o, ged_o, outs_o, dins_o,
        xk, wq, wo, gain_land, gain_v, g_all, n2, in_s, do_s, send_in, send_do,
        wg, wu, wd, act_s, dg_s, du_s, stage_g, stage_u, stage_d,
        *sems,
    ) = refs
    dense_sems, sems = sems[:6], sems[6:]
    expert_sems, sems = sems[:4], sems[4:]
    (
        line_send, line_recv, load_sem, ai_send, ai_recv, ad_send, ad_recv,
        chunk_sem, store_sem, out_sem,
    ) = sems
    micro_count, rows, features = tokens.shape
    prompt = depth * PB
    length = prompt + CONT
    local_count, _, width = eg_in.shape
    total = owners * local_count
    capacity = rows * 8 // (3 * total)
    slots = in_s.shape[1]
    me = place.e

    def dense(i, own, slot):
        return DenseGather(place, own, slot, [s.at[i] for s in dense_sems])

    def rows_of(ref, count):
        return lambda s: ref.at[pl.ds(pl.multiple_of(s * count, 16), count)]

    def columns_of(ref, count):
        return lambda s: ref.at[:, pl.ds(pl.multiple_of(s * count, 128), count)]

    early = [
        dense(0, qkv_in, rows_of(wq, qkv_in.shape[0])),
        dense(1, out_in, rows_of(wo, out_in.shape[0])),
        dense(2, gain_in, rows_of(gain_land, gain_in.shape[0])),
    ]
    late = [
        dense(3, sg_in, columns_of(sg_o, sg_in.shape[1])),
        dense(4, su_in, columns_of(su_o, su_in.shape[1])),
        dense(5, sd_in, rows_of(sd_o, sd_in.shape[0])),
    ]
    experts = ExpertGather(place, (eg_in, eu_in, ed_in), (eg_o, eu_o, ed_o), expert_sems)
    own_prompt = pl.ds(pl.multiple_of(place.z * PB, PB), PB)
    prompts = [
        Line(
            place,
            tokens.at[m, pl.ds(0, PB)],
            lambda z, m=m: xk.at[m, pl.ds(pl.multiple_of(z * PB, PB), PB)],
            line_send.at[m],
            line_recv.at[m],
        )
        for m in range(micro_count)
    ]
    own_at = (place.z * high_count + place.high) * 2 + place.low
    loads = [
        (tokens.at[:, pl.ds(0, PB)], xk.at[:, own_prompt]),
        (tokens.at[:, pl.ds(PB, CONT)], xk.at[:, pl.ds(prompt, CONT)]),
    ]
    loads += [(cot.at[m], g_all.at[pl.ds(m * rows, rows)]) for m in range(micro_count)]
    loads += [(d.own, d.slot_of(own_at)) for d in early]
    bounce = [
        (sg_in, wg.at[0, :, pl.ds(0, sg_in.shape[1])], late[0].slot_of(own_at)),
        (su_in, wu.at[0, :, pl.ds(0, su_in.shape[1])], late[1].slot_of(own_at)),
        (sd_in, wd.at[0, pl.ds(0, sd_in.shape[0])], late[2].slot_of(own_at)),
    ]
    loads += [(source, middle) for source, middle, _ in bounce]
    load_copies = [
        pltpu.make_async_copy(source, target, load_sem.at[i])
        for i, (source, target) in enumerate(loads)
    ]
    bounce_copies = [
        pltpu.make_async_copy(middle, target, load_sem.at[i])
        for i, (_, middle, target) in enumerate(bounce)
    ]
    for copy in load_copies:
        copy.start()
    place.greet()
    for d in early:
        d.start()
    experts.start_x()
    for copy in load_copies:
        copy.wait()
    for copy in bounce_copies:
        copy.start()
    stores = []

    def store(source, target):
        copy = pltpu.make_async_copy(source, target, out_sem.at[len(stores)])
        copy.start()
        stores.append(copy)

    def slot_rows(m, sender):
        return pl.ds(pl.multiple_of((m * owners + sender) * capacity, 16), capacity)

    def exchange(buffer, land, send_sem, recv_sem, m, step):
        return remote(
            buffer.at[step - 1, m],
            land.at[:, slot_rows(m, me)],
            send_sem.at[step - 1, m],
            recv_sem.at[step - 1, m],
            experts=place.peer_owner(step),
        )

    def exchanged(land, recv_sem, m, step):
        sender = lax.rem(me - step + owners, owners)
        arrived(land.at[:, slot_rows(m, sender)], recv_sem.at[step - 1, m])

    def put(buffer, land, m, i, value):
        if i < local_count:
            land[i, slot_rows(m, me), :] = value
        else:
            buffer[i // local_count - 1, m, i % local_count] = value

    def expert_gradients(m):
        g_rows = g_all[pl.ds(m * rows, rows), :]
        for i, hit, weight in one_hots(routes.at[m], gates.at[m], me, local_count, total):
            gate = jnp.sum(jnp.where(hit, weight, 0.0), -1, keepdims=True)
            value = mdot(hit.astype(F32).astype(BF), g_rows)
            put(send_do, do_s, m, i, (gate * value).astype(BF))

    def early_hop(step):
        for d in early:
            d.hop(step)

    for step in range(depth - 2):
        if step < micro_count:
            expert_gradients(step)
        early_hop(step)
    for m in range(max(depth - 2, 0), micro_count):
        expert_gradients(m)
    prompts[0].start()
    early_hop(depth - 2)
    for m in range(micro_count):
        for step in range(1, owners):
            exchange(send_do, do_s, ad_send, ad_recv, m, step).start()
    prompts[0].hop(0)
    for z in range(depth):
        for d in early:
            d.cross(z)
    for step in range(1, depth - 1):
        prompts[0].hop(step)
        if step == 1:
            for prompt_line in prompts[1:]:
                prompt_line.start()
    for z in range(depth):
        for d in early:
            d.finish(z)
    store(wq, qkv_o)
    store(wo, out_o)
    shards = depth * owners
    gain_rows = gain_in.shape[0]
    gain_sum = jnp.zeros((8, features), F32)
    for s in range(shards):
        gain_sum += gain_land[pl.ds(s * gain_rows, gain_rows), :].astype(F32)[:8]
    gain_v[...] = gain_sum
    store(gain_v, gain_o)

    def own_rows(i):
        start = place.z * PB if i == 0 else prompt + (i - 1) * PB
        return start, pl.ds(start if i else pl.multiple_of(start, PB), PB)

    def front(n1, k, v, q, att, hid, lse):
        lse[...] = jnp.zeros_like(lse)
        pairs = features // (2 * HD)

        def prompt_hop(step):
            for prompt_line in prompts[1:]:
                prompt_line.hop(step)
            if step == depth - 2:
                experts.start_z()

        def project_all(m):
            def project(here):
                normed = norm_rows(xk[m, here, :].astype(F32), gain_v[0:1, :])
                n1[m, here, :] = normed
                key = ndot(normed, wq[pl.ds(features, features), :])
                k[m, here, :] = rope(key, cosine[here, :], sine_part[here, :]).astype(BF)
                v[m, here, :] = ndot(normed, wq[pl.ds(2 * features, features), :]).astype(BF)

            tiles(length, 256, project)
            for i in range(rows // PB):
                _, here = own_rows(i)
                query = ndot(n1[m, here, :], wq[pl.ds(0, features), :])
                query = rope(query, cosine[here, :], sine_part[here, :]).astype(BF)
                q[m, pl.ds(i * PB, PB), :] = query * jnp.asarray(HD**-0.5, BF)
        lane = lax.broadcasted_iota(jnp.int32, (PB, 2 * HD), 1)
        for m in range(micro_count):
            project_all(m)

            def pair(index, carry):
                if m == 0:
                    for step in range(depth - 1):
                        pl.when(index == min(step, pairs - 1))(lambda step=step: prompt_hop(step))
                lanes = pl.ds(pl.multiple_of(index * 2 * HD, 2 * HD), 2 * HD)
                for i in range(rows // PB):
                    here = pl.ds(i * PB, PB)
                    query = q[m, here, lanes]
                    seen = prompt + i * PB
                    keys, values = k[m, pl.ds(0, seen), lanes], v[m, pl.ds(0, seen), lanes]
                    column = lax.broadcasted_iota(jnp.int32, (PB, seen), 1)
                    row = lax.broadcasted_iota(jnp.int32, (PB, seen), 0)
                    allowed = column <= row + own_rows(i)[0]
                    parts = []
                    logs = lse[m, here, :]
                    for sub in range(2):
                        only = jnp.where(lane // HD == sub, query, jnp.zeros_like(query))
                        scores = jnp.where(allowed, ndot(only, keys), -1000000000.0)
                        highest = jnp.max(scores, -1, keepdims=True)
                        weights = jnp.exp(scores - highest)
                        sums = jnp.sum(weights, -1, keepdims=True)
                        parts.append(mdot((weights * (1.0 / sums)).astype(BF), values))
                        logs = jnp.where(lane == 2 * index + sub, highest + jnp.log(sums), logs)
                    lse[m, here, :] = logs
                    att[m, here, lanes] = jnp.where(lane < HD, parts[0], parts[1]).astype(BF)
                return carry

            lax.fori_loop(0, pairs, pair, 0)
            if m == 0:
                for copy in bounce_copies:
                    copy.wait()
                for d in late:
                    d.start()
            if m == micro_count - 1:
                experts.hop(0, 0)
                for d in late:
                    d.cross(place.z)
            for i in range(rows // PB):
                here = pl.ds(i * PB, PB)
                hidden = xk[m, own_rows(i)[1], :].astype(F32) + mdot(att[m, here, :], wo[...])
                hid[m, here, :] = hidden
                n2[pl.ds(m * rows + i * PB, PB), :] = norm_rows(hidden, gain_v[1:2, :])
            normed = n2[pl.ds(m * rows, rows), :]
            for i, hit, _ in one_hots(routes.at[m], gates.at[m], me, local_count, total):
                value = mdot(hit.astype(F32).astype(BF), normed)
                put(send_in, in_s, m, i, value.astype(BF))
            for step in range(1, owners):
                exchange(send_in, in_s, ai_send, ai_recv, m, step).start()
        store(n1, n1_o)
        store(k, k_o)
        store(v, v_o)
        store(q, q_o)
        store(att, att_o)
        store(hid, hid_o)
        store(lse, lse_o)
        for copy in stores:
            copy.wait()

    pl.run_scoped(
        front,
        pltpu.VMEM((micro_count, length, features), BF),
        pltpu.VMEM((micro_count, length, features), BF),
        pltpu.VMEM((micro_count, length, features), BF),
        pltpu.VMEM((micro_count, rows, features), BF),
        pltpu.VMEM((micro_count, rows, features), BF),
        pltpu.VMEM((micro_count, rows, features), F32),
        pltpu.VMEM((micro_count, rows, 2 * HD), F32),
    )
    saved = (act_s, dg_s, du_s)
    staged = (stage_g, stage_u, stage_d)

    def chunk_loads(sources, slot):
        return [
            pltpu.make_async_copy(source, buffer.at[slot], chunk_sem.at[slot, kind])
            for kind, (source, buffer) in enumerate(zip(sources, (wg, wu, wd)))
        ]

    def chunk_stores(targets, slot):
        return [
            pltpu.make_async_copy(buffer.at[slot], target, store_sem.at[slot, kind])
            for kind, (target, buffer) in enumerate(zip(targets, staged))
        ]

    def wait_rows():
        for m in range(micro_count):
            for step in range(1, owners):
                exchanged(in_s, ai_recv, m, step)
                exchanged(do_s, ad_recv, m, step)

    def returns(local):
        return [
            pltpu.make_async_copy(source.at[local], target.at[local], out_sem.at[2 + 2 * local + i])
            for i, (source, target) in enumerate(((in_s, outs_o), (do_s, dins_o)))
        ]

    def both(out_sum, in_sum, side_sum, normed_sum):
        out_sum[...] = jnp.zeros_like(out_sum)
        in_sum[...] = jnp.zeros_like(in_sum)
        side_sum[...] = jnp.zeros_like(side_sum)
        normed_sum[...] = jnp.zeros_like(normed_sum)
        group = late[0].own.shape[1] * owners // width

        def store_grads(targets, slot, stored):
            def previous():
                for copy in chunk_stores(targets, slot):
                    copy.wait()

            pl.when(stored)(previous)
            return lambda: [copy.start() for copy in chunk_stores(targets, slot)]

        def shared_part(refs, c):
            here = pl.ds(pl.multiple_of(c * width, 128), width)
            return [refs[0].at[:, here], refs[1].at[:, here], refs[2].at[here]]

        def shared_item(w, z):
            for d in late:
                d.finish(z)

            def one(i, carry):
                c = z * group + i
                loads = chunk_loads(shared_part((sg_o, su_o, sd_o), c), 2 * local_count + i)
                for copy in loads:
                    copy.wait()
                send = store_grads(shared_part((gsg_o, gsu_o, gsd_o), c), i, w > 0)
                ffn_chunk(
                    n2,
                    g_all,
                    [buffer.at[2 * local_count + i] for buffer in (wg, wu, wd)],
                    saved,
                    (side_sum, normed_sum),
                    [buffer.at[i] for buffer in staged],
                    micro_count * rows,
                )
                send()
                return carry

            for i in range(group):
                for copy in chunk_loads(
                    shared_part((sg_o, su_o, sd_o), z * group + i), 2 * local_count + i
                ):
                    copy.start()
            lax.fori_loop(0, group, one, 0)

        def expert_item(w, z, crossed, local, side, ahead):
            shard = jnp.where(crossed, place.other_shard(z), place.shard(z))

            def load(n):
                sources = [
                    expert_slab(ref, k, n, shard, width) for k, ref in enumerate((eg_o, eu_o, ed_o))
                ]
                return chunk_loads(sources, side * local_count + n)

            def begin(n):
                def own():
                    mine = [ref.at[n] for ref in (eg_in, eu_in, ed_in)]
                    for copy in chunk_loads(mine, side * local_count + n):
                        copy.start()

                def landed():
                    pl.when(crossed)(lambda: experts.wait_x(n, z))
                    for copy in load(n):
                        copy.start()

                pl.when(w == 1)(own)
                pl.when(w > 1)(landed)

            def begin_rest():
                for n in range(1, local_count):
                    begin(n)

            pl.when(w == 1)(wait_rows)
            pl.when(local == 0)(lambda: begin(0))
            pl.when(ahead & (local == 0))(begin_rest)
            pl.when(jnp.logical_not(ahead) & (local > 0))(lambda: begin(local))
            for copy in load(local):
                copy.wait()
            targets = [
                expert_slab(ref, k, local, shard, width) for k, ref in enumerate((geg_o, geu_o, ged_o))
            ]
            send = store_grads(targets, local, True)
            ffn_chunk(
                in_s.at[local],
                do_s.at[local],
                [buffer.at[side * local_count + local] for buffer in (wg, wu, wd)],
                saved,
                (out_sum.at[local], in_sum.at[local]),
                [buffer.at[local] for buffer in staged],
                slots,
            )
            send()

        def crossing(step):
            for d in late:
                for z in (place.z - 1 - step, place.z + 1 + step):
                    pl.when(place.on_line(z))(lambda d=d, z=z: d.cross(z))

        def late_hop(step):
            for d in late:
                d.hop(step)

        heads = 2 * local_count + 1
        in_step = 2 * heads
        after_item = [(local, lambda local=local: experts.hop(local, 0)) for local in range(1, local_count)]
        after_item = [(local - 1, run) for local, run in after_item]
        after_item += [(local_count, lambda: late_hop(0)), (heads - 1, lambda: crossing(0))]
        for step in range(1, depth - 1):
            here = heads + in_step * step
            first = here - in_step + 3
            spots = [first, here - 1] if step == 1 else [here - 1, here + 1]
            for local in range(local_count):
                at = spots[min(local, 1)]
                after_item.append((at, lambda local=local, step=step: experts.hop(local, step)))
            after_item.append((here + 3, lambda step=step: late_hop(step)))
            after_item.append((here + 5, lambda step=step: crossing(step)))

        def item(w, carry):
            head = w < heads
            after = jnp.maximum(w - heads, 0)
            step, spot = after // in_step, lax.rem(after, in_step)
            kind = jnp.where(head, w - 1, spot // 2)
            turn = jnp.where(head, kind, jnp.where(kind > local_count, kind - 1, kind))
            is_shared = kind == jnp.where(head, -1, local_count + 1)
            crossed = turn >= local_count
            local = jnp.clip(jnp.where(crossed, turn - local_count, turn), 0, local_count - 1)
            z = jnp.where(head, place.z, place.z + (2 * lax.rem(spot, 2) - 1) * (1 + step))
            valid = place.on_line(z)
            pl.when(valid & is_shared)(lambda: shared_item(w, z))
            ahead = head | (step < depth - 2)
            side = jnp.where(head, 0, lax.rem(spot, 2))
            pl.when(valid & jnp.logical_not(is_shared))(
                lambda: expert_item(w, z, crossed, local, side, ahead)
            )
            for at, run in after_item:
                pl.when(w == at)(run)
            return carry

        lax.fori_loop(0, heads + in_step * (depth - 1), item, 0)
        sums = [
            pltpu.make_async_copy(side_sum, side_o, out_sem.at[0]),
            pltpu.make_async_copy(normed_sum, dn2_o, out_sem.at[1]),
        ]
        for copy in sums:
            copy.start()
        for local in range(local_count):
            targets = [expert_slab(ref, k, local, 0, width) for k, ref in enumerate((geg_o, geu_o, ged_o))]
            for copy in chunk_stores(targets, local):
                copy.wait()

            def finish(here, local=local):
                in_s[local, here, :] = out_sum[local, here, :].astype(BF)
                do_s[local, here, :] = in_sum[local, here, :].astype(BF)

            tiles(slots, 256, finish)
            for copy in returns(local):
                copy.start()
        for copy in sums:
            copy.wait()

    pl.run_scoped(
        both,
        pltpu.VMEM((local_count, slots, features), F32),
        pltpu.VMEM((local_count, slots, features), F32),
        pltpu.VMEM((micro_count * rows, features), F32),
        pltpu.VMEM((micro_count * rows, features), F32),
    )
    for local in range(local_count):
        for copy in returns(local):
            copy.wait()
    for line in prompts:
        line.drain()
    for d in early + late:
        d.drain()
    experts.drain()
    for m in range(micro_count):
        for step in range(1, owners):
            exchange(send_do, do_s, ad_send, ad_recv, m, step).wait_send()
            exchange(send_in, in_s, ai_send, ai_recv, m, step).wait_send()


def rope_tables(prompt):
    positions = np.arange(prompt + CONT, dtype=np.float64)
    frequency = 10000.0 ** (-2.0 * np.arange(HD // 2) / HD)
    angles = positions[:, None] * frequency
    cosine, sine_part = np.cos(angles), np.sin(angles)
    return (
        np.concatenate([cosine] * 4, 1).astype(np.float32),
        np.concatenate([-sine_part, sine_part] * 2, 1).astype(np.float32),
    )


def run_forward(sizes, tokens, cot, gates, routes, dense, experts):
    depth, high_count = sizes
    micro_count, rows, features = tokens.shape
    owners = high_count * 2
    line = depth * owners
    prompt = depth * PB
    length = prompt + CONT
    local_count, _, width = experts[0].shape
    hidden_units = dense[3].shape[1] * line
    capacity = rows * 8 // (3 * owners * local_count)
    slots = micro_count * owners * capacity
    cosine, sine_part = rope_tables(prompt)
    hbm, vmem = pl.BlockSpec(memory_space=pltpu.HBM), pl.BlockSpec(memory_space=pltpu.VMEM)

    def shape(dtype, *dims):
        return jax.ShapeDtypeStruct(dims, dtype)

    token_rows = micro_count * rows
    wide, tall = (features, hidden_units), (hidden_units, features)
    out_shape = [
        shape(BF, dense[0].shape[0] * line, features),
        shape(BF, dense[1].shape[0] * line, features),
        shape(F32, 8, features),
        shape(BF, *wide), shape(BF, *wide), shape(BF, *tall),
        shape(BF, local_count, *wide), shape(BF, local_count, *wide), shape(BF, local_count, *tall),
        shape(BF, micro_count, length, features),
        shape(BF, micro_count, length, features),
        shape(BF, micro_count, length, features),
        shape(BF, micro_count, rows, features),
        shape(BF, micro_count, rows, features),
        shape(F32, micro_count, rows, features),
        shape(F32, micro_count, rows, 2 * HD),
        shape(F32, token_rows, features),
        shape(F32, token_rows, features),
        shape(BF, *wide), shape(BF, *wide), shape(BF, *tall),
        shape(BF, local_count, *wide), shape(BF, local_count, *wide), shape(BF, local_count, *tall),
        shape(BF, local_count, slots, features),
        shape(BF, local_count, slots, features),
    ]
    dma = pltpu.SemaphoreType.DMA
    buffers = max(2, local_count)
    loads = 2 * local_count + 2
    send = pltpu.VMEM((owners - 1, micro_count, local_count, capacity, features), BF)
    scratch = [
        pltpu.VMEM((micro_count, length, features), BF),
        pltpu.VMEM(out_shape[0].shape, BF),
        pltpu.VMEM(out_shape[1].shape, BF),
        pltpu.VMEM((dense[2].shape[0] * line, features), BF),
        pltpu.VMEM((8, features), F32),
        pltpu.VMEM((token_rows, features), BF),
        pltpu.VMEM((token_rows, features), BF),
        pltpu.VMEM((local_count, slots, features), BF),
        pltpu.VMEM((local_count, slots, features), BF),
        send,
        send,
        pltpu.VMEM((loads, features, width), BF),
        pltpu.VMEM((loads, features, width), BF),
        pltpu.VMEM((loads, width, features), BF),
        pltpu.VMEM((max(slots, token_rows), width), BF),
        pltpu.VMEM((max(slots, token_rows), width), BF),
        pltpu.VMEM((max(slots, token_rows), width), BF),
        pltpu.VMEM((buffers, features, width), BF),
        pltpu.VMEM((buffers, features, width), BF),
        pltpu.VMEM((buffers, width, features), BF),
    ]
    scratch += DenseGather.semaphores(len(dense), depth, high_count)
    scratch += ExpertGather.semaphores(depth, local_count)
    scratch += [
        dma((micro_count, 2, depth)),
        dma((micro_count, depth)),
        dma((10 + micro_count,)),
        dma((owners - 1, micro_count)),
        dma((owners - 1, micro_count)),
        dma((owners - 1, micro_count)),
        dma((owners - 1, micro_count)),
        dma((loads, 3)),
        dma((buffers, 3)),
        dma((12 + 2 * local_count,)),
    ]
    return pl.pallas_call(
        functools.partial(forward_kernel, sizes),
        out_shape=out_shape,
        in_specs=[hbm] * 2 + [vmem] * 4 + [hbm] * 9,
        out_specs=[hbm] * len(out_shape),
        scratch_shapes=scratch,
        compiler_params=pltpu.CompilerParams(
            collective_id=0, has_side_effects=True, vmem_limit_bytes=60 * MIB
        ),
        name="gather_and_forward",
    )(tokens, cot, gates, routes, cosine, sine_part, *dense, *experts)


def add_into(target, sources, step):
    def body(here):
        value = target[here, :].astype(F32)
        for source in sources:
            value = value + source[here, :].astype(F32)
        target[here, :] = value.astype(target.dtype)

    tiles(target.shape[0], step, body)


class LineSum:
    def __init__(self, place, part, land, send_sem, recv_sem):
        self.place, self.part, self.land = place, part, land
        self.send_sem, self.recv_sem = send_sem, recv_sem

    def copy(self, z, direction):
        place = self.place
        slot = z if direction > 0 else jnp.where(z == place.z - 1, place.depth, z)
        return remote(
            self.part(z),
            self.land(slot),
            self.send_sem.at[z],
            self.recv_sem.at[slot],
            context=place.z + direction,
        )

    def upstream(self, direction):
        return self.place.z > 0 if direction > 0 else self.place.z < self.place.depth - 1

    def arrive(self, slot):
        arrived(self.land(slot), self.recv_sem.at[slot])

    def at(self, direction, step, body):
        z = self.place.z + direction * step
        pl.when(self.place.on_line(z))(lambda: body(z))

    def pass_on(self, direction, step, add):
        def body(z):
            def more():
                self.arrive(z)
                add(self.part(z), self.land(z))

            pl.when(self.upstream(direction))(more)
            self.copy(z, direction).start()

        self.at(direction, step, body)

    def end(self, add):
        for direction, slot in ((1, self.place.z), (-1, self.place.depth)):

            def body(slot=slot):
                self.arrive(slot)
                add(self.part(self.place.z), self.land(slot))

            pl.when(self.upstream(direction))(body)

    def drain(self):
        for step in range(1, self.place.depth):
            for direction in (1, -1):
                self.at(direction, step, lambda z, d=direction: self.copy(z, d).wait_send())


class DenseScatter:
    def __init__(self, place, source, low, high, line, cross, spare, out, sems):
        self.place, self.source, self.spare, self.out = place, source, spare, out
        self.low, self.high, self.cross = low, high, cross
        (
            self.l_send, self.l_recv, self.h_send, self.h_recv, z_send, z_recv,
            self.x_send, self.x_recv, self.own_sem,
        ) = sems
        self.step = min(64, low.shape[2]) if low.shape[2] % 64 == 0 else 16
        self.line = LineSum(
            place, lambda z: low.at[z, place.high], lambda slot: line.at[slot], z_send, z_recv
        )

    @staticmethod
    def semaphores(count, depth, high_count):
        dma = pltpu.SemaphoreType.DMA
        cross = dma((count, depth, high_count))
        return [
            cross, cross, dma((count, high_count)), dma((count, high_count)),
            dma((count, depth + 1)), dma((count, depth + 1)),
            dma((count,)), dma((count,)), dma((count, 2)),
        ]

    def _index(self, z, high, low):
        return (z * self.place.high_count + high) * 2 + low

    def _to_low(self, z, high):
        place = self.place
        return remote(
            self.source(self._index(z, high, 1 - place.low)),
            self.low.at[z, high],
            self.l_send.at[z, high],
            self.l_recv.at[z, high],
            experts=place.e + 1 - 2 * place.low,
        )

    def _each(self, body):
        for z in range(self.place.depth):
            for high in range(self.place.high_count):
                body(z, high)

    def start(self):
        self._each(lambda z, high: self._to_low(z, high).start())

    def add_low(self):
        place = self.place
        places = [(z, high) for z in range(place.depth) for high in range(place.high_count)]

        def load(i):
            z, high = places[i]
            return pltpu.make_async_copy(
                self.source(self._index(z, high, place.low)),
                self.spare.at[i % 2],
                self.own_sem.at[i % 2],
            )

        if self.spare is not None:
            load(0).start()
        for i, (z, high) in enumerate(places):
            self._to_low(z, high).wait_recv()
            if self.spare is None:
                own = self.source(self._index(z, high, place.low))
            else:
                if i + 1 < len(places):
                    load(i + 1).start()
                load(i).wait()
                own = self.spare.at[i % 2]
            add_into(self.low.at[z, high], [own], self.step)
        for step in range(1, place.high_count):
            self._to_high(step).start()

    def _to_high(self, step):
        place = self.place
        peer = place.peer_high(step)
        return remote(
            self.low.at[:, peer],
            self.high.at[step - 1],
            self.h_send.at[step],
            self.h_recv.at[step],
            experts=peer * 2 + place.low,
        )

    def add_high(self):
        place = self.place
        for step in range(1, place.high_count):
            self._to_high(step).wait_recv()
        for z in range(place.depth):
            add_into(
                self.low.at[z, place.high],
                [self.high.at[step - 1, z] for step in range(1, place.high_count)],
                self.step,
            )

    def _add(self, target, more):
        add_into(target, [more], self.step)

    def pass_on(self, direction, step):
        self.line.pass_on(direction, step, self._add)

    def _across(self):
        place = self.place
        return remote(
            self.low.at[place.z, place.high], self.cross, self.x_send, self.x_recv, dp=1 - place.x
        )

    def end(self):
        self.line.end(self._add)
        self._across().start()

    def _store(self):
        return pltpu.make_async_copy(self.cross, self.out, self.own_sem.at[0])

    def finish(self):
        self._across().wait_recv()
        self._add(self.cross, self.low.at[self.place.z, self.place.high])
        self._store().start()

    def drain(self):
        self._each(lambda z, high: self._to_low(z, high).wait_send())
        for step in range(1, self.place.high_count):
            self._to_high(step).wait_send()
        self.line.drain()
        self._across().wait_send()
        self._store().wait()


class ExpertScatter:
    def __init__(self, place, sums, cross, land, own, more, outs, sems):
        self.place, self.sums, self.cross, self.land = place, sums, cross, land
        self.own, self.more, self.outs = own, more, outs
        self.x_send, self.x_recv, self.z_send, self.z_recv, self.load_sem, self.out_sem = sems
        self.local_count, self.width = cross[0].shape[1], cross[0].shape[3]

    @staticmethod
    def semaphores(depth, local_count):
        dma = pltpu.SemaphoreType.DMA
        return [
            dma((local_count, 3, depth)),
            dma((local_count, 3, depth)),
            dma((local_count, 3, depth + 1)),
            dma((local_count, 3, depth + 1)),
            dma((3, 3)),
            dma((local_count, 3)),
        ]

    def _line(self, local, kind):
        return LineSum(
            self.place,
            lambda z: self.cross[kind].at[z, local],
            lambda slot: self.land[kind].at[slot, local],
            self.z_send.at[local, kind],
            self.z_recv.at[local, kind],
        )

    def _across(self, local, kind, z):
        return remote(
            expert_slab(self.sums[kind], kind, local, self.place.other_shard(z), self.width),
            self.cross[kind].at[z, local],
            self.x_send.at[local, kind, z],
            self.x_recv.at[local, kind, z],
            dp=1 - self.place.x,
        )

    def _order(self, body):
        place = self.place
        for step in range(place.depth - 1, 0, -1):
            for direction in (1, -1):
                z = place.z + direction * step
                pl.when(place.on_line(z))(lambda z=z: body(z))
        body(place.z)

    def start(self):
        def body(z):
            for local in range(self.local_count):
                for kind in range(3):
                    self._across(local, kind, z).start()

        self._order(body)

    def _own_load(self, local, kind, z):
        return pltpu.make_async_copy(
            expert_slab(self.sums[kind], kind, local, self.place.shard(z), self.width),
            self.own[kind],
            self.load_sem.at[0, kind],
        )

    def _more_load(self, local, kind, slot, which):
        return pltpu.make_async_copy(
            self.land[kind].at[slot, local], self.more[kind].at[which], self.load_sem.at[1 + which, kind]
        )

    def pass_on(self, direction, step, local, kinds=(0, 1, 2)):
        def body(z):
            for kind in kinds:
                self._own_load(local, kind, z).start()
            for kind in kinds:
                line = self._line(local, kind)
                target = self.cross[kind].at[z, local]

                def come(line=line, kind=kind):
                    line.arrive(z)
                    self._more_load(local, kind, z, 0).start()

                pl.when(line.upstream(direction))(come)
                self._across(local, kind, z).wait_recv()
                self._own_load(local, kind, z).wait()

                def both(target=target, kind=kind):
                    self._more_load(local, kind, z, 0).wait()
                    add_into(target, [self.own[kind], self.more[kind].at[0]], 64)

                def single(target=target, kind=kind):
                    add_into(target, [self.own[kind]], 64)

                pl.when(line.upstream(direction))(both)
                pl.when(jnp.logical_not(line.upstream(direction)))(single)
                line.copy(z, direction).start()

        self._line(local, 0).at(direction, step, body)

    def end(self, local):
        place = self.place
        z = place.z
        for kind in range(3):
            self._own_load(local, kind, z).start()
        for kind in range(3):
            line = self._line(local, kind)
            target = self.cross[kind].at[z, local]
            for which, (direction, slot) in enumerate(((1, z), (-1, place.depth))):

                def come(slot=slot, which=which, line=line, kind=kind):
                    line.arrive(slot)
                    self._more_load(local, kind, slot, which).start()

                pl.when(line.upstream(direction))(come)
            self._across(local, kind, z).wait_recv()
            self._own_load(local, kind, z).wait()
            add_into(target, [self.own[kind]], 64)
            for which, (direction, slot) in enumerate(((1, z), (-1, place.depth))):

                def more(slot=slot, which=which, kind=kind, target=target):
                    self._more_load(local, kind, slot, which).wait()
                    add_into(target, [self.more[kind].at[which]], 64)

                pl.when(line.upstream(direction))(more)
            self._store(local, kind).start()

    def _store(self, local, kind):
        return pltpu.make_async_copy(
            self.cross[kind].at[self.place.z, local],
            self.outs[kind].at[local],
            self.out_sem.at[local, kind],
        )

    def drain(self):
        for local in range(self.local_count):
            for kind in range(3):
                for z in range(self.place.depth):
                    self._across(local, kind, z).wait_send()
                self._line(local, kind).drain()
                self._store(local, kind).wait()


def backward_kernel(sizes, *refs):
    place = Place(sizes)
    depth, high_count = sizes
    owners = place.owners
    (
        tokens, cot, gates, routes, gate_rows, cosine, sine_part,
        qkv_w, out_w, gain_v, n1_i, k_i, v_i, q_i, att_i, hid_i, lse_i, side_i, dn2_i,
        gsg, gsu, gsd, geg, geu, ged, outs_i, dins_i,
        mixed_o, input_o, gqkv_o, gout_o, gsg_o, gsu_o, gsd_o, geg_o, geu_o, ged_o, gain_o,
        eland_g, eland_u, eland_d, ret_in, ret_out, d_hidden_o, dn1_o,
        *rest,
    ) = refs
    count = 5
    low, rest = rest[:count], rest[count:]
    high, rest = rest[:count], rest[count:]
    line, rest = rest[:count], rest[count:]
    cross, rest = rest[:count], rest[count:]
    (
        spare_w, spare_t, ecross_g, ecross_u, ecross_d, eown_g, eown_u, eown_d,
        emore_g, emore_u, emore_d,
        d_att, dpq, dpk, dpv, g_qkv, g_out, part, part_land,
        gain_own, gain_low, gain_high, gain_line, gain_cross, out_rows,
        *sems,
    ) = rest
    dense_sems, sems = sems[:9], sems[9:]
    expert_sems, sems = sems[:6], sems[6:]
    (
        part_send, part_recv, ri_send, ri_recv, ro_send, ro_recv,
        gain_send, gain_recv, load_sem, wq_sem, out_sem,
    ) = sems
    micro_count, rows, features = tokens.shape
    prompt = depth * PB
    length = prompt + CONT
    local_count, slots = outs_i.shape[0], outs_i.shape[1]
    total = owners * local_count
    capacity = rows * 8 // (3 * total)
    me = place.e

    def rows_of(ref, size):
        return lambda s: ref.at[pl.ds(pl.multiple_of(s * size, 16), size)]

    def columns_of(ref, size):
        return lambda s: ref.at[:, pl.ds(pl.multiple_of(s * size, 128), size)]

    sources = [
        columns_of(gsg, gsg_o.shape[1]),
        columns_of(gsu, gsu_o.shape[1]),
        rows_of(gsd, gsd_o.shape[0]),
        rows_of(g_qkv, gqkv_o.shape[0]),
        rows_of(g_out, gout_o.shape[0]),
    ]
    spares = [spare_w, spare_w, spare_t, None, None]
    dense = [
        DenseScatter(
            place, sources[i], low[i], high[i], line[i], cross[i], spares[i], out,
            [s.at[i] for s in dense_sems],
        )
        for i, out in enumerate((gsg_o, gsu_o, gsd_o, gqkv_o, gout_o))
    ]
    early, late = dense[:3], dense[3:]
    experts = ExpertScatter(
        place,
        (geg, geu, ged),
        (ecross_g, ecross_u, ecross_d),
        (eland_g, eland_u, eland_d),
        (eown_g, eown_u, eown_d),
        (emore_g, emore_u, emore_d),
        (geg_o, geu_o, ged_o),
        expert_sems,
    )
    prompts = [
        LineSum(
            place,
            lambda z, m=m: part.at[m, z],
            lambda slot, m=m: part_land.at[m, slot],
            part_send.at[m],
            part_recv.at[m],
        )
        for m in range(micro_count)
    ]

    def slot_rows(m, owner_of_rows):
        return pl.ds(pl.multiple_of((m * owners + owner_of_rows) * capacity, 16), capacity)

    def hand_back(source, land, send_sem, recv_sem, m, step):
        peer = place.peer_owner(step)
        return remote(
            source.at[:, slot_rows(m, peer)],
            land.at[m, owners - step],
            send_sem.at[step, m],
            recv_sem.at[owners - step, m],
            experts=peer,
        )

    returns = [(dins_i, ret_in, ri_send, ri_recv), (outs_i, ret_out, ro_send, ro_recv)]
    place.greet()
    for m in range(micro_count):
        for step in range(1, owners):
            hand_back(*returns[0], m, step).start()
    for d in early:
        d.start()
    experts.start()

    def fetch(pairs):
        copies = [
            pltpu.make_async_copy(source, target, load_sem.at[i])
            for i, (source, target) in enumerate(pairs)
        ]
        for copy in copies:
            copy.start()
        for copy in copies:
            copy.wait()

    def fetch_returned(source, land, recv_sem, target, m):
        for step in range(1, owners):
            arrived(land.at[m, step], recv_sem.at[step, m])
        pairs = []
        for step in range(owners):
            for local in range(local_count):
                at = pl.ds((step * local_count + local) * capacity, capacity)
                if step == 0:
                    piece = source.at[local, slot_rows(m, me)]
                else:
                    piece = land.at[m, step, local]
                pairs.append((piece, target.at[at]))
        fetch(pairs)

    for kind, d in enumerate(early):
        for direction in (1, -1):
            experts.pass_on(direction, depth - 1, 0, (kind,))
        d.add_low()
    for m in range(micro_count):
        for step in range(1, owners):
            hand_back(*returns[1], m, step).start()
    gain_own[...] = jnp.zeros_like(gain_own)

    def mark_pairs(first, second, m):
        for i, hit, _ in one_hots(routes.at[m], gates.at[m], me, local_count, total):
            here = pl.ds(i * capacity, capacity)
            expert = lax.rem(me * local_count + i, total)
            hit_first = either(hit, routes[m, 0:1, :] == expert)
            hit_second = either(hit, routes[m, 1:2, :] == expert)
            first[here, :] = hit_first.astype(F32).astype(BF)
            second[here, :] = hit_second.astype(F32).astype(BF)

    def after_experts(hidden, extra, back, first, second, g_rows, att, d_attn, wo):
        fetch([(out_w, wo)] + [(att_i.at[m], att.at[pl.ds(m * rows, rows)]) for m in range(micro_count)])
        for m in range(micro_count):
            fetch([(hid_i.at[m], hidden), (cot.at[m], g_rows), (dn2_i.at[pl.ds(m * rows, rows)], extra)])
            mark_pairs(first, second, m)
            fetch_returned(dins_i, ret_in, ri_recv, back, m)
            gain = gain_v[1:2, :]
            for i in range(rows // PB):
                here = pl.ds(i * PB, PB)
                both = first[:, here] + second[:, here]
                d_normed = extra[here, :] + tdot(both, back[...])
                values = hidden[here, :]
                root = lax.rsqrt(jnp.mean(values * values, -1, keepdims=True) + EPSILON)
                scaled = gain * d_normed
                d_values = (
                    g_rows[here, :].astype(F32)
                    + root * scaled
                    - values * (root * root * root) * jnp.mean(values * scaled, -1, keepdims=True)
                )
                gain_own[1:2, :] += jnp.sum(d_normed * values * root, 0, keepdims=True)
                there = pl.ds(m * rows + i * PB, PB)
                extra[here, :] = d_values
                low_part = d_values.astype(BF)
                d_attn[there, :] = low_part
                d_att[there, :] = ndot(low_part, wo[...]).astype(BF)
            fetch([(extra, d_hidden_o.at[m])])
            for kind in ((0,), (1, 2))[m] if m < 2 else ():
                for direction in (1, -1):
                    experts.pass_on(direction, depth - 1, 1, (kind,))

        def out_grad(here):
            g_out[here, :] = tdot(att[:, here], d_attn[...]).astype(BF)

        tiles(features, 256, out_grad)

    pl.run_scoped(
        after_experts,
        pltpu.VMEM((rows, features), F32),
        pltpu.VMEM((rows, features), F32),
        pltpu.VMEM((total * capacity, features), BF),
        pltpu.VMEM((total * capacity, rows), BF),
        pltpu.VMEM((total * capacity, rows), BF),
        pltpu.VMEM((rows, features), BF),
        pltpu.VMEM((micro_count * rows, features), BF),
        pltpu.VMEM((micro_count * rows, features), BF),
        pltpu.VMEM((features, features), BF),
    )

    def both_ways(items, step):
        for direction in (1, -1):
            for item in items:
                item.pass_on(direction, step)

    def prompts_on(m, step):
        for direction in (1, -1):
            prompts[m].pass_on(direction, step, lambda t, s: add_into(t, [s], 64))

    def experts_on(step, local):
        for direction in (1, -1):
            experts.pass_on(direction, step, local)

    def own_rows(i):
        start = place.z * PB if i == 0 else prompt + (i - 1) * PB
        return start, pl.ds(start if i else pl.multiple_of(start, PB), PB)

    def attention(k, v, q, lse, ds_s, p_s, wq, dn1):
        load_wq = pltpu.make_async_copy(qkv_w, wq, wq_sem.at[0])
        load_wq.start()
        lane = lax.broadcasted_iota(jnp.int32, (PB, 2 * HD), 1)
        wide_lane = lax.broadcasted_iota(jnp.int32, (rows, 2 * HD), 1)
        ds_s[...] = jnp.zeros_like(ds_s)
        p_s[...] = jnp.zeros_like(p_s)
        for m in range(micro_count):
            fetch([(k_i.at[m], k), (v_i.at[m], v), (q_i.at[m], q), (lse_i.at[m], lse)])
            whole = pl.ds(m * rows, rows)

            def pair(index, carry):
                lanes = pl.ds(pl.multiple_of(index * 2 * HD, 2 * HD), 2 * HD)
                for i in range(rows // PB):
                    here = pl.ds(i * PB, PB)
                    there = pl.ds(m * rows + i * PB, PB)
                    query, d_out, logs = q[here, lanes], d_att[there, lanes], lse[here, :]
                    start, table = own_rows(i)
                    seen = prompt + i * PB
                    keys, values = k[pl.ds(0, seen), lanes], v[pl.ds(0, seen), lanes]
                    column = lax.broadcasted_iota(jnp.int32, (PB, seen), 1)
                    row = lax.broadcasted_iota(jnp.int32, (PB, seen), 0)
                    allowed = column <= row + start
                    parts = []
                    for sub in range(2):
                        mine = lane // HD == sub
                        scores = ndot(jnp.where(mine, query, jnp.zeros_like(query)), keys)
                        log = jnp.sum(
                            jnp.where(lane == 2 * index + sub, logs, 0.0), -1, keepdims=True
                        )
                        probs = jnp.where(allowed, jnp.exp(scores - log), 0.0)
                        d_probs = ndot(jnp.where(mine, d_out, jnp.zeros_like(d_out)), values)
                        centre = jnp.sum(probs * d_probs, -1, keepdims=True)
                        d_scores = (probs * (d_probs - centre)).astype(BF)
                        ds_s[sub, here, pl.ds(0, seen)] = d_scores
                        p_s[sub, here, pl.ds(0, seen)] = probs.astype(BF)
                        parts.append(mdot(d_scores, keys))
                    d_query = jnp.where(lane < HD, parts[0], parts[1]) * HD**-0.5
                    d_query = rope(d_query, cosine[table, :], -sine_part[table, :])
                    dpq[there, lanes] = d_query.astype(BF)
                d_key = jnp.zeros((length, 2 * HD), F32)
                d_value = jnp.zeros((length, 2 * HD), F32)
                query, d_out = q[:, lanes], d_att[whole, lanes]
                for sub in range(2):
                    mine = wide_lane // HD == sub
                    d_key += tdot(ds_s[sub], jnp.where(mine, query, jnp.zeros_like(query)))
                    d_value += tdot(p_s[sub], jnp.where(mine, d_out, jnp.zeros_like(d_out)))
                keys_here = pl.ds(m * length, length)
                d_key = rope(d_key, cosine[...], -sine_part[...])
                dpk[keys_here, lanes] = d_key.astype(BF)
                dpv[keys_here, lanes] = d_value.astype(BF)
                return carry

            lax.fori_loop(0, features // (2 * HD), pair, 0)
            if m == 0:
                load_wq.wait()
            key_w, value_w = wq[pl.ds(features, features), :], wq[pl.ds(2 * features, features), :]
            for z in range(depth):
                here = pl.ds(m * length + z * PB, PB)
                part[m, z] = (mdot(dpk[here, :], key_w) + mdot(dpv[here, :], value_w)).astype(BF)
            prompts_on(m, depth - 1)
            for i in range(rows // PB):
                _, table = own_rows(i)
                start = own_rows(i)[0] + m * length
                here = pl.ds(pl.multiple_of(start, PB), PB)
                there = pl.ds(m * rows + i * PB, PB)
                dn1[pl.ds(i * PB, PB), :] = (
                    mdot(dpq[there, :], wq[pl.ds(0, features), :])
                    + mdot(dpk[here, :], key_w)
                    + mdot(dpv[here, :], value_w)
                )
            fetch([(dn1, dn1_o.at[m])])
            experts_on(depth - 2, m)
            if m == 0:
                for d in early:
                    d.add_high()
                both_ways(early, depth - 1)

    pl.run_scoped(
        attention,
        pltpu.VMEM((length, features), BF),
        pltpu.VMEM((length, features), BF),
        pltpu.VMEM((rows, features), BF),
        pltpu.VMEM((rows, 2 * HD), F32),
        pltpu.VMEM((2, rows, length), BF),
        pltpu.VMEM((2, rows, length), BF),
        pltpu.VMEM(qkv_w.shape, BF),
        pltpu.VMEM((rows, features), F32),
    )

    def weight_grads(n1, n1_own):
        pairs = []
        for m in range(micro_count):
            pairs.append((n1_i.at[m], n1.at[pl.ds(m * length, length)]))
            for i in range(rows // PB):
                _, here = own_rows(i)
                pairs.append((n1_i.at[m, here], n1_own.at[pl.ds(m * rows + i * PB, PB)]))
        fetch(pairs)

        def make(here):
            g_qkv[here, :] = tdot(dpq[:, here], n1_own[...]).astype(BF)

        def make_key(here):
            there = pl.ds(pl.multiple_of(here.start + features, 256), 256)
            g_qkv[there, :] = tdot(dpk[:, here], n1[...]).astype(BF)

        def make_value(here):
            there = pl.ds(pl.multiple_of(here.start + 2 * features, 256), 256)
            g_qkv[there, :] = tdot(dpv[:, here], n1[...]).astype(BF)

        tiles(features, 256, make)
        tiles(features, 256, make_key)
        tiles(features, 256, make_value)

    pl.run_scoped(
        weight_grads,
        pltpu.VMEM((micro_count * length, features), BF),
        pltpu.VMEM((micro_count * rows, features), BF),
    )
    for d in late:
        d.start()

    for step in range(depth - 2, 1, -1):
        for m in range(micro_count):
            prompts_on(m, step)
    for d in late:
        d.add_low()

    def outputs(hidden, side, back, first, second):
        for m in range(micro_count):
            fetch([(hid_i.at[m], hidden), (side_i.at[pl.ds(m * rows, rows)], side)])
            mark_pairs(first, second, m)
            fetch_returned(outs_i, ret_out, ro_recv, back, m)
            for i in range(rows // PB):
                here = pl.ds(i * PB, PB)
                routed = gate_rows[m, here, 0:1] * tdot(first[:, here], back[...])
                routed += gate_rows[m, here, 1:2] * tdot(second[:, here], back[...])
                out_rows[here, :] = (hidden[here, :] + side[here, :] + routed).astype(BF)
            fetch([(out_rows, mixed_o.at[m])])
            if m == 0:
                for step in range(depth - 2, 1, -1):
                    both_ways(early, step)
                for d in late:
                    d.add_high()
                both_ways(late, depth - 1)
                for step in range(depth - 3, 0, -1):
                    experts_on(step, 0)

    pl.run_scoped(
        outputs,
        pltpu.VMEM((rows, features), F32),
        pltpu.VMEM((rows, features), F32),
        pltpu.VMEM((total * capacity, features), BF),
        pltpu.VMEM((total * capacity, rows), BF),
        pltpu.VMEM((total * capacity, rows), BF),
    )

    def last_on(kind):
        for step in range(depth - 3, 0, -1):
            for local in range(1, local_count):
                for direction in (1, -1):
                    experts.pass_on(direction, step, local, (kind,))

    for m in range(micro_count):
        prompts_on(m, 1)
    both_ways(early, 1)
    last_on(0)
    for step in range(depth - 2, 1, -1):
        both_ways(late, step)

    def inputs(x_rows, d_hidden, dn1):
        for m in range(micro_count):
            fetch([(tokens.at[m], x_rows), (d_hidden_o.at[m], d_hidden), (dn1_o.at[m], dn1)])
            for direction, slot in ((1, place.z), (-1, depth)):

                def body(m=m, slot=slot):
                    prompts[m].arrive(slot)
                    dn1[pl.ds(0, PB), :] += part_land[m, slot].astype(F32)

                pl.when(prompts[m].upstream(direction))(body)
            gain = gain_v[0:1, :]
            for i in range(rows // PB):
                here = pl.ds(i * PB, PB)
                values, d_normed = x_rows[here, :].astype(F32), dn1[here, :]
                root = lax.rsqrt(jnp.mean(values * values, -1, keepdims=True) + EPSILON)
                scaled = gain * d_normed
                d_values = (
                    d_hidden[here, :]
                    + root * scaled
                    - values * (root * root * root) * jnp.mean(values * scaled, -1, keepdims=True)
                )
                gain_own[0:1, :] += jnp.sum(d_normed * values * root, 0, keepdims=True)
                out_rows[here, :] = d_values.astype(BF)
            fetch([(out_rows, input_o.at[m])])

    pl.run_scoped(
        inputs,
        pltpu.VMEM((rows, features), BF),
        pltpu.VMEM((rows, features), F32),
        pltpu.VMEM((rows, features), F32),
    )
    last_on(1)
    both_ways(late, 1)
    last_on(2)
    for d in early:
        d.end()

    def gain_copies(first, targets, lands):
        return [
            remote(gain_own, land, gain_send.at[first + i], gain_recv.at[first + i], **target)
            for i, (target, land) in enumerate(zip(targets, lands))
        ]

    def gain_add(copies, lands):
        for copy in copies:
            copy.wait()
        total_gain = gain_own[...]
        for land in lands:
            total_gain = total_gain + land[...]
        gain_own[...] = total_gain

    peers = range(1, high_count)
    places = range(1, depth)
    stages = [
        (0, [dict(experts=place.e + 1 - 2 * place.low)], [gain_low]),
        (
            1,
            [dict(experts=place.peer_high(s) * 2 + place.low) for s in peers],
            [gain_high.at[s - 1] for s in peers],
        ),
        (
            high_count,
            [dict(context=lax.rem(place.z + s, depth)) for s in places],
            [gain_line.at[s - 1] for s in places],
        ),
        (high_count + depth - 1, [dict(dp=1 - place.x)], [gain_cross]),
    ]

    def gain_start(i):
        copies = gain_copies(*stages[i])
        for copy in copies:
            copy.start()
        return copies

    for i in range(2):
        gain_add(gain_start(i), stages[i][2])
    line_copies = gain_start(2)
    experts.end(0)
    for d in late:
        d.end()
    gain_add(line_copies, stages[2][2])
    cross_copies = gain_start(3)
    for d in early:
        d.finish()
    for d in late:
        d.finish()
    for local in range(1, local_count):
        experts.end(local)
    gain_add(cross_copies, stages[3][2])
    fetch([(gain_own, gain_o)])
    for d in dense:
        d.drain()
    experts.drain()
    for p in prompts:
        p.drain()
    for m in range(micro_count):
        for step in range(1, owners):
            for entry in returns:
                hand_back(*entry, m, step).wait_send()


def run_backward(sizes, tokens, cot, gates, routes, gate_rows, forward):
    depth, high_count = sizes
    micro_count, rows, features = tokens.shape
    owners = high_count * 2
    line = depth * owners
    prompt = depth * PB
    length = prompt + CONT
    cosine, sine_part = rope_tables(prompt)
    gsg, geg, outs = forward[12], forward[15], forward[18]
    local_count, slots, _ = outs.shape
    total = owners * local_count
    capacity = rows * 8 // (3 * total)
    part = gsg.shape[1] // line
    width = geg.shape[2] // (2 * depth)
    hbm, vmem = pl.BlockSpec(memory_space=pltpu.HBM), pl.BlockSpec(memory_space=pltpu.VMEM)
    shapes = [(features, part), (features, part), (part, features)]
    shapes += [(forward[0].shape[0] // line, features), (forward[1].shape[0] // line, features)]
    expert_shapes = [(features, width), (features, width), (width, features)]
    returned = (micro_count, owners, local_count, capacity, features)
    out_dims = [(micro_count, rows, features)] * 2
    out_dims += [shapes[3], shapes[4], shapes[0], shapes[1], shapes[2]]
    out_dims += [(local_count,) + s for s in expert_shapes]
    out_shape = [jax.ShapeDtypeStruct(dims, BF) for dims in out_dims]
    out_shape += [jax.ShapeDtypeStruct((8, features), F32)]
    out_shape += [jax.ShapeDtypeStruct((depth + 1, local_count) + s, BF) for s in expert_shapes]
    out_shape += [jax.ShapeDtypeStruct(returned, BF)] * 2
    out_shape += [jax.ShapeDtypeStruct((micro_count, rows, features), F32)] * 2
    scratch = [pltpu.VMEM((depth, high_count) + s, BF) for s in shapes]
    scratch += [pltpu.VMEM((high_count - 1, depth) + s, BF) for s in shapes]
    scratch += [pltpu.VMEM((depth + 1,) + s, BF) for s in shapes]
    scratch += [pltpu.VMEM(s, BF) for s in shapes]
    scratch += [pltpu.VMEM((2,) + shapes[0], BF), pltpu.VMEM((2,) + shapes[2], BF)]
    scratch += [pltpu.VMEM((depth, local_count) + s, BF) for s in expert_shapes]
    scratch += [pltpu.VMEM(s, BF) for s in expert_shapes]
    scratch += [pltpu.VMEM((2,) + s, BF) for s in expert_shapes]
    token_rows, key_rows = micro_count * rows, micro_count * length
    gain = (8, features)
    scratch += [
        pltpu.VMEM((token_rows, features), BF),
        pltpu.VMEM((token_rows, features), BF),
        pltpu.VMEM((key_rows, features), BF),
        pltpu.VMEM((key_rows, features), BF),
        pltpu.VMEM(forward[0].shape, BF),
        pltpu.VMEM(forward[1].shape, BF),
        pltpu.VMEM((micro_count, depth, PB, features), BF),
        pltpu.VMEM((micro_count, depth + 1, PB, features), BF),
        pltpu.VMEM(gain, F32),
        pltpu.VMEM(gain, F32),
        pltpu.VMEM((high_count - 1,) + gain, F32),
        pltpu.VMEM((depth - 1,) + gain, F32),
        pltpu.VMEM(gain, F32),
        pltpu.VMEM((rows, features), BF),
    ]
    dma = pltpu.SemaphoreType.DMA
    scratch += DenseScatter.semaphores(len(shapes), depth, high_count)
    scratch += ExpertScatter.semaphores(depth, local_count)
    stages = 1 + high_count + depth
    scratch += [
        dma((micro_count, depth + 1)),
        dma((micro_count, depth + 1)),
        dma((owners, micro_count)),
        dma((owners, micro_count)),
        dma((owners, micro_count)),
        dma((owners, micro_count)),
        dma((stages,)),
        dma((stages,)),
        dma((max(total, 2 + micro_count, 4 * micro_count + micro_count),)),
        dma((1,)),
        dma((1,)),
    ]
    return pl.pallas_call(
        functools.partial(backward_kernel, sizes),
        out_shape=out_shape,
        in_specs=[hbm] * 2 + [vmem] * 5 + [hbm] * 2 + [vmem] + [hbm] * 17,
        out_specs=[hbm] * len(out_shape),
        scratch_shapes=scratch,
        compiler_params=pltpu.CompilerParams(
            collective_id=1, has_side_effects=True, vmem_limit_bytes=60 * MIB
        ),
        name="backward_and_sum",
    )(tokens, cot, gates, routes, gate_rows, cosine, sine_part, *forward)


def on_device_plain(
    tokens,
    cotangent,
    gates,
    routes,
    qkv_weight,
    out_weight,
    shared_gate,
    shared_up,
    shared_down,
    gains,
    expert_gate,
    expert_up,
    expert_down,
):
    micro_count = tokens.shape[2]
    row_count = tokens.shape[4]
    feature_count = tokens.shape[5]
    owners = lax.axis_size(EXPERTS)
    local_experts = expert_gate.shape[0]
    total_experts = owners * local_experts
    capacity = row_count * 8 // (3 * total_experts)
    blocks = lax.axis_size(CONTEXT)
    prompt = blocks * PB
    scaling = HD ** (-0.5)
    w_qkv, w_out, w_sgate, w_sup, w_sdown, w_gains = (
        lax.all_gather(qkv_weight, (CONTEXT, EXPERTS), axis=1, tiled=True),
        lax.all_gather(out_weight, (CONTEXT, EXPERTS), axis=0, tiled=True),
        lax.all_gather(shared_gate, (CONTEXT, EXPERTS), axis=1, tiled=True),
        lax.all_gather(shared_up, (CONTEXT, EXPERTS), axis=1, tiled=True),
        lax.all_gather(shared_down, (CONTEXT, EXPERTS), axis=0, tiled=True),
        lax.all_gather(gains, (CONTEXT, EXPERTS), axis=1, tiled=True),
    )
    e_gate, expert_up_weight, e_down = (
        lax.all_gather(expert_gate, (DP, CONTEXT), axis=2, tiled=True),
        lax.all_gather(expert_up, (DP, CONTEXT), axis=2, tiled=True),
        lax.all_gather(expert_down, (DP, CONTEXT), axis=1, tiled=True),
    )
    gain_one = w_gains[0].astype(jnp.float32)
    gain_two = w_gains[1].astype(jnp.float32)
    here_index = lax.axis_index(CONTEXT)
    row_ids = jnp.arange(row_count, dtype=jnp.int32)
    query_pos = jnp.where(row_ids < PB, here_index * PB + row_ids, prompt + row_ids - PB)
    key_pos = jnp.arange(prompt + CONT, dtype=jnp.int32)
    allowed = key_pos[None, None, :] <= query_pos[None, :, None]
    half_size = HD // 2
    frequency = 10000.0 ** (-2.0 * jnp.arange(half_size, dtype=jnp.float32) / HD)
    angles = query_pos.astype(jnp.float32)[:, None] * frequency
    cosine = jnp.cos(angles)[:, None, :]
    sine_part = jnp.sin(angles)[:, None, :]
    kept_list = []
    mixed_list = []
    for step_index in range(micro_count):
        inputs = tokens[0, 0, step_index, 0].astype(jnp.float32)
        root_one = lax.rsqrt(jnp.mean(inputs * inputs, -1, keepdims=True) + EPSILON)
        normed_one = (inputs * root_one * gain_one).astype(jnp.bfloat16)
        projected = mdot(normed_one, w_qkv)
        query = rotate(projected[:, :feature_count], cosine, sine_part).astype(jnp.bfloat16)
        key_rows = rotate(
            projected[:, feature_count : 2 * feature_count], cosine, sine_part
        ).astype(jnp.bfloat16)
        value_rows = projected[:, 2 * feature_count :].astype(jnp.bfloat16)
        prompt_key, prompt_value = (
            lax.all_gather(key_rows[:PB], CONTEXT, axis=0, tiled=True),
            lax.all_gather(value_rows[:PB], CONTEXT, axis=0, tiled=True),
        )
        key_heads = jnp.concatenate([prompt_key, key_rows[PB:]], 0).reshape(prompt + CONT, H, HD)
        value_heads = jnp.concatenate([prompt_value, value_rows[PB:]], 0).reshape(
            prompt + CONT, H, HD
        )
        query_heads = query.reshape(row_count, H, HD)
        scores = (
            jnp.einsum("qhd,khd->hqk", query_heads, key_heads, preferred_element_type=jnp.float32)
            * scaling
        )
        scores = jnp.where(allowed, scores, -1000000000.0)
        highest = jnp.max(scores, -1, keepdims=True)
        weights = jnp.exp(scores - highest)
        total = jnp.sum(weights, -1, keepdims=True)
        log_total = highest + jnp.log(total)
        probs = (weights / total).astype(jnp.bfloat16)
        attended = (
            jnp.einsum("hqk,khd->qhd", probs, value_heads, preferred_element_type=jnp.float32)
            .reshape(row_count, feature_count)
            .astype(jnp.bfloat16)
        )
        hidden = inputs + mdot(attended, w_out)
        root_two = lax.rsqrt(jnp.mean(hidden * hidden, -1, keepdims=True) + EPSILON)
        normed_two = (hidden * root_two * gain_two).astype(jnp.bfloat16)
        side_gate = mdot(normed_two, w_sgate)
        side_up = mdot(normed_two, w_sup)
        side_act = (jax.nn.silu(side_gate) * side_up).astype(jnp.bfloat16)
        side = mdot(side_act, w_sdown)
        route_rows = routes[0, 0, step_index, 0]
        slots = slot_table(route_rows, total_experts)
        flat_dest = (route_rows * capacity + slots).reshape(-1)
        source = (
            jnp.full((total_experts * capacity,), 2 * row_count, jnp.int32)
            .at[flat_dest]
            .set(jnp.arange(2 * row_count, dtype=jnp.int32))
        )
        padded = jnp.concatenate([normed_two, jnp.zeros((1, feature_count), jnp.bfloat16)], 0)
        send = padded[source // 2].reshape(total_experts, capacity, feature_count)
        received = lax.all_to_all(send, EXPERTS, split_axis=0, concat_axis=0, tiled=True)
        count = received.shape[1]
        expert_grouped = received.reshape(owners, local_experts, count, feature_count)
        expert_gate_act = jnp.einsum(
            "send,edf->senf", expert_grouped, e_gate, preferred_element_type=jnp.float32
        )
        expert_up_act = jnp.einsum(
            "send,edf->senf", expert_grouped, expert_up_weight, preferred_element_type=jnp.float32
        )
        expert_hidden_act = (jax.nn.silu(expert_gate_act) * expert_up_act).astype(jnp.bfloat16)
        result = jnp.einsum(
            "senf,efd->send", expert_hidden_act, e_down, preferred_element_type=jnp.float32
        ).astype(jnp.bfloat16)
        expert_out = result.reshape(owners * local_experts, count, feature_count)
        expert_in = received
        returned = lax.all_to_all(
            expert_out, EXPERTS, split_axis=0, concat_axis=0, tiled=True
        ).reshape(-1, feature_count)
        gate_rows = gates[0, 0, step_index, 0]
        picked = returned[flat_dest].reshape(row_count, 2, feature_count).astype(jnp.float32)
        routed = jnp.sum(gate_rows[:, :, None] * picked, 1)
        mixed_list.append((hidden + routed + side).astype(jnp.bfloat16))
        cached = (prompt_key, prompt_value)
        kept_list.append(
            (
                inputs,
                root_one,
                normed_one,
                query,
                key_rows,
                value_rows,
                cached,
                log_total,
                attended,
                hidden,
                root_two,
                normed_two,
                side_gate,
                side_up,
                side_act,
                flat_dest,
                source,
                expert_in,
                gate_rows,
            )
        )
    acc_qkv = jnp.zeros(w_qkv.shape, jnp.float32)
    acc_out = jnp.zeros(w_out.shape, jnp.float32)
    acc_sgate = jnp.zeros(w_sgate.shape, jnp.float32)
    acc_sup = jnp.zeros(w_sup.shape, jnp.float32)
    acc_sdown = jnp.zeros(w_sdown.shape, jnp.float32)
    acc_gain_one = jnp.zeros((feature_count,), jnp.float32)
    acc_gain_two = jnp.zeros((feature_count,), jnp.float32)
    local_egate = jnp.zeros(e_gate.shape, jnp.float32)
    local_expert_up_weight = jnp.zeros(expert_up_weight.shape, jnp.float32)
    local_edown = jnp.zeros(e_down.shape, jnp.float32)
    input_list = []
    for step_index in range(micro_count):
        (
            inputs,
            root_one,
            normed_one,
            query,
            key_rows,
            value_rows,
            cached,
            log_total,
            attended,
            hidden,
            root_two,
            normed_two,
            side_gate,
            side_up,
            side_act,
            flat_dest,
            source,
            expert_in,
            gate_rows,
        ) = kept_list[step_index]
        grad_rows = cotangent[0, 0, step_index, 0].astype(jnp.float32)
        grad_low = grad_rows.astype(jnp.bfloat16)
        acc_sdown = acc_sdown + tdot(side_act, grad_low)
        d_side_act = ndot(grad_low, w_sdown).astype(jnp.bfloat16).astype(jnp.float32)
        silu_side, slope_side = silu_parts(side_gate)
        d_side_gate = (d_side_act * side_up * slope_side).astype(jnp.bfloat16)
        d_side_up = (d_side_act * silu_side).astype(jnp.bfloat16)
        acc_sgate = acc_sgate + tdot(normed_two, d_side_gate)
        acc_sup = acc_sup + tdot(normed_two, d_side_up)
        d_normed_two = ndot(d_side_gate, w_sgate) + ndot(d_side_up, w_sup)
        d_pairs = (
            (gate_rows[:, :, None] * grad_rows[:, None, :])
            .astype(jnp.bfloat16)
            .reshape(2 * row_count, feature_count)
        )
        padded_grad = jnp.concatenate([d_pairs, jnp.zeros((1, feature_count), jnp.bfloat16)], 0)
        grad_send = padded_grad[source].reshape(total_experts, capacity, feature_count)
        grad_in = lax.all_to_all(grad_send, EXPERTS, split_axis=0, concat_axis=0, tiled=True)
        grouped_grad = grad_in.reshape(owners, local_experts, capacity, feature_count)
        grouped = expert_in.reshape(owners, local_experts, capacity, feature_count)
        gate_act = jnp.einsum("send,edf->senf", grouped, e_gate, preferred_element_type=jnp.float32)
        up_act = jnp.einsum(
            "send,edf->senf", grouped, expert_up_weight, preferred_element_type=jnp.float32
        )
        silu_gate, slope_gate = silu_parts(gate_act)
        hidden_act = (silu_gate * up_act).astype(jnp.bfloat16)
        d_hidden_act = (
            jnp.einsum("send,efd->senf", grouped_grad, e_down, preferred_element_type=jnp.float32)
            .astype(jnp.bfloat16)
            .astype(jnp.float32)
        )
        d_gate_act = (d_hidden_act * up_act * slope_gate).astype(jnp.bfloat16)
        d_up_act = (d_hidden_act * silu_gate).astype(jnp.bfloat16)
        step_edown = jnp.einsum(
            "senf,send->efd", hidden_act, grouped_grad, preferred_element_type=jnp.float32
        )
        step_egate = jnp.einsum(
            "send,senf->edf", grouped, d_gate_act, preferred_element_type=jnp.float32
        )
        stepwise_expert_up = jnp.einsum(
            "send,senf->edf", grouped, d_up_act, preferred_element_type=jnp.float32
        )
        local_egate = local_egate + step_egate
        local_expert_up_weight = local_expert_up_weight + stepwise_expert_up
        local_edown = local_edown + step_edown
        d_expert_in = jnp.einsum(
            "senf,edf->send", d_gate_act, e_gate, preferred_element_type=jnp.float32
        ) + jnp.einsum(
            "senf,edf->send", d_up_act, expert_up_weight, preferred_element_type=jnp.float32
        )
        d_expert_in = d_expert_in.astype(jnp.bfloat16).reshape(
            total_experts, capacity, feature_count
        )
        back = lax.all_to_all(
            d_expert_in, EXPERTS, split_axis=0, concat_axis=0, tiled=True
        ).reshape(-1, feature_count)
        d_normed_two = d_normed_two + jnp.sum(
            back[flat_dest].reshape(row_count, 2, feature_count).astype(jnp.float32), 1
        )
        scaled_two = gain_two * d_normed_two
        d_hidden = (
            grad_rows
            + root_two * scaled_two
            - hidden * root_two**3 * jnp.mean(hidden * scaled_two, -1, keepdims=True)
        )
        acc_gain_two = acc_gain_two + jnp.sum(d_normed_two * hidden * root_two, 0)
        d_attn = d_hidden.astype(jnp.bfloat16)
        acc_out = acc_out + tdot(attended, d_attn)
        d_attended = ndot(d_attn, w_out).astype(jnp.bfloat16)
        prompt_key, prompt_value = cached
        key_heads = jnp.concatenate([prompt_key, key_rows[PB:]], 0).reshape(prompt + CONT, H, HD)
        value_heads = jnp.concatenate([prompt_value, value_rows[PB:]], 0).reshape(
            prompt + CONT, H, HD
        )
        query_heads = query.reshape(row_count, H, HD)
        scores = (
            jnp.einsum("qhd,khd->hqk", query_heads, key_heads, preferred_element_type=jnp.float32)
            * scaling
        )
        scores = jnp.where(allowed, scores, -1000000000.0)
        probs = jnp.exp(scores - log_total)
        d_heads = d_attended.reshape(row_count, H, HD)
        d_probs = jnp.einsum(
            "qhd,khd->hqk", d_heads, value_heads, preferred_element_type=jnp.float32
        )
        centre = jnp.sum(probs * d_probs, -1, keepdims=True)
        d_scores = (probs * (d_probs - centre)).astype(jnp.bfloat16)
        d_query = (
            jnp.einsum(
                "hqk,khd->qhd", d_scores, key_heads, preferred_element_type=jnp.float32
            ).reshape(row_count, feature_count)
            * scaling
        )
        d_keys = (
            jnp.einsum(
                "hqk,qhd->khd", d_scores, query_heads, preferred_element_type=jnp.float32
            ).reshape(prompt + CONT, feature_count)
            * scaling
        )
        d_values = jnp.einsum(
            "hqk,qhd->khd", probs.astype(jnp.bfloat16), d_heads, preferred_element_type=jnp.float32
        ).reshape(prompt + CONT, feature_count)
        own_dkey, own_dvalue = (
            lax.psum_scatter(
                d_keys[:prompt].astype(jnp.bfloat16), CONTEXT, scatter_dimension=0, tiled=True
            ).astype(jnp.float32),
            lax.psum_scatter(
                d_values[:prompt].astype(jnp.bfloat16), CONTEXT, scatter_dimension=0, tiled=True
            ).astype(jnp.float32),
        )
        d_key_rows = jnp.concatenate([own_dkey, d_keys[prompt:]], 0)
        d_value_rows = jnp.concatenate([own_dvalue, d_values[prompt:]], 0)
        d_projected = jnp.concatenate(
            [
                rotate(d_query, cosine, -sine_part).astype(jnp.bfloat16),
                rotate(d_key_rows, cosine, -sine_part).astype(jnp.bfloat16),
                d_value_rows.astype(jnp.bfloat16),
            ],
            1,
        )
        acc_qkv = acc_qkv + tdot(normed_one, d_projected)
        d_normed_one = ndot(d_projected, w_qkv)
        scaled_one = gain_one * d_normed_one
        d_inputs = (
            d_hidden
            + root_one * scaled_one
            - inputs * root_one**3 * jnp.mean(inputs * scaled_one, -1, keepdims=True)
        )
        acc_gain_one = acc_gain_one + jnp.sum(d_normed_one * inputs * root_one, 0)
        input_list.append(d_inputs.astype(jnp.bfloat16))
    sharded_expert_gate, sharded_expert_up, sharded_expert_down = (
        lax.psum_scatter(
            local_egate.astype(jnp.bfloat16), (DP, CONTEXT), scatter_dimension=2, tiled=True
        ).astype(jnp.float32),
        lax.psum_scatter(
            local_expert_up_weight.astype(jnp.bfloat16),
            (DP, CONTEXT),
            scatter_dimension=2,
            tiled=True,
        ).astype(jnp.float32),
        lax.psum_scatter(
            local_edown.astype(jnp.bfloat16), (DP, CONTEXT), scatter_dimension=1, tiled=True
        ).astype(jnp.float32),
    )
    acc_gains = jnp.stack([acc_gain_one, acc_gain_two], 0)
    dense_shards = (
        lax.psum_scatter(acc_qkv, (CONTEXT, EXPERTS), scatter_dimension=1, tiled=True),
        lax.psum_scatter(acc_out, (CONTEXT, EXPERTS), scatter_dimension=0, tiled=True),
        lax.psum_scatter(acc_sgate, (CONTEXT, EXPERTS), scatter_dimension=1, tiled=True),
        lax.psum_scatter(acc_sup, (CONTEXT, EXPERTS), scatter_dimension=1, tiled=True),
        lax.psum_scatter(acc_sdown, (CONTEXT, EXPERTS), scatter_dimension=0, tiled=True),
        lax.psum_scatter(acc_gains, (CONTEXT, EXPERTS), scatter_dimension=1, tiled=True),
    )
    grad_qkv, grad_out, grad_sgate, grad_sup, grad_sdown, grad_gains = (
        lax.psum(dense_shards[0].astype(jnp.bfloat16), DP).astype(jnp.float32),
        lax.psum(dense_shards[1].astype(jnp.bfloat16), DP).astype(jnp.float32),
        lax.psum(dense_shards[2].astype(jnp.bfloat16), DP).astype(jnp.float32),
        lax.psum(dense_shards[3].astype(jnp.bfloat16), DP).astype(jnp.float32),
        lax.psum(dense_shards[4].astype(jnp.bfloat16), DP).astype(jnp.float32),
        lax.psum(dense_shards[5].astype(jnp.bfloat16), DP).astype(jnp.float32),
    )
    mixed = jnp.stack(mixed_list, 0).reshape(tokens.shape)
    input_grad = jnp.stack(input_list, 0).reshape(tokens.shape)
    return (
        mixed,
        input_grad,
        grad_qkv,
        grad_out,
        grad_sgate,
        grad_sup,
        grad_sdown,
        grad_gains,
        sharded_expert_gate,
        sharded_expert_up,
        sharded_expert_down,
    )


def on_device(
    tokens,
    cotangent,
    gates,
    routes,
    qkv_weight,
    out_weight,
    shared_gate,
    shared_up,
    shared_down,
    gains,
    expert_gate,
    expert_up,
    expert_down,
):
    owners = lax.axis_size(EXPERTS)
    sizes = (lax.axis_size(CONTEXT), owners // 2)
    own_at = lax.axis_index(CONTEXT) * owners + lax.axis_index(EXPERTS)
    gain_width, features = gains.shape[1], tokens.shape[5]
    gain_rows = lax.dynamic_update_slice(
        jnp.zeros((16, features), jnp.bfloat16), gains, (0, own_at * gain_width)
    )
    rows, cot = tokens[0, 0, :, 0], cotangent[0, 0, :, 0]
    gate_rows, route_rows = gates[0, 0, :, 0], routes[0, 0, :, 0]
    gate_columns, route_columns = gate_rows.transpose(0, 2, 1), route_rows.transpose(0, 2, 1)
    forward = run_forward(
        sizes,
        rows,
        cot,
        gate_columns,
        route_columns,
        (qkv_weight.T, out_weight, gain_rows, shared_gate, shared_up, shared_down),
        (expert_gate, expert_up, expert_down),
    )
    (
        mixed, input_grad, grad_qkv, grad_out, grad_sgate, grad_sup, grad_sdown,
        grad_egate, grad_eup, grad_edown, gain_sum, *_,
    ) = run_backward(
        sizes, rows, cot, gate_columns, route_columns, gate_rows, forward[:3] + forward[9:]
    )
    return (
        mixed.reshape(tokens.shape),
        input_grad.reshape(tokens.shape),
        grad_qkv.T.astype(F32),
        grad_out.astype(F32),
        grad_sgate.astype(F32),
        grad_sup.astype(F32),
        grad_sdown.astype(F32),
        lax.dynamic_slice(gain_sum, (0, own_at * gain_width), (2, gain_width)),
        grad_egate.astype(F32),
        grad_eup.astype(F32),
        grad_edown.astype(F32),
    )


def kernels_fit(mesh_shape, arrays):
    qkv_weight, out_weight, shared_gate, _, shared_down = arrays[4:9]
    rows = (qkv_weight.shape[1], out_weight.shape[0], shared_gate.shape[1], shared_down.shape[0])
    return (
        mesh_shape[DP] == 2
        and mesh_shape[EXPERTS] % 2 == 0
        and all(count % 16 == 0 for count in rows)
        and shared_gate.shape[1] % 128 == 0
        and arrays[10].shape[2] % 128 == 0
    )


def solution(mesh):
    def device_program(*arrays):
        return (on_device if kernels_fit(mesh.shape, arrays) else on_device_plain)(*arrays)

    return jax.shard_map(
        device_program,
        mesh=mesh,
        in_specs=(
            P(DP, EXPERTS, None, CONTEXT, None, None),
            P(DP, EXPERTS, None, CONTEXT, None, None),
            P(DP, EXPERTS, None, CONTEXT, None, None),
            P(DP, EXPERTS, None, CONTEXT, None, None),
            P(None, (CONTEXT, EXPERTS)),
            P((CONTEXT, EXPERTS), None),
            P(None, (CONTEXT, EXPERTS)),
            P(None, (CONTEXT, EXPERTS)),
            P((CONTEXT, EXPERTS), None),
            P(None, (CONTEXT, EXPERTS)),
            P(EXPERTS, None, (DP, CONTEXT)),
            P(EXPERTS, None, (DP, CONTEXT)),
            P(EXPERTS, (DP, CONTEXT), None),
        ),
        out_specs=(
            P(DP, EXPERTS, None, CONTEXT, None, None),
            P(DP, EXPERTS, None, CONTEXT, None, None),
            P(None, (CONTEXT, EXPERTS)),
            P((CONTEXT, EXPERTS), None),
            P(None, (CONTEXT, EXPERTS)),
            P(None, (CONTEXT, EXPERTS)),
            P((CONTEXT, EXPERTS), None),
            P(None, (CONTEXT, EXPERTS)),
            P(EXPERTS, None, (DP, CONTEXT)),
            P(EXPERTS, None, (DP, CONTEXT)),
            P(EXPERTS, (DP, CONTEXT), None),
        ),
        check_vma=False,
    )
```

```python
import functools

import jax
import jax.numpy as jnp
import numpy as np
from jax import lax
from jax.experimental import pallas as pl
from jax.experimental.pallas import tpu as pltpu
from jax.sharding import PartitionSpec as P

DP, CONTEXT, EXPERTS = "dp", "context", "experts"

H = 12
HD = 64
PB = 128
CONT = 256


EPSILON = 1e-06


def mdot(former, latter):
    return jnp.dot(former, latter, preferred_element_type=jnp.float32)


def tdot(former, latter):
    return lax.dot_general(
        former, latter, (((0,), (0,)), ((), ())), preferred_element_type=jnp.float32
    )


def ndot(former, latter):
    return lax.dot_general(
        former, latter, (((1,), (1,)), ((), ())), preferred_element_type=jnp.float32
    )


def rotate(values, cosine, sine_part):
    half_size = HD // 2
    shaped = values.reshape(values.shape[0], H, HD)
    former = shaped[..., :half_size]
    latter = shaped[..., half_size:]
    turned = jnp.concatenate(
        [former * cosine - latter * sine_part, latter * cosine + former * sine_part], -1
    )
    return turned.reshape(values.shape)


def slot_table(routes_block, expert_count):
    flat_routes = routes_block.reshape(-1)
    onehot = (flat_routes[:, None] == jnp.arange(expert_count, dtype=jnp.int32)[None, :]).astype(
        jnp.int32
    )
    before = jnp.cumsum(onehot, 0) - onehot
    return jnp.sum(before * onehot, 1).reshape(routes_block.shape)


def silu_parts(values):
    sigma = jax.nn.sigmoid(values)
    return (values * sigma, sigma * (1.0 + values * (1.0 - sigma)))


MESH = pl.DeviceIdType.MESH
MIB = 1024 * 1024
BF = jnp.bfloat16
F32 = jnp.float32


def remote(source, target, send_sem, recv_sem, **device):
    return pltpu.make_async_remote_copy(
        src_ref=source,
        dst_ref=target,
        send_sem=send_sem,
        recv_sem=recv_sem,
        device_id=device,
        device_id_type=MESH,
    )


def arrived(slot, recv_sem):
    remote(slot, slot, recv_sem, recv_sem, context=0).wait_recv()


def either(first, second):
    return jnp.logical_and(first, second)


class Place:
    def __init__(self, sizes):
        self.depth, self.high_count = sizes
        self.owners = self.high_count * 2
        self.x = lax.axis_index(DP)
        self.z = lax.axis_index(CONTEXT)
        self.e = lax.axis_index(EXPERTS)
        self.high = self.e // 2
        self.low = self.e % 2

    def shard(self, z):
        return self.x * self.depth + z

    def other_shard(self, z):
        return (1 - self.x) * self.depth + z

    def peer_high(self, step):
        return lax.rem(self.high + step, self.high_count)

    def peer_owner(self, step):
        return lax.rem(self.e + step, self.owners)

    def on_line(self, z):
        return (z >= 0) & (z < self.depth)

    def greet(self):
        barrier = pltpu.get_barrier_semaphore()

        def signal(**device):
            pl.semaphore_signal(barrier, inc=1, device_id=device, device_id_type=MESH)

        signal(dp=1 - self.x)
        for step in range(1, self.owners):
            signal(experts=self.peer_owner(step))
        for step in range(1, self.depth):
            signal(context=lax.rem(self.z + step, self.depth))
        count = self.owners + self.depth - 1
        pl.semaphore_wait(barrier, count)


class Line:
    def __init__(self, place, own, slot, send_sem, recv_sem):
        self.place, self.own, self.slot = place, own, slot
        self.send_sem, self.recv_sem = send_sem, recv_sem

    def _copy(self, direction, step):
        place = self.place
        z = place.z - direction * step
        source = self.own if step == 0 else self.slot(z)
        return remote(
            source,
            self.slot(z),
            self.send_sem.at[(direction + 1) // 2, step],
            self.recv_sem.at[z],
            context=place.z + direction,
        )

    def _valid(self, direction, step):
        place = self.place
        return place.on_line(place.z - direction * step) & place.on_line(place.z + direction)

    def send(self, direction, step):
        if step < self.place.depth - 1:
            pl.when(self._valid(direction, step))(lambda: self._copy(direction, step).start())

    def start(self):
        self.send(1, 0)
        self.send(-1, 0)

    def hop(self, step, then=None):
        for direction in (1, -1):
            z = self.place.z - direction * (step + 1)

            def body(direction=direction, z=z):
                arrived(self.slot(z), self.recv_sem.at[z])
                self.send(direction, step + 1)
                if then is not None:
                    then(z)

            pl.when(self.place.on_line(z))(body)

    def drain(self):
        for direction in (1, -1):
            for step in range(self.place.depth - 1):
                pl.when(self._valid(direction, step))(
                    lambda d=direction, s=step: self._copy(d, s).wait_send()
                )


class DenseGather:
    def __init__(self, place, own, slot, sems):
        self.place, self.own, self.slot_of = place, own, slot
        zs, zr, self.h_send, self.h_recv, self.l_send, self.l_recv = sems
        self.line = Line(place, own, lambda z: self.slot(z, place.high, place.low), zs, zr)

    @staticmethod
    def semaphores(count, depth, high_count):
        dma = pltpu.SemaphoreType.DMA
        cross = dma((count, high_count, depth))
        return [dma((count, 2, depth)), dma((count, depth)), cross, cross, cross, cross]

    def slot(self, z, high, low):
        return self.slot_of((z * self.place.high_count + high) * 2 + low)

    def _to_high(self, z, step, own):
        place = self.place
        target = self.slot(z, place.high, place.low)
        return remote(
            self.own if own else target,
            target,
            self.h_send.at[step, z],
            self.h_recv.at[place.high, z],
            experts=place.peer_high(step) * 2 + place.low,
        )

    def _to_low(self, z, high, own):
        place = self.place
        target = self.slot(z, high, place.low)
        return remote(
            self.own if own else target,
            target,
            self.l_send.at[high, z],
            self.l_recv.at[high, z],
            experts=place.e + 1 - 2 * place.low,
        )

    def _spread(self, z, own=False):
        for step in range(1, self.place.high_count):
            self._to_high(z, step, own).start()
        self._to_low(z, self.place.high, own).start()

    def start(self):
        self.line.start()
        self._spread(self.place.z, True)

    def hop(self, step):
        self.line.hop(step, self._spread)

    def cross(self, z):
        place = self.place
        for step in range(1, place.high_count):
            high = place.peer_high(step)
            arrived(self.slot(z, high, place.low), self.h_recv.at[high, z])
            self._to_low(z, high, False).start()

    def finish(self, z):
        place = self.place
        for high in range(place.high_count):
            arrived(self.slot(z, high, 1 - place.low), self.l_recv.at[high, z])

    def drain(self):
        place = self.place
        self.line.drain()
        for z in range(place.depth):
            for step in range(1, place.high_count):
                self._to_high(z, step, False).wait_send()
            for high in range(place.high_count):
                self._to_low(z, high, False).wait_send()


def expert_slab(ref, kind, local, shard, width):
    start = pl.multiple_of(shard * width, 128)
    if kind == 2:
        return ref.at[local, pl.ds(start, width)]
    return ref.at[local, :, pl.ds(start, width)]


class ExpertGather:
    def __init__(self, place, own, out, sems):
        self.place, self.own, self.out = place, own, out
        self.z_send, self.z_recv, self.x_send, self.x_recv = sems
        self.local_count, self.width = own[0].shape[0], own[0].shape[2]

    @staticmethod
    def semaphores(depth, local_count):
        dma = pltpu.SemaphoreType.DMA
        return [
            dma((local_count, 3, 2, depth)),
            dma((local_count, 3, depth)),
            dma((local_count, 3, depth)),
            dma((local_count, 3, depth)),
        ]

    def slot(self, local, kind, shard):
        return expert_slab(self.out[kind], kind, local, shard, self.width)

    def _line(self, local, kind):
        return Line(
            self.place,
            self.own[kind].at[local],
            lambda z: self.slot(local, kind, self.place.shard(z)),
            self.z_send.at[local, kind],
            self.z_recv.at[local, kind],
        )

    def _across(self, local, kind, z, own=False):
        target = self.slot(local, kind, self.place.shard(z))
        return remote(
            self.own[kind].at[local] if own else target,
            target,
            self.x_send.at[local, kind, z],
            self.x_recv.at[local, kind, z],
            dp=1 - self.place.x,
        )

    def start_x(self):
        for local in range(self.local_count):
            for kind in range(3):
                self._across(local, kind, self.place.z, True).start()

    def start_z(self):
        for local in range(self.local_count):
            for kind in range(3):
                self._line(local, kind).start()

    def hop(self, local, step):
        for kind in range(3):
            self._line(local, kind).hop(
                step, lambda z, kind=kind: self._across(local, kind, z).start()
            )

    def wait_x(self, local, z):
        for kind in range(3):
            arrived(
                self.slot(local, kind, self.place.other_shard(z)), self.x_recv.at[local, kind, z]
            )

    def drain(self):
        for local in range(self.local_count):
            for kind in range(3):
                self._line(local, kind).drain()
                for z in range(self.place.depth):
                    self._across(local, kind, z).wait_send()


def rope(values, cosine, sine_part):
    lane = lax.broadcasted_iota(jnp.int32, cosine.shape, 1)
    first = lax.rem(lane, HD) < HD // 2
    turned = []
    for start in range(0, values.shape[1], 2 * HD):
        part = values[:, start : start + 2 * HD]
        partner = jnp.where(
            first, pltpu.roll(part, 2 * HD - HD // 2, 1), pltpu.roll(part, HD // 2, 1)
        )
        turned.append(part * cosine + partner * sine_part)
    return jnp.concatenate(turned, 1)


def norm_rows(values, gain):
    root = lax.rsqrt(jnp.mean(values * values, -1, keepdims=True) + EPSILON)
    return (values * root * gain).astype(BF)


def tiles(total, size, body):
    def run(i, carry):
        body(pl.ds(pl.multiple_of(i * size, size), size))
        return carry

    lax.fori_loop(0, total // size, run, 0)


def one_hots(routes, gates, me, local_count, total):
    rows = routes.shape[1]
    capacity = rows * 8 // (3 * total)
    first, second = routes[0:1, :], routes[1:2, :]
    ids = lax.rem(
        lax.broadcasted_iota(jnp.int32, (total, rows), 0) + me * local_count, total
    )
    named = (first == ids) | (second == ids)
    earlier = (
        lax.broadcasted_iota(jnp.int32, (rows, rows), 0)
        < lax.broadcasted_iota(jnp.int32, (rows, rows), 1)
    ).astype(F32).astype(BF)
    counts = mdot(named.astype(F32).astype(BF), earlier).astype(jnp.int32)
    places = jnp.where(named, counts, -1)
    weights = jnp.where(first == ids, gates[0:1, :], 0.0) + jnp.where(
        second == ids, gates[1:2, :], 0.0
    )
    slot = lax.broadcasted_iota(jnp.int32, (capacity, rows), 0)
    for i in range(total):
        yield i, slot == places[i : i + 1, :], weights[i : i + 1, :]


def ffn_chunk(x, g, weights, saved, sums, grads, tile):
    gate_w, up_w, down_w = weights
    act_s, d_gate_s, d_up_s = saved
    out_sum, in_sum = sums

    def forward(here):
        x_rows, g_rows = x[here, :], g[here, :]
        gate = mdot(x_rows, gate_w[...])
        up = mdot(x_rows, up_w[...])
        d_act = ndot(g_rows, down_w[...]).astype(BF).astype(F32)
        sigma = jax.nn.sigmoid(gate)
        silu = gate * sigma
        act = (silu * up).astype(BF)
        d_gate = (d_act * up * (sigma * (1.0 + gate * (1.0 - sigma)))).astype(BF)
        d_up = (d_act * silu).astype(BF)
        act_s[here, :] = act
        d_gate_s[here, :] = d_gate
        d_up_s[here, :] = d_up
        out_sum[here, :] += mdot(act, down_w[...])
        in_sum[here, :] += ndot(d_gate, gate_w[...]) + ndot(d_up, up_w[...])

    rows = x.shape[0]
    tiles(rows, tile, forward)
    used = pl.ds(0, rows)

    def weight_grads(here):
        grads[0][here, :] = tdot(x[:, here], d_gate_s[used, :]).astype(BF)
        grads[1][here, :] = tdot(x[:, here], d_up_s[used, :]).astype(BF)
        grads[2][:, here] = tdot(act_s[used, :], g[:, here]).astype(BF)

    tiles(x.shape[1], 256, weight_grads)


def forward_kernel(sizes, *refs):
    place = Place(sizes)
    depth, high_count = sizes
    owners = place.owners
    (
        tokens, cot, gates, routes, cosine, sine_part,
        qkv_in, out_in, gain_in, sg_in, su_in, sd_in, eg_in, eu_in, ed_in,
        qkv_o, out_o, gain_o, sg_o, su_o, sd_o, eg_o, eu_o, ed_o,
        n1_o, k_o, v_o, q_o, att_o, hid_o, lse_o, side_o, dn2_o,
        gsg_o, gsu_o, gsd_o, geg_o, geu_o, ged_o, outs_o, dins_o, pre_g, pre_u, pre_d,
        xk, wq, wo, gain_land, gain_v, g_all, n2, in_s, do_s, send_in, send_do,
        wg, wu, wd, act_s, dg_s, du_s, stage_g, stage_u, stage_d,
        *sems,
    ) = refs
    dense_sems, sems = sems[:6], sems[6:]
    expert_sems, sems = sems[:4], sems[4:]
    (
        line_send, line_recv, load_sem, ai_send, ai_recv, ad_send, ad_recv,
        chunk_sem, store_sem, out_sem, pre_send, pre_recv,
    ) = sems
    micro_count, rows, features = tokens.shape
    prompt = depth * PB
    length = prompt + CONT
    local_count, _, width = eg_in.shape
    total = owners * local_count
    capacity = rows * 8 // (3 * total)
    slots = in_s.shape[1]
    me = place.e

    def dense(i, own, slot):
        return DenseGather(place, own, slot, [s.at[i] for s in dense_sems])

    def rows_of(ref, count):
        return lambda s: ref.at[pl.ds(pl.multiple_of(s * count, 16), count)]

    def columns_of(ref, count):
        return lambda s: ref.at[:, pl.ds(pl.multiple_of(s * count, 128), count)]

    early = [
        dense(0, qkv_in, rows_of(wq, qkv_in.shape[0])),
        dense(1, out_in, rows_of(wo, out_in.shape[0])),
        dense(2, gain_in, rows_of(gain_land, gain_in.shape[0])),
    ]
    late = [
        dense(3, sg_in, columns_of(sg_o, sg_in.shape[1])),
        dense(4, su_in, columns_of(su_o, su_in.shape[1])),
        dense(5, sd_in, rows_of(sd_o, sd_in.shape[0])),
    ]
    experts = ExpertGather(place, (eg_in, eu_in, ed_in), (eg_o, eu_o, ed_o), expert_sems)
    own_prompt = pl.ds(pl.multiple_of(place.z * PB, PB), PB)
    prompts = [
        Line(
            place,
            tokens.at[m, pl.ds(0, PB)],
            lambda z, m=m: xk.at[m, pl.ds(pl.multiple_of(z * PB, PB), PB)],
            line_send.at[m],
            line_recv.at[m],
        )
        for m in range(micro_count)
    ]
    own_at = (place.z * high_count + place.high) * 2 + place.low
    loads = [
        (tokens.at[:, pl.ds(0, PB)], xk.at[:, own_prompt]),
        (tokens.at[:, pl.ds(PB, CONT)], xk.at[:, pl.ds(prompt, CONT)]),
    ]
    loads += [(cot.at[m], g_all.at[pl.ds(m * rows, rows)]) for m in range(micro_count)]
    loads += [(d.own, d.slot_of(own_at)) for d in early]
    bounce = [
        (sg_in, wg.at[0, :, pl.ds(0, sg_in.shape[1])], late[0].slot_of(own_at)),
        (su_in, wu.at[0, :, pl.ds(0, su_in.shape[1])], late[1].slot_of(own_at)),
        (sd_in, wd.at[0, pl.ds(0, sd_in.shape[0])], late[2].slot_of(own_at)),
    ]
    loads += [(source, middle) for source, middle, _ in bounce]
    load_copies = [
        pltpu.make_async_copy(source, target, load_sem.at[i])
        for i, (source, target) in enumerate(loads)
    ]
    bounce_copies = [
        pltpu.make_async_copy(middle, target, load_sem.at[i])
        for i, (_, middle, target) in enumerate(bounce)
    ]
    for copy in load_copies:
        copy.start()
    place.greet()
    for d in early:
        d.start()
    experts.start_x()
    for copy in load_copies:
        copy.wait()
    for copy in bounce_copies:
        copy.start()
    stores = []

    def store(source, target):
        copy = pltpu.make_async_copy(source, target, out_sem.at[len(stores)])
        copy.start()
        stores.append(copy)

    def slot_rows(m, sender):
        return pl.ds(pl.multiple_of((m * owners + sender) * capacity, 16), capacity)

    def exchange(buffer, land, send_sem, recv_sem, m, step):
        return remote(
            buffer.at[step - 1, m],
            land.at[:, slot_rows(m, me)],
            send_sem.at[step - 1, m],
            recv_sem.at[step - 1, m],
            experts=place.peer_owner(step),
        )

    def exchanged(land, recv_sem, m, step):
        sender = lax.rem(me - step + owners, owners)
        arrived(land.at[:, slot_rows(m, sender)], recv_sem.at[step - 1, m])

    def put(buffer, land, m, i, value):
        if i < local_count:
            land[i, slot_rows(m, me), :] = value
        else:
            buffer[i // local_count - 1, m, i % local_count] = value

    def expert_gradients(m):
        g_rows = g_all[pl.ds(m * rows, rows), :]
        for i, hit, weight in one_hots(routes.at[m], gates.at[m], me, local_count, total):
            gate = jnp.sum(jnp.where(hit, weight, 0.0), -1, keepdims=True)
            value = mdot(hit.astype(F32).astype(BF), g_rows)
            put(send_do, do_s, m, i, (gate * value).astype(BF))

    def early_hop(step):
        for d in early:
            d.hop(step)

    for step in range(depth - 2):
        if step < micro_count:
            expert_gradients(step)
        early_hop(step)
    for m in range(max(depth - 2, 0), micro_count):
        expert_gradients(m)
    prompts[0].start()
    early_hop(depth - 2)
    for m in range(micro_count):
        for step in range(1, owners):
            exchange(send_do, do_s, ad_send, ad_recv, m, step).start()
    prompts[0].hop(0)
    for z in range(depth):
        for d in early:
            d.cross(z)
    for step in range(1, depth - 1):
        prompts[0].hop(step)
        if step == 1:
            for prompt_line in prompts[1:]:
                prompt_line.start()
    for z in range(depth):
        for d in early:
            d.finish(z)
    store(wq, qkv_o)
    store(wo, out_o)
    shards = depth * owners
    gain_rows = gain_in.shape[0]
    gain_sum = jnp.zeros((8, features), F32)
    for s in range(shards):
        gain_sum += gain_land[pl.ds(s * gain_rows, gain_rows), :].astype(F32)[:8]
    gain_v[...] = gain_sum
    store(gain_v, gain_o)

    def own_rows(i):
        start = place.z * PB if i == 0 else prompt + (i - 1) * PB
        return start, pl.ds(start if i else pl.multiple_of(start, PB), PB)

    def front(n1, k, v, q, att, hid, lse):
        lse[...] = jnp.zeros_like(lse)
        pairs = features // (2 * HD)

        def prompt_hop(step):
            for prompt_line in prompts[1:]:
                prompt_line.hop(step)
            if step == depth - 2:
                experts.start_z()

        def project_all(m):
            def project(here):
                normed = norm_rows(xk[m, here, :].astype(F32), gain_v[0:1, :])
                n1[m, here, :] = normed
                key = ndot(normed, wq[pl.ds(features, features), :])
                k[m, here, :] = rope(key, cosine[here, :], sine_part[here, :]).astype(BF)
                v[m, here, :] = ndot(normed, wq[pl.ds(2 * features, features), :]).astype(BF)

            tiles(length, 256, project)
            for i in range(rows // PB):
                _, here = own_rows(i)
                query = ndot(n1[m, here, :], wq[pl.ds(0, features), :])
                query = rope(query, cosine[here, :], sine_part[here, :]).astype(BF)
                q[m, pl.ds(i * PB, PB), :] = query * jnp.asarray(HD**-0.5, BF)
        lane = lax.broadcasted_iota(jnp.int32, (PB, 2 * HD), 1)
        for m in range(micro_count):
            project_all(m)

            def pair(index, carry):
                if m == 0:
                    for step in range(depth - 1):
                        pl.when(index == min(step, pairs - 1))(lambda step=step: prompt_hop(step))
                lanes = pl.ds(pl.multiple_of(index * 2 * HD, 2 * HD), 2 * HD)
                for i in range(rows // PB):
                    here = pl.ds(i * PB, PB)
                    query = q[m, here, lanes]
                    seen = prompt + i * PB
                    keys, values = k[m, pl.ds(0, seen), lanes], v[m, pl.ds(0, seen), lanes]
                    column = lax.broadcasted_iota(jnp.int32, (PB, seen), 1)
                    row = lax.broadcasted_iota(jnp.int32, (PB, seen), 0)
                    allowed = column <= row + own_rows(i)[0]
                    parts = []
                    logs = lse[m, here, :]
                    for sub in range(2):
                        only = jnp.where(lane // HD == sub, query, jnp.zeros_like(query))
                        scores = jnp.where(allowed, ndot(only, keys), -1000000000.0)
                        highest = jnp.max(scores, -1, keepdims=True)
                        weights = jnp.exp(scores - highest)
                        sums = jnp.sum(weights, -1, keepdims=True)
                        parts.append(mdot((weights * (1.0 / sums)).astype(BF), values))
                        logs = jnp.where(lane == 2 * index + sub, highest + jnp.log(sums), logs)
                    lse[m, here, :] = logs
                    att[m, here, lanes] = jnp.where(lane < HD, parts[0], parts[1]).astype(BF)
                return carry

            lax.fori_loop(0, pairs, pair, 0)
            if m == 0:
                for copy in bounce_copies:
                    copy.wait()
                for d in late:
                    d.start()
            if m == micro_count - 1:
                experts.hop(0, 0)
                for d in late:
                    d.cross(place.z)
            for i in range(rows // PB):
                here = pl.ds(i * PB, PB)
                hidden = xk[m, own_rows(i)[1], :].astype(F32) + mdot(att[m, here, :], wo[...])
                hid[m, here, :] = hidden
                n2[pl.ds(m * rows + i * PB, PB), :] = norm_rows(hidden, gain_v[1:2, :])
            normed = n2[pl.ds(m * rows, rows), :]
            for i, hit, _ in one_hots(routes.at[m], gates.at[m], me, local_count, total):
                value = mdot(hit.astype(F32).astype(BF), normed)
                put(send_in, in_s, m, i, value.astype(BF))
            for step in range(1, owners):
                exchange(send_in, in_s, ai_send, ai_recv, m, step).start()
        store(n1, n1_o)
        store(k, k_o)
        store(v, v_o)
        store(q, q_o)
        store(att, att_o)
        store(hid, hid_o)
        store(lse, lse_o)
        for copy in stores:
            copy.wait()

    pl.run_scoped(
        front,
        pltpu.VMEM((micro_count, length, features), BF),
        pltpu.VMEM((micro_count, length, features), BF),
        pltpu.VMEM((micro_count, length, features), BF),
        pltpu.VMEM((micro_count, rows, features), BF),
        pltpu.VMEM((micro_count, rows, features), BF),
        pltpu.VMEM((micro_count, rows, features), F32),
        pltpu.VMEM((micro_count, rows, 2 * HD), F32),
    )
    saved = (act_s, dg_s, du_s)
    staged = (stage_g, stage_u, stage_d)

    def chunk_loads(sources, slot):
        return [
            pltpu.make_async_copy(source, buffer.at[slot], chunk_sem.at[slot, kind])
            for kind, (source, buffer) in enumerate(zip(sources, (wg, wu, wd)))
        ]

    def chunk_stores(targets, slot):
        return [
            pltpu.make_async_copy(buffer.at[slot], target, store_sem.at[slot, kind])
            for kind, (target, buffer) in enumerate(zip(targets, staged))
        ]

    def wait_rows():
        for m in range(micro_count):
            for step in range(1, owners):
                exchanged(in_s, ai_recv, m, step)
                exchanged(do_s, ad_recv, m, step)

    at_end = (place.z == 0) | (place.z == depth - 1)
    beside_end = (place.z == 1) | (place.z == depth - 2)

    def sums_to_neighbour(which):
        z = jnp.where(place.z == 0, 1, depth - 2)
        return [
            remote(
                expert_slab(
                    ref, kind, local, (place.other_shard if crossed else place.shard)(z), width
                ),
                land.at[crossed, local],
                pre_send.at[crossed, local, kind],
                pre_recv.at[crossed, local, kind],
                context=z,
            )
            for crossed in which
            for local in range(local_count)
            for kind, (ref, land) in enumerate(
                ((geg_o, pre_g), (geu_o, pre_u), (ged_o, pre_d))
            )
        ]

    def send_sums(crossed):
        def body():
            for copy in sums_to_neighbour((crossed,)):
                copy.start()

        pl.when(at_end)(body)

    def sums_sent():
        for copy in sums_to_neighbour((0, 1)):
            copy.wait_send()

    def sums_arrived():
        for crossed in (1, 0):
            for local in range(local_count):
                for kind, land in enumerate((pre_g, pre_u, pre_d)):
                    arrived(land.at[crossed, local], pre_recv.at[crossed, local, kind])

    def returns(local):
        return [
            pltpu.make_async_copy(source.at[local], target.at[local], out_sem.at[2 + 2 * local + i])
            for i, (source, target) in enumerate(((in_s, outs_o), (do_s, dins_o)))
        ]

    def both(out_sum, in_sum, side_sum, normed_sum):
        out_sum[...] = jnp.zeros_like(out_sum)
        in_sum[...] = jnp.zeros_like(in_sum)
        side_sum[...] = jnp.zeros_like(side_sum)
        normed_sum[...] = jnp.zeros_like(normed_sum)
        group = late[0].own.shape[1] * owners // width

        def store_grads(targets, slot, stored):
            def previous():
                for copy in chunk_stores(targets, slot):
                    copy.wait()

            pl.when(stored)(previous)
            return lambda: [copy.start() for copy in chunk_stores(targets, slot)]

        def shared_part(refs, c):
            here = pl.ds(pl.multiple_of(c * width, 128), width)
            return [refs[0].at[:, here], refs[1].at[:, here], refs[2].at[here]]

        def shared_item(w, z):
            for d in late:
                d.finish(z)

            def one(i, carry):
                c = z * group + i
                loads = chunk_loads(shared_part((sg_o, su_o, sd_o), c), 2 * local_count + i)
                for copy in loads:
                    copy.wait()
                send = store_grads(shared_part((gsg_o, gsu_o, gsd_o), c), i, w > 0)
                ffn_chunk(
                    n2,
                    g_all,
                    [buffer.at[2 * local_count + i] for buffer in (wg, wu, wd)],
                    saved,
                    (side_sum, normed_sum),
                    [buffer.at[i] for buffer in staged],
                    micro_count * rows,
                )
                send()
                return carry

            for i in range(group):
                for copy in chunk_loads(
                    shared_part((sg_o, su_o, sd_o), z * group + i), 2 * local_count + i
                ):
                    copy.start()
            lax.fori_loop(0, group, one, 0)

        def expert_item(w, z, crossed, local, side, ahead):
            shard = jnp.where(crossed, place.other_shard(z), place.shard(z))

            def load(n):
                sources = [
                    expert_slab(ref, k, n, shard, width) for k, ref in enumerate((eg_o, eu_o, ed_o))
                ]
                return chunk_loads(sources, side * local_count + n)

            def begin(n):
                def own():
                    mine = [ref.at[n] for ref in (eg_in, eu_in, ed_in)]
                    for copy in chunk_loads(mine, side * local_count + n):
                        copy.start()

                def landed():
                    pl.when(crossed)(lambda: experts.wait_x(n, z))
                    for copy in load(n):
                        copy.start()

                pl.when(w == 1)(own)
                pl.when(w > 1)(landed)

            def begin_rest():
                for n in range(1, local_count):
                    begin(n)

            pl.when(w == 1)(wait_rows)
            pl.when(local == 0)(lambda: begin(0))
            pl.when(ahead & (local == 0))(begin_rest)
            pl.when(jnp.logical_not(ahead) & (local > 0))(lambda: begin(local))
            for copy in load(local):
                copy.wait()
            targets = [
                expert_slab(ref, k, local, shard, width) for k, ref in enumerate((geg_o, geu_o, ged_o))
            ]
            send = store_grads(targets, local, True)
            ffn_chunk(
                in_s.at[local],
                do_s.at[local],
                [buffer.at[side * local_count + local] for buffer in (wg, wu, wd)],
                saved,
                (out_sum.at[local], in_sum.at[local]),
                [buffer.at[local] for buffer in staged],
                slots,
            )
            send()

        def crossing(step):
            for d in late:
                for z in (place.z - 1 - step, place.z + 1 + step):
                    pl.when(place.on_line(z))(lambda d=d, z=z: d.cross(z))

        def late_hop(step):
            for d in late:
                d.hop(step)

        heads = 2 * local_count + 1
        in_step = 2 * heads
        after_item = [(local, lambda local=local: experts.hop(local, 0)) for local in range(1, local_count)]
        after_item = [(local - 1, run) for local, run in after_item]
        after_item += [(local_count, lambda: late_hop(0)), (heads - 1, lambda: crossing(0))]
        for step in range(1, depth - 1):
            here = heads + in_step * step
            if step == 1:
                spots = [heads + 3, jnp.where(at_end, here - 1, heads + 5)]
                late_spot = jnp.where(at_end, here + 3, heads + 7)
            else:
                spots = [here - 3, here + 1 if step == depth - 2 else here - 1]
                late_spot = here + 3
            for local in range(local_count):
                at = spots[min(local, 1)]
                after_item.append((at, lambda local=local, step=step: experts.hop(local, step)))
            after_item.append((late_spot, lambda step=step: late_hop(step)))
            after_item.append((here + 5, lambda step=step: crossing(step)))
        after_item.append((heads + in_step - 3, lambda: send_sums(0)))
        after_item.append((heads + in_step - 1, lambda: send_sums(1)))
        count = heads + in_step * (depth - 1)

        def finish(local):
            def convert(here):
                in_s[local, here, :] = out_sum[local, here, :].astype(BF)
                do_s[local, here, :] = in_sum[local, here, :].astype(BF)

            tiles(slots, 256, convert)
            for copy in returns(local):
                copy.start()

        def side_sums():
            return [
                pltpu.make_async_copy(side_sum, side_o, out_sem.at[0]),
                pltpu.make_async_copy(normed_sum, dn2_o, out_sem.at[1]),
            ]

        def finish_first():
            for copy in side_sums():
                copy.start()
            finish(0)

        after_item.append((count - 2 * (local_count - 1) - 1, finish_first))

        def item(w, carry):
            head = w < heads
            after = jnp.maximum(w - heads, 0)
            step, spot = after // in_step, lax.rem(after, in_step)
            kind = jnp.where(head, w - 1, spot // 2)
            last = jnp.logical_not(head) & (step == depth - 2)
            turn = jnp.where(last & (kind > local_count), kind - 1, kind)
            is_shared = kind == jnp.where(
                head, -1, jnp.where(last, local_count + 1, 2 * local_count)
            )
            crossed = turn >= local_count
            local = jnp.clip(jnp.where(crossed, turn - local_count, turn), 0, local_count - 1)
            z = jnp.where(head, place.z, place.z + (2 * lax.rem(spot, 2) - 1) * (1 + step))
            valid = place.on_line(z)
            pl.when(valid & is_shared)(lambda: shared_item(w, z))
            ahead = head | (step < depth - 2)
            side = jnp.where(head, 0, lax.rem(spot, 2))
            pl.when(valid & jnp.logical_not(is_shared))(
                lambda: expert_item(w, z, crossed, local, side, ahead)
            )
            for at, run in after_item:
                pl.when(w == at)(run)
            return carry

        lax.fori_loop(0, count, item, 0)
        for local in range(local_count):
            targets = [expert_slab(ref, k, local, 0, width) for k, ref in enumerate((geg_o, geu_o, ged_o))]
            for copy in chunk_stores(targets, local):
                copy.wait()
        for local in range(1, local_count):
            finish(local)
        for copy in side_sums():
            copy.wait()

    pl.run_scoped(
        both,
        pltpu.VMEM((local_count, slots, features), F32),
        pltpu.VMEM((local_count, slots, features), F32),
        pltpu.VMEM((micro_count * rows, features), F32),
        pltpu.VMEM((micro_count * rows, features), F32),
    )
    for local in range(local_count):
        for copy in returns(local):
            copy.wait()
    pl.when(beside_end)(sums_arrived)
    pl.when(at_end)(sums_sent)
    for line in prompts:
        line.drain()
    for d in early + late:
        d.drain()
    experts.drain()
    for m in range(micro_count):
        for step in range(1, owners):
            exchange(send_do, do_s, ad_send, ad_recv, m, step).wait_send()
            exchange(send_in, in_s, ai_send, ai_recv, m, step).wait_send()


def rope_tables(prompt):
    positions = np.arange(prompt + CONT, dtype=np.float64)
    frequency = 10000.0 ** (-2.0 * np.arange(HD // 2) / HD)
    angles = positions[:, None] * frequency
    cosine, sine_part = np.cos(angles), np.sin(angles)
    return (
        np.concatenate([cosine] * 4, 1).astype(np.float32),
        np.concatenate([-sine_part, sine_part] * 2, 1).astype(np.float32),
    )


def run_forward(sizes, tokens, cot, gates, routes, dense, experts):
    depth, high_count = sizes
    micro_count, rows, features = tokens.shape
    owners = high_count * 2
    line = depth * owners
    prompt = depth * PB
    length = prompt + CONT
    local_count, _, width = experts[0].shape
    hidden_units = dense[3].shape[1] * line
    capacity = rows * 8 // (3 * owners * local_count)
    slots = micro_count * owners * capacity
    cosine, sine_part = rope_tables(prompt)
    hbm, vmem = pl.BlockSpec(memory_space=pltpu.HBM), pl.BlockSpec(memory_space=pltpu.VMEM)

    def shape(dtype, *dims):
        return jax.ShapeDtypeStruct(dims, dtype)

    token_rows = micro_count * rows
    wide, tall = (features, hidden_units), (hidden_units, features)
    out_shape = [
        shape(BF, dense[0].shape[0] * line, features),
        shape(BF, dense[1].shape[0] * line, features),
        shape(F32, 8, features),
        shape(BF, *wide), shape(BF, *wide), shape(BF, *tall),
        shape(BF, local_count, *wide), shape(BF, local_count, *wide), shape(BF, local_count, *tall),
        shape(BF, micro_count, length, features),
        shape(BF, micro_count, length, features),
        shape(BF, micro_count, length, features),
        shape(BF, micro_count, rows, features),
        shape(BF, micro_count, rows, features),
        shape(F32, micro_count, rows, features),
        shape(F32, micro_count, rows, 2 * HD),
        shape(F32, token_rows, features),
        shape(F32, token_rows, features),
        shape(BF, *wide), shape(BF, *wide), shape(BF, *tall),
        shape(BF, local_count, *wide), shape(BF, local_count, *wide), shape(BF, local_count, *tall),
        shape(BF, local_count, slots, features),
        shape(BF, local_count, slots, features),
        shape(BF, 2, local_count, features, width),
        shape(BF, 2, local_count, features, width),
        shape(BF, 2, local_count, width, features),
    ]
    dma = pltpu.SemaphoreType.DMA
    buffers = max(2, local_count)
    loads = 2 * local_count + 2
    send = pltpu.VMEM((owners - 1, micro_count, local_count, capacity, features), BF)
    scratch = [
        pltpu.VMEM((micro_count, length, features), BF),
        pltpu.VMEM(out_shape[0].shape, BF),
        pltpu.VMEM(out_shape[1].shape, BF),
        pltpu.VMEM((dense[2].shape[0] * line, features), BF),
        pltpu.VMEM((8, features), F32),
        pltpu.VMEM((token_rows, features), BF),
        pltpu.VMEM((token_rows, features), BF),
        pltpu.VMEM((local_count, slots, features), BF),
        pltpu.VMEM((local_count, slots, features), BF),
        send,
        send,
        pltpu.VMEM((loads, features, width), BF),
        pltpu.VMEM((loads, features, width), BF),
        pltpu.VMEM((loads, width, features), BF),
        pltpu.VMEM((max(slots, token_rows), width), BF),
        pltpu.VMEM((max(slots, token_rows), width), BF),
        pltpu.VMEM((max(slots, token_rows), width), BF),
        pltpu.VMEM((buffers, features, width), BF),
        pltpu.VMEM((buffers, features, width), BF),
        pltpu.VMEM((buffers, width, features), BF),
    ]
    scratch += DenseGather.semaphores(len(dense), depth, high_count)
    scratch += ExpertGather.semaphores(depth, local_count)
    scratch += [
        dma((micro_count, 2, depth)),
        dma((micro_count, depth)),
        dma((10 + micro_count,)),
        dma((owners - 1, micro_count)),
        dma((owners - 1, micro_count)),
        dma((owners - 1, micro_count)),
        dma((owners - 1, micro_count)),
        dma((loads, 3)),
        dma((buffers, 3)),
        dma((12 + 2 * local_count,)),
        dma((2, local_count, 3)),
        dma((2, local_count, 3)),
    ]
    return pl.pallas_call(
        functools.partial(forward_kernel, sizes),
        out_shape=out_shape,
        in_specs=[hbm] * 2 + [vmem] * 4 + [hbm] * 9,
        out_specs=[hbm] * len(out_shape),
        scratch_shapes=scratch,
        compiler_params=pltpu.CompilerParams(
            collective_id=0, has_side_effects=True, vmem_limit_bytes=60 * MIB
        ),
        name="gather_and_forward",
    )(tokens, cot, gates, routes, cosine, sine_part, *dense, *experts)


def add_into(target, sources, step):
    def body(here):
        value = target[here, :].astype(F32)
        for source in sources:
            value = value + source[here, :].astype(F32)
        target[here, :] = value.astype(target.dtype)

    tiles(target.shape[0], step, body)


class LineSum:
    def __init__(self, place, part, land, send_sem, recv_sem):
        self.place, self.part, self.land = place, part, land
        self.send_sem, self.recv_sem = send_sem, recv_sem

    def copy(self, z, direction):
        place = self.place
        slot = z if direction > 0 else jnp.where(z == place.z - 1, place.depth, z)
        return remote(
            self.part(z),
            self.land(slot),
            self.send_sem.at[z],
            self.recv_sem.at[slot],
            context=place.z + direction,
        )

    def upstream(self, direction):
        return self.place.z > 0 if direction > 0 else self.place.z < self.place.depth - 1

    def arrive(self, slot):
        arrived(self.land(slot), self.recv_sem.at[slot])

    def at(self, direction, step, body):
        z = self.place.z + direction * step
        pl.when(self.place.on_line(z))(lambda: body(z))

    def pass_on(self, direction, step, add):
        def body(z):
            def more():
                self.arrive(z)
                add(self.part(z), self.land(z))

            pl.when(self.upstream(direction))(more)
            self.copy(z, direction).start()

        self.at(direction, step, body)

    def end(self, add):
        for direction, slot in ((1, self.place.z), (-1, self.place.depth)):

            def body(slot=slot):
                self.arrive(slot)
                add(self.part(self.place.z), self.land(slot))

            pl.when(self.upstream(direction))(body)

    def drain(self):
        for step in range(1, self.place.depth):
            for direction in (1, -1):
                self.at(direction, step, lambda z, d=direction: self.copy(z, d).wait_send())


class DenseScatter:
    def __init__(self, place, source, low, high, line, cross, spare, out, sems):
        self.place, self.source, self.spare, self.out = place, source, spare, out
        self.low, self.high, self.cross = low, high, cross
        (
            self.l_send, self.l_recv, self.h_send, self.h_recv, z_send, z_recv,
            self.x_send, self.x_recv, self.own_sem,
        ) = sems
        self.step = min(64, low.shape[2]) if low.shape[2] % 64 == 0 else 16
        self.line = LineSum(
            place, lambda z: low.at[z, place.high], lambda slot: line.at[slot], z_send, z_recv
        )

    @staticmethod
    def semaphores(count, depth, high_count):
        dma = pltpu.SemaphoreType.DMA
        cross = dma((count, depth, high_count))
        return [
            cross, cross, dma((count, high_count)), dma((count, high_count)),
            dma((count, depth + 1)), dma((count, depth + 1)),
            dma((count,)), dma((count,)), dma((count, 2)),
        ]

    def _index(self, z, high, low):
        return (z * self.place.high_count + high) * 2 + low

    def _to_low(self, z, high):
        place = self.place
        return remote(
            self.source(self._index(z, high, 1 - place.low)),
            self.low.at[z, high],
            self.l_send.at[z, high],
            self.l_recv.at[z, high],
            experts=place.e + 1 - 2 * place.low,
        )

    def _each(self, body):
        for z in range(self.place.depth):
            for high in range(self.place.high_count):
                body(z, high)

    def start(self):
        self._each(lambda z, high: self._to_low(z, high).start())

    def add_low(self):
        place = self.place
        places = [(z, high) for z in range(place.depth) for high in range(place.high_count)]

        def load(i):
            z, high = places[i]
            return pltpu.make_async_copy(
                self.source(self._index(z, high, place.low)),
                self.spare.at[i % 2],
                self.own_sem.at[i % 2],
            )

        if self.spare is not None:
            load(0).start()
        for i, (z, high) in enumerate(places):
            self._to_low(z, high).wait_recv()
            if self.spare is None:
                own = self.source(self._index(z, high, place.low))
            else:
                if i + 1 < len(places):
                    load(i + 1).start()
                load(i).wait()
                own = self.spare.at[i % 2]
            add_into(self.low.at[z, high], [own], self.step)
        for step in range(1, place.high_count):
            self._to_high(step).start()

    def _to_high(self, step):
        place = self.place
        peer = place.peer_high(step)
        return remote(
            self.low.at[:, peer],
            self.high.at[step - 1],
            self.h_send.at[step],
            self.h_recv.at[step],
            experts=peer * 2 + place.low,
        )

    def add_high(self):
        place = self.place
        for step in range(1, place.high_count):
            self._to_high(step).wait_recv()
        for z in range(place.depth):
            add_into(
                self.low.at[z, place.high],
                [self.high.at[step - 1, z] for step in range(1, place.high_count)],
                self.step,
            )

    def _add(self, target, more):
        add_into(target, [more], self.step)

    def pass_on(self, direction, step):
        self.line.pass_on(direction, step, self._add)

    def _across(self):
        place = self.place
        return remote(
            self.low.at[place.z, place.high], self.cross, self.x_send, self.x_recv, dp=1 - place.x
        )

    def end(self):
        self.line.end(self._add)
        self._across().start()

    def _store(self):
        return pltpu.make_async_copy(self.cross, self.out, self.own_sem.at[0])

    def finish(self):
        self._across().wait_recv()
        self._add(self.cross, self.low.at[self.place.z, self.place.high])
        self._store().start()

    def drain(self):
        self._each(lambda z, high: self._to_low(z, high).wait_send())
        for step in range(1, self.place.high_count):
            self._to_high(step).wait_send()
        self.line.drain()
        self._across().wait_send()
        self._store().wait()


class ExpertScatter:
    def __init__(self, place, sums, cross, land, own, more, early, absorbed, outs, sems):
        self.early, self.absorbed = early, absorbed
        self.at_end = (place.z == 0) | (place.z == place.depth - 1)
        self.beside_end = (place.z == 1) | (place.z == place.depth - 2)
        self.place, self.sums, self.cross, self.land = place, sums, cross, land
        self.own, self.more, self.outs = own, more, outs
        self.x_send, self.x_recv, self.z_send, self.z_recv, self.load_sem, self.out_sem = sems
        self.local_count, self.width = cross[0].shape[1], cross[0].shape[3]

    @staticmethod
    def semaphores(depth, local_count):
        dma = pltpu.SemaphoreType.DMA
        return [
            dma((local_count, 3, depth)),
            dma((local_count, 3, depth)),
            dma((local_count, 3, depth + 1)),
            dma((local_count, 3, depth + 1)),
            dma((3, 3)),
            dma((local_count, 3)),
        ]

    def _line(self, local, kind):
        return LineSum(
            self.place,
            lambda z: self.cross[kind].at[z, local],
            lambda slot: self.land[kind].at[slot, local],
            self.z_send.at[local, kind],
            self.z_recv.at[local, kind],
        )

    def _across(self, local, kind, z):
        return remote(
            expert_slab(self.sums[kind], kind, local, self.place.other_shard(z), self.width),
            self.cross[kind].at[z, local],
            self.x_send.at[local, kind, z],
            self.x_recv.at[local, kind, z],
            dp=1 - self.place.x,
        )

    def _order(self, body):
        place = self.place
        for step in range(place.depth - 1, 0, -1):
            for direction in (1, -1):
                z = place.z + direction * step
                here = place.on_line(z)
                if step == 1:
                    here = here & jnp.logical_not(self.at_end)
                pl.when(here)(lambda z=z: body(z))

    def start(self):
        def body(z):
            for local in range(self.local_count):
                for kind in range(3):
                    self._across(local, kind, z).start()

        self._order(body)
        pl.when(jnp.logical_not(self.beside_end))(lambda: body(self.place.z))

    def absorb(self):
        z = self.place.z

        def body():
            for local in range(self.local_count):
                loads = []
                for kind in range(3):
                    source = expert_slab(
                        self.sums[kind], kind, local, self.place.other_shard(z), self.width
                    )
                    early = self.early[kind].at[1, local]
                    loads.append(
                        [
                            pltpu.make_async_copy(source, self.own[kind], self.load_sem.at[0, kind]),
                            pltpu.make_async_copy(
                                early, self.more[kind].at[0], self.load_sem.at[1, kind]
                            ),
                        ]
                    )
                stores = [
                    pltpu.make_async_copy(
                        self.own[kind], self.absorbed[kind].at[local], self.load_sem.at[0, kind]
                    )
                    for kind in range(3)
                ]
                for pair in loads:
                    for copy in pair:
                        copy.start()
                for kind in range(3):
                    for copy in loads[kind]:
                        copy.wait()
                    add_into(self.own[kind], [self.more[kind].at[0]], 64)
                    stores[kind].start()
                for kind in range(3):
                    stores[kind].wait()
                    remote(
                        self.absorbed[kind].at[local],
                        self.cross[kind].at[z, local],
                        self.x_send.at[local, kind, z],
                        self.x_recv.at[local, kind, z],
                        dp=1 - self.place.x,
                    ).start()

        pl.when(self.beside_end)(body)

    def _own_load(self, local, kind, z):
        return pltpu.make_async_copy(
            expert_slab(self.sums[kind], kind, local, self.place.shard(z), self.width),
            self.own[kind],
            self.load_sem.at[0, kind],
        )

    def _more_load(self, local, kind, slot, which):
        return pltpu.make_async_copy(
            self.land[kind].at[slot, local], self.more[kind].at[which], self.load_sem.at[1 + which, kind]
        )

    def pass_on(self, direction, step, local, kinds=(0, 1, 2)):
        def body(z):
            for kind in kinds:
                self._own_load(local, kind, z).start()
            for kind in kinds:
                line = self._line(local, kind)
                target = self.cross[kind].at[z, local]

                def come(line=line, kind=kind):
                    line.arrive(z)
                    self._more_load(local, kind, z, 0).start()

                pl.when(line.upstream(direction))(come)
                self._across(local, kind, z).wait_recv()
                self._own_load(local, kind, z).wait()

                def both(target=target, kind=kind):
                    self._more_load(local, kind, z, 0).wait()
                    add_into(target, [self.own[kind], self.more[kind].at[0]], 64)

                def single(target=target, kind=kind):
                    add_into(target, [self.own[kind]], 64)

                pl.when(line.upstream(direction))(both)
                pl.when(jnp.logical_not(line.upstream(direction)))(single)
                line.copy(z, direction).start()

        def there(z):
            if step == 1:
                pl.when(jnp.logical_not(self.at_end))(lambda: body(z))
            else:
                body(z)

        self._line(local, 0).at(direction, step, there)

    def _early_load(self, local, kind, which):
        return pltpu.make_async_copy(
            self.early[kind].at[0, local], self.more[kind].at[which], self.load_sem.at[1 + which, kind]
        )

    def end(self, local):
        place = self.place
        z = place.z
        for kind in range(3):
            self._own_load(local, kind, z).start()
        for kind in range(3):
            line = self._line(local, kind)
            target = self.cross[kind].at[z, local]
            for which, (direction, slot) in enumerate(((1, z), (-1, place.depth))):

                def come(slot=slot, which=which, line=line, kind=kind):
                    line.arrive(slot)
                    self._more_load(local, kind, slot, which).start()

                def came(which=which, kind=kind):
                    self._early_load(local, kind, which).start()

                from_end = z - direction == (0 if direction > 0 else place.depth - 1)
                pl.when(line.upstream(direction) & jnp.logical_not(from_end))(come)
                pl.when(from_end)(came)
            self._across(local, kind, z).wait_recv()
            self._own_load(local, kind, z).wait()
            add_into(target, [self.own[kind]], 64)
            for which, (direction, slot) in enumerate(((1, z), (-1, place.depth))):

                def more(slot=slot, which=which, kind=kind, target=target):
                    self._more_load(local, kind, slot, which).wait()
                    add_into(target, [self.more[kind].at[which]], 64)

                pl.when(line.upstream(direction))(more)
            self._store(local, kind).start()

    def _store(self, local, kind):
        return pltpu.make_async_copy(
            self.cross[kind].at[self.place.z, local],
            self.outs[kind].at[local],
            self.out_sem.at[local, kind],
        )

    def drain(self):
        for local in range(self.local_count):
            for kind in range(3):
                self._order(lambda z, p=(local, kind): self._across(*p, z).wait_send())
                self._across(local, kind, self.place.z).wait_send()
                line = self._line(local, kind)
                for step in range(1, self.place.depth):
                    for direction in (1, -1):

                        def sent(z, line=line, direction=direction):
                            line.copy(z, direction).wait_send()

                        def there(z, step=step, sent=sent):
                            if step == 1:
                                pl.when(jnp.logical_not(self.at_end))(lambda: sent(z))
                            else:
                                sent(z)

                        line.at(direction, step, there)
                self._store(local, kind).wait()


def backward_kernel(sizes, *refs):
    place = Place(sizes)
    depth, high_count = sizes
    owners = place.owners
    (
        tokens, cot, gates, routes, gate_rows, cosine, sine_part,
        qkv_w, out_w, gain_v, n1_i, k_i, v_i, q_i, att_i, hid_i, lse_i, side_i, dn2_i,
        gsg, gsu, gsd, geg, geu, ged, outs_i, dins_i, pre_g, pre_u, pre_d,
        mixed_o, input_o, gqkv_o, gout_o, gsg_o, gsu_o, gsd_o, geg_o, geu_o, ged_o, gain_o,
        eland_g, eland_u, eland_d, ret_in, ret_out, d_hidden_o, dn1_o, abs_g, abs_u, abs_d,
        *rest,
    ) = refs
    count = 5
    low, rest = rest[:count], rest[count:]
    high, rest = rest[:count], rest[count:]
    line, rest = rest[:count], rest[count:]
    cross, rest = rest[:count], rest[count:]
    (
        spare_w, spare_t, ecross_g, ecross_u, ecross_d, eown_g, eown_u, eown_d,
        emore_g, emore_u, emore_d,
        d_att, dpq, dpk, dpv, g_qkv, g_out, part, part_land,
        gain_own, gain_low, gain_high, gain_line, gain_cross, out_rows,
        *sems,
    ) = rest
    dense_sems, sems = sems[:9], sems[9:]
    expert_sems, sems = sems[:6], sems[6:]
    (
        part_send, part_recv, ri_send, ri_recv, ro_send, ro_recv,
        gain_send, gain_recv, load_sem, wq_sem, out_sem,
    ) = sems
    micro_count, rows, features = tokens.shape
    prompt = depth * PB
    length = prompt + CONT
    local_count, slots = outs_i.shape[0], outs_i.shape[1]
    total = owners * local_count
    capacity = rows * 8 // (3 * total)
    me = place.e

    def rows_of(ref, size):
        return lambda s: ref.at[pl.ds(pl.multiple_of(s * size, 16), size)]

    def columns_of(ref, size):
        return lambda s: ref.at[:, pl.ds(pl.multiple_of(s * size, 128), size)]

    sources = [
        columns_of(gsg, gsg_o.shape[1]),
        columns_of(gsu, gsu_o.shape[1]),
        rows_of(gsd, gsd_o.shape[0]),
        rows_of(g_qkv, gqkv_o.shape[0]),
        rows_of(g_out, gout_o.shape[0]),
    ]
    spares = [spare_w, spare_w, spare_t, None, None]
    dense = [
        DenseScatter(
            place, sources[i], low[i], high[i], line[i], cross[i], spares[i], out,
            [s.at[i] for s in dense_sems],
        )
        for i, out in enumerate((gsg_o, gsu_o, gsd_o, gqkv_o, gout_o))
    ]
    early, late = dense[:3], dense[3:]
    experts = ExpertScatter(
        place,
        (geg, geu, ged),
        (ecross_g, ecross_u, ecross_d),
        (eland_g, eland_u, eland_d),
        (eown_g, eown_u, eown_d),
        (emore_g, emore_u, emore_d),
        (pre_g, pre_u, pre_d),
        (abs_g, abs_u, abs_d),
        (geg_o, geu_o, ged_o),
        expert_sems,
    )
    prompts = [
        LineSum(
            place,
            lambda z, m=m: part.at[m, z],
            lambda slot, m=m: part_land.at[m, slot],
            part_send.at[m],
            part_recv.at[m],
        )
        for m in range(micro_count)
    ]

    def slot_rows(m, owner_of_rows):
        return pl.ds(pl.multiple_of((m * owners + owner_of_rows) * capacity, 16), capacity)

    def hand_back(source, land, send_sem, recv_sem, m, step):
        peer = place.peer_owner(step)
        return remote(
            source.at[:, slot_rows(m, peer)],
            land.at[m, owners - step],
            send_sem.at[step, m],
            recv_sem.at[owners - step, m],
            experts=peer,
        )

    returns = [(dins_i, ret_in, ri_send, ri_recv), (outs_i, ret_out, ro_send, ro_recv)]
    place.greet()
    for m in range(micro_count):
        for step in range(1, owners):
            hand_back(*returns[0], m, step).start()
    for d in early:
        d.start()
    experts.start()

    def fetch(pairs):
        copies = [
            pltpu.make_async_copy(source, target, load_sem.at[i])
            for i, (source, target) in enumerate(pairs)
        ]
        for copy in copies:
            copy.start()
        for copy in copies:
            copy.wait()

    def fetch_returned(source, land, recv_sem, target, m):
        for step in range(1, owners):
            arrived(land.at[m, step], recv_sem.at[step, m])
        pairs = []
        for step in range(owners):
            for local in range(local_count):
                at = pl.ds((step * local_count + local) * capacity, capacity)
                if step == 0:
                    piece = source.at[local, slot_rows(m, me)]
                else:
                    piece = land.at[m, step, local]
                pairs.append((piece, target.at[at]))
        fetch(pairs)

    for kind, d in enumerate(early):
        for direction in (1, -1):
            experts.pass_on(direction, depth - 1, 0, (kind,))
        d.add_low()
    for m in range(micro_count):
        for step in range(1, owners):
            hand_back(*returns[1], m, step).start()
    experts.absorb()
    gain_own[...] = jnp.zeros_like(gain_own)

    def mark_pairs(first, second, m):
        for i, hit, _ in one_hots(routes.at[m], gates.at[m], me, local_count, total):
            here = pl.ds(i * capacity, capacity)
            expert = lax.rem(me * local_count + i, total)
            hit_first = either(hit, routes[m, 0:1, :] == expert)
            hit_second = either(hit, routes[m, 1:2, :] == expert)
            first[here, :] = hit_first.astype(F32).astype(BF)
            second[here, :] = hit_second.astype(F32).astype(BF)

    def after_experts(hidden, extra, back, first, second, g_rows, att, d_attn, wo):
        fetch([(out_w, wo)] + [(att_i.at[m], att.at[pl.ds(m * rows, rows)]) for m in range(micro_count)])
        for m in range(micro_count):
            fetch([(hid_i.at[m], hidden), (cot.at[m], g_rows), (dn2_i.at[pl.ds(m * rows, rows)], extra)])
            mark_pairs(first, second, m)
            fetch_returned(dins_i, ret_in, ri_recv, back, m)
            gain = gain_v[1:2, :]
            for i in range(rows // PB):
                here = pl.ds(i * PB, PB)
                both = first[:, here] + second[:, here]
                d_normed = extra[here, :] + tdot(both, back[...])
                values = hidden[here, :]
                root = lax.rsqrt(jnp.mean(values * values, -1, keepdims=True) + EPSILON)
                scaled = gain * d_normed
                d_values = (
                    g_rows[here, :].astype(F32)
                    + root * scaled
                    - values * (root * root * root) * jnp.mean(values * scaled, -1, keepdims=True)
                )
                gain_own[1:2, :] += jnp.sum(d_normed * values * root, 0, keepdims=True)
                there = pl.ds(m * rows + i * PB, PB)
                extra[here, :] = d_values
                low_part = d_values.astype(BF)
                d_attn[there, :] = low_part
                d_att[there, :] = ndot(low_part, wo[...]).astype(BF)
            fetch([(extra, d_hidden_o.at[m])])
            for kind in ((0,), (1, 2))[m] if m < 2 else ():
                for direction in (1, -1):
                    experts.pass_on(direction, depth - 1, 1, (kind,))

        def out_grad(here):
            g_out[here, :] = tdot(att[:, here], d_attn[...]).astype(BF)

        tiles(features, 256, out_grad)

    pl.run_scoped(
        after_experts,
        pltpu.VMEM((rows, features), F32),
        pltpu.VMEM((rows, features), F32),
        pltpu.VMEM((total * capacity, features), BF),
        pltpu.VMEM((total * capacity, rows), BF),
        pltpu.VMEM((total * capacity, rows), BF),
        pltpu.VMEM((rows, features), BF),
        pltpu.VMEM((micro_count * rows, features), BF),
        pltpu.VMEM((micro_count * rows, features), BF),
        pltpu.VMEM((features, features), BF),
    )

    def both_ways(items, step):
        for direction in (1, -1):
            for item in items:
                item.pass_on(direction, step)

    def prompts_on(m, step):
        for direction in (1, -1):
            prompts[m].pass_on(direction, step, lambda t, s: add_into(t, [s], 64))

    def experts_on(step, local, where=True):
        def body():
            for direction in (1, -1):
                experts.pass_on(direction, step, local)

        pl.when(where)(body)

    inside = jnp.logical_not(experts.at_end)
    experts_on(depth - 2, 0, inside)

    def own_rows(i):
        start = place.z * PB if i == 0 else prompt + (i - 1) * PB
        return start, pl.ds(start if i else pl.multiple_of(start, PB), PB)

    def attention(k, v, q, lse, ds_s, p_s, wq, dn1):
        load_wq = pltpu.make_async_copy(qkv_w, wq, wq_sem.at[0])
        load_wq.start()
        lane = lax.broadcasted_iota(jnp.int32, (PB, 2 * HD), 1)
        wide_lane = lax.broadcasted_iota(jnp.int32, (rows, 2 * HD), 1)
        ds_s[...] = jnp.zeros_like(ds_s)
        p_s[...] = jnp.zeros_like(p_s)
        for m in range(micro_count):
            fetch([(k_i.at[m], k), (v_i.at[m], v), (q_i.at[m], q), (lse_i.at[m], lse)])
            whole = pl.ds(m * rows, rows)

            def pair(index, carry):
                lanes = pl.ds(pl.multiple_of(index * 2 * HD, 2 * HD), 2 * HD)
                for i in range(rows // PB):
                    here = pl.ds(i * PB, PB)
                    there = pl.ds(m * rows + i * PB, PB)
                    query, d_out, logs = q[here, lanes], d_att[there, lanes], lse[here, :]
                    start, table = own_rows(i)
                    seen = prompt + i * PB
                    keys, values = k[pl.ds(0, seen), lanes], v[pl.ds(0, seen), lanes]
                    column = lax.broadcasted_iota(jnp.int32, (PB, seen), 1)
                    row = lax.broadcasted_iota(jnp.int32, (PB, seen), 0)
                    allowed = column <= row + start
                    parts = []
                    for sub in range(2):
                        mine = lane // HD == sub
                        scores = ndot(jnp.where(mine, query, jnp.zeros_like(query)), keys)
                        log = jnp.sum(
                            jnp.where(lane == 2 * index + sub, logs, 0.0), -1, keepdims=True
                        )
                        probs = jnp.where(allowed, jnp.exp(scores - log), 0.0)
                        d_probs = ndot(jnp.where(mine, d_out, jnp.zeros_like(d_out)), values)
                        centre = jnp.sum(probs * d_probs, -1, keepdims=True)
                        d_scores = (probs * (d_probs - centre)).astype(BF)
                        ds_s[sub, here, pl.ds(0, seen)] = d_scores
                        p_s[sub, here, pl.ds(0, seen)] = probs.astype(BF)
                        parts.append(mdot(d_scores, keys))
                    d_query = jnp.where(lane < HD, parts[0], parts[1]) * HD**-0.5
                    d_query = rope(d_query, cosine[table, :], -sine_part[table, :])
                    dpq[there, lanes] = d_query.astype(BF)
                d_key = jnp.zeros((length, 2 * HD), F32)
                d_value = jnp.zeros((length, 2 * HD), F32)
                query, d_out = q[:, lanes], d_att[whole, lanes]
                for sub in range(2):
                    mine = wide_lane // HD == sub
                    d_key += tdot(ds_s[sub], jnp.where(mine, query, jnp.zeros_like(query)))
                    d_value += tdot(p_s[sub], jnp.where(mine, d_out, jnp.zeros_like(d_out)))
                keys_here = pl.ds(m * length, length)
                d_key = rope(d_key, cosine[...], -sine_part[...])
                dpk[keys_here, lanes] = d_key.astype(BF)
                dpv[keys_here, lanes] = d_value.astype(BF)
                return carry

            lax.fori_loop(0, features // (2 * HD), pair, 0)
            if m == 0:
                load_wq.wait()
            key_w, value_w = wq[pl.ds(features, features), :], wq[pl.ds(2 * features, features), :]
            for z in range(depth):
                here = pl.ds(m * length + z * PB, PB)
                part[m, z] = (mdot(dpk[here, :], key_w) + mdot(dpv[here, :], value_w)).astype(BF)
            prompts_on(m, depth - 1)
            for i in range(rows // PB):
                _, table = own_rows(i)
                start = own_rows(i)[0] + m * length
                here = pl.ds(pl.multiple_of(start, PB), PB)
                there = pl.ds(m * rows + i * PB, PB)
                dn1[pl.ds(i * PB, PB), :] = (
                    mdot(dpq[there, :], wq[pl.ds(0, features), :])
                    + mdot(dpk[here, :], key_w)
                    + mdot(dpv[here, :], value_w)
                )
            fetch([(dn1, dn1_o.at[m])])
            experts_on(depth - 2, m, experts.at_end)
            if m == 0:
                experts_on(depth - 2, 1, inside)
                for d in early:
                    d.add_high()
                both_ways(early, depth - 1)

    pl.run_scoped(
        attention,
        pltpu.VMEM((length, features), BF),
        pltpu.VMEM((length, features), BF),
        pltpu.VMEM((rows, features), BF),
        pltpu.VMEM((rows, 2 * HD), F32),
        pltpu.VMEM((2, rows, length), BF),
        pltpu.VMEM((2, rows, length), BF),
        pltpu.VMEM(qkv_w.shape, BF),
        pltpu.VMEM((rows, features), F32),
    )

    def weight_grads(n1, n1_own):
        pairs = []
        for m in range(micro_count):
            pairs.append((n1_i.at[m], n1.at[pl.ds(m * length, length)]))
            for i in range(rows // PB):
                _, here = own_rows(i)
                pairs.append((n1_i.at[m, here], n1_own.at[pl.ds(m * rows + i * PB, PB)]))
        fetch(pairs)

        def make(here):
            g_qkv[here, :] = tdot(dpq[:, here], n1_own[...]).astype(BF)

        def make_key(here):
            there = pl.ds(pl.multiple_of(here.start + features, 256), 256)
            g_qkv[there, :] = tdot(dpk[:, here], n1[...]).astype(BF)

        def make_value(here):
            there = pl.ds(pl.multiple_of(here.start + 2 * features, 256), 256)
            g_qkv[there, :] = tdot(dpv[:, here], n1[...]).astype(BF)

        tiles(features, 256, make)
        tiles(features, 256, make_key)
        tiles(features, 256, make_value)

    pl.run_scoped(
        weight_grads,
        pltpu.VMEM((micro_count * length, features), BF),
        pltpu.VMEM((micro_count * rows, features), BF),
    )
    for d in late:
        d.start()

    for step in range(depth - 2, 1, -1):
        for m in range(micro_count):
            prompts_on(m, step)
    for d in late:
        d.add_low()

    def outputs(hidden, side, back, first, second):
        for m in range(micro_count):
            fetch([(hid_i.at[m], hidden), (side_i.at[pl.ds(m * rows, rows)], side)])
            mark_pairs(first, second, m)
            fetch_returned(outs_i, ret_out, ro_recv, back, m)
            for i in range(rows // PB):
                here = pl.ds(i * PB, PB)
                routed = gate_rows[m, here, 0:1] * tdot(first[:, here], back[...])
                routed += gate_rows[m, here, 1:2] * tdot(second[:, here], back[...])
                out_rows[here, :] = (hidden[here, :] + side[here, :] + routed).astype(BF)
            fetch([(out_rows, mixed_o.at[m])])
            if m == 0:
                for step in range(depth - 2, 1, -1):
                    both_ways(early, step)
                for step in range(depth - 3, 0, -1):
                    experts_on(step, 0)
                for n in range(micro_count):
                    prompts_on(n, 1)
                both_ways(early, 1)

    pl.run_scoped(
        outputs,
        pltpu.VMEM((rows, features), F32),
        pltpu.VMEM((rows, features), F32),
        pltpu.VMEM((total * capacity, features), BF),
        pltpu.VMEM((total * capacity, rows), BF),
        pltpu.VMEM((total * capacity, rows), BF),
    )

    def last_on(kind):
        for step in range(depth - 3, 0, -1):
            for local in range(1, local_count):
                for direction in (1, -1):
                    experts.pass_on(direction, step, local, (kind,))

    for d in late:
        d.add_high()
    both_ways(late, depth - 1)
    last_on(0)
    last_on(1)
    for step in range(depth - 2, 1, -1):
        both_ways(late, step)

    def inputs(x_rows, d_hidden, dn1):
        for m in range(micro_count):
            fetch([(tokens.at[m], x_rows), (d_hidden_o.at[m], d_hidden), (dn1_o.at[m], dn1)])
            for direction, slot in ((1, place.z), (-1, depth)):

                def body(m=m, slot=slot):
                    prompts[m].arrive(slot)
                    dn1[pl.ds(0, PB), :] += part_land[m, slot].astype(F32)

                pl.when(prompts[m].upstream(direction))(body)
            gain = gain_v[0:1, :]
            for i in range(rows // PB):
                here = pl.ds(i * PB, PB)
                values, d_normed = x_rows[here, :].astype(F32), dn1[here, :]
                root = lax.rsqrt(jnp.mean(values * values, -1, keepdims=True) + EPSILON)
                scaled = gain * d_normed
                d_values = (
                    d_hidden[here, :]
                    + root * scaled
                    - values * (root * root * root) * jnp.mean(values * scaled, -1, keepdims=True)
                )
                gain_own[0:1, :] += jnp.sum(d_normed * values * root, 0, keepdims=True)
                out_rows[here, :] = d_values.astype(BF)
            fetch([(out_rows, input_o.at[m])])

    pl.run_scoped(
        inputs,
        pltpu.VMEM((rows, features), BF),
        pltpu.VMEM((rows, features), F32),
        pltpu.VMEM((rows, features), F32),
    )
    last_on(2)
    for d in early:
        d.end()
    both_ways(late, 1)

    def gain_copies(first, targets, lands):
        return [
            remote(gain_own, land, gain_send.at[first + i], gain_recv.at[first + i], **target)
            for i, (target, land) in enumerate(zip(targets, lands))
        ]

    def gain_add(copies, lands):
        for copy in copies:
            copy.wait()
        total_gain = gain_own[...]
        for land in lands:
            total_gain = total_gain + land[...]
        gain_own[...] = total_gain

    peers = range(1, high_count)
    places = range(1, depth)
    stages = [
        (0, [dict(experts=place.e + 1 - 2 * place.low)], [gain_low]),
        (
            1,
            [dict(experts=place.peer_high(s) * 2 + place.low) for s in peers],
            [gain_high.at[s - 1] for s in peers],
        ),
        (
            high_count,
            [dict(context=lax.rem(place.z + s, depth)) for s in places],
            [gain_line.at[s - 1] for s in places],
        ),
        (high_count + depth - 1, [dict(dp=1 - place.x)], [gain_cross]),
    ]

    def gain_start(i):
        copies = gain_copies(*stages[i])
        for copy in copies:
            copy.start()
        return copies

    for i in range(2):
        gain_add(gain_start(i), stages[i][2])
    line_copies = gain_start(2)
    experts.end(0)
    for d in late:
        d.end()
    gain_add(line_copies, stages[2][2])
    cross_copies = gain_start(3)
    for d in early:
        d.finish()
    for d in late:
        d.finish()
    for local in range(1, local_count):
        experts.end(local)
    gain_add(cross_copies, stages[3][2])
    fetch([(gain_own, gain_o)])
    for d in dense:
        d.drain()
    experts.drain()
    for p in prompts:
        p.drain()
    for m in range(micro_count):
        for step in range(1, owners):
            for entry in returns:
                hand_back(*entry, m, step).wait_send()


def run_backward(sizes, tokens, cot, gates, routes, gate_rows, forward):
    depth, high_count = sizes
    micro_count, rows, features = tokens.shape
    owners = high_count * 2
    line = depth * owners
    prompt = depth * PB
    length = prompt + CONT
    cosine, sine_part = rope_tables(prompt)
    gsg, geg, outs = forward[12], forward[15], forward[18]
    local_count, slots, _ = outs.shape
    total = owners * local_count
    capacity = rows * 8 // (3 * total)
    part = gsg.shape[1] // line
    width = geg.shape[2] // (2 * depth)
    hbm, vmem = pl.BlockSpec(memory_space=pltpu.HBM), pl.BlockSpec(memory_space=pltpu.VMEM)
    shapes = [(features, part), (features, part), (part, features)]
    shapes += [(forward[0].shape[0] // line, features), (forward[1].shape[0] // line, features)]
    expert_shapes = [(features, width), (features, width), (width, features)]
    returned = (micro_count, owners, local_count, capacity, features)
    out_dims = [(micro_count, rows, features)] * 2
    out_dims += [shapes[3], shapes[4], shapes[0], shapes[1], shapes[2]]
    out_dims += [(local_count,) + s for s in expert_shapes]
    out_shape = [jax.ShapeDtypeStruct(dims, BF) for dims in out_dims]
    out_shape += [jax.ShapeDtypeStruct((8, features), F32)]
    out_shape += [jax.ShapeDtypeStruct((depth + 1, local_count) + s, BF) for s in expert_shapes]
    out_shape += [jax.ShapeDtypeStruct(returned, BF)] * 2
    out_shape += [jax.ShapeDtypeStruct((micro_count, rows, features), F32)] * 2
    out_shape += [jax.ShapeDtypeStruct((local_count,) + s, BF) for s in expert_shapes]
    scratch = [pltpu.VMEM((depth, high_count) + s, BF) for s in shapes]
    scratch += [pltpu.VMEM((high_count - 1, depth) + s, BF) for s in shapes]
    scratch += [pltpu.VMEM((depth + 1,) + s, BF) for s in shapes]
    scratch += [pltpu.VMEM(s, BF) for s in shapes]
    scratch += [pltpu.VMEM((2,) + shapes[0], BF), pltpu.VMEM((2,) + shapes[2], BF)]
    scratch += [pltpu.VMEM((depth, local_count) + s, BF) for s in expert_shapes]
    scratch += [pltpu.VMEM(s, BF) for s in expert_shapes]
    scratch += [pltpu.VMEM((2,) + s, BF) for s in expert_shapes]
    token_rows, key_rows = micro_count * rows, micro_count * length
    gain = (8, features)
    scratch += [
        pltpu.VMEM((token_rows, features), BF),
        pltpu.VMEM((token_rows, features), BF),
        pltpu.VMEM((key_rows, features), BF),
        pltpu.VMEM((key_rows, features), BF),
        pltpu.VMEM(forward[0].shape, BF),
        pltpu.VMEM(forward[1].shape, BF),
        pltpu.VMEM((micro_count, depth, PB, features), BF),
        pltpu.VMEM((micro_count, depth + 1, PB, features), BF),
        pltpu.VMEM(gain, F32),
        pltpu.VMEM(gain, F32),
        pltpu.VMEM((high_count - 1,) + gain, F32),
        pltpu.VMEM((depth - 1,) + gain, F32),
        pltpu.VMEM(gain, F32),
        pltpu.VMEM((rows, features), BF),
    ]
    dma = pltpu.SemaphoreType.DMA
    scratch += DenseScatter.semaphores(len(shapes), depth, high_count)
    scratch += ExpertScatter.semaphores(depth, local_count)
    stages = 1 + high_count + depth
    scratch += [
        dma((micro_count, depth + 1)),
        dma((micro_count, depth + 1)),
        dma((owners, micro_count)),
        dma((owners, micro_count)),
        dma((owners, micro_count)),
        dma((owners, micro_count)),
        dma((stages,)),
        dma((stages,)),
        dma((max(total, 2 + micro_count, 4 * micro_count + micro_count),)),
        dma((1,)),
        dma((1,)),
    ]
    return pl.pallas_call(
        functools.partial(backward_kernel, sizes),
        out_shape=out_shape,
        in_specs=[hbm] * 2 + [vmem] * 5 + [hbm] * 2 + [vmem] + [hbm] * 20,
        out_specs=[hbm] * len(out_shape),
        scratch_shapes=scratch,
        compiler_params=pltpu.CompilerParams(
            collective_id=1, has_side_effects=True, vmem_limit_bytes=60 * MIB
        ),
        name="backward_and_sum",
    )(tokens, cot, gates, routes, gate_rows, cosine, sine_part, *forward)


def finish_kernel(count, gain_width, *refs):
    low, refs = refs[:count], refs[count:]
    rows, refs = refs[:2], refs[2:]
    gain, refs = refs[0], refs[1:]
    rows_o, refs = refs[:2], refs[2:]
    wide_o, refs = refs[:count], refs[count:]
    gain_o, refs = refs[0], refs[1:]
    low_s, refs = refs[:count], refs[count:]
    wide_s, refs = refs[:count], refs[count:]
    rows_s, sem_in, sem_out = refs[:2], refs[2], refs[3]
    loads = [
        pltpu.make_async_copy(source, target, sem_in.at[i])
        for i, (source, target) in enumerate(zip(low + rows, low_s + rows_s))
    ]
    for copy in loads:
        copy.start()
    stores = [
        pltpu.make_async_copy(source, target, sem_out.at[i])
        for i, (source, target) in enumerate(zip(wide_s + rows_s, wide_o + rows_o))
    ]
    place = (lax.axis_index(CONTEXT) * lax.axis_size(EXPERTS) + lax.axis_index(EXPERTS)) * gain_width
    features = gain.shape[1]
    gain_o[...] = pltpu.roll(gain[...], lax.rem(features - place, features), 1)[:2, :gain_width]
    for i in range(count):
        loads[i].wait()
        wide_s[i][...] = low_s[i][...].astype(F32)
        stores[i].start()
    for i in range(count, count + 2):
        loads[i].wait()
        stores[i].start()
    for copy in stores:
        copy.wait()


def finish_outputs(low, rows, gain, gain_width):
    count = len(low)
    hbm, vmem = pl.BlockSpec(memory_space=pltpu.HBM), pl.BlockSpec(memory_space=pltpu.VMEM)
    wide = [item.shape for item in low]
    out_shape = [jax.ShapeDtypeStruct(item.shape, BF) for item in rows]
    out_shape += [jax.ShapeDtypeStruct(dims, F32) for dims in wide]
    out_shape += [jax.ShapeDtypeStruct((2, gain_width), F32)]
    dma = pltpu.SemaphoreType.DMA
    return pl.pallas_call(
        functools.partial(finish_kernel, count, gain_width),
        out_shape=out_shape,
        in_specs=[hbm] * (count + 2) + [vmem],
        out_specs=[hbm] * (count + 2) + [vmem],
        scratch_shapes=[pltpu.VMEM(item.shape, BF) for item in low]
        + [pltpu.VMEM(dims, F32) for dims in wide]
        + [pltpu.VMEM(item.shape, BF) for item in rows]
        + [dma((count + 2,)), dma((count + 2,))],
        compiler_params=pltpu.CompilerParams(vmem_limit_bytes=60 * MIB),
        name="finish_outputs",
    )(*low, *rows, gain)


def on_device_plain(
    tokens,
    cotangent,
    gates,
    routes,
    qkv_weight,
    out_weight,
    shared_gate,
    shared_up,
    shared_down,
    gains,
    expert_gate,
    expert_up,
    expert_down,
):
    micro_count = tokens.shape[2]
    row_count = tokens.shape[4]
    feature_count = tokens.shape[5]
    owners = lax.axis_size(EXPERTS)
    local_experts = expert_gate.shape[0]
    total_experts = owners * local_experts
    capacity = row_count * 8 // (3 * total_experts)
    blocks = lax.axis_size(CONTEXT)
    prompt = blocks * PB
    scaling = HD ** (-0.5)
    w_qkv, w_out, w_sgate, w_sup, w_sdown, w_gains = (
        lax.all_gather(qkv_weight, (CONTEXT, EXPERTS), axis=1, tiled=True),
        lax.all_gather(out_weight, (CONTEXT, EXPERTS), axis=0, tiled=True),
        lax.all_gather(shared_gate, (CONTEXT, EXPERTS), axis=1, tiled=True),
        lax.all_gather(shared_up, (CONTEXT, EXPERTS), axis=1, tiled=True),
        lax.all_gather(shared_down, (CONTEXT, EXPERTS), axis=0, tiled=True),
        lax.all_gather(gains, (CONTEXT, EXPERTS), axis=1, tiled=True),
    )
    e_gate, expert_up_weight, e_down = (
        lax.all_gather(expert_gate, (DP, CONTEXT), axis=2, tiled=True),
        lax.all_gather(expert_up, (DP, CONTEXT), axis=2, tiled=True),
        lax.all_gather(expert_down, (DP, CONTEXT), axis=1, tiled=True),
    )
    gain_one = w_gains[0].astype(jnp.float32)
    gain_two = w_gains[1].astype(jnp.float32)
    here_index = lax.axis_index(CONTEXT)
    row_ids = jnp.arange(row_count, dtype=jnp.int32)
    query_pos = jnp.where(row_ids < PB, here_index * PB + row_ids, prompt + row_ids - PB)
    key_pos = jnp.arange(prompt + CONT, dtype=jnp.int32)
    allowed = key_pos[None, None, :] <= query_pos[None, :, None]
    half_size = HD // 2
    frequency = 10000.0 ** (-2.0 * jnp.arange(half_size, dtype=jnp.float32) / HD)
    angles = query_pos.astype(jnp.float32)[:, None] * frequency
    cosine = jnp.cos(angles)[:, None, :]
    sine_part = jnp.sin(angles)[:, None, :]
    kept_list = []
    mixed_list = []
    for step_index in range(micro_count):
        inputs = tokens[0, 0, step_index, 0].astype(jnp.float32)
        root_one = lax.rsqrt(jnp.mean(inputs * inputs, -1, keepdims=True) + EPSILON)
        normed_one = (inputs * root_one * gain_one).astype(jnp.bfloat16)
        projected = mdot(normed_one, w_qkv)
        query = rotate(projected[:, :feature_count], cosine, sine_part).astype(jnp.bfloat16)
        key_rows = rotate(
            projected[:, feature_count : 2 * feature_count], cosine, sine_part
        ).astype(jnp.bfloat16)
        value_rows = projected[:, 2 * feature_count :].astype(jnp.bfloat16)
        prompt_key, prompt_value = (
            lax.all_gather(key_rows[:PB], CONTEXT, axis=0, tiled=True),
            lax.all_gather(value_rows[:PB], CONTEXT, axis=0, tiled=True),
        )
        key_heads = jnp.concatenate([prompt_key, key_rows[PB:]], 0).reshape(prompt + CONT, H, HD)
        value_heads = jnp.concatenate([prompt_value, value_rows[PB:]], 0).reshape(
            prompt + CONT, H, HD
        )
        query_heads = query.reshape(row_count, H, HD)
        scores = (
            jnp.einsum("qhd,khd->hqk", query_heads, key_heads, preferred_element_type=jnp.float32)
            * scaling
        )
        scores = jnp.where(allowed, scores, -1000000000.0)
        highest = jnp.max(scores, -1, keepdims=True)
        weights = jnp.exp(scores - highest)
        total = jnp.sum(weights, -1, keepdims=True)
        log_total = highest + jnp.log(total)
        probs = (weights / total).astype(jnp.bfloat16)
        attended = (
            jnp.einsum("hqk,khd->qhd", probs, value_heads, preferred_element_type=jnp.float32)
            .reshape(row_count, feature_count)
            .astype(jnp.bfloat16)
        )
        hidden = inputs + mdot(attended, w_out)
        root_two = lax.rsqrt(jnp.mean(hidden * hidden, -1, keepdims=True) + EPSILON)
        normed_two = (hidden * root_two * gain_two).astype(jnp.bfloat16)
        side_gate = mdot(normed_two, w_sgate)
        side_up = mdot(normed_two, w_sup)
        side_act = (jax.nn.silu(side_gate) * side_up).astype(jnp.bfloat16)
        side = mdot(side_act, w_sdown)
        route_rows = routes[0, 0, step_index, 0]
        slots = slot_table(route_rows, total_experts)
        flat_dest = (route_rows * capacity + slots).reshape(-1)
        source = (
            jnp.full((total_experts * capacity,), 2 * row_count, jnp.int32)
            .at[flat_dest]
            .set(jnp.arange(2 * row_count, dtype=jnp.int32))
        )
        padded = jnp.concatenate([normed_two, jnp.zeros((1, feature_count), jnp.bfloat16)], 0)
        send = padded[source // 2].reshape(total_experts, capacity, feature_count)
        received = lax.all_to_all(send, EXPERTS, split_axis=0, concat_axis=0, tiled=True)
        count = received.shape[1]
        expert_grouped = received.reshape(owners, local_experts, count, feature_count)
        expert_gate_act = jnp.einsum(
            "send,edf->senf", expert_grouped, e_gate, preferred_element_type=jnp.float32
        )
        expert_up_act = jnp.einsum(
            "send,edf->senf", expert_grouped, expert_up_weight, preferred_element_type=jnp.float32
        )
        expert_hidden_act = (jax.nn.silu(expert_gate_act) * expert_up_act).astype(jnp.bfloat16)
        result = jnp.einsum(
            "senf,efd->send", expert_hidden_act, e_down, preferred_element_type=jnp.float32
        ).astype(jnp.bfloat16)
        expert_out = result.reshape(owners * local_experts, count, feature_count)
        expert_in = received
        returned = lax.all_to_all(
            expert_out, EXPERTS, split_axis=0, concat_axis=0, tiled=True
        ).reshape(-1, feature_count)
        gate_rows = gates[0, 0, step_index, 0]
        picked = returned[flat_dest].reshape(row_count, 2, feature_count).astype(jnp.float32)
        routed = jnp.sum(gate_rows[:, :, None] * picked, 1)
        mixed_list.append((hidden + routed + side).astype(jnp.bfloat16))
        cached = (prompt_key, prompt_value)
        kept_list.append(
            (
                inputs,
                root_one,
                normed_one,
                query,
                key_rows,
                value_rows,
                cached,
                log_total,
                attended,
                hidden,
                root_two,
                normed_two,
                side_gate,
                side_up,
                side_act,
                flat_dest,
                source,
                expert_in,
                gate_rows,
            )
        )
    acc_qkv = jnp.zeros(w_qkv.shape, jnp.float32)
    acc_out = jnp.zeros(w_out.shape, jnp.float32)
    acc_sgate = jnp.zeros(w_sgate.shape, jnp.float32)
    acc_sup = jnp.zeros(w_sup.shape, jnp.float32)
    acc_sdown = jnp.zeros(w_sdown.shape, jnp.float32)
    acc_gain_one = jnp.zeros((feature_count,), jnp.float32)
    acc_gain_two = jnp.zeros((feature_count,), jnp.float32)
    local_egate = jnp.zeros(e_gate.shape, jnp.float32)
    local_expert_up_weight = jnp.zeros(expert_up_weight.shape, jnp.float32)
    local_edown = jnp.zeros(e_down.shape, jnp.float32)
    input_list = []
    for step_index in range(micro_count):
        (
            inputs,
            root_one,
            normed_one,
            query,
            key_rows,
            value_rows,
            cached,
            log_total,
            attended,
            hidden,
            root_two,
            normed_two,
            side_gate,
            side_up,
            side_act,
            flat_dest,
            source,
            expert_in,
            gate_rows,
        ) = kept_list[step_index]
        grad_rows = cotangent[0, 0, step_index, 0].astype(jnp.float32)
        grad_low = grad_rows.astype(jnp.bfloat16)
        acc_sdown = acc_sdown + tdot(side_act, grad_low)
        d_side_act = ndot(grad_low, w_sdown).astype(jnp.bfloat16).astype(jnp.float32)
        silu_side, slope_side = silu_parts(side_gate)
        d_side_gate = (d_side_act * side_up * slope_side).astype(jnp.bfloat16)
        d_side_up = (d_side_act * silu_side).astype(jnp.bfloat16)
        acc_sgate = acc_sgate + tdot(normed_two, d_side_gate)
        acc_sup = acc_sup + tdot(normed_two, d_side_up)
        d_normed_two = ndot(d_side_gate, w_sgate) + ndot(d_side_up, w_sup)
        d_pairs = (
            (gate_rows[:, :, None] * grad_rows[:, None, :])
            .astype(jnp.bfloat16)
            .reshape(2 * row_count, feature_count)
        )
        padded_grad = jnp.concatenate([d_pairs, jnp.zeros((1, feature_count), jnp.bfloat16)], 0)
        grad_send = padded_grad[source].reshape(total_experts, capacity, feature_count)
        grad_in = lax.all_to_all(grad_send, EXPERTS, split_axis=0, concat_axis=0, tiled=True)
        grouped_grad = grad_in.reshape(owners, local_experts, capacity, feature_count)
        grouped = expert_in.reshape(owners, local_experts, capacity, feature_count)
        gate_act = jnp.einsum("send,edf->senf", grouped, e_gate, preferred_element_type=jnp.float32)
        up_act = jnp.einsum(
            "send,edf->senf", grouped, expert_up_weight, preferred_element_type=jnp.float32
        )
        silu_gate, slope_gate = silu_parts(gate_act)
        hidden_act = (silu_gate * up_act).astype(jnp.bfloat16)
        d_hidden_act = (
            jnp.einsum("send,efd->senf", grouped_grad, e_down, preferred_element_type=jnp.float32)
            .astype(jnp.bfloat16)
            .astype(jnp.float32)
        )
        d_gate_act = (d_hidden_act * up_act * slope_gate).astype(jnp.bfloat16)
        d_up_act = (d_hidden_act * silu_gate).astype(jnp.bfloat16)
        step_edown = jnp.einsum(
            "senf,send->efd", hidden_act, grouped_grad, preferred_element_type=jnp.float32
        )
        step_egate = jnp.einsum(
            "send,senf->edf", grouped, d_gate_act, preferred_element_type=jnp.float32
        )
        stepwise_expert_up = jnp.einsum(
            "send,senf->edf", grouped, d_up_act, preferred_element_type=jnp.float32
        )
        local_egate = local_egate + step_egate
        local_expert_up_weight = local_expert_up_weight + stepwise_expert_up
        local_edown = local_edown + step_edown
        d_expert_in = jnp.einsum(
            "senf,edf->send", d_gate_act, e_gate, preferred_element_type=jnp.float32
        ) + jnp.einsum(
            "senf,edf->send", d_up_act, expert_up_weight, preferred_element_type=jnp.float32
        )
        d_expert_in = d_expert_in.astype(jnp.bfloat16).reshape(
            total_experts, capacity, feature_count
        )
        back = lax.all_to_all(
            d_expert_in, EXPERTS, split_axis=0, concat_axis=0, tiled=True
        ).reshape(-1, feature_count)
        d_normed_two = d_normed_two + jnp.sum(
            back[flat_dest].reshape(row_count, 2, feature_count).astype(jnp.float32), 1
        )
        scaled_two = gain_two * d_normed_two
        d_hidden = (
            grad_rows
            + root_two * scaled_two
            - hidden * root_two**3 * jnp.mean(hidden * scaled_two, -1, keepdims=True)
        )
        acc_gain_two = acc_gain_two + jnp.sum(d_normed_two * hidden * root_two, 0)
        d_attn = d_hidden.astype(jnp.bfloat16)
        acc_out = acc_out + tdot(attended, d_attn)
        d_attended = ndot(d_attn, w_out).astype(jnp.bfloat16)
        prompt_key, prompt_value = cached
        key_heads = jnp.concatenate([prompt_key, key_rows[PB:]], 0).reshape(prompt + CONT, H, HD)
        value_heads = jnp.concatenate([prompt_value, value_rows[PB:]], 0).reshape(
            prompt + CONT, H, HD
        )
        query_heads = query.reshape(row_count, H, HD)
        scores = (
            jnp.einsum("qhd,khd->hqk", query_heads, key_heads, preferred_element_type=jnp.float32)
            * scaling
        )
        scores = jnp.where(allowed, scores, -1000000000.0)
        probs = jnp.exp(scores - log_total)
        d_heads = d_attended.reshape(row_count, H, HD)
        d_probs = jnp.einsum(
            "qhd,khd->hqk", d_heads, value_heads, preferred_element_type=jnp.float32
        )
        centre = jnp.sum(probs * d_probs, -1, keepdims=True)
        d_scores = (probs * (d_probs - centre)).astype(jnp.bfloat16)
        d_query = (
            jnp.einsum(
                "hqk,khd->qhd", d_scores, key_heads, preferred_element_type=jnp.float32
            ).reshape(row_count, feature_count)
            * scaling
        )
        d_keys = (
            jnp.einsum(
                "hqk,qhd->khd", d_scores, query_heads, preferred_element_type=jnp.float32
            ).reshape(prompt + CONT, feature_count)
            * scaling
        )
        d_values = jnp.einsum(
            "hqk,qhd->khd", probs.astype(jnp.bfloat16), d_heads, preferred_element_type=jnp.float32
        ).reshape(prompt + CONT, feature_count)
        own_dkey, own_dvalue = (
            lax.psum_scatter(
                d_keys[:prompt].astype(jnp.bfloat16), CONTEXT, scatter_dimension=0, tiled=True
            ).astype(jnp.float32),
            lax.psum_scatter(
                d_values[:prompt].astype(jnp.bfloat16), CONTEXT, scatter_dimension=0, tiled=True
            ).astype(jnp.float32),
        )
        d_key_rows = jnp.concatenate([own_dkey, d_keys[prompt:]], 0)
        d_value_rows = jnp.concatenate([own_dvalue, d_values[prompt:]], 0)
        d_projected = jnp.concatenate(
            [
                rotate(d_query, cosine, -sine_part).astype(jnp.bfloat16),
                rotate(d_key_rows, cosine, -sine_part).astype(jnp.bfloat16),
                d_value_rows.astype(jnp.bfloat16),
            ],
            1,
        )
        acc_qkv = acc_qkv + tdot(normed_one, d_projected)
        d_normed_one = ndot(d_projected, w_qkv)
        scaled_one = gain_one * d_normed_one
        d_inputs = (
            d_hidden
            + root_one * scaled_one
            - inputs * root_one**3 * jnp.mean(inputs * scaled_one, -1, keepdims=True)
        )
        acc_gain_one = acc_gain_one + jnp.sum(d_normed_one * inputs * root_one, 0)
        input_list.append(d_inputs.astype(jnp.bfloat16))
    sharded_expert_gate, sharded_expert_up, sharded_expert_down = (
        lax.psum_scatter(
            local_egate.astype(jnp.bfloat16), (DP, CONTEXT), scatter_dimension=2, tiled=True
        ).astype(jnp.float32),
        lax.psum_scatter(
            local_expert_up_weight.astype(jnp.bfloat16),
            (DP, CONTEXT),
            scatter_dimension=2,
            tiled=True,
        ).astype(jnp.float32),
        lax.psum_scatter(
            local_edown.astype(jnp.bfloat16), (DP, CONTEXT), scatter_dimension=1, tiled=True
        ).astype(jnp.float32),
    )
    acc_gains = jnp.stack([acc_gain_one, acc_gain_two], 0)
    dense_shards = (
        lax.psum_scatter(acc_qkv, (CONTEXT, EXPERTS), scatter_dimension=1, tiled=True),
        lax.psum_scatter(acc_out, (CONTEXT, EXPERTS), scatter_dimension=0, tiled=True),
        lax.psum_scatter(acc_sgate, (CONTEXT, EXPERTS), scatter_dimension=1, tiled=True),
        lax.psum_scatter(acc_sup, (CONTEXT, EXPERTS), scatter_dimension=1, tiled=True),
        lax.psum_scatter(acc_sdown, (CONTEXT, EXPERTS), scatter_dimension=0, tiled=True),
        lax.psum_scatter(acc_gains, (CONTEXT, EXPERTS), scatter_dimension=1, tiled=True),
    )
    grad_qkv, grad_out, grad_sgate, grad_sup, grad_sdown, grad_gains = (
        lax.psum(dense_shards[0].astype(jnp.bfloat16), DP).astype(jnp.float32),
        lax.psum(dense_shards[1].astype(jnp.bfloat16), DP).astype(jnp.float32),
        lax.psum(dense_shards[2].astype(jnp.bfloat16), DP).astype(jnp.float32),
        lax.psum(dense_shards[3].astype(jnp.bfloat16), DP).astype(jnp.float32),
        lax.psum(dense_shards[4].astype(jnp.bfloat16), DP).astype(jnp.float32),
        lax.psum(dense_shards[5].astype(jnp.bfloat16), DP).astype(jnp.float32),
    )
    mixed = jnp.stack(mixed_list, 0).reshape(tokens.shape)
    input_grad = jnp.stack(input_list, 0).reshape(tokens.shape)
    return (
        mixed,
        input_grad,
        grad_qkv,
        grad_out,
        grad_sgate,
        grad_sup,
        grad_sdown,
        grad_gains,
        sharded_expert_gate,
        sharded_expert_up,
        sharded_expert_down,
    )


def on_device(
    tokens,
    cotangent,
    gates,
    routes,
    qkv_weight,
    out_weight,
    shared_gate,
    shared_up,
    shared_down,
    gains,
    expert_gate,
    expert_up,
    expert_down,
):
    owners = lax.axis_size(EXPERTS)
    sizes = (lax.axis_size(CONTEXT), owners // 2)
    own_at = lax.axis_index(CONTEXT) * owners + lax.axis_index(EXPERTS)
    gain_width, features = gains.shape[1], tokens.shape[5]
    gain_rows = lax.dynamic_update_slice(
        jnp.zeros((16, features), jnp.bfloat16), gains, (0, own_at * gain_width)
    )
    rows, cot = tokens[0, 0, :, 0], cotangent[0, 0, :, 0]
    gate_rows, route_rows = gates[0, 0, :, 0], routes[0, 0, :, 0]
    gate_columns, route_columns = gate_rows.transpose(0, 2, 1), route_rows.transpose(0, 2, 1)
    forward = run_forward(
        sizes,
        rows,
        cot,
        gate_columns,
        route_columns,
        (qkv_weight.T, out_weight, gain_rows, shared_gate, shared_up, shared_down),
        (expert_gate, expert_up, expert_down),
    )
    (
        mixed, input_grad, grad_qkv, grad_out, grad_sgate, grad_sup, grad_sdown,
        grad_egate, grad_eup, grad_edown, gain_sum, *_,
    ) = run_backward(
        sizes, rows, cot, gate_columns, route_columns, gate_rows, forward[:3] + forward[9:]
    )
    mixed, input_grad, grad_qkv, *rest = finish_outputs(
        (grad_qkv, grad_out, grad_sgate, grad_sup, grad_sdown, grad_egate, grad_eup, grad_edown),
        (mixed, input_grad),
        gain_sum,
        gain_width,
    )
    grad_out, grad_sgate, grad_sup, grad_sdown, grad_egate, grad_eup, grad_edown, grad_gains = rest
    return (
        mixed.reshape(tokens.shape),
        input_grad.reshape(tokens.shape),
        grad_qkv.T,
        grad_out,
        grad_sgate,
        grad_sup,
        grad_sdown,
        grad_gains,
        grad_egate,
        grad_eup,
        grad_edown,
    )


def kernels_fit(mesh_shape, arrays):
    qkv_weight, out_weight, shared_gate, _, shared_down = arrays[4:9]
    rows = (qkv_weight.shape[1], out_weight.shape[0], shared_gate.shape[1], shared_down.shape[0])
    return (
        mesh_shape[DP] == 2
        and mesh_shape[CONTEXT] >= 4
        and mesh_shape[EXPERTS] % 2 == 0
        and all(count % 16 == 0 for count in rows)
        and shared_gate.shape[1] % 128 == 0
        and arrays[10].shape[2] % 128 == 0
        and shared_gate.shape[1] * mesh_shape[EXPERTS] == 2 * arrays[10].shape[2]
    )


def solution(mesh):
    def device_program(*arrays):
        return (on_device if kernels_fit(mesh.shape, arrays) else on_device_plain)(*arrays)

    return jax.shard_map(
        device_program,
        mesh=mesh,
        in_specs=(
            P(DP, EXPERTS, None, CONTEXT, None, None),
            P(DP, EXPERTS, None, CONTEXT, None, None),
            P(DP, EXPERTS, None, CONTEXT, None, None),
            P(DP, EXPERTS, None, CONTEXT, None, None),
            P(None, (CONTEXT, EXPERTS)),
            P((CONTEXT, EXPERTS), None),
            P(None, (CONTEXT, EXPERTS)),
            P(None, (CONTEXT, EXPERTS)),
            P((CONTEXT, EXPERTS), None),
            P(None, (CONTEXT, EXPERTS)),
            P(EXPERTS, None, (DP, CONTEXT)),
            P(EXPERTS, None, (DP, CONTEXT)),
            P(EXPERTS, (DP, CONTEXT), None),
        ),
        out_specs=(
            P(DP, EXPERTS, None, CONTEXT, None, None),
            P(DP, EXPERTS, None, CONTEXT, None, None),
            P(None, (CONTEXT, EXPERTS)),
            P((CONTEXT, EXPERTS), None),
            P(None, (CONTEXT, EXPERTS)),
            P(None, (CONTEXT, EXPERTS)),
            P((CONTEXT, EXPERTS), None),
            P(None, (CONTEXT, EXPERTS)),
            P(EXPERTS, None, (DP, CONTEXT)),
            P(EXPERTS, None, (DP, CONTEXT)),
            P(EXPERTS, (DP, CONTEXT), None),
        ),
        check_vma=False,
    )
```

```python
import functools

import jax
import jax.numpy as jnp
import numpy as np
from jax import lax
from jax.experimental import pallas as pl
from jax.experimental.pallas import tpu as pltpu
from jax.sharding import PartitionSpec as P

DP, CONTEXT, EXPERTS = "dp", "context", "experts"

H = 12
HD = 64
PB = 128
CONT = 256


EPSILON = 1e-06


def mdot(former, latter):
    return jnp.dot(former, latter, preferred_element_type=jnp.float32)


def tdot(former, latter):
    return lax.dot_general(
        former, latter, (((0,), (0,)), ((), ())), preferred_element_type=jnp.float32
    )


def ndot(former, latter):
    return lax.dot_general(
        former, latter, (((1,), (1,)), ((), ())), preferred_element_type=jnp.float32
    )


def rotate(values, cosine, sine_part):
    half_size = HD // 2
    shaped = values.reshape(values.shape[0], H, HD)
    former = shaped[..., :half_size]
    latter = shaped[..., half_size:]
    turned = jnp.concatenate(
        [former * cosine - latter * sine_part, latter * cosine + former * sine_part], -1
    )
    return turned.reshape(values.shape)


def slot_table(routes_block, expert_count):
    flat_routes = routes_block.reshape(-1)
    onehot = (flat_routes[:, None] == jnp.arange(expert_count, dtype=jnp.int32)[None, :]).astype(
        jnp.int32
    )
    before = jnp.cumsum(onehot, 0) - onehot
    return jnp.sum(before * onehot, 1).reshape(routes_block.shape)


def silu_parts(values):
    sigma = jax.nn.sigmoid(values)
    return (values * sigma, sigma * (1.0 + values * (1.0 - sigma)))


MESH = pl.DeviceIdType.MESH
MIB = 1024 * 1024
BF = jnp.bfloat16
F32 = jnp.float32


def remote(source, target, send_sem, recv_sem, **device):
    return pltpu.make_async_remote_copy(
        src_ref=source,
        dst_ref=target,
        send_sem=send_sem,
        recv_sem=recv_sem,
        device_id=device,
        device_id_type=MESH,
    )


def arrived(slot, recv_sem):
    remote(slot, slot, recv_sem, recv_sem, context=0).wait_recv()


def either(first, second):
    return jnp.logical_and(first, second)


class Place:
    def __init__(self, sizes):
        self.depth, self.high_count = sizes
        self.owners = self.high_count * 2
        self.x = lax.axis_index(DP)
        self.z = lax.axis_index(CONTEXT)
        self.e = lax.axis_index(EXPERTS)
        self.high = self.e // 2
        self.low = self.e % 2

    def shard(self, z):
        return self.x * self.depth + z

    def other_shard(self, z):
        return (1 - self.x) * self.depth + z

    def peer_high(self, step):
        return lax.rem(self.high + step, self.high_count)

    def peer_owner(self, step):
        return lax.rem(self.e + step, self.owners)

    def on_line(self, z):
        return (z >= 0) & (z < self.depth)

    def greet(self):
        barrier = pltpu.get_barrier_semaphore()

        def signal(**device):
            pl.semaphore_signal(barrier, inc=1, device_id=device, device_id_type=MESH)

        signal(dp=1 - self.x)
        for step in range(1, self.owners):
            signal(experts=self.peer_owner(step))
        for step in range(1, self.depth):
            signal(context=lax.rem(self.z + step, self.depth))
        count = self.owners + self.depth - 1
        pl.semaphore_wait(barrier, count)


class Line:
    def __init__(self, place, own, slot, send_sem, recv_sem):
        self.place, self.own, self.slot = place, own, slot
        self.send_sem, self.recv_sem = send_sem, recv_sem

    def _copy(self, direction, step):
        place = self.place
        z = place.z - direction * step
        source = self.own if step == 0 else self.slot(z)
        return remote(
            source,
            self.slot(z),
            self.send_sem.at[(direction + 1) // 2, step],
            self.recv_sem.at[z],
            context=place.z + direction,
        )

    def _valid(self, direction, step):
        place = self.place
        return place.on_line(place.z - direction * step) & place.on_line(place.z + direction)

    def send(self, direction, step):
        if step < self.place.depth - 1:
            pl.when(self._valid(direction, step))(lambda: self._copy(direction, step).start())

    def start(self):
        self.send(1, 0)
        self.send(-1, 0)

    def hop(self, step, then=None):
        for direction in (1, -1):
            z = self.place.z - direction * (step + 1)

            def body(direction=direction, z=z):
                arrived(self.slot(z), self.recv_sem.at[z])
                self.send(direction, step + 1)
                if then is not None:
                    then(z)

            pl.when(self.place.on_line(z))(body)

    def drain(self):
        for direction in (1, -1):
            for step in range(self.place.depth - 1):
                pl.when(self._valid(direction, step))(
                    lambda d=direction, s=step: self._copy(d, s).wait_send()
                )


class DenseGather:
    def __init__(self, place, own, slot, sems):
        self.place, self.own, self.slot_of = place, own, slot
        zs, zr, self.h_send, self.h_recv, self.l_send, self.l_recv = sems
        self.line = Line(place, own, lambda z: self.slot(z, place.high, place.low), zs, zr)

    @staticmethod
    def semaphores(count, depth, high_count):
        dma = pltpu.SemaphoreType.DMA
        cross = dma((count, high_count, depth))
        return [dma((count, 2, depth)), dma((count, depth)), cross, cross, cross, cross]

    def slot(self, z, high, low):
        return self.slot_of((z * self.place.high_count + high) * 2 + low)

    def _to_high(self, z, step, own):
        place = self.place
        target = self.slot(z, place.high, place.low)
        return remote(
            self.own if own else target,
            target,
            self.h_send.at[step, z],
            self.h_recv.at[place.high, z],
            experts=place.peer_high(step) * 2 + place.low,
        )

    def _to_low(self, z, high, own):
        place = self.place
        target = self.slot(z, high, place.low)
        return remote(
            self.own if own else target,
            target,
            self.l_send.at[high, z],
            self.l_recv.at[high, z],
            experts=place.e + 1 - 2 * place.low,
        )

    def _spread(self, z, own=False):
        for step in range(1, self.place.high_count):
            self._to_high(z, step, own).start()
        self._to_low(z, self.place.high, own).start()

    def start(self):
        self.line.start()
        self._spread(self.place.z, True)

    def hop(self, step):
        self.line.hop(step, self._spread)

    def cross(self, z):
        place = self.place
        for step in range(1, place.high_count):
            high = place.peer_high(step)
            arrived(self.slot(z, high, place.low), self.h_recv.at[high, z])
            self._to_low(z, high, False).start()

    def finish(self, z):
        place = self.place
        for high in range(place.high_count):
            arrived(self.slot(z, high, 1 - place.low), self.l_recv.at[high, z])

    def drain(self):
        place = self.place
        self.line.drain()
        for z in range(place.depth):
            for step in range(1, place.high_count):
                self._to_high(z, step, False).wait_send()
            for high in range(place.high_count):
                self._to_low(z, high, False).wait_send()


def expert_slab(ref, kind, local, shard, width):
    start = pl.multiple_of(shard * width, 128)
    if kind == 2:
        return ref.at[local, pl.ds(start, width)]
    return ref.at[local, :, pl.ds(start, width)]


class ExpertGather:
    def __init__(self, place, own, out, sems):
        self.place, self.own, self.out = place, own, out
        self.z_send, self.z_recv, self.x_send, self.x_recv = sems
        self.local_count, self.width = own[0].shape[0], own[0].shape[2]

    @staticmethod
    def semaphores(depth, local_count):
        dma = pltpu.SemaphoreType.DMA
        return [
            dma((local_count, 3, 2, depth)),
            dma((local_count, 3, depth)),
            dma((local_count, 3, depth)),
            dma((local_count, 3, depth)),
        ]

    def slot(self, local, kind, shard):
        return expert_slab(self.out[kind], kind, local, shard, self.width)

    def _line(self, local, kind):
        return Line(
            self.place,
            self.own[kind].at[local],
            lambda z: self.slot(local, kind, self.place.shard(z)),
            self.z_send.at[local, kind],
            self.z_recv.at[local, kind],
        )

    def _across(self, local, kind, z, own=False):
        target = self.slot(local, kind, self.place.shard(z))
        return remote(
            self.own[kind].at[local] if own else target,
            target,
            self.x_send.at[local, kind, z],
            self.x_recv.at[local, kind, z],
            dp=1 - self.place.x,
        )

    def start_x(self):
        for local in range(self.local_count):
            for kind in range(3):
                self._across(local, kind, self.place.z, True).start()

    def start_z(self):
        for local in range(self.local_count):
            for kind in range(3):
                self._line(local, kind).start()

    def hop(self, local, step, kinds=(0, 1, 2)):
        for kind in kinds:
            self._line(local, kind).hop(
                step, lambda z, kind=kind: self._across(local, kind, z).start()
            )

    def wait_x(self, local, z):
        for kind in range(3):
            arrived(
                self.slot(local, kind, self.place.other_shard(z)), self.x_recv.at[local, kind, z]
            )

    def drain(self):
        for local in range(self.local_count):
            for kind in range(3):
                self._line(local, kind).drain()
                for z in range(self.place.depth):
                    self._across(local, kind, z).wait_send()


def rope(values, cosine, sine_part):
    lane = lax.broadcasted_iota(jnp.int32, cosine.shape, 1)
    first = lax.rem(lane, HD) < HD // 2
    turned = []
    for start in range(0, values.shape[1], 2 * HD):
        part = values[:, start : start + 2 * HD]
        partner = jnp.where(
            first, pltpu.roll(part, 2 * HD - HD // 2, 1), pltpu.roll(part, HD // 2, 1)
        )
        turned.append(part * cosine + partner * sine_part)
    return jnp.concatenate(turned, 1)


def norm_rows(values, gain):
    root = lax.rsqrt(jnp.mean(values * values, -1, keepdims=True) + EPSILON)
    return (values * root * gain).astype(BF)


def tiles(total, size, body):
    def run(i, carry):
        body(pl.ds(pl.multiple_of(i * size, size), size))
        return carry

    lax.fori_loop(0, total // size, run, 0)


def one_hots(routes, gates, me, local_count, total):
    rows = routes.shape[1]
    capacity = rows * 8 // (3 * total)
    first, second = routes[0:1, :], routes[1:2, :]
    ids = lax.rem(
        lax.broadcasted_iota(jnp.int32, (total, rows), 0) + me * local_count, total
    )
    named = (first == ids) | (second == ids)
    earlier = (
        lax.broadcasted_iota(jnp.int32, (rows, rows), 0)
        < lax.broadcasted_iota(jnp.int32, (rows, rows), 1)
    ).astype(F32).astype(BF)
    counts = mdot(named.astype(F32).astype(BF), earlier).astype(jnp.int32)
    places = jnp.where(named, counts, -1)
    weights = jnp.where(first == ids, gates[0:1, :], 0.0) + jnp.where(
        second == ids, gates[1:2, :], 0.0
    )
    slot = lax.broadcasted_iota(jnp.int32, (capacity, rows), 0)
    for i in range(total):
        yield i, slot == places[i : i + 1, :], weights[i : i + 1, :]


def ffn_chunk(x, g, weights, saved, sums, grads, tile):
    gate_w, up_w, down_w = weights
    act_s, d_gate_s, d_up_s = saved
    out_sum, in_sum = sums

    def forward(here):
        x_rows, g_rows = x[here, :], g[here, :]
        gate = mdot(x_rows, gate_w[...])
        up = mdot(x_rows, up_w[...])
        d_act = ndot(g_rows, down_w[...]).astype(BF).astype(F32)
        sigma = jax.nn.sigmoid(gate)
        silu = gate * sigma
        act = (silu * up).astype(BF)
        d_gate = (d_act * up * (sigma * (1.0 + gate * (1.0 - sigma)))).astype(BF)
        d_up = (d_act * silu).astype(BF)
        act_s[here, :] = act
        d_gate_s[here, :] = d_gate
        d_up_s[here, :] = d_up
        out_sum[here, :] += mdot(act, down_w[...])
        in_sum[here, :] += ndot(d_gate, gate_w[...]) + ndot(d_up, up_w[...])

    rows = x.shape[0]
    tiles(rows, tile, forward)
    used = pl.ds(0, rows)

    def weight_grads(here):
        grads[0][here, :] = tdot(x[:, here], d_gate_s[used, :]).astype(BF)
        grads[1][here, :] = tdot(x[:, here], d_up_s[used, :]).astype(BF)
        grads[2][:, here] = tdot(act_s[used, :], g[:, here]).astype(BF)

    tiles(x.shape[1], 256, weight_grads)


def forward_kernel(sizes, *refs):
    place = Place(sizes)
    depth, high_count = sizes
    owners = place.owners
    (
        tokens, cot, gates, routes, cosine, sine_part,
        qkv_in, out_in, gain_in, sg_in, su_in, sd_in, eg_in, eu_in, ed_in,
        qkv_o, out_o, gain_o, sg_o, su_o, sd_o, eg_o, eu_o, ed_o,
        n1_o, k_o, v_o, q_o, att_o, hid_o, lse_o, side_o, dn2_o,
        gsg_o, gsu_o, gsd_o, geg_o, geu_o, ged_o, outs_o, dins_o, pre_g, pre_u, pre_d,
        xk, wq, wo, gain_land, gain_v, g_all, n2, in_s, do_s, send_in, send_do,
        wg, wu, wd, act_s, dg_s, du_s, stage_g, stage_u, stage_d,
        *sems,
    ) = refs
    dense_sems, sems = sems[:6], sems[6:]
    expert_sems, sems = sems[:4], sems[4:]
    (
        line_send, line_recv, load_sem, ai_send, ai_recv, ad_send, ad_recv,
        chunk_sem, store_sem, out_sem, pre_send, pre_recv,
    ) = sems
    micro_count, rows, features = tokens.shape
    prompt = depth * PB
    length = prompt + CONT
    local_count, _, width = eg_in.shape
    total = owners * local_count
    capacity = rows * 8 // (3 * total)
    slots = in_s.shape[1]
    me = place.e

    def dense(i, own, slot):
        return DenseGather(place, own, slot, [s.at[i] for s in dense_sems])

    def rows_of(ref, count):
        return lambda s: ref.at[pl.ds(pl.multiple_of(s * count, 16), count)]

    def columns_of(ref, count):
        return lambda s: ref.at[:, pl.ds(pl.multiple_of(s * count, 128), count)]

    early = [
        dense(0, qkv_in, rows_of(wq, qkv_in.shape[0])),
        dense(1, out_in, rows_of(wo, out_in.shape[0])),
        dense(2, gain_in, rows_of(gain_land, gain_in.shape[0])),
    ]
    late = [
        dense(3, sg_in, columns_of(sg_o, sg_in.shape[1])),
        dense(4, su_in, columns_of(su_o, su_in.shape[1])),
        dense(5, sd_in, rows_of(sd_o, sd_in.shape[0])),
    ]
    experts = ExpertGather(place, (eg_in, eu_in, ed_in), (eg_o, eu_o, ed_o), expert_sems)
    own_prompt = pl.ds(pl.multiple_of(place.z * PB, PB), PB)
    prompts = [
        Line(
            place,
            tokens.at[m, pl.ds(0, PB)],
            lambda z, m=m: xk.at[m, pl.ds(pl.multiple_of(z * PB, PB), PB)],
            line_send.at[m],
            line_recv.at[m],
        )
        for m in range(micro_count)
    ]
    own_at = (place.z * high_count + place.high) * 2 + place.low
    loads = [
        (tokens.at[:, pl.ds(0, PB)], xk.at[:, own_prompt]),
        (tokens.at[:, pl.ds(PB, CONT)], xk.at[:, pl.ds(prompt, CONT)]),
    ]
    loads += [(cot.at[m], g_all.at[pl.ds(m * rows, rows)]) for m in range(micro_count)]
    loads += [(d.own, d.slot_of(own_at)) for d in early]
    bounce = [
        (sg_in, wg.at[0, :, pl.ds(0, sg_in.shape[1])], late[0].slot_of(own_at)),
        (su_in, wu.at[0, :, pl.ds(0, su_in.shape[1])], late[1].slot_of(own_at)),
        (sd_in, wd.at[0, pl.ds(0, sd_in.shape[0])], late[2].slot_of(own_at)),
    ]
    loads += [(source, middle) for source, middle, _ in bounce]
    load_copies = [
        pltpu.make_async_copy(source, target, load_sem.at[i])
        for i, (source, target) in enumerate(loads)
    ]
    bounce_copies = [
        pltpu.make_async_copy(middle, target, load_sem.at[i])
        for i, (_, middle, target) in enumerate(bounce)
    ]
    for copy in load_copies:
        copy.start()
    place.greet()
    for d in early:
        d.start()
    experts.start_x()
    for copy in load_copies:
        copy.wait()
    for copy in bounce_copies:
        copy.start()
    stores = []

    def store(source, target):
        copy = pltpu.make_async_copy(source, target, out_sem.at[len(stores)])
        copy.start()
        stores.append(copy)

    def slot_rows(m, sender):
        return pl.ds(pl.multiple_of((m * owners + sender) * capacity, 16), capacity)

    def exchange(buffer, land, send_sem, recv_sem, m, step):
        return remote(
            buffer.at[step - 1, m],
            land.at[:, slot_rows(m, me)],
            send_sem.at[step - 1, m],
            recv_sem.at[step - 1, m],
            experts=place.peer_owner(step),
        )

    def exchanged(land, recv_sem, m, step):
        sender = lax.rem(me - step + owners, owners)
        arrived(land.at[:, slot_rows(m, sender)], recv_sem.at[step - 1, m])

    def put(buffer, land, m, i, value):
        if i < local_count:
            land[i, slot_rows(m, me), :] = value
        else:
            buffer[i // local_count - 1, m, i % local_count] = value

    def expert_gradients(m):
        g_rows = g_all[pl.ds(m * rows, rows), :]
        for i, hit, weight in one_hots(routes.at[m], gates.at[m], me, local_count, total):
            gate = jnp.sum(jnp.where(hit, weight, 0.0), -1, keepdims=True)
            value = mdot(hit.astype(F32).astype(BF), g_rows)
            put(send_do, do_s, m, i, (gate * value).astype(BF))

    def early_hop(step):
        for d in early:
            d.hop(step)

    for step in range(depth - 2):
        if step < micro_count:
            expert_gradients(step)
        early_hop(step)
    for m in range(max(depth - 2, 0), micro_count):
        expert_gradients(m)
    prompts[0].start()
    early_hop(depth - 2)
    for m in range(micro_count):
        for step in range(1, owners):
            exchange(send_do, do_s, ad_send, ad_recv, m, step).start()
    prompts[0].hop(0)
    for z in range(depth):
        for d in early:
            d.cross(z)
    for step in range(1, depth - 1):
        prompts[0].hop(step)
        if step == 1:
            for prompt_line in prompts[1:]:
                prompt_line.start()
    for z in range(depth):
        for d in early:
            d.finish(z)
    store(wq, qkv_o)
    store(wo, out_o)
    shards = depth * owners
    gain_rows = gain_in.shape[0]
    gain_sum = jnp.zeros((8, features), F32)
    for s in range(shards):
        gain_sum += gain_land[pl.ds(s * gain_rows, gain_rows), :].astype(F32)[:8]
    gain_v[...] = gain_sum
    store(gain_v, gain_o)

    def own_rows(i):
        start = place.z * PB if i == 0 else prompt + (i - 1) * PB
        return start, pl.ds(start if i else pl.multiple_of(start, PB), PB)

    def front(n1, k, v, q, att, hid, lse):
        lse[...] = jnp.zeros_like(lse)
        pairs = features // (2 * HD)

        def prompt_hop(step):
            for prompt_line in prompts[1:]:
                prompt_line.hop(step)
            if step == depth - 2:
                experts.start_z()

        def project_all(m):
            def project(here):
                normed = norm_rows(xk[m, here, :].astype(F32), gain_v[0:1, :])
                n1[m, here, :] = normed
                key = ndot(normed, wq[pl.ds(features, features), :])
                k[m, here, :] = rope(key, cosine[here, :], sine_part[here, :]).astype(BF)
                v[m, here, :] = ndot(normed, wq[pl.ds(2 * features, features), :]).astype(BF)

            tiles(length, 256, project)
            for i in range(rows // PB):
                _, here = own_rows(i)
                query = ndot(n1[m, here, :], wq[pl.ds(0, features), :])
                query = rope(query, cosine[here, :], sine_part[here, :]).astype(BF)
                q[m, pl.ds(i * PB, PB), :] = query * jnp.asarray(HD**-0.5, BF)
        lane = lax.broadcasted_iota(jnp.int32, (PB, 2 * HD), 1)
        for m in range(micro_count):
            project_all(m)

            def pair(index, carry):
                if m == 0:
                    for step in range(depth - 1):
                        pl.when(index == min(step, pairs - 1))(lambda step=step: prompt_hop(step))
                lanes = pl.ds(pl.multiple_of(index * 2 * HD, 2 * HD), 2 * HD)
                for i in range(rows // PB):
                    here = pl.ds(i * PB, PB)
                    query = q[m, here, lanes]
                    seen = prompt + i * PB
                    keys, values = k[m, pl.ds(0, seen), lanes], v[m, pl.ds(0, seen), lanes]
                    column = lax.broadcasted_iota(jnp.int32, (PB, seen), 1)
                    row = lax.broadcasted_iota(jnp.int32, (PB, seen), 0)
                    allowed = column <= row + own_rows(i)[0]
                    parts = []
                    logs = lse[m, here, :]
                    for sub in range(2):
                        only = jnp.where(lane // HD == sub, query, jnp.zeros_like(query))
                        scores = jnp.where(allowed, ndot(only, keys), -1000000000.0)
                        highest = jnp.max(scores, -1, keepdims=True)
                        weights = jnp.exp(scores - highest)
                        sums = jnp.sum(weights, -1, keepdims=True)
                        parts.append(mdot((weights * (1.0 / sums)).astype(BF), values))
                        logs = jnp.where(lane == 2 * index + sub, highest + jnp.log(sums), logs)
                    lse[m, here, :] = logs
                    att[m, here, lanes] = jnp.where(lane < HD, parts[0], parts[1]).astype(BF)
                return carry

            lax.fori_loop(0, pairs, pair, 0)
            if m == 0:
                for copy in bounce_copies:
                    copy.wait()
                for d in late:
                    d.start()
            if m == micro_count - 1:
                experts.hop(0, 0)
                for d in late:
                    d.cross(place.z)
            for i in range(rows // PB):
                here = pl.ds(i * PB, PB)
                hidden = xk[m, own_rows(i)[1], :].astype(F32) + mdot(att[m, here, :], wo[...])
                hid[m, here, :] = hidden
                n2[pl.ds(m * rows + i * PB, PB), :] = norm_rows(hidden, gain_v[1:2, :])
            normed = n2[pl.ds(m * rows, rows), :]
            for i, hit, _ in one_hots(routes.at[m], gates.at[m], me, local_count, total):
                value = mdot(hit.astype(F32).astype(BF), normed)
                put(send_in, in_s, m, i, value.astype(BF))
            for step in range(1, owners):
                exchange(send_in, in_s, ai_send, ai_recv, m, step).start()
        store(n1, n1_o)
        store(k, k_o)
        store(v, v_o)
        store(q, q_o)
        store(att, att_o)
        store(hid, hid_o)
        store(lse, lse_o)
        for copy in stores:
            copy.wait()

    pl.run_scoped(
        front,
        pltpu.VMEM((micro_count, length, features), BF),
        pltpu.VMEM((micro_count, length, features), BF),
        pltpu.VMEM((micro_count, length, features), BF),
        pltpu.VMEM((micro_count, rows, features), BF),
        pltpu.VMEM((micro_count, rows, features), BF),
        pltpu.VMEM((micro_count, rows, features), F32),
        pltpu.VMEM((micro_count, rows, 2 * HD), F32),
    )
    saved = (act_s, dg_s, du_s)
    staged = (stage_g, stage_u, stage_d)

    def chunk_loads(sources, slot):
        return [
            pltpu.make_async_copy(source, buffer.at[slot], chunk_sem.at[slot, kind])
            for kind, (source, buffer) in enumerate(zip(sources, (wg, wu, wd)))
        ]

    def chunk_stores(targets, slot):
        return [
            pltpu.make_async_copy(buffer.at[slot], target, store_sem.at[slot, kind])
            for kind, (target, buffer) in enumerate(zip(targets, staged))
        ]

    def wait_rows():
        for m in range(micro_count):
            for step in range(1, owners):
                exchanged(in_s, ai_recv, m, step)
                exchanged(do_s, ad_recv, m, step)

    at_end = (place.z == 0) | (place.z == depth - 1)
    beside_end = (place.z == 1) | (place.z == depth - 2)

    def sums_to_neighbour(which):
        z = jnp.where(place.z == 0, 1, depth - 2)
        return [
            remote(
                expert_slab(
                    ref, kind, local, (place.other_shard if crossed else place.shard)(z), width
                ),
                land.at[crossed, local],
                pre_send.at[crossed, local, kind],
                pre_recv.at[crossed, local, kind],
                context=z,
            )
            for crossed in which
            for local in range(local_count)
            for kind, (ref, land) in enumerate(
                ((geg_o, pre_g), (geu_o, pre_u), (ged_o, pre_d))
            )
        ]

    def send_sums(crossed):
        def body():
            for copy in sums_to_neighbour((crossed,)):
                copy.start()

        pl.when(at_end)(body)

    def sums_sent():
        for copy in sums_to_neighbour((0, 1)):
            copy.wait_send()

    def sums_arrived():
        for crossed in (1, 0):
            for local in range(local_count):
                for kind, land in enumerate((pre_g, pre_u, pre_d)):
                    arrived(land.at[crossed, local], pre_recv.at[crossed, local, kind])

    def returns(local):
        return [
            pltpu.make_async_copy(source.at[local], target.at[local], out_sem.at[2 + 2 * local + i])
            for i, (source, target) in enumerate(((in_s, outs_o), (do_s, dins_o)))
        ]

    def both(out_sum, in_sum, side_sum, normed_sum):
        out_sum[...] = jnp.zeros_like(out_sum)
        in_sum[...] = jnp.zeros_like(in_sum)
        side_sum[...] = jnp.zeros_like(side_sum)
        normed_sum[...] = jnp.zeros_like(normed_sum)
        group = late[0].own.shape[1] * owners // width

        def store_grads(targets, slot, stored):
            def previous():
                for copy in chunk_stores(targets, slot):
                    copy.wait()

            pl.when(stored)(previous)
            return lambda: [copy.start() for copy in chunk_stores(targets, slot)]

        def shared_part(refs, c):
            here = pl.ds(pl.multiple_of(c * width, 128), width)
            return [refs[0].at[:, here], refs[1].at[:, here], refs[2].at[here]]

        def shared_item(w, z):
            for d in late:
                d.finish(z)

            def one(i, carry):
                c = z * group + i
                loads = chunk_loads(shared_part((sg_o, su_o, sd_o), c), 2 * local_count + i)
                for copy in loads:
                    copy.wait()
                send = store_grads(shared_part((gsg_o, gsu_o, gsd_o), c), i, w > 0)
                ffn_chunk(
                    n2,
                    g_all,
                    [buffer.at[2 * local_count + i] for buffer in (wg, wu, wd)],
                    saved,
                    (side_sum, normed_sum),
                    [buffer.at[i] for buffer in staged],
                    micro_count * rows,
                )
                send()
                return carry

            for i in range(group):
                for copy in chunk_loads(
                    shared_part((sg_o, su_o, sd_o), z * group + i), 2 * local_count + i
                ):
                    copy.start()
            lax.fori_loop(0, group, one, 0)

        def expert_item(w, z, crossed, local, side, ahead):
            shard = jnp.where(crossed, place.other_shard(z), place.shard(z))

            def load(n):
                sources = [
                    expert_slab(ref, k, n, shard, width) for k, ref in enumerate((eg_o, eu_o, ed_o))
                ]
                return chunk_loads(sources, side * local_count + n)

            def begin(n):
                def own():
                    mine = [ref.at[n] for ref in (eg_in, eu_in, ed_in)]
                    for copy in chunk_loads(mine, side * local_count + n):
                        copy.start()

                def landed():
                    pl.when(crossed)(lambda: experts.wait_x(n, z))
                    for copy in load(n):
                        copy.start()

                pl.when(w == 1)(own)
                pl.when(w > 1)(landed)

            def begin_rest():
                for n in range(1, local_count):
                    begin(n)

            pl.when(w == 1)(wait_rows)
            pl.when(local == 0)(lambda: begin(0))
            pl.when(ahead & (local == 0))(begin_rest)
            pl.when(jnp.logical_not(ahead) & (local > 0))(lambda: begin(local))
            for copy in load(local):
                copy.wait()
            targets = [
                expert_slab(ref, k, local, shard, width) for k, ref in enumerate((geg_o, geu_o, ged_o))
            ]
            send = store_grads(targets, local, True)
            ffn_chunk(
                in_s.at[local],
                do_s.at[local],
                [buffer.at[side * local_count + local] for buffer in (wg, wu, wd)],
                saved,
                (out_sum.at[local], in_sum.at[local]),
                [buffer.at[local] for buffer in staged],
                slots,
            )
            send()

        def crossing(step):
            for d in late:
                for z in (place.z - 1 - step, place.z + 1 + step):
                    pl.when(place.on_line(z))(lambda d=d, z=z: d.cross(z))

        def late_hop(step):
            for d in late:
                d.hop(step)

        heads = 2 * local_count + 1
        in_step = 2 * heads
        after_item = [(local, lambda local=local: experts.hop(local, 0)) for local in range(1, local_count)]
        after_item = [(local - 1, run) for local, run in after_item]
        after_item += [(local_count, lambda: late_hop(0)), (heads - 1, lambda: crossing(0))]
        for step in range(1, depth - 1):
            here = heads + in_step * step
            late_spot, cross_spot = here + 3, here + 5
            if step == depth - 2:
                before = here - in_step
                spots = [(0, before + 3), (0, before + 5), (0, before + 7)]
                spots += [(local, here - 1) for local in range(1, local_count)]
                spots += [(local, here + 1) for local in range(1, local_count)] * 2
                late_spot, cross_spot = here + 5, here + 7
                kinds = {}
                for local, at in spots:
                    kind = kinds.get(local, 0)
                    kinds[local] = kind + 1
                    after_item.append(
                        (at, lambda p=(local, step, (kind,)): experts.hop(*p))
                    )
            else:
                if step == 1:
                    spots = [heads + 3, jnp.where(at_end, here - 1, heads + 5)]
                    late_spot = jnp.where(at_end, here + 3, heads + 7)
                else:
                    spots = [here - 3, here - 1]
                for local in range(local_count):
                    at = spots[min(local, 1)]
                    after_item.append((at, lambda p=(local, step): experts.hop(*p)))
            after_item.append((late_spot, lambda step=step: late_hop(step)))
            after_item.append((cross_spot, lambda step=step: crossing(step)))
        after_item.append((heads + in_step - 3, lambda: send_sums(0)))
        after_item.append((heads + in_step - 1, lambda: send_sums(1)))
        count = heads + in_step * (depth - 1)

        def finish(local):
            def convert(here):
                in_s[local, here, :] = out_sum[local, here, :].astype(BF)
                do_s[local, here, :] = in_sum[local, here, :].astype(BF)

            tiles(slots, 256, convert)
            for copy in returns(local):
                copy.start()

        def side_sums():
            return [
                pltpu.make_async_copy(side_sum, side_o, out_sem.at[0]),
                pltpu.make_async_copy(normed_sum, dn2_o, out_sem.at[1]),
            ]

        def finish_routed():
            for local in range(local_count):
                finish(local)

        def early_drain():
            for line in prompts:
                line.drain()
            for d in early:
                d.drain()
            for m in range(micro_count):
                for step in range(1, owners):
                    exchange(send_do, do_s, ad_send, ad_recv, m, step).wait_send()
                    exchange(send_in, in_s, ai_send, ai_recv, m, step).wait_send()

        after_item.append((count - in_step, early_drain))
        after_item.append((count - 3, finish_routed))

        def item(w, carry):
            head = w < heads
            after = jnp.maximum(w - heads, 0)
            step, spot = after // in_step, lax.rem(after, in_step)
            kind = jnp.where(head, w - 1, spot // 2)
            is_shared = kind == jnp.where(head, -1, 2 * local_count)
            crossed = kind >= local_count
            local = jnp.clip(jnp.where(crossed, kind - local_count, kind), 0, local_count - 1)
            z = jnp.where(head, place.z, place.z + (2 * lax.rem(spot, 2) - 1) * (1 + step))
            valid = place.on_line(z)
            pl.when(valid & is_shared)(lambda: shared_item(w, z))
            ahead = head | (step < depth - 2)
            side = jnp.where(head, 0, lax.rem(spot, 2))
            pl.when(valid & jnp.logical_not(is_shared))(
                lambda: expert_item(w, z, crossed, local, side, ahead)
            )
            for at, run in after_item:
                pl.when(w == at)(run)
            return carry

        lax.fori_loop(0, count, item, 0)
        for copy in side_sums():
            copy.start()
        for local in range(local_count):
            targets = [expert_slab(ref, k, local, 0, width) for k, ref in enumerate((geg_o, geu_o, ged_o))]
            for copy in chunk_stores(targets, local):
                copy.wait()
        for copy in side_sums():
            copy.wait()

    pl.run_scoped(
        both,
        pltpu.VMEM((local_count, slots, features), F32),
        pltpu.VMEM((local_count, slots, features), F32),
        pltpu.VMEM((micro_count * rows, features), F32),
        pltpu.VMEM((micro_count * rows, features), F32),
    )
    for local in range(local_count):
        for copy in returns(local):
            copy.wait()
    pl.when(beside_end)(sums_arrived)
    pl.when(at_end)(sums_sent)
    for d in late:
        d.drain()
    experts.drain()


def rope_tables(prompt):
    positions = np.arange(prompt + CONT, dtype=np.float64)
    frequency = 10000.0 ** (-2.0 * np.arange(HD // 2) / HD)
    angles = positions[:, None] * frequency
    cosine, sine_part = np.cos(angles), np.sin(angles)
    return (
        np.concatenate([cosine] * 4, 1).astype(np.float32),
        np.concatenate([-sine_part, sine_part] * 2, 1).astype(np.float32),
    )


def run_forward(sizes, tokens, cot, gates, routes, dense, experts):
    depth, high_count = sizes
    micro_count, rows, features = tokens.shape
    owners = high_count * 2
    line = depth * owners
    prompt = depth * PB
    length = prompt + CONT
    local_count, _, width = experts[0].shape
    hidden_units = dense[3].shape[1] * line
    capacity = rows * 8 // (3 * owners * local_count)
    slots = micro_count * owners * capacity
    cosine, sine_part = rope_tables(prompt)
    hbm, vmem = pl.BlockSpec(memory_space=pltpu.HBM), pl.BlockSpec(memory_space=pltpu.VMEM)

    def shape(dtype, *dims):
        return jax.ShapeDtypeStruct(dims, dtype)

    token_rows = micro_count * rows
    wide, tall = (features, hidden_units), (hidden_units, features)
    out_shape = [
        shape(BF, dense[0].shape[0] * line, features),
        shape(BF, dense[1].shape[0] * line, features),
        shape(F32, 8, features),
        shape(BF, *wide), shape(BF, *wide), shape(BF, *tall),
        shape(BF, local_count, *wide), shape(BF, local_count, *wide), shape(BF, local_count, *tall),
        shape(BF, micro_count, length, features),
        shape(BF, micro_count, length, features),
        shape(BF, micro_count, length, features),
        shape(BF, micro_count, rows, features),
        shape(BF, micro_count, rows, features),
        shape(F32, micro_count, rows, features),
        shape(F32, micro_count, rows, 2 * HD),
        shape(F32, token_rows, features),
        shape(F32, token_rows, features),
        shape(BF, *wide), shape(BF, *wide), shape(BF, *tall),
        shape(BF, local_count, *wide), shape(BF, local_count, *wide), shape(BF, local_count, *tall),
        shape(BF, local_count, slots, features),
        shape(BF, local_count, slots, features),
        shape(BF, 2, local_count, features, width),
        shape(BF, 2, local_count, features, width),
        shape(BF, 2, local_count, width, features),
    ]
    dma = pltpu.SemaphoreType.DMA
    buffers = max(2, local_count)
    loads = 2 * local_count + 2
    send = pltpu.VMEM((owners - 1, micro_count, local_count, capacity, features), BF)
    scratch = [
        pltpu.VMEM((micro_count, length, features), BF),
        pltpu.VMEM(out_shape[0].shape, BF),
        pltpu.VMEM(out_shape[1].shape, BF),
        pltpu.VMEM((dense[2].shape[0] * line, features), BF),
        pltpu.VMEM((8, features), F32),
        pltpu.VMEM((token_rows, features), BF),
        pltpu.VMEM((token_rows, features), BF),
        pltpu.VMEM((local_count, slots, features), BF),
        pltpu.VMEM((local_count, slots, features), BF),
        send,
        send,
        pltpu.VMEM((loads, features, width), BF),
        pltpu.VMEM((loads, features, width), BF),
        pltpu.VMEM((loads, width, features), BF),
        pltpu.VMEM((max(slots, token_rows), width), BF),
        pltpu.VMEM((max(slots, token_rows), width), BF),
        pltpu.VMEM((max(slots, token_rows), width), BF),
        pltpu.VMEM((buffers, features, width), BF),
        pltpu.VMEM((buffers, features, width), BF),
        pltpu.VMEM((buffers, width, features), BF),
    ]
    scratch += DenseGather.semaphores(len(dense), depth, high_count)
    scratch += ExpertGather.semaphores(depth, local_count)
    scratch += [
        dma((micro_count, 2, depth)),
        dma((micro_count, depth)),
        dma((10 + micro_count,)),
        dma((owners - 1, micro_count)),
        dma((owners - 1, micro_count)),
        dma((owners - 1, micro_count)),
        dma((owners - 1, micro_count)),
        dma((loads, 3)),
        dma((buffers, 3)),
        dma((12 + 2 * local_count,)),
        dma((2, local_count, 3)),
        dma((2, local_count, 3)),
    ]
    return pl.pallas_call(
        functools.partial(forward_kernel, sizes),
        out_shape=out_shape,
        in_specs=[hbm] * 2 + [vmem] * 4 + [hbm] * 9,
        out_specs=[hbm] * len(out_shape),
        scratch_shapes=scratch,
        compiler_params=pltpu.CompilerParams(
            collective_id=0, has_side_effects=True, vmem_limit_bytes=60 * MIB
        ),
        name="gather_and_forward",
    )(tokens, cot, gates, routes, cosine, sine_part, *dense, *experts)


def add_into(target, sources, step):
    def body(here):
        value = target[here, :].astype(F32)
        for source in sources:
            value = value + source[here, :].astype(F32)
        target[here, :] = value.astype(target.dtype)

    tiles(target.shape[0], step, body)


class LineSum:
    def __init__(self, place, part, land, send_sem, recv_sem):
        self.place, self.part, self.land = place, part, land
        self.send_sem, self.recv_sem = send_sem, recv_sem

    def copy(self, z, direction):
        place = self.place
        slot = z if direction > 0 else jnp.where(z == place.z - 1, place.depth, z)
        return remote(
            self.part(z),
            self.land(slot),
            self.send_sem.at[z],
            self.recv_sem.at[slot],
            context=place.z + direction,
        )

    def upstream(self, direction):
        return self.place.z > 0 if direction > 0 else self.place.z < self.place.depth - 1

    def arrive(self, slot):
        arrived(self.land(slot), self.recv_sem.at[slot])

    def at(self, direction, step, body):
        z = self.place.z + direction * step
        pl.when(self.place.on_line(z))(lambda: body(z))

    def pass_on(self, direction, step, add):
        def body(z):
            def more():
                self.arrive(z)
                add(self.part(z), self.land(z))

            pl.when(self.upstream(direction))(more)
            self.copy(z, direction).start()

        self.at(direction, step, body)

    def end(self, add):
        for direction, slot in ((1, self.place.z), (-1, self.place.depth)):

            def body(slot=slot):
                self.arrive(slot)
                add(self.part(self.place.z), self.land(slot))

            pl.when(self.upstream(direction))(body)

    def drain(self):
        for step in range(1, self.place.depth):
            for direction in (1, -1):
                self.at(direction, step, lambda z, d=direction: self.copy(z, d).wait_send())


class DenseScatter:
    def __init__(self, place, source, low, high, line, cross, spare, out, sems):
        self.place, self.source, self.spare, self.out = place, source, spare, out
        self.low, self.high, self.cross = low, high, cross
        (
            self.l_send, self.l_recv, self.h_send, self.h_recv, z_send, z_recv,
            self.x_send, self.x_recv, self.own_sem,
        ) = sems
        self.step = min(64, low.shape[2]) if low.shape[2] % 64 == 0 else 16
        self.line = LineSum(
            place, lambda z: low.at[z, place.high], lambda slot: line.at[slot], z_send, z_recv
        )

    @staticmethod
    def semaphores(count, depth, high_count):
        dma = pltpu.SemaphoreType.DMA
        cross = dma((count, depth, high_count))
        return [
            cross, cross, dma((count, high_count)), dma((count, high_count)),
            dma((count, depth + 1)), dma((count, depth + 1)),
            dma((count,)), dma((count,)), dma((count, 2)),
        ]

    def _index(self, z, high, low):
        return (z * self.place.high_count + high) * 2 + low

    def _to_low(self, z, high):
        place = self.place
        return remote(
            self.source(self._index(z, high, 1 - place.low)),
            self.low.at[z, high],
            self.l_send.at[z, high],
            self.l_recv.at[z, high],
            experts=place.e + 1 - 2 * place.low,
        )

    def _each(self, body):
        for z in range(self.place.depth):
            for high in range(self.place.high_count):
                body(z, high)

    def start(self):
        self._each(lambda z, high: self._to_low(z, high).start())

    def add_low(self):
        place = self.place
        places = [(z, high) for z in range(place.depth) for high in range(place.high_count)]

        def load(i):
            z, high = places[i]
            return pltpu.make_async_copy(
                self.source(self._index(z, high, place.low)),
                self.spare.at[i % 2],
                self.own_sem.at[i % 2],
            )

        if self.spare is not None:
            load(0).start()
        for i, (z, high) in enumerate(places):
            self._to_low(z, high).wait_recv()
            if self.spare is None:
                own = self.source(self._index(z, high, place.low))
            else:
                if i + 1 < len(places):
                    load(i + 1).start()
                load(i).wait()
                own = self.spare.at[i % 2]
            add_into(self.low.at[z, high], [own], self.step)
        for step in range(1, place.high_count):
            self._to_high(step).start()

    def _to_high(self, step):
        place = self.place
        peer = place.peer_high(step)
        return remote(
            self.low.at[:, peer],
            self.high.at[step - 1],
            self.h_send.at[step],
            self.h_recv.at[step],
            experts=peer * 2 + place.low,
        )

    def add_high(self):
        place = self.place
        for step in range(1, place.high_count):
            self._to_high(step).wait_recv()
        for z in range(place.depth):
            add_into(
                self.low.at[z, place.high],
                [self.high.at[step - 1, z] for step in range(1, place.high_count)],
                self.step,
            )

    def _add(self, target, more):
        add_into(target, [more], self.step)

    def pass_on(self, direction, step):
        self.line.pass_on(direction, step, self._add)

    def _across(self):
        place = self.place
        return remote(
            self.low.at[place.z, place.high], self.cross, self.x_send, self.x_recv, dp=1 - place.x
        )

    def end(self):
        self.line.end(self._add)
        self._across().start()

    def _store(self):
        return pltpu.make_async_copy(self.cross, self.out, self.own_sem.at[0])

    def finish(self):
        self._across().wait_recv()
        self._add(self.cross, self.low.at[self.place.z, self.place.high])
        self._store().start()

    def drain_first(self):
        self._each(lambda z, high: self._to_low(z, high).wait_send())
        for step in range(1, self.place.high_count):
            self._to_high(step).wait_send()

    def drain(self):
        self.line.drain()
        self._across().wait_send()
        self._store().wait()


class ExpertScatter:
    def __init__(self, place, sums, cross, land, own, more, early, absorbed, outs, sems):
        self.early, self.absorbed = early, absorbed
        self.at_end = (place.z == 0) | (place.z == place.depth - 1)
        self.beside_end = (place.z == 1) | (place.z == place.depth - 2)
        self.place, self.sums, self.cross, self.land = place, sums, cross, land
        self.own, self.more, self.outs = own, more, outs
        self.x_send, self.x_recv, self.z_send, self.z_recv, self.load_sem, self.out_sem = sems
        self.local_count, self.width = cross[0].shape[1], cross[0].shape[3]

    @staticmethod
    def semaphores(depth, local_count):
        dma = pltpu.SemaphoreType.DMA
        return [
            dma((local_count, 3, depth)),
            dma((local_count, 3, depth)),
            dma((local_count, 3, depth + 1)),
            dma((local_count, 3, depth + 1)),
            dma((3, 3)),
            dma((local_count, 3)),
        ]

    def _line(self, local, kind):
        return LineSum(
            self.place,
            lambda z: self.cross[kind].at[z, local],
            lambda slot: self.land[kind].at[slot, local],
            self.z_send.at[local, kind],
            self.z_recv.at[local, kind],
        )

    def _across(self, local, kind, z):
        return remote(
            expert_slab(self.sums[kind], kind, local, self.place.other_shard(z), self.width),
            self.cross[kind].at[z, local],
            self.x_send.at[local, kind, z],
            self.x_recv.at[local, kind, z],
            dp=1 - self.place.x,
        )

    def _order(self, body):
        place = self.place
        for step in range(place.depth - 1, 0, -1):
            for direction in (1, -1):
                z = place.z + direction * step
                here = place.on_line(z)
                if step == 1:
                    here = here & jnp.logical_not(self.at_end)
                pl.when(here)(lambda z=z: body(z))

    def start(self):
        def body(z):
            for local in range(self.local_count):
                for kind in range(3):
                    self._across(local, kind, z).start()

        self._order(body)
        pl.when(jnp.logical_not(self.beside_end))(lambda: body(self.place.z))

    def absorb(self):
        z = self.place.z

        def body():
            for local in range(self.local_count):
                loads = []
                for kind in range(3):
                    source = expert_slab(
                        self.sums[kind], kind, local, self.place.other_shard(z), self.width
                    )
                    early = self.early[kind].at[1, local]
                    loads.append(
                        [
                            pltpu.make_async_copy(source, self.own[kind], self.load_sem.at[0, kind]),
                            pltpu.make_async_copy(
                                early, self.more[kind].at[0], self.load_sem.at[1, kind]
                            ),
                        ]
                    )
                stores = [
                    pltpu.make_async_copy(
                        self.own[kind], self.absorbed[kind].at[local], self.load_sem.at[0, kind]
                    )
                    for kind in range(3)
                ]
                for pair in loads:
                    for copy in pair:
                        copy.start()
                for kind in range(3):
                    for copy in loads[kind]:
                        copy.wait()
                    add_into(self.own[kind], [self.more[kind].at[0]], 64)
                    stores[kind].start()
                for kind in range(3):
                    stores[kind].wait()
                    remote(
                        self.absorbed[kind].at[local],
                        self.cross[kind].at[z, local],
                        self.x_send.at[local, kind, z],
                        self.x_recv.at[local, kind, z],
                        dp=1 - self.place.x,
                    ).start()

        pl.when(self.beside_end)(body)

    def _own_load(self, local, kind, z):
        return pltpu.make_async_copy(
            expert_slab(self.sums[kind], kind, local, self.place.shard(z), self.width),
            self.own[kind],
            self.load_sem.at[0, kind],
        )

    def _more_load(self, local, kind, slot, which):
        return pltpu.make_async_copy(
            self.land[kind].at[slot, local], self.more[kind].at[which], self.load_sem.at[1 + which, kind]
        )

    def pass_on(self, direction, step, local, kinds=(0, 1, 2)):
        def body(z):
            for kind in kinds:
                self._own_load(local, kind, z).start()
            for kind in kinds:
                line = self._line(local, kind)
                target = self.cross[kind].at[z, local]

                def come(line=line, kind=kind):
                    line.arrive(z)
                    self._more_load(local, kind, z, 0).start()

                pl.when(line.upstream(direction))(come)
                self._across(local, kind, z).wait_recv()
                self._own_load(local, kind, z).wait()

                def both(target=target, kind=kind):
                    self._more_load(local, kind, z, 0).wait()
                    add_into(target, [self.own[kind], self.more[kind].at[0]], 64)

                def single(target=target, kind=kind):
                    add_into(target, [self.own[kind]], 64)

                pl.when(line.upstream(direction))(both)
                pl.when(jnp.logical_not(line.upstream(direction)))(single)
                line.copy(z, direction).start()

        def there(z):
            if step == 1:
                pl.when(jnp.logical_not(self.at_end))(lambda: body(z))
            else:
                body(z)

        self._line(local, 0).at(direction, step, there)

    def _early_load(self, local, kind, which):
        return pltpu.make_async_copy(
            self.early[kind].at[0, local], self.more[kind].at[which], self.load_sem.at[1 + which, kind]
        )

    def end(self, local):
        place = self.place
        z = place.z
        for kind in range(3):
            self._own_load(local, kind, z).start()
        for kind in range(3):
            line = self._line(local, kind)
            target = self.cross[kind].at[z, local]
            for which, (direction, slot) in enumerate(((1, z), (-1, place.depth))):

                def come(slot=slot, which=which, line=line, kind=kind):
                    line.arrive(slot)
                    self._more_load(local, kind, slot, which).start()

                def came(which=which, kind=kind):
                    self._early_load(local, kind, which).start()

                from_end = z - direction == (0 if direction > 0 else place.depth - 1)
                pl.when(line.upstream(direction) & jnp.logical_not(from_end))(come)
                pl.when(from_end)(came)
            self._across(local, kind, z).wait_recv()
            self._own_load(local, kind, z).wait()
            add_into(target, [self.own[kind]], 64)
            for which, (direction, slot) in enumerate(((1, z), (-1, place.depth))):

                def more(slot=slot, which=which, kind=kind, target=target):
                    self._more_load(local, kind, slot, which).wait()
                    add_into(target, [self.more[kind].at[which]], 64)

                pl.when(line.upstream(direction))(more)
            self._store(local, kind).start()

    def _store(self, local, kind):
        return pltpu.make_async_copy(
            self.cross[kind].at[self.place.z, local],
            self.outs[kind].at[local],
            self.out_sem.at[local, kind],
        )

    def drain(self):
        for local in range(self.local_count):
            for kind in range(3):
                self._order(lambda z, p=(local, kind): self._across(*p, z).wait_send())
                self._across(local, kind, self.place.z).wait_send()
                line = self._line(local, kind)
                for step in range(1, self.place.depth):
                    for direction in (1, -1):

                        def sent(z, line=line, direction=direction):
                            line.copy(z, direction).wait_send()

                        def there(z, step=step, sent=sent):
                            if step == 1:
                                pl.when(jnp.logical_not(self.at_end))(lambda: sent(z))
                            else:
                                sent(z)

                        line.at(direction, step, there)
                self._store(local, kind).wait()


def backward_kernel(sizes, *refs):
    place = Place(sizes)
    depth, high_count = sizes
    owners = place.owners
    (
        tokens, cot, gates, routes, gate_rows, cosine, sine_part,
        qkv_w, out_w, gain_v, n1_i, k_i, v_i, q_i, att_i, hid_i, lse_i, side_i, dn2_i,
        gsg, gsu, gsd, geg, geu, ged, outs_i, dins_i, pre_g, pre_u, pre_d,
        mixed_o, input_o, gqkv_o, gout_o, gsg_o, gsu_o, gsd_o, geg_o, geu_o, ged_o, gain_o,
        eland_g, eland_u, eland_d, ret_in, ret_out, d_hidden_o, dn1_o, abs_g, abs_u, abs_d,
        *rest,
    ) = refs
    count = 5
    low, rest = rest[:count], rest[count:]
    high, rest = rest[:count], rest[count:]
    line, rest = rest[:count], rest[count:]
    cross, rest = rest[:count], rest[count:]
    (
        spare_w, spare_t, ecross_g, ecross_u, ecross_d, eown_g, eown_u, eown_d,
        emore_g, emore_u, emore_d,
        d_att, dpq, dpk, dpv, g_qkv, g_out, part, part_land,
        gain_own, gain_low, gain_high, gain_line, gain_cross, out_rows,
        *sems,
    ) = rest
    dense_sems, sems = sems[:9], sems[9:]
    expert_sems, sems = sems[:6], sems[6:]
    (
        part_send, part_recv, ri_send, ri_recv, ro_send, ro_recv,
        gain_send, gain_recv, load_sem, wq_sem, out_sem,
    ) = sems
    micro_count, rows, features = tokens.shape
    prompt = depth * PB
    length = prompt + CONT
    local_count, slots = outs_i.shape[0], outs_i.shape[1]
    total = owners * local_count
    capacity = rows * 8 // (3 * total)
    me = place.e

    def rows_of(ref, size):
        return lambda s: ref.at[pl.ds(pl.multiple_of(s * size, 16), size)]

    def columns_of(ref, size):
        return lambda s: ref.at[:, pl.ds(pl.multiple_of(s * size, 128), size)]

    sources = [
        columns_of(gsg, gsg_o.shape[1]),
        columns_of(gsu, gsu_o.shape[1]),
        rows_of(gsd, gsd_o.shape[0]),
        rows_of(g_qkv, gqkv_o.shape[0]),
        rows_of(g_out, gout_o.shape[0]),
    ]
    spares = [spare_w, spare_w, spare_t, None, None]
    dense = [
        DenseScatter(
            place, sources[i], low[i], high[i], line[i], cross[i], spares[i], out,
            [s.at[i] for s in dense_sems],
        )
        for i, out in enumerate((gsg_o, gsu_o, gsd_o, gqkv_o, gout_o))
    ]
    early, late = dense[:3], dense[3:]
    experts = ExpertScatter(
        place,
        (geg, geu, ged),
        (ecross_g, ecross_u, ecross_d),
        (eland_g, eland_u, eland_d),
        (eown_g, eown_u, eown_d),
        (emore_g, emore_u, emore_d),
        (pre_g, pre_u, pre_d),
        (abs_g, abs_u, abs_d),
        (geg_o, geu_o, ged_o),
        expert_sems,
    )
    prompts = [
        LineSum(
            place,
            lambda z, m=m: part.at[m, z],
            lambda slot, m=m: part_land.at[m, slot],
            part_send.at[m],
            part_recv.at[m],
        )
        for m in range(micro_count)
    ]

    def slot_rows(m, owner_of_rows):
        return pl.ds(pl.multiple_of((m * owners + owner_of_rows) * capacity, 16), capacity)

    def hand_back(source, land, send_sem, recv_sem, m, step):
        peer = place.peer_owner(step)
        return remote(
            source.at[:, slot_rows(m, peer)],
            land.at[m, owners - step],
            send_sem.at[step, m],
            recv_sem.at[owners - step, m],
            experts=peer,
        )

    returns = [(dins_i, ret_in, ri_send, ri_recv), (outs_i, ret_out, ro_send, ro_recv)]
    place.greet()
    for m in range(micro_count):
        for step in range(1, owners):
            hand_back(*returns[0], m, step).start()
    for d in early:
        d.start()
    experts.start()

    def fetch(pairs):
        copies = [
            pltpu.make_async_copy(source, target, load_sem.at[i])
            for i, (source, target) in enumerate(pairs)
        ]
        for copy in copies:
            copy.start()
        for copy in copies:
            copy.wait()

    def fetch_returned(source, land, recv_sem, target, m):
        for step in range(1, owners):
            arrived(land.at[m, step], recv_sem.at[step, m])
        pairs = []
        for step in range(owners):
            for local in range(local_count):
                at = pl.ds((step * local_count + local) * capacity, capacity)
                if step == 0:
                    piece = source.at[local, slot_rows(m, me)]
                else:
                    piece = land.at[m, step, local]
                pairs.append((piece, target.at[at]))
        fetch(pairs)

    for kind, d in enumerate(early):
        for direction in (1, -1):
            experts.pass_on(direction, depth - 1, 0, (kind,))
        d.add_low()
    for m in range(micro_count):
        for step in range(1, owners):
            hand_back(*returns[1], m, step).start()
    experts.absorb()
    gain_own[...] = jnp.zeros_like(gain_own)

    def mark_pairs(first, second, m):
        for i, hit, _ in one_hots(routes.at[m], gates.at[m], me, local_count, total):
            here = pl.ds(i * capacity, capacity)
            expert = lax.rem(me * local_count + i, total)
            hit_first = either(hit, routes[m, 0:1, :] == expert)
            hit_second = either(hit, routes[m, 1:2, :] == expert)
            first[here, :] = hit_first.astype(F32).astype(BF)
            second[here, :] = hit_second.astype(F32).astype(BF)

    def after_experts(hidden, extra, back, first, second, g_rows, att, d_attn, wo):
        fetch([(out_w, wo)] + [(att_i.at[m], att.at[pl.ds(m * rows, rows)]) for m in range(micro_count)])
        for m in range(micro_count):
            fetch([(hid_i.at[m], hidden), (cot.at[m], g_rows), (dn2_i.at[pl.ds(m * rows, rows)], extra)])
            mark_pairs(first, second, m)
            fetch_returned(dins_i, ret_in, ri_recv, back, m)
            gain = gain_v[1:2, :]
            for i in range(rows // PB):
                here = pl.ds(i * PB, PB)
                both = first[:, here] + second[:, here]
                d_normed = extra[here, :] + tdot(both, back[...])
                values = hidden[here, :]
                root = lax.rsqrt(jnp.mean(values * values, -1, keepdims=True) + EPSILON)
                scaled = gain * d_normed
                d_values = (
                    g_rows[here, :].astype(F32)
                    + root * scaled
                    - values * (root * root * root) * jnp.mean(values * scaled, -1, keepdims=True)
                )
                gain_own[1:2, :] += jnp.sum(d_normed * values * root, 0, keepdims=True)
                there = pl.ds(m * rows + i * PB, PB)
                extra[here, :] = d_values
                low_part = d_values.astype(BF)
                d_attn[there, :] = low_part
                d_att[there, :] = ndot(low_part, wo[...]).astype(BF)
            fetch([(extra, d_hidden_o.at[m])])
            for kind in ((0,), (1, 2))[m] if m < 2 else ():
                for direction in (1, -1):
                    experts.pass_on(direction, depth - 1, 1, (kind,))

        def out_grad(here):
            g_out[here, :] = tdot(att[:, here], d_attn[...]).astype(BF)

        tiles(features, 256, out_grad)

    pl.run_scoped(
        after_experts,
        pltpu.VMEM((rows, features), F32),
        pltpu.VMEM((rows, features), F32),
        pltpu.VMEM((total * capacity, features), BF),
        pltpu.VMEM((total * capacity, rows), BF),
        pltpu.VMEM((total * capacity, rows), BF),
        pltpu.VMEM((rows, features), BF),
        pltpu.VMEM((micro_count * rows, features), BF),
        pltpu.VMEM((micro_count * rows, features), BF),
        pltpu.VMEM((features, features), BF),
    )

    def both_ways(items, step):
        for direction in (1, -1):
            for item in items:
                item.pass_on(direction, step)

    def prompts_on(m, step):
        for direction in (1, -1):
            prompts[m].pass_on(direction, step, lambda t, s: add_into(t, [s], 64))

    def experts_on(step, local, where=True):
        def body():
            for direction in (1, -1):
                experts.pass_on(direction, step, local)

        pl.when(where)(body)

    inside = jnp.logical_not(experts.at_end)
    experts_on(depth - 2, 0, inside)

    def own_rows(i):
        start = place.z * PB if i == 0 else prompt + (i - 1) * PB
        return start, pl.ds(start if i else pl.multiple_of(start, PB), PB)

    def attention(k, v, q, lse, ds_s, p_s, wq, dn1):
        load_wq = pltpu.make_async_copy(qkv_w, wq, wq_sem.at[0])
        load_wq.start()
        lane = lax.broadcasted_iota(jnp.int32, (PB, 2 * HD), 1)
        wide_lane = lax.broadcasted_iota(jnp.int32, (rows, 2 * HD), 1)
        ds_s[...] = jnp.zeros_like(ds_s)
        p_s[...] = jnp.zeros_like(p_s)
        for m in range(micro_count):
            fetch([(k_i.at[m], k), (v_i.at[m], v), (q_i.at[m], q), (lse_i.at[m], lse)])
            whole = pl.ds(m * rows, rows)

            def pair(index, carry):
                lanes = pl.ds(pl.multiple_of(index * 2 * HD, 2 * HD), 2 * HD)
                for i in range(rows // PB):
                    here = pl.ds(i * PB, PB)
                    there = pl.ds(m * rows + i * PB, PB)
                    query, d_out, logs = q[here, lanes], d_att[there, lanes], lse[here, :]
                    start, table = own_rows(i)
                    seen = prompt + i * PB
                    keys, values = k[pl.ds(0, seen), lanes], v[pl.ds(0, seen), lanes]
                    column = lax.broadcasted_iota(jnp.int32, (PB, seen), 1)
                    row = lax.broadcasted_iota(jnp.int32, (PB, seen), 0)
                    allowed = column <= row + start
                    parts = []
                    for sub in range(2):
                        mine = lane // HD == sub
                        scores = ndot(jnp.where(mine, query, jnp.zeros_like(query)), keys)
                        log = jnp.sum(
                            jnp.where(lane == 2 * index + sub, logs, 0.0), -1, keepdims=True
                        )
                        probs = jnp.where(allowed, jnp.exp(scores - log), 0.0)
                        d_probs = ndot(jnp.where(mine, d_out, jnp.zeros_like(d_out)), values)
                        centre = jnp.sum(probs * d_probs, -1, keepdims=True)
                        d_scores = (probs * (d_probs - centre)).astype(BF)
                        ds_s[sub, here, pl.ds(0, seen)] = d_scores
                        p_s[sub, here, pl.ds(0, seen)] = probs.astype(BF)
                        parts.append(mdot(d_scores, keys))
                    d_query = jnp.where(lane < HD, parts[0], parts[1]) * HD**-0.5
                    d_query = rope(d_query, cosine[table, :], -sine_part[table, :])
                    dpq[there, lanes] = d_query.astype(BF)
                d_key = jnp.zeros((length, 2 * HD), F32)
                d_value = jnp.zeros((length, 2 * HD), F32)
                query, d_out = q[:, lanes], d_att[whole, lanes]
                for sub in range(2):
                    mine = wide_lane // HD == sub
                    d_key += tdot(ds_s[sub], jnp.where(mine, query, jnp.zeros_like(query)))
                    d_value += tdot(p_s[sub], jnp.where(mine, d_out, jnp.zeros_like(d_out)))
                keys_here = pl.ds(m * length, length)
                d_key = rope(d_key, cosine[...], -sine_part[...])
                dpk[keys_here, lanes] = d_key.astype(BF)
                dpv[keys_here, lanes] = d_value.astype(BF)
                return carry

            lax.fori_loop(0, features // (2 * HD), pair, 0)
            if m == 0:
                load_wq.wait()
            key_w, value_w = wq[pl.ds(features, features), :], wq[pl.ds(2 * features, features), :]
            for z in range(depth):
                here = pl.ds(m * length + z * PB, PB)
                part[m, z] = (mdot(dpk[here, :], key_w) + mdot(dpv[here, :], value_w)).astype(BF)
            prompts_on(m, depth - 1)
            for i in range(rows // PB):
                _, table = own_rows(i)
                start = own_rows(i)[0] + m * length
                here = pl.ds(pl.multiple_of(start, PB), PB)
                there = pl.ds(m * rows + i * PB, PB)
                dn1[pl.ds(i * PB, PB), :] = (
                    mdot(dpq[there, :], wq[pl.ds(0, features), :])
                    + mdot(dpk[here, :], key_w)
                    + mdot(dpv[here, :], value_w)
                )
            fetch([(dn1, dn1_o.at[m])])
            experts_on(depth - 2, m, experts.at_end)
            if m == 0:
                experts_on(depth - 2, 1, inside)
                for d in early:
                    d.add_high()
                both_ways(early, depth - 1)

    pl.run_scoped(
        attention,
        pltpu.VMEM((length, features), BF),
        pltpu.VMEM((length, features), BF),
        pltpu.VMEM((rows, features), BF),
        pltpu.VMEM((rows, 2 * HD), F32),
        pltpu.VMEM((2, rows, length), BF),
        pltpu.VMEM((2, rows, length), BF),
        pltpu.VMEM(qkv_w.shape, BF),
        pltpu.VMEM((rows, features), F32),
    )

    def weight_grads(n1, n1_own):
        pairs = []
        for m in range(micro_count):
            pairs.append((n1_i.at[m], n1.at[pl.ds(m * length, length)]))
            for i in range(rows // PB):
                _, here = own_rows(i)
                pairs.append((n1_i.at[m, here], n1_own.at[pl.ds(m * rows + i * PB, PB)]))
        fetch(pairs)

        def make(here):
            g_qkv[here, :] = tdot(dpq[:, here], n1_own[...]).astype(BF)

        def make_key(here):
            there = pl.ds(pl.multiple_of(here.start + features, 256), 256)
            g_qkv[there, :] = tdot(dpk[:, here], n1[...]).astype(BF)

        def make_value(here):
            there = pl.ds(pl.multiple_of(here.start + 2 * features, 256), 256)
            g_qkv[there, :] = tdot(dpv[:, here], n1[...]).astype(BF)

        tiles(features, 256, make)
        tiles(features, 256, make_key)
        tiles(features, 256, make_value)

    pl.run_scoped(
        weight_grads,
        pltpu.VMEM((micro_count * length, features), BF),
        pltpu.VMEM((micro_count * rows, features), BF),
    )
    for d in late:
        d.start()

    for step in range(depth - 2, 1, -1):
        for m in range(micro_count):
            prompts_on(m, step)
    for d in late:
        d.add_low()

    def outputs(hidden, side, back, first, second):
        for m in range(micro_count):
            fetch([(hid_i.at[m], hidden), (side_i.at[pl.ds(m * rows, rows)], side)])
            mark_pairs(first, second, m)
            fetch_returned(outs_i, ret_out, ro_recv, back, m)
            for i in range(rows // PB):
                here = pl.ds(i * PB, PB)
                routed = gate_rows[m, here, 0:1] * tdot(first[:, here], back[...])
                routed += gate_rows[m, here, 1:2] * tdot(second[:, here], back[...])
                out_rows[here, :] = (hidden[here, :] + side[here, :] + routed).astype(BF)
            fetch([(out_rows, mixed_o.at[m])])
            if m == 0:
                for step in range(depth - 3, 0, -1):
                    experts_on(step, 0)

    pl.run_scoped(
        outputs,
        pltpu.VMEM((rows, features), F32),
        pltpu.VMEM((rows, features), F32),
        pltpu.VMEM((total * capacity, features), BF),
        pltpu.VMEM((total * capacity, rows), BF),
        pltpu.VMEM((total * capacity, rows), BF),
    )

    def last_on(kind):
        for step in range(depth - 3, 0, -1):
            for local in range(1, local_count):
                for direction in (1, -1):
                    experts.pass_on(direction, step, local, (kind,))

    for d in late:
        d.add_high()
    both_ways(late, depth - 1)
    for m in range(micro_count):
        prompts_on(m, 1)
    for step in range(depth - 2, 1, -1):
        both_ways(early, step)
        both_ways(late, step)
    both_ways(early, 1)
    last_on(0)
    last_on(1)

    def inputs(x_rows, d_hidden, dn1):
        for m in range(micro_count):
            fetch([(tokens.at[m], x_rows), (d_hidden_o.at[m], d_hidden), (dn1_o.at[m], dn1)])
            for direction, slot in ((1, place.z), (-1, depth)):

                def body(m=m, slot=slot):
                    prompts[m].arrive(slot)
                    dn1[pl.ds(0, PB), :] += part_land[m, slot].astype(F32)

                pl.when(prompts[m].upstream(direction))(body)
            gain = gain_v[0:1, :]
            for i in range(rows // PB):
                here = pl.ds(i * PB, PB)
                values, d_normed = x_rows[here, :].astype(F32), dn1[here, :]
                root = lax.rsqrt(jnp.mean(values * values, -1, keepdims=True) + EPSILON)
                scaled = gain * d_normed
                d_values = (
                    d_hidden[here, :]
                    + root * scaled
                    - values * (root * root * root) * jnp.mean(values * scaled, -1, keepdims=True)
                )
                gain_own[0:1, :] += jnp.sum(d_normed * values * root, 0, keepdims=True)
                out_rows[here, :] = d_values.astype(BF)
            fetch([(out_rows, input_o.at[m])])

    pl.run_scoped(
        inputs,
        pltpu.VMEM((rows, features), BF),
        pltpu.VMEM((rows, features), F32),
        pltpu.VMEM((rows, features), F32),
    )
    both_ways(late, 1)
    last_on(2)
    for d in early:
        d.end()

    def gain_copies(first, targets, lands):
        return [
            remote(gain_own, land, gain_send.at[first + i], gain_recv.at[first + i], **target)
            for i, (target, land) in enumerate(zip(targets, lands))
        ]

    def gain_add(copies, lands):
        for copy in copies:
            copy.wait()
        total_gain = gain_own[...]
        for land in lands:
            total_gain = total_gain + land[...]
        gain_own[...] = total_gain

    peers = range(1, high_count)
    places = range(1, depth)
    stages = [
        (0, [dict(experts=place.e + 1 - 2 * place.low)], [gain_low]),
        (
            1,
            [dict(experts=place.peer_high(s) * 2 + place.low) for s in peers],
            [gain_high.at[s - 1] for s in peers],
        ),
        (
            high_count,
            [dict(context=lax.rem(place.z + s, depth)) for s in places],
            [gain_line.at[s - 1] for s in places],
        ),
        (high_count + depth - 1, [dict(dp=1 - place.x)], [gain_cross]),
    ]

    def gain_start(i):
        copies = gain_copies(*stages[i])
        for copy in copies:
            copy.start()
        return copies

    for i in range(2):
        gain_add(gain_start(i), stages[i][2])
    line_copies = gain_start(2)
    experts.end(0)
    for d in dense:
        d.drain_first()
    for m in range(micro_count):
        for step in range(1, owners):
            for entry in returns:
                hand_back(*entry, m, step).wait_send()
    for d in late:
        d.end()
    gain_add(line_copies, stages[2][2])
    cross_copies = gain_start(3)
    for d in early:
        d.finish()
    for d in late:
        d.finish()
    for local in range(1, local_count):
        experts.end(local)
    gain_add(cross_copies, stages[3][2])
    fetch([(gain_own, gain_o)])
    for d in dense:
        d.drain()
    experts.drain()
    for p in prompts:
        p.drain()


def run_backward(sizes, tokens, cot, gates, routes, gate_rows, forward):
    depth, high_count = sizes
    micro_count, rows, features = tokens.shape
    owners = high_count * 2
    line = depth * owners
    prompt = depth * PB
    length = prompt + CONT
    cosine, sine_part = rope_tables(prompt)
    gsg, geg, outs = forward[12], forward[15], forward[18]
    local_count, slots, _ = outs.shape
    total = owners * local_count
    capacity = rows * 8 // (3 * total)
    part = gsg.shape[1] // line
    width = geg.shape[2] // (2 * depth)
    hbm, vmem = pl.BlockSpec(memory_space=pltpu.HBM), pl.BlockSpec(memory_space=pltpu.VMEM)
    shapes = [(features, part), (features, part), (part, features)]
    shapes += [(forward[0].shape[0] // line, features), (forward[1].shape[0] // line, features)]
    expert_shapes = [(features, width), (features, width), (width, features)]
    returned = (micro_count, owners, local_count, capacity, features)
    out_dims = [(micro_count, rows, features)] * 2
    out_dims += [shapes[3], shapes[4], shapes[0], shapes[1], shapes[2]]
    out_dims += [(local_count,) + s for s in expert_shapes]
    out_shape = [jax.ShapeDtypeStruct(dims, BF) for dims in out_dims]
    out_shape += [jax.ShapeDtypeStruct((8, features), F32)]
    out_shape += [jax.ShapeDtypeStruct((depth + 1, local_count) + s, BF) for s in expert_shapes]
    out_shape += [jax.ShapeDtypeStruct(returned, BF)] * 2
    out_shape += [jax.ShapeDtypeStruct((micro_count, rows, features), F32)] * 2
    out_shape += [jax.ShapeDtypeStruct((local_count,) + s, BF) for s in expert_shapes]
    scratch = [pltpu.VMEM((depth, high_count) + s, BF) for s in shapes]
    scratch += [pltpu.VMEM((high_count - 1, depth) + s, BF) for s in shapes]
    scratch += [pltpu.VMEM((depth + 1,) + s, BF) for s in shapes]
    scratch += [pltpu.VMEM(s, BF) for s in shapes]
    scratch += [pltpu.VMEM((2,) + shapes[0], BF), pltpu.VMEM((2,) + shapes[2], BF)]
    scratch += [pltpu.VMEM((depth, local_count) + s, BF) for s in expert_shapes]
    scratch += [pltpu.VMEM(s, BF) for s in expert_shapes]
    scratch += [pltpu.VMEM((2,) + s, BF) for s in expert_shapes]
    token_rows, key_rows = micro_count * rows, micro_count * length
    gain = (8, features)
    scratch += [
        pltpu.VMEM((token_rows, features), BF),
        pltpu.VMEM((token_rows, features), BF),
        pltpu.VMEM((key_rows, features), BF),
        pltpu.VMEM((key_rows, features), BF),
        pltpu.VMEM(forward[0].shape, BF),
        pltpu.VMEM(forward[1].shape, BF),
        pltpu.VMEM((micro_count, depth, PB, features), BF),
        pltpu.VMEM((micro_count, depth + 1, PB, features), BF),
        pltpu.VMEM(gain, F32),
        pltpu.VMEM(gain, F32),
        pltpu.VMEM((high_count - 1,) + gain, F32),
        pltpu.VMEM((depth - 1,) + gain, F32),
        pltpu.VMEM(gain, F32),
        pltpu.VMEM((rows, features), BF),
    ]
    dma = pltpu.SemaphoreType.DMA
    scratch += DenseScatter.semaphores(len(shapes), depth, high_count)
    scratch += ExpertScatter.semaphores(depth, local_count)
    stages = 1 + high_count + depth
    scratch += [
        dma((micro_count, depth + 1)),
        dma((micro_count, depth + 1)),
        dma((owners, micro_count)),
        dma((owners, micro_count)),
        dma((owners, micro_count)),
        dma((owners, micro_count)),
        dma((stages,)),
        dma((stages,)),
        dma((max(total, 2 + micro_count, 4 * micro_count + micro_count),)),
        dma((1,)),
        dma((1,)),
    ]
    return pl.pallas_call(
        functools.partial(backward_kernel, sizes),
        out_shape=out_shape,
        in_specs=[hbm] * 2 + [vmem] * 5 + [hbm] * 2 + [vmem] + [hbm] * 20,
        out_specs=[hbm] * len(out_shape),
        scratch_shapes=scratch,
        compiler_params=pltpu.CompilerParams(
            collective_id=1, has_side_effects=True, vmem_limit_bytes=60 * MIB
        ),
        name="backward_and_sum",
    )(tokens, cot, gates, routes, gate_rows, cosine, sine_part, *forward)


def finish_kernel(count, gain_width, *refs):
    low, refs = refs[:count], refs[count:]
    rows, refs = refs[:2], refs[2:]
    gain, refs = refs[0], refs[1:]
    rows_o, refs = refs[:2], refs[2:]
    wide_o, refs = refs[:count], refs[count:]
    gain_o, refs = refs[0], refs[1:]
    low_s, refs = refs[:count], refs[count:]
    wide_s, refs = refs[:count], refs[count:]
    rows_s, sem_in, sem_out = refs[:2], refs[2], refs[3]
    loads = [
        pltpu.make_async_copy(source, target, sem_in.at[i])
        for i, (source, target) in enumerate(zip(low + rows, low_s + rows_s))
    ]
    for copy in loads:
        copy.start()
    stores = [
        pltpu.make_async_copy(source, target, sem_out.at[i])
        for i, (source, target) in enumerate(zip(wide_s + rows_s, wide_o + rows_o))
    ]
    place = (lax.axis_index(CONTEXT) * lax.axis_size(EXPERTS) + lax.axis_index(EXPERTS)) * gain_width
    features = gain.shape[1]
    gain_o[...] = pltpu.roll(gain[...], lax.rem(features - place, features), 1)[:2, :gain_width]
    for i in range(count):
        loads[i].wait()
        wide_s[i][...] = low_s[i][...].astype(F32)
        stores[i].start()
    for i in range(count, count + 2):
        loads[i].wait()
        stores[i].start()
    for copy in stores:
        copy.wait()


def finish_outputs(low, rows, gain, gain_width):
    count = len(low)
    hbm, vmem = pl.BlockSpec(memory_space=pltpu.HBM), pl.BlockSpec(memory_space=pltpu.VMEM)
    wide = [item.shape for item in low]
    out_shape = [jax.ShapeDtypeStruct(item.shape, BF) for item in rows]
    out_shape += [jax.ShapeDtypeStruct(dims, F32) for dims in wide]
    out_shape += [jax.ShapeDtypeStruct((2, gain_width), F32)]
    dma = pltpu.SemaphoreType.DMA
    return pl.pallas_call(
        functools.partial(finish_kernel, count, gain_width),
        out_shape=out_shape,
        in_specs=[hbm] * (count + 2) + [vmem],
        out_specs=[hbm] * (count + 2) + [vmem],
        scratch_shapes=[pltpu.VMEM(item.shape, BF) for item in low]
        + [pltpu.VMEM(dims, F32) for dims in wide]
        + [pltpu.VMEM(item.shape, BF) for item in rows]
        + [dma((count + 2,)), dma((count + 2,))],
        compiler_params=pltpu.CompilerParams(vmem_limit_bytes=60 * MIB),
        name="finish_outputs",
    )(*low, *rows, gain)


def on_device_plain(
    tokens,
    cotangent,
    gates,
    routes,
    qkv_weight,
    out_weight,
    shared_gate,
    shared_up,
    shared_down,
    gains,
    expert_gate,
    expert_up,
    expert_down,
):
    micro_count = tokens.shape[2]
    row_count = tokens.shape[4]
    feature_count = tokens.shape[5]
    owners = lax.axis_size(EXPERTS)
    local_experts = expert_gate.shape[0]
    total_experts = owners * local_experts
    capacity = row_count * 8 // (3 * total_experts)
    blocks = lax.axis_size(CONTEXT)
    prompt = blocks * PB
    scaling = HD ** (-0.5)
    w_qkv, w_out, w_sgate, w_sup, w_sdown, w_gains = (
        lax.all_gather(qkv_weight, (CONTEXT, EXPERTS), axis=1, tiled=True),
        lax.all_gather(out_weight, (CONTEXT, EXPERTS), axis=0, tiled=True),
        lax.all_gather(shared_gate, (CONTEXT, EXPERTS), axis=1, tiled=True),
        lax.all_gather(shared_up, (CONTEXT, EXPERTS), axis=1, tiled=True),
        lax.all_gather(shared_down, (CONTEXT, EXPERTS), axis=0, tiled=True),
        lax.all_gather(gains, (CONTEXT, EXPERTS), axis=1, tiled=True),
    )
    e_gate, expert_up_weight, e_down = (
        lax.all_gather(expert_gate, (DP, CONTEXT), axis=2, tiled=True),
        lax.all_gather(expert_up, (DP, CONTEXT), axis=2, tiled=True),
        lax.all_gather(expert_down, (DP, CONTEXT), axis=1, tiled=True),
    )
    gain_one = w_gains[0].astype(jnp.float32)
    gain_two = w_gains[1].astype(jnp.float32)
    here_index = lax.axis_index(CONTEXT)
    row_ids = jnp.arange(row_count, dtype=jnp.int32)
    query_pos = jnp.where(row_ids < PB, here_index * PB + row_ids, prompt + row_ids - PB)
    key_pos = jnp.arange(prompt + CONT, dtype=jnp.int32)
    allowed = key_pos[None, None, :] <= query_pos[None, :, None]
    half_size = HD // 2
    frequency = 10000.0 ** (-2.0 * jnp.arange(half_size, dtype=jnp.float32) / HD)
    angles = query_pos.astype(jnp.float32)[:, None] * frequency
    cosine = jnp.cos(angles)[:, None, :]
    sine_part = jnp.sin(angles)[:, None, :]
    kept_list = []
    mixed_list = []
    for step_index in range(micro_count):
        inputs = tokens[0, 0, step_index, 0].astype(jnp.float32)
        root_one = lax.rsqrt(jnp.mean(inputs * inputs, -1, keepdims=True) + EPSILON)
        normed_one = (inputs * root_one * gain_one).astype(jnp.bfloat16)
        projected = mdot(normed_one, w_qkv)
        query = rotate(projected[:, :feature_count], cosine, sine_part).astype(jnp.bfloat16)
        key_rows = rotate(
            projected[:, feature_count : 2 * feature_count], cosine, sine_part
        ).astype(jnp.bfloat16)
        value_rows = projected[:, 2 * feature_count :].astype(jnp.bfloat16)
        prompt_key, prompt_value = (
            lax.all_gather(key_rows[:PB], CONTEXT, axis=0, tiled=True),
            lax.all_gather(value_rows[:PB], CONTEXT, axis=0, tiled=True),
        )
        key_heads = jnp.concatenate([prompt_key, key_rows[PB:]], 0).reshape(prompt + CONT, H, HD)
        value_heads = jnp.concatenate([prompt_value, value_rows[PB:]], 0).reshape(
            prompt + CONT, H, HD
        )
        query_heads = query.reshape(row_count, H, HD)
        scores = (
            jnp.einsum("qhd,khd->hqk", query_heads, key_heads, preferred_element_type=jnp.float32)
            * scaling
        )
        scores = jnp.where(allowed, scores, -1000000000.0)
        highest = jnp.max(scores, -1, keepdims=True)
        weights = jnp.exp(scores - highest)
        total = jnp.sum(weights, -1, keepdims=True)
        log_total = highest + jnp.log(total)
        probs = (weights / total).astype(jnp.bfloat16)
        attended = (
            jnp.einsum("hqk,khd->qhd", probs, value_heads, preferred_element_type=jnp.float32)
            .reshape(row_count, feature_count)
            .astype(jnp.bfloat16)
        )
        hidden = inputs + mdot(attended, w_out)
        root_two = lax.rsqrt(jnp.mean(hidden * hidden, -1, keepdims=True) + EPSILON)
        normed_two = (hidden * root_two * gain_two).astype(jnp.bfloat16)
        side_gate = mdot(normed_two, w_sgate)
        side_up = mdot(normed_two, w_sup)
        side_act = (jax.nn.silu(side_gate) * side_up).astype(jnp.bfloat16)
        side = mdot(side_act, w_sdown)
        route_rows = routes[0, 0, step_index, 0]
        slots = slot_table(route_rows, total_experts)
        flat_dest = (route_rows * capacity + slots).reshape(-1)
        source = (
            jnp.full((total_experts * capacity,), 2 * row_count, jnp.int32)
            .at[flat_dest]
            .set(jnp.arange(2 * row_count, dtype=jnp.int32))
        )
        padded = jnp.concatenate([normed_two, jnp.zeros((1, feature_count), jnp.bfloat16)], 0)
        send = padded[source // 2].reshape(total_experts, capacity, feature_count)
        received = lax.all_to_all(send, EXPERTS, split_axis=0, concat_axis=0, tiled=True)
        count = received.shape[1]
        expert_grouped = received.reshape(owners, local_experts, count, feature_count)
        expert_gate_act = jnp.einsum(
            "send,edf->senf", expert_grouped, e_gate, preferred_element_type=jnp.float32
        )
        expert_up_act = jnp.einsum(
            "send,edf->senf", expert_grouped, expert_up_weight, preferred_element_type=jnp.float32
        )
        expert_hidden_act = (jax.nn.silu(expert_gate_act) * expert_up_act).astype(jnp.bfloat16)
        result = jnp.einsum(
            "senf,efd->send", expert_hidden_act, e_down, preferred_element_type=jnp.float32
        ).astype(jnp.bfloat16)
        expert_out = result.reshape(owners * local_experts, count, feature_count)
        expert_in = received
        returned = lax.all_to_all(
            expert_out, EXPERTS, split_axis=0, concat_axis=0, tiled=True
        ).reshape(-1, feature_count)
        gate_rows = gates[0, 0, step_index, 0]
        picked = returned[flat_dest].reshape(row_count, 2, feature_count).astype(jnp.float32)
        routed = jnp.sum(gate_rows[:, :, None] * picked, 1)
        mixed_list.append((hidden + routed + side).astype(jnp.bfloat16))
        cached = (prompt_key, prompt_value)
        kept_list.append(
            (
                inputs,
                root_one,
                normed_one,
                query,
                key_rows,
                value_rows,
                cached,
                log_total,
                attended,
                hidden,
                root_two,
                normed_two,
                side_gate,
                side_up,
                side_act,
                flat_dest,
                source,
                expert_in,
                gate_rows,
            )
        )
    acc_qkv = jnp.zeros(w_qkv.shape, jnp.float32)
    acc_out = jnp.zeros(w_out.shape, jnp.float32)
    acc_sgate = jnp.zeros(w_sgate.shape, jnp.float32)
    acc_sup = jnp.zeros(w_sup.shape, jnp.float32)
    acc_sdown = jnp.zeros(w_sdown.shape, jnp.float32)
    acc_gain_one = jnp.zeros((feature_count,), jnp.float32)
    acc_gain_two = jnp.zeros((feature_count,), jnp.float32)
    local_egate = jnp.zeros(e_gate.shape, jnp.float32)
    local_expert_up_weight = jnp.zeros(expert_up_weight.shape, jnp.float32)
    local_edown = jnp.zeros(e_down.shape, jnp.float32)
    input_list = []
    for step_index in range(micro_count):
        (
            inputs,
            root_one,
            normed_one,
            query,
            key_rows,
            value_rows,
            cached,
            log_total,
            attended,
            hidden,
            root_two,
            normed_two,
            side_gate,
            side_up,
            side_act,
            flat_dest,
            source,
            expert_in,
            gate_rows,
        ) = kept_list[step_index]
        grad_rows = cotangent[0, 0, step_index, 0].astype(jnp.float32)
        grad_low = grad_rows.astype(jnp.bfloat16)
        acc_sdown = acc_sdown + tdot(side_act, grad_low)
        d_side_act = ndot(grad_low, w_sdown).astype(jnp.bfloat16).astype(jnp.float32)
        silu_side, slope_side = silu_parts(side_gate)
        d_side_gate = (d_side_act * side_up * slope_side).astype(jnp.bfloat16)
        d_side_up = (d_side_act * silu_side).astype(jnp.bfloat16)
        acc_sgate = acc_sgate + tdot(normed_two, d_side_gate)
        acc_sup = acc_sup + tdot(normed_two, d_side_up)
        d_normed_two = ndot(d_side_gate, w_sgate) + ndot(d_side_up, w_sup)
        d_pairs = (
            (gate_rows[:, :, None] * grad_rows[:, None, :])
            .astype(jnp.bfloat16)
            .reshape(2 * row_count, feature_count)
        )
        padded_grad = jnp.concatenate([d_pairs, jnp.zeros((1, feature_count), jnp.bfloat16)], 0)
        grad_send = padded_grad[source].reshape(total_experts, capacity, feature_count)
        grad_in = lax.all_to_all(grad_send, EXPERTS, split_axis=0, concat_axis=0, tiled=True)
        grouped_grad = grad_in.reshape(owners, local_experts, capacity, feature_count)
        grouped = expert_in.reshape(owners, local_experts, capacity, feature_count)
        gate_act = jnp.einsum("send,edf->senf", grouped, e_gate, preferred_element_type=jnp.float32)
        up_act = jnp.einsum(
            "send,edf->senf", grouped, expert_up_weight, preferred_element_type=jnp.float32
        )
        silu_gate, slope_gate = silu_parts(gate_act)
        hidden_act = (silu_gate * up_act).astype(jnp.bfloat16)
        d_hidden_act = (
            jnp.einsum("send,efd->senf", grouped_grad, e_down, preferred_element_type=jnp.float32)
            .astype(jnp.bfloat16)
            .astype(jnp.float32)
        )
        d_gate_act = (d_hidden_act * up_act * slope_gate).astype(jnp.bfloat16)
        d_up_act = (d_hidden_act * silu_gate).astype(jnp.bfloat16)
        step_edown = jnp.einsum(
            "senf,send->efd", hidden_act, grouped_grad, preferred_element_type=jnp.float32
        )
        step_egate = jnp.einsum(
            "send,senf->edf", grouped, d_gate_act, preferred_element_type=jnp.float32
        )
        stepwise_expert_up = jnp.einsum(
            "send,senf->edf", grouped, d_up_act, preferred_element_type=jnp.float32
        )
        local_egate = local_egate + step_egate
        local_expert_up_weight = local_expert_up_weight + stepwise_expert_up
        local_edown = local_edown + step_edown
        d_expert_in = jnp.einsum(
            "senf,edf->send", d_gate_act, e_gate, preferred_element_type=jnp.float32
        ) + jnp.einsum(
            "senf,edf->send", d_up_act, expert_up_weight, preferred_element_type=jnp.float32
        )
        d_expert_in = d_expert_in.astype(jnp.bfloat16).reshape(
            total_experts, capacity, feature_count
        )
        back = lax.all_to_all(
            d_expert_in, EXPERTS, split_axis=0, concat_axis=0, tiled=True
        ).reshape(-1, feature_count)
        d_normed_two = d_normed_two + jnp.sum(
            back[flat_dest].reshape(row_count, 2, feature_count).astype(jnp.float32), 1
        )
        scaled_two = gain_two * d_normed_two
        d_hidden = (
            grad_rows
            + root_two * scaled_two
            - hidden * root_two**3 * jnp.mean(hidden * scaled_two, -1, keepdims=True)
        )
        acc_gain_two = acc_gain_two + jnp.sum(d_normed_two * hidden * root_two, 0)
        d_attn = d_hidden.astype(jnp.bfloat16)
        acc_out = acc_out + tdot(attended, d_attn)
        d_attended = ndot(d_attn, w_out).astype(jnp.bfloat16)
        prompt_key, prompt_value = cached
        key_heads = jnp.concatenate([prompt_key, key_rows[PB:]], 0).reshape(prompt + CONT, H, HD)
        value_heads = jnp.concatenate([prompt_value, value_rows[PB:]], 0).reshape(
            prompt + CONT, H, HD
        )
        query_heads = query.reshape(row_count, H, HD)
        scores = (
            jnp.einsum("qhd,khd->hqk", query_heads, key_heads, preferred_element_type=jnp.float32)
            * scaling
        )
        scores = jnp.where(allowed, scores, -1000000000.0)
        probs = jnp.exp(scores - log_total)
        d_heads = d_attended.reshape(row_count, H, HD)
        d_probs = jnp.einsum(
            "qhd,khd->hqk", d_heads, value_heads, preferred_element_type=jnp.float32
        )
        centre = jnp.sum(probs * d_probs, -1, keepdims=True)
        d_scores = (probs * (d_probs - centre)).astype(jnp.bfloat16)
        d_query = (
            jnp.einsum(
                "hqk,khd->qhd", d_scores, key_heads, preferred_element_type=jnp.float32
            ).reshape(row_count, feature_count)
            * scaling
        )
        d_keys = (
            jnp.einsum(
                "hqk,qhd->khd", d_scores, query_heads, preferred_element_type=jnp.float32
            ).reshape(prompt + CONT, feature_count)
            * scaling
        )
        d_values = jnp.einsum(
            "hqk,qhd->khd", probs.astype(jnp.bfloat16), d_heads, preferred_element_type=jnp.float32
        ).reshape(prompt + CONT, feature_count)
        own_dkey, own_dvalue = (
            lax.psum_scatter(
                d_keys[:prompt].astype(jnp.bfloat16), CONTEXT, scatter_dimension=0, tiled=True
            ).astype(jnp.float32),
            lax.psum_scatter(
                d_values[:prompt].astype(jnp.bfloat16), CONTEXT, scatter_dimension=0, tiled=True
            ).astype(jnp.float32),
        )
        d_key_rows = jnp.concatenate([own_dkey, d_keys[prompt:]], 0)
        d_value_rows = jnp.concatenate([own_dvalue, d_values[prompt:]], 0)
        d_projected = jnp.concatenate(
            [
                rotate(d_query, cosine, -sine_part).astype(jnp.bfloat16),
                rotate(d_key_rows, cosine, -sine_part).astype(jnp.bfloat16),
                d_value_rows.astype(jnp.bfloat16),
            ],
            1,
        )
        acc_qkv = acc_qkv + tdot(normed_one, d_projected)
        d_normed_one = ndot(d_projected, w_qkv)
        scaled_one = gain_one * d_normed_one
        d_inputs = (
            d_hidden
            + root_one * scaled_one
            - inputs * root_one**3 * jnp.mean(inputs * scaled_one, -1, keepdims=True)
        )
        acc_gain_one = acc_gain_one + jnp.sum(d_normed_one * inputs * root_one, 0)
        input_list.append(d_inputs.astype(jnp.bfloat16))
    sharded_expert_gate, sharded_expert_up, sharded_expert_down = (
        lax.psum_scatter(
            local_egate.astype(jnp.bfloat16), (DP, CONTEXT), scatter_dimension=2, tiled=True
        ).astype(jnp.float32),
        lax.psum_scatter(
            local_expert_up_weight.astype(jnp.bfloat16),
            (DP, CONTEXT),
            scatter_dimension=2,
            tiled=True,
        ).astype(jnp.float32),
        lax.psum_scatter(
            local_edown.astype(jnp.bfloat16), (DP, CONTEXT), scatter_dimension=1, tiled=True
        ).astype(jnp.float32),
    )
    acc_gains = jnp.stack([acc_gain_one, acc_gain_two], 0)
    dense_shards = (
        lax.psum_scatter(acc_qkv, (CONTEXT, EXPERTS), scatter_dimension=1, tiled=True),
        lax.psum_scatter(acc_out, (CONTEXT, EXPERTS), scatter_dimension=0, tiled=True),
        lax.psum_scatter(acc_sgate, (CONTEXT, EXPERTS), scatter_dimension=1, tiled=True),
        lax.psum_scatter(acc_sup, (CONTEXT, EXPERTS), scatter_dimension=1, tiled=True),
        lax.psum_scatter(acc_sdown, (CONTEXT, EXPERTS), scatter_dimension=0, tiled=True),
        lax.psum_scatter(acc_gains, (CONTEXT, EXPERTS), scatter_dimension=1, tiled=True),
    )
    grad_qkv, grad_out, grad_sgate, grad_sup, grad_sdown, grad_gains = (
        lax.psum(dense_shards[0].astype(jnp.bfloat16), DP).astype(jnp.float32),
        lax.psum(dense_shards[1].astype(jnp.bfloat16), DP).astype(jnp.float32),
        lax.psum(dense_shards[2].astype(jnp.bfloat16), DP).astype(jnp.float32),
        lax.psum(dense_shards[3].astype(jnp.bfloat16), DP).astype(jnp.float32),
        lax.psum(dense_shards[4].astype(jnp.bfloat16), DP).astype(jnp.float32),
        lax.psum(dense_shards[5].astype(jnp.bfloat16), DP).astype(jnp.float32),
    )
    mixed = jnp.stack(mixed_list, 0).reshape(tokens.shape)
    input_grad = jnp.stack(input_list, 0).reshape(tokens.shape)
    return (
        mixed,
        input_grad,
        grad_qkv,
        grad_out,
        grad_sgate,
        grad_sup,
        grad_sdown,
        grad_gains,
        sharded_expert_gate,
        sharded_expert_up,
        sharded_expert_down,
    )


def on_device(
    tokens,
    cotangent,
    gates,
    routes,
    qkv_weight,
    out_weight,
    shared_gate,
    shared_up,
    shared_down,
    gains,
    expert_gate,
    expert_up,
    expert_down,
):
    owners = lax.axis_size(EXPERTS)
    sizes = (lax.axis_size(CONTEXT), owners // 2)
    own_at = lax.axis_index(CONTEXT) * owners + lax.axis_index(EXPERTS)
    gain_width, features = gains.shape[1], tokens.shape[5]
    gain_rows = lax.dynamic_update_slice(
        jnp.zeros((16, features), jnp.bfloat16), gains, (0, own_at * gain_width)
    )
    rows, cot = tokens[0, 0, :, 0], cotangent[0, 0, :, 0]
    gate_rows, route_rows = gates[0, 0, :, 0], routes[0, 0, :, 0]
    gate_columns, route_columns = gate_rows.transpose(0, 2, 1), route_rows.transpose(0, 2, 1)
    forward = run_forward(
        sizes,
        rows,
        cot,
        gate_columns,
        route_columns,
        (qkv_weight.T, out_weight, gain_rows, shared_gate, shared_up, shared_down),
        (expert_gate, expert_up, expert_down),
    )
    (
        mixed, input_grad, grad_qkv, grad_out, grad_sgate, grad_sup, grad_sdown,
        grad_egate, grad_eup, grad_edown, gain_sum, *_,
    ) = run_backward(
        sizes, rows, cot, gate_columns, route_columns, gate_rows, forward[:3] + forward[9:]
    )
    mixed, input_grad, grad_qkv, *rest = finish_outputs(
        (grad_qkv, grad_out, grad_sgate, grad_sup, grad_sdown, grad_egate, grad_eup, grad_edown),
        (mixed, input_grad),
        gain_sum,
        gain_width,
    )
    grad_out, grad_sgate, grad_sup, grad_sdown, grad_egate, grad_eup, grad_edown, grad_gains = rest
    return (
        mixed.reshape(tokens.shape),
        input_grad.reshape(tokens.shape),
        grad_qkv.T,
        grad_out,
        grad_sgate,
        grad_sup,
        grad_sdown,
        grad_gains,
        grad_egate,
        grad_eup,
        grad_edown,
    )


def kernels_fit(mesh_shape, arrays):
    qkv_weight, out_weight, shared_gate, _, shared_down = arrays[4:9]
    rows = (qkv_weight.shape[1], out_weight.shape[0], shared_gate.shape[1], shared_down.shape[0])
    return (
        mesh_shape[DP] == 2
        and mesh_shape[CONTEXT] >= 4
        and mesh_shape[EXPERTS] % 2 == 0
        and all(count % 16 == 0 for count in rows)
        and shared_gate.shape[1] % 128 == 0
        and arrays[10].shape[2] % 128 == 0
        and shared_gate.shape[1] * mesh_shape[EXPERTS] == 2 * arrays[10].shape[2]
    )


def solution(mesh):
    def device_program(*arrays):
        return (on_device if kernels_fit(mesh.shape, arrays) else on_device_plain)(*arrays)

    return jax.shard_map(
        device_program,
        mesh=mesh,
        in_specs=(
            P(DP, EXPERTS, None, CONTEXT, None, None),
            P(DP, EXPERTS, None, CONTEXT, None, None),
            P(DP, EXPERTS, None, CONTEXT, None, None),
            P(DP, EXPERTS, None, CONTEXT, None, None),
            P(None, (CONTEXT, EXPERTS)),
            P((CONTEXT, EXPERTS), None),
            P(None, (CONTEXT, EXPERTS)),
            P(None, (CONTEXT, EXPERTS)),
            P((CONTEXT, EXPERTS), None),
            P(None, (CONTEXT, EXPERTS)),
            P(EXPERTS, None, (DP, CONTEXT)),
            P(EXPERTS, None, (DP, CONTEXT)),
            P(EXPERTS, (DP, CONTEXT), None),
        ),
        out_specs=(
            P(DP, EXPERTS, None, CONTEXT, None, None),
            P(DP, EXPERTS, None, CONTEXT, None, None),
            P(None, (CONTEXT, EXPERTS)),
            P((CONTEXT, EXPERTS), None),
            P(None, (CONTEXT, EXPERTS)),
            P(None, (CONTEXT, EXPERTS)),
            P((CONTEXT, EXPERTS), None),
            P(None, (CONTEXT, EXPERTS)),
            P(EXPERTS, None, (DP, CONTEXT)),
            P(EXPERTS, None, (DP, CONTEXT)),
            P(EXPERTS, (DP, CONTEXT), None),
        ),
        check_vma=False,
    )
```

```python
import functools

import jax
import jax.numpy as jnp
import numpy as np
from jax import lax
from jax.experimental import pallas as pl
from jax.experimental.pallas import tpu as pltpu
from jax.sharding import PartitionSpec as P

DP, CONTEXT, EXPERTS = "dp", "context", "experts"

H = 12
HD = 64
PB = 128
CONT = 256


EPSILON = 1e-06


def mdot(former, latter):
    return jnp.dot(former, latter, preferred_element_type=jnp.float32)


def tdot(former, latter):
    return lax.dot_general(
        former, latter, (((0,), (0,)), ((), ())), preferred_element_type=jnp.float32
    )


def ndot(former, latter):
    return lax.dot_general(
        former, latter, (((1,), (1,)), ((), ())), preferred_element_type=jnp.float32
    )


def rotate(values, cosine, sine_part):
    half_size = HD // 2
    shaped = values.reshape(values.shape[0], H, HD)
    former = shaped[..., :half_size]
    latter = shaped[..., half_size:]
    turned = jnp.concatenate(
        [former * cosine - latter * sine_part, latter * cosine + former * sine_part], -1
    )
    return turned.reshape(values.shape)


def slot_table(routes_block, expert_count):
    flat_routes = routes_block.reshape(-1)
    onehot = (flat_routes[:, None] == jnp.arange(expert_count, dtype=jnp.int32)[None, :]).astype(
        jnp.int32
    )
    before = jnp.cumsum(onehot, 0) - onehot
    return jnp.sum(before * onehot, 1).reshape(routes_block.shape)


def silu_parts(values):
    sigma = jax.nn.sigmoid(values)
    return (values * sigma, sigma * (1.0 + values * (1.0 - sigma)))


MESH = pl.DeviceIdType.MESH
MIB = 1024 * 1024
BF = jnp.bfloat16
F32 = jnp.float32


def remote(source, target, send_sem, recv_sem, **device):
    return pltpu.make_async_remote_copy(
        src_ref=source,
        dst_ref=target,
        send_sem=send_sem,
        recv_sem=recv_sem,
        device_id=device,
        device_id_type=MESH,
    )


def arrived(slot, recv_sem):
    remote(slot, slot, recv_sem, recv_sem, context=0).wait_recv()


def either(first, second):
    return jnp.logical_and(first, second)


class Place:
    def __init__(self, sizes):
        self.depth, self.high_count = sizes
        self.owners = self.high_count * 2
        self.x = lax.axis_index(DP)
        self.z = lax.axis_index(CONTEXT)
        self.e = lax.axis_index(EXPERTS)
        self.high = self.e // 2
        self.low = self.e % 2

    def shard(self, z):
        return self.x * self.depth + z

    def other_shard(self, z):
        return (1 - self.x) * self.depth + z

    def peer_high(self, step):
        return lax.rem(self.high + step, self.high_count)

    def peer_owner(self, step):
        return lax.rem(self.e + step, self.owners)

    def on_line(self, z):
        return (z >= 0) & (z < self.depth)

    def greet(self):
        barrier = pltpu.get_barrier_semaphore()

        def signal(**device):
            pl.semaphore_signal(barrier, inc=1, device_id=device, device_id_type=MESH)

        signal(dp=1 - self.x)
        for step in range(1, self.owners):
            signal(experts=self.peer_owner(step))
        for step in range(1, self.depth):
            signal(context=lax.rem(self.z + step, self.depth))
        count = self.owners + self.depth - 1
        pl.semaphore_wait(barrier, count)


class Line:
    def __init__(self, place, own, slot, send_sem, recv_sem):
        self.place, self.own, self.slot = place, own, slot
        self.send_sem, self.recv_sem = send_sem, recv_sem

    def _copy(self, direction, step):
        place = self.place
        z = place.z - direction * step
        source = self.own if step == 0 else self.slot(z)
        return remote(
            source,
            self.slot(z),
            self.send_sem.at[(direction + 1) // 2, step],
            self.recv_sem.at[z],
            context=place.z + direction,
        )

    def _valid(self, direction, step):
        place = self.place
        return place.on_line(place.z - direction * step) & place.on_line(place.z + direction)

    def send(self, direction, step):
        if step < self.place.depth - 1:
            pl.when(self._valid(direction, step))(lambda: self._copy(direction, step).start())

    def start(self):
        self.send(1, 0)
        self.send(-1, 0)

    def hop(self, step, then=None):
        for direction in (1, -1):
            z = self.place.z - direction * (step + 1)

            def body(direction=direction, z=z):
                arrived(self.slot(z), self.recv_sem.at[z])
                self.send(direction, step + 1)
                if then is not None:
                    then(z)

            pl.when(self.place.on_line(z))(body)

    def drain(self):
        for direction in (1, -1):
            for step in range(self.place.depth - 1):
                pl.when(self._valid(direction, step))(
                    lambda d=direction, s=step: self._copy(d, s).wait_send()
                )


class DenseGather:
    def __init__(self, place, own, slot, sems):
        self.place, self.own, self.slot_of = place, own, slot
        zs, zr, self.h_send, self.h_recv, self.l_send, self.l_recv = sems
        self.line = Line(place, own, lambda z: self.slot(z, place.high, place.low), zs, zr)

    @staticmethod
    def semaphores(count, depth, high_count):
        dma = pltpu.SemaphoreType.DMA
        cross = dma((count, high_count, depth))
        return [dma((count, 2, depth)), dma((count, depth)), cross, cross, cross, cross]

    def slot(self, z, high, low):
        return self.slot_of((z * self.place.high_count + high) * 2 + low)

    def _to_high(self, z, step, own):
        place = self.place
        target = self.slot(z, place.high, place.low)
        return remote(
            self.own if own else target,
            target,
            self.h_send.at[step, z],
            self.h_recv.at[place.high, z],
            experts=place.peer_high(step) * 2 + place.low,
        )

    def _to_low(self, z, high, own):
        place = self.place
        target = self.slot(z, high, place.low)
        return remote(
            self.own if own else target,
            target,
            self.l_send.at[high, z],
            self.l_recv.at[high, z],
            experts=place.e + 1 - 2 * place.low,
        )

    def _spread(self, z, own=False):
        for step in range(1, self.place.high_count):
            self._to_high(z, step, own).start()
        self._to_low(z, self.place.high, own).start()

    def start(self):
        self.line.start()
        self._spread(self.place.z, True)

    def hop(self, step):
        self.line.hop(step, self._spread)

    def cross(self, z):
        place = self.place
        for step in range(1, place.high_count):
            high = place.peer_high(step)
            arrived(self.slot(z, high, place.low), self.h_recv.at[high, z])
            self._to_low(z, high, False).start()

    def finish(self, z):
        place = self.place
        for high in range(place.high_count):
            arrived(self.slot(z, high, 1 - place.low), self.l_recv.at[high, z])

    def drain(self):
        place = self.place
        self.line.drain()
        for z in range(place.depth):
            for step in range(1, place.high_count):
                self._to_high(z, step, False).wait_send()
            for high in range(place.high_count):
                self._to_low(z, high, False).wait_send()


def expert_slab(ref, kind, local, shard, width):
    start = pl.multiple_of(shard * width, 128)
    if kind == 2:
        return ref.at[local, pl.ds(start, width)]
    return ref.at[local, :, pl.ds(start, width)]


class ExpertGather:
    def __init__(self, place, own, out, sems):
        self.place, self.own, self.out = place, own, out
        self.z_send, self.z_recv, self.x_send, self.x_recv = sems
        self.local_count, self.width = own[0].shape[0], own[0].shape[2]

    @staticmethod
    def semaphores(depth, local_count):
        dma = pltpu.SemaphoreType.DMA
        return [
            dma((local_count, 3, 2, depth)),
            dma((local_count, 3, depth)),
            dma((local_count, 3, depth)),
            dma((local_count, 3, depth)),
        ]

    def slot(self, local, kind, shard):
        return expert_slab(self.out[kind], kind, local, shard, self.width)

    def _line(self, local, kind):
        return Line(
            self.place,
            self.own[kind].at[local],
            lambda z: self.slot(local, kind, self.place.shard(z)),
            self.z_send.at[local, kind],
            self.z_recv.at[local, kind],
        )

    def _across(self, local, kind, z, own=False):
        target = self.slot(local, kind, self.place.shard(z))
        return remote(
            self.own[kind].at[local] if own else target,
            target,
            self.x_send.at[local, kind, z],
            self.x_recv.at[local, kind, z],
            dp=1 - self.place.x,
        )

    def start_x(self):
        for local in range(self.local_count):
            for kind in range(3):
                self._across(local, kind, self.place.z, True).start()

    def start_z(self):
        for local in range(self.local_count):
            for kind in range(3):
                self._line(local, kind).start()

    def hop(self, local, step, kinds=(0, 1, 2)):
        for kind in kinds:
            self._line(local, kind).hop(
                step, lambda z, kind=kind: self._across(local, kind, z).start()
            )

    def wait_x(self, local, z):
        for kind in range(3):
            arrived(
                self.slot(local, kind, self.place.other_shard(z)), self.x_recv.at[local, kind, z]
            )

    def drain(self):
        for local in range(self.local_count):
            for kind in range(3):
                self._line(local, kind).drain()
                for z in range(self.place.depth):
                    self._across(local, kind, z).wait_send()


def rope(values, cosine, sine_part):
    lane = lax.broadcasted_iota(jnp.int32, cosine.shape, 1)
    first = lax.rem(lane, HD) < HD // 2
    turned = []
    for start in range(0, values.shape[1], 2 * HD):
        part = values[:, start : start + 2 * HD]
        partner = jnp.where(
            first, pltpu.roll(part, 2 * HD - HD // 2, 1), pltpu.roll(part, HD // 2, 1)
        )
        turned.append(part * cosine + partner * sine_part)
    return jnp.concatenate(turned, 1)


def norm_rows(values, gain):
    root = lax.rsqrt(jnp.mean(values * values, -1, keepdims=True) + EPSILON)
    return (values * root * gain).astype(BF)


def tiles(total, size, body):
    def run(i, carry):
        body(pl.ds(pl.multiple_of(i * size, size), size))
        return carry

    lax.fori_loop(0, total // size, run, 0)


def one_hots(routes, gates, me, local_count, total):
    rows = routes.shape[1]
    capacity = rows * 8 // (3 * total)
    first, second = routes[0:1, :], routes[1:2, :]
    ids = lax.rem(
        lax.broadcasted_iota(jnp.int32, (total, rows), 0) + me * local_count, total
    )
    named = (first == ids) | (second == ids)
    earlier = (
        lax.broadcasted_iota(jnp.int32, (rows, rows), 0)
        < lax.broadcasted_iota(jnp.int32, (rows, rows), 1)
    ).astype(F32).astype(BF)
    counts = mdot(named.astype(F32).astype(BF), earlier).astype(jnp.int32)
    places = jnp.where(named, counts, -1)
    weights = jnp.where(first == ids, gates[0:1, :], 0.0) + jnp.where(
        second == ids, gates[1:2, :], 0.0
    )
    slot = lax.broadcasted_iota(jnp.int32, (capacity, rows), 0)
    for i in range(total):
        yield i, slot == places[i : i + 1, :], weights[i : i + 1, :]


def ffn_chunk(x, g, weights, saved, sums, grads, tile):
    gate_w, up_w, down_w = weights
    act_s, d_gate_s, d_up_s = saved
    out_sum, in_sum = sums

    def forward(here):
        x_rows, g_rows = x[here, :], g[here, :]
        gate = mdot(x_rows, gate_w[...])
        up = mdot(x_rows, up_w[...])
        d_act = ndot(g_rows, down_w[...]).astype(BF).astype(F32)
        sigma = jax.nn.sigmoid(gate)
        silu = gate * sigma
        act = (silu * up).astype(BF)
        d_gate = (d_act * up * (sigma * (1.0 + gate * (1.0 - sigma)))).astype(BF)
        d_up = (d_act * silu).astype(BF)
        act_s[here, :] = act
        d_gate_s[here, :] = d_gate
        d_up_s[here, :] = d_up
        out_sum[here, :] += mdot(act, down_w[...])
        in_sum[here, :] += ndot(d_gate, gate_w[...]) + ndot(d_up, up_w[...])

    rows = x.shape[0]
    tiles(rows, tile, forward)
    used = pl.ds(0, rows)

    def weight_grads(here):
        grads[0][here, :] = tdot(x[:, here], d_gate_s[used, :]).astype(BF)
        grads[1][here, :] = tdot(x[:, here], d_up_s[used, :]).astype(BF)
        grads[2][:, here] = tdot(act_s[used, :], g[:, here]).astype(BF)

    tiles(x.shape[1], 256, weight_grads)


def forward_kernel(sizes, *refs):
    place = Place(sizes)
    depth, high_count = sizes
    owners = place.owners
    (
        tokens, cot, gates, routes, cosine, sine_part,
        qkv_in, out_in, gain_in, sg_in, su_in, sd_in, eg_in, eu_in, ed_in,
        qkv_o, out_o, gain_o, sg_o, su_o, sd_o, eg_o, eu_o, ed_o,
        n1_o, k_o, v_o, q_o, att_o, hid_o, lse_o, side_o, dn2_o,
        gsg_o, gsu_o, gsd_o, geg_o, geu_o, ged_o, outs_o, dins_o, pre_g, pre_u, pre_d,
        xk, wq, wo, gain_land, gain_v, g_all, n2, in_s, do_s, send_in, send_do,
        wg, wu, wd, act_s, dg_s, du_s, stage_g, stage_u, stage_d,
        *sems,
    ) = refs
    dense_sems, sems = sems[:6], sems[6:]
    expert_sems, sems = sems[:4], sems[4:]
    (
        line_send, line_recv, load_sem, ai_send, ai_recv, ad_send, ad_recv,
        chunk_sem, store_sem, out_sem, pre_send, pre_recv,
    ) = sems
    micro_count, rows, features = tokens.shape
    prompt = depth * PB
    length = prompt + CONT
    local_count, _, width = eg_in.shape
    total = owners * local_count
    capacity = rows * 8 // (3 * total)
    slots = in_s.shape[1]
    me = place.e

    def dense(i, own, slot):
        return DenseGather(place, own, slot, [s.at[i] for s in dense_sems])

    def rows_of(ref, count):
        return lambda s: ref.at[pl.ds(pl.multiple_of(s * count, 16), count)]

    def columns_of(ref, count):
        return lambda s: ref.at[:, pl.ds(pl.multiple_of(s * count, 128), count)]

    early = [
        dense(0, qkv_in, rows_of(wq, qkv_in.shape[0])),
        dense(1, out_in, rows_of(wo, out_in.shape[0])),
        dense(2, gain_in, rows_of(gain_land, gain_in.shape[0])),
    ]
    late = [
        dense(3, sg_in, columns_of(sg_o, sg_in.shape[1])),
        dense(4, su_in, columns_of(su_o, su_in.shape[1])),
        dense(5, sd_in, rows_of(sd_o, sd_in.shape[0])),
    ]
    experts = ExpertGather(place, (eg_in, eu_in, ed_in), (eg_o, eu_o, ed_o), expert_sems)
    own_prompt = pl.ds(pl.multiple_of(place.z * PB, PB), PB)
    prompts = [
        Line(
            place,
            tokens.at[m, pl.ds(0, PB)],
            lambda z, m=m: xk.at[m, pl.ds(pl.multiple_of(z * PB, PB), PB)],
            line_send.at[m],
            line_recv.at[m],
        )
        for m in range(micro_count)
    ]
    own_at = (place.z * high_count + place.high) * 2 + place.low
    loads = [
        (tokens.at[:, pl.ds(0, PB)], xk.at[:, own_prompt]),
        (tokens.at[:, pl.ds(PB, CONT)], xk.at[:, pl.ds(prompt, CONT)]),
    ]
    loads += [(cot.at[m], g_all.at[pl.ds(m * rows, rows)]) for m in range(micro_count)]
    loads += [(d.own, d.slot_of(own_at)) for d in early]
    bounce = [
        (sg_in, wg.at[0, :, pl.ds(0, sg_in.shape[1])], late[0].slot_of(own_at)),
        (su_in, wu.at[0, :, pl.ds(0, su_in.shape[1])], late[1].slot_of(own_at)),
        (sd_in, wd.at[0, pl.ds(0, sd_in.shape[0])], late[2].slot_of(own_at)),
    ]
    loads += [(source, middle) for source, middle, _ in bounce]
    load_copies = [
        pltpu.make_async_copy(source, target, load_sem.at[i])
        for i, (source, target) in enumerate(loads)
    ]
    bounce_copies = [
        pltpu.make_async_copy(middle, target, load_sem.at[i])
        for i, (_, middle, target) in enumerate(bounce)
    ]
    for copy in load_copies:
        copy.start()
    place.greet()
    for d in early:
        d.start()
    experts.start_x()
    for copy in load_copies:
        copy.wait()
    for copy in bounce_copies:
        copy.start()
    stores = []

    def store(source, target):
        copy = pltpu.make_async_copy(source, target, out_sem.at[len(stores)])
        copy.start()
        stores.append(copy)

    def slot_rows(m, sender):
        return pl.ds(pl.multiple_of((m * owners + sender) * capacity, 16), capacity)

    def exchange(buffer, land, send_sem, recv_sem, m, step):
        return remote(
            buffer.at[step - 1, m],
            land.at[:, slot_rows(m, me)],
            send_sem.at[step - 1, m],
            recv_sem.at[step - 1, m],
            experts=place.peer_owner(step),
        )

    def exchanged(land, recv_sem, m, step):
        sender = lax.rem(me - step + owners, owners)
        arrived(land.at[:, slot_rows(m, sender)], recv_sem.at[step - 1, m])

    def put(buffer, land, m, i, value):
        if i < local_count:
            land[i, slot_rows(m, me), :] = value
        else:
            buffer[i // local_count - 1, m, i % local_count] = value

    def expert_gradients(m):
        g_rows = g_all[pl.ds(m * rows, rows), :]
        for i, hit, weight in one_hots(routes.at[m], gates.at[m], me, local_count, total):
            gate = jnp.sum(jnp.where(hit, weight, 0.0), -1, keepdims=True)
            value = mdot(hit.astype(F32).astype(BF), g_rows)
            put(send_do, do_s, m, i, (gate * value).astype(BF))

    def early_hop(step):
        for d in early:
            d.hop(step)

    for step in range(depth - 2):
        if step < micro_count:
            expert_gradients(step)
        early_hop(step)
    for m in range(max(depth - 2, 0), micro_count):
        expert_gradients(m)
    prompts[0].start()
    early_hop(depth - 2)
    for m in range(micro_count):
        for step in range(1, owners):
            exchange(send_do, do_s, ad_send, ad_recv, m, step).start()
    prompts[0].hop(0)
    for z in range(depth):
        for d in early:
            d.cross(z)
    for step in range(1, depth - 1):
        prompts[0].hop(step)
        if step == 1:
            for prompt_line in prompts[1:]:
                prompt_line.start()
    for z in range(depth):
        for d in early:
            d.finish(z)
    store(wq, qkv_o)
    store(wo, out_o)
    shards = depth * owners
    gain_rows = gain_in.shape[0]
    gain_sum = jnp.zeros((8, features), F32)
    for s in range(shards):
        gain_sum += gain_land[pl.ds(s * gain_rows, gain_rows), :].astype(F32)[:8]
    gain_v[...] = gain_sum
    store(gain_v, gain_o)

    def own_rows(i):
        start = place.z * PB if i == 0 else prompt + (i - 1) * PB
        return start, pl.ds(start if i else pl.multiple_of(start, PB), PB)

    def front(n1, k, v, q, att, hid, lse):
        lse[...] = jnp.zeros_like(lse)
        pairs = features // (2 * HD)

        def prompt_hop(step):
            for prompt_line in prompts[1:]:
                prompt_line.hop(step)
            if step == depth - 2:
                experts.start_z()

        def project_all(m):
            def project(here):
                normed = norm_rows(xk[m, here, :].astype(F32), gain_v[0:1, :])
                n1[m, here, :] = normed
                key = ndot(normed, wq[pl.ds(features, features), :])
                k[m, here, :] = rope(key, cosine[here, :], sine_part[here, :]).astype(BF)
                v[m, here, :] = ndot(normed, wq[pl.ds(2 * features, features), :]).astype(BF)

            tiles(length, 256, project)
            for i in range(rows // PB):
                _, here = own_rows(i)
                query = ndot(n1[m, here, :], wq[pl.ds(0, features), :])
                query = rope(query, cosine[here, :], sine_part[here, :]).astype(BF)
                q[m, pl.ds(i * PB, PB), :] = query * jnp.asarray(HD**-0.5, BF)
        lane = lax.broadcasted_iota(jnp.int32, (PB, 2 * HD), 1)
        for m in range(micro_count):
            project_all(m)

            def pair(index, carry):
                if m == 0:
                    for step in range(depth - 1):
                        pl.when(index == min(step, pairs - 1))(lambda step=step: prompt_hop(step))
                lanes = pl.ds(pl.multiple_of(index * 2 * HD, 2 * HD), 2 * HD)
                for i in range(rows // PB):
                    here = pl.ds(i * PB, PB)
                    query = q[m, here, lanes]
                    seen = prompt + i * PB
                    keys, values = k[m, pl.ds(0, seen), lanes], v[m, pl.ds(0, seen), lanes]
                    column = lax.broadcasted_iota(jnp.int32, (PB, seen), 1)
                    row = lax.broadcasted_iota(jnp.int32, (PB, seen), 0)
                    allowed = column <= row + own_rows(i)[0]
                    parts = []
                    logs = lse[m, here, :]
                    for sub in range(2):
                        only = jnp.where(lane // HD == sub, query, jnp.zeros_like(query))
                        scores = jnp.where(allowed, ndot(only, keys), -1000000000.0)
                        highest = jnp.max(scores, -1, keepdims=True)
                        weights = jnp.exp(scores - highest)
                        sums = jnp.sum(weights, -1, keepdims=True)
                        parts.append(mdot((weights * (1.0 / sums)).astype(BF), values))
                        logs = jnp.where(lane == 2 * index + sub, highest + jnp.log(sums), logs)
                    lse[m, here, :] = logs
                    att[m, here, lanes] = jnp.where(lane < HD, parts[0], parts[1]).astype(BF)
                return carry

            lax.fori_loop(0, pairs, pair, 0)
            if m == 0:
                for copy in bounce_copies:
                    copy.wait()
                for d in late:
                    d.start()
            if m == micro_count - 1:
                experts.hop(0, 0)
                for d in late:
                    d.cross(place.z)
            for i in range(rows // PB):
                here = pl.ds(i * PB, PB)
                hidden = xk[m, own_rows(i)[1], :].astype(F32) + mdot(att[m, here, :], wo[...])
                hid[m, here, :] = hidden
                n2[pl.ds(m * rows + i * PB, PB), :] = norm_rows(hidden, gain_v[1:2, :])
            normed = n2[pl.ds(m * rows, rows), :]
            for i, hit, _ in one_hots(routes.at[m], gates.at[m], me, local_count, total):
                value = mdot(hit.astype(F32).astype(BF), normed)
                put(send_in, in_s, m, i, value.astype(BF))
            for step in range(1, owners):
                exchange(send_in, in_s, ai_send, ai_recv, m, step).start()
        store(n1, n1_o)
        store(k, k_o)
        store(v, v_o)
        store(q, q_o)
        store(att, att_o)
        store(hid, hid_o)
        store(lse, lse_o)
        for copy in stores:
            copy.wait()

    pl.run_scoped(
        front,
        pltpu.VMEM((micro_count, length, features), BF),
        pltpu.VMEM((micro_count, length, features), BF),
        pltpu.VMEM((micro_count, length, features), BF),
        pltpu.VMEM((micro_count, rows, features), BF),
        pltpu.VMEM((micro_count, rows, features), BF),
        pltpu.VMEM((micro_count, rows, features), F32),
        pltpu.VMEM((micro_count, rows, 2 * HD), F32),
    )
    saved = (act_s, dg_s, du_s)
    staged = (stage_g, stage_u, stage_d)

    def chunk_loads(sources, slot):
        return [
            pltpu.make_async_copy(source, buffer.at[slot], chunk_sem.at[slot, kind])
            for kind, (source, buffer) in enumerate(zip(sources, (wg, wu, wd)))
        ]

    def chunk_stores(targets, slot):
        return [
            pltpu.make_async_copy(buffer.at[slot], target, store_sem.at[slot, kind])
            for kind, (target, buffer) in enumerate(zip(targets, staged))
        ]

    def wait_rows():
        for m in range(micro_count):
            for step in range(1, owners):
                exchanged(in_s, ai_recv, m, step)
                exchanged(do_s, ad_recv, m, step)

    at_end = (place.z == 0) | (place.z == depth - 1)
    beside_end = (place.z == 1) | (place.z == depth - 2)

    def sums_to_neighbour(which):
        z = jnp.where(place.z == 0, 1, depth - 2)
        return [
            remote(
                expert_slab(
                    ref, kind, local, (place.other_shard if crossed else place.shard)(z), width
                ),
                land.at[crossed, local],
                pre_send.at[crossed, local, kind],
                pre_recv.at[crossed, local, kind],
                context=z,
            )
            for crossed in which
            for local in range(local_count)
            for kind, (ref, land) in enumerate(
                ((geg_o, pre_g), (geu_o, pre_u), (ged_o, pre_d))
            )
        ]

    def send_sums(crossed):
        def body():
            for copy in sums_to_neighbour((crossed,)):
                copy.start()

        pl.when(at_end)(body)

    def sums_sent():
        for copy in sums_to_neighbour((0, 1)):
            copy.wait_send()

    def sums_arrived():
        for crossed in (1, 0):
            for local in range(local_count):
                for kind, land in enumerate((pre_g, pre_u, pre_d)):
                    arrived(land.at[crossed, local], pre_recv.at[crossed, local, kind])

    def returns(local):
        return [
            pltpu.make_async_copy(source.at[local], target.at[local], out_sem.at[2 + 2 * local + i])
            for i, (source, target) in enumerate(((in_s, outs_o), (do_s, dins_o)))
        ]

    def both(out_sum, in_sum, side_sum, normed_sum):
        out_sum[...] = jnp.zeros_like(out_sum)
        in_sum[...] = jnp.zeros_like(in_sum)
        side_sum[...] = jnp.zeros_like(side_sum)
        normed_sum[...] = jnp.zeros_like(normed_sum)
        group = late[0].own.shape[1] * owners // width

        def store_grads(targets, slot, stored):
            def previous():
                for copy in chunk_stores(targets, slot):
                    copy.wait()

            pl.when(stored)(previous)
            return lambda: [copy.start() for copy in chunk_stores(targets, slot)]

        def shared_part(refs, c):
            here = pl.ds(pl.multiple_of(c * width, 128), width)
            return [refs[0].at[:, here], refs[1].at[:, here], refs[2].at[here]]

        def shared_item(w, z):
            for d in late:
                d.finish(z)

            def one(i, carry):
                c = z * group + i
                loads = chunk_loads(shared_part((sg_o, su_o, sd_o), c), 2 * local_count + i)
                for copy in loads:
                    copy.wait()
                send = store_grads(shared_part((gsg_o, gsu_o, gsd_o), c), i, w > 0)
                ffn_chunk(
                    n2,
                    g_all,
                    [buffer.at[2 * local_count + i] for buffer in (wg, wu, wd)],
                    saved,
                    (side_sum, normed_sum),
                    [buffer.at[i] for buffer in staged],
                    micro_count * rows,
                )
                send()
                return carry

            for i in range(group):
                for copy in chunk_loads(
                    shared_part((sg_o, su_o, sd_o), z * group + i), 2 * local_count + i
                ):
                    copy.start()
            lax.fori_loop(0, group, one, 0)

        def expert_item(w, z, crossed, local, side, ahead):
            shard = jnp.where(crossed, place.other_shard(z), place.shard(z))

            def load(n):
                sources = [
                    expert_slab(ref, k, n, shard, width) for k, ref in enumerate((eg_o, eu_o, ed_o))
                ]
                return chunk_loads(sources, side * local_count + n)

            def begin(n):
                def own():
                    mine = [ref.at[n] for ref in (eg_in, eu_in, ed_in)]
                    for copy in chunk_loads(mine, side * local_count + n):
                        copy.start()

                def landed():
                    pl.when(crossed)(lambda: experts.wait_x(n, z))
                    for copy in load(n):
                        copy.start()

                pl.when(w == 1)(own)
                pl.when(w > 1)(landed)

            def begin_rest():
                for n in range(1, local_count):
                    begin(n)

            pl.when(w == 1)(wait_rows)
            pl.when(local == 0)(lambda: begin(0))
            pl.when(ahead & (local == 0))(begin_rest)
            pl.when(jnp.logical_not(ahead) & (local > 0))(lambda: begin(local))
            for copy in load(local):
                copy.wait()
            targets = [
                expert_slab(ref, k, local, shard, width) for k, ref in enumerate((geg_o, geu_o, ged_o))
            ]
            send = store_grads(targets, local, True)
            ffn_chunk(
                in_s.at[local],
                do_s.at[local],
                [buffer.at[side * local_count + local] for buffer in (wg, wu, wd)],
                saved,
                (out_sum.at[local], in_sum.at[local]),
                [buffer.at[local] for buffer in staged],
                slots,
            )
            send()

        def crossing(step):
            for d in late:
                for z in (place.z - 1 - step, place.z + 1 + step):
                    pl.when(place.on_line(z))(lambda d=d, z=z: d.cross(z))

        def late_hop(step, which=late):
            for d in which:
                d.hop(step)

        heads = 2 * local_count + 1
        in_step = 2 * heads
        after_item = [(local, lambda local=local: experts.hop(local, 0)) for local in range(1, local_count)]
        after_item = [(local - 1, run) for local, run in after_item]
        after_item += [(local_count, lambda: late_hop(0)), (heads - 1, lambda: crossing(0))]
        for step in range(1, depth - 1):
            here = heads + in_step * step
            late_spot, cross_spot = here + 3, here + 5
            if step == depth - 2:
                before = here - in_step
                spots = [(0, before + 3), (0, before + 5), (0, before + 7)]
                spots += [(local, here - 1) for local in range(1, local_count)]
                spots += [(local, here + 1) for local in range(1, local_count)] * 2
                late_spot, cross_spot = here + 5, here + 7
                after_item.append((here + 3, lambda step=step: late_hop(step, late[:1])))
                kinds = {}
                for local, at in spots:
                    kind = kinds.get(local, 0)
                    kinds[local] = kind + 1
                    after_item.append(
                        (at, lambda p=(local, step, (kind,)): experts.hop(*p))
                    )
            else:
                if step == 1:
                    spots = [heads + 3, jnp.where(at_end, here - 1, heads + 5)]
                    late_spot = jnp.where(at_end, here + 3, heads + 7)
                else:
                    spots = [here - 3, here - 1]
                for local in range(local_count):
                    at = spots[min(local, 1)]
                    after_item.append((at, lambda p=(local, step): experts.hop(*p)))
            rest = late[1:] if step == depth - 2 else late
            after_item.append((late_spot, lambda p=(step, rest): late_hop(*p)))
            after_item.append((cross_spot, lambda step=step: crossing(step)))
        after_item.append((heads + in_step - 3, lambda: send_sums(0)))
        after_item.append((heads + in_step - 1, lambda: send_sums(1)))
        count = heads + in_step * (depth - 1)

        def finish(local):
            def convert(here):
                in_s[local, here, :] = out_sum[local, here, :].astype(BF)
                do_s[local, here, :] = in_sum[local, here, :].astype(BF)

            tiles(slots, 256, convert)
            for copy in returns(local):
                copy.start()

        def side_sums():
            return [
                pltpu.make_async_copy(side_sum, side_o, out_sem.at[0]),
                pltpu.make_async_copy(normed_sum, dn2_o, out_sem.at[1]),
            ]

        def finish_routed():
            for local in range(local_count):
                finish(local)

        def early_drain():
            for line in prompts:
                line.drain()
            for d in early:
                d.drain()
            for m in range(micro_count):
                for step in range(1, owners):
                    exchange(send_do, do_s, ad_send, ad_recv, m, step).wait_send()
                    exchange(send_in, in_s, ai_send, ai_recv, m, step).wait_send()

        after_item.append((count - in_step, early_drain))
        after_item.append((count - 3, finish_routed))

        def item(w, carry):
            head = w < heads
            after = jnp.maximum(w - heads, 0)
            step, spot = after // in_step, lax.rem(after, in_step)
            kind = jnp.where(head, w - 1, spot // 2)
            is_shared = kind == jnp.where(head, -1, 2 * local_count)
            crossed = kind >= local_count
            local = jnp.clip(jnp.where(crossed, kind - local_count, kind), 0, local_count - 1)
            z = jnp.where(head, place.z, place.z + (2 * lax.rem(spot, 2) - 1) * (1 + step))
            valid = place.on_line(z)
            pl.when(valid & is_shared)(lambda: shared_item(w, z))
            ahead = head | (step < depth - 2)
            side = jnp.where(head, 0, lax.rem(spot, 2))
            pl.when(valid & jnp.logical_not(is_shared))(
                lambda: expert_item(w, z, crossed, local, side, ahead)
            )
            for at, run in after_item:
                pl.when(w == at)(run)
            return carry

        lax.fori_loop(0, count, item, 0)
        for copy in side_sums():
            copy.start()
        for d in late:
            d.drain()
        experts.drain()
        for local in range(local_count):
            targets = [expert_slab(ref, k, local, 0, width) for k, ref in enumerate((geg_o, geu_o, ged_o))]
            for copy in chunk_stores(targets, local):
                copy.wait()
        for copy in side_sums():
            copy.wait()

    pl.run_scoped(
        both,
        pltpu.VMEM((local_count, slots, features), F32),
        pltpu.VMEM((local_count, slots, features), F32),
        pltpu.VMEM((micro_count * rows, features), F32),
        pltpu.VMEM((micro_count * rows, features), F32),
    )
    for local in range(local_count):
        for copy in returns(local):
            copy.wait()
    pl.when(beside_end)(sums_arrived)
    pl.when(at_end)(sums_sent)


def rope_tables(prompt):
    positions = np.arange(prompt + CONT, dtype=np.float64)
    frequency = 10000.0 ** (-2.0 * np.arange(HD // 2) / HD)
    angles = positions[:, None] * frequency
    cosine, sine_part = np.cos(angles), np.sin(angles)
    return (
        np.concatenate([cosine] * 4, 1).astype(np.float32),
        np.concatenate([-sine_part, sine_part] * 2, 1).astype(np.float32),
    )


def run_forward(sizes, tokens, cot, gates, routes, dense, experts):
    depth, high_count = sizes
    micro_count, rows, features = tokens.shape
    owners = high_count * 2
    line = depth * owners
    prompt = depth * PB
    length = prompt + CONT
    local_count, _, width = experts[0].shape
    hidden_units = dense[3].shape[1] * line
    capacity = rows * 8 // (3 * owners * local_count)
    slots = micro_count * owners * capacity
    cosine, sine_part = rope_tables(prompt)
    hbm, vmem = pl.BlockSpec(memory_space=pltpu.HBM), pl.BlockSpec(memory_space=pltpu.VMEM)

    def shape(dtype, *dims):
        return jax.ShapeDtypeStruct(dims, dtype)

    token_rows = micro_count * rows
    wide, tall = (features, hidden_units), (hidden_units, features)
    out_shape = [
        shape(BF, dense[0].shape[0] * line, features),
        shape(BF, dense[1].shape[0] * line, features),
        shape(F32, 8, features),
        shape(BF, *wide), shape(BF, *wide), shape(BF, *tall),
        shape(BF, local_count, *wide), shape(BF, local_count, *wide), shape(BF, local_count, *tall),
        shape(BF, micro_count, length, features),
        shape(BF, micro_count, length, features),
        shape(BF, micro_count, length, features),
        shape(BF, micro_count, rows, features),
        shape(BF, micro_count, rows, features),
        shape(F32, micro_count, rows, features),
        shape(F32, micro_count, rows, 2 * HD),
        shape(F32, token_rows, features),
        shape(F32, token_rows, features),
        shape(BF, *wide), shape(BF, *wide), shape(BF, *tall),
        shape(BF, local_count, *wide), shape(BF, local_count, *wide), shape(BF, local_count, *tall),
        shape(BF, local_count, slots, features),
        shape(BF, local_count, slots, features),
        shape(BF, 2, local_count, features, width),
        shape(BF, 2, local_count, features, width),
        shape(BF, 2, local_count, width, features),
    ]
    dma = pltpu.SemaphoreType.DMA
    buffers = max(2, local_count)
    loads = 2 * local_count + 2
    send = pltpu.VMEM((owners - 1, micro_count, local_count, capacity, features), BF)
    scratch = [
        pltpu.VMEM((micro_count, length, features), BF),
        pltpu.VMEM(out_shape[0].shape, BF),
        pltpu.VMEM(out_shape[1].shape, BF),
        pltpu.VMEM((dense[2].shape[0] * line, features), BF),
        pltpu.VMEM((8, features), F32),
        pltpu.VMEM((token_rows, features), BF),
        pltpu.VMEM((token_rows, features), BF),
        pltpu.VMEM((local_count, slots, features), BF),
        pltpu.VMEM((local_count, slots, features), BF),
        send,
        send,
        pltpu.VMEM((loads, features, width), BF),
        pltpu.VMEM((loads, features, width), BF),
        pltpu.VMEM((loads, width, features), BF),
        pltpu.VMEM((max(slots, token_rows), width), BF),
        pltpu.VMEM((max(slots, token_rows), width), BF),
        pltpu.VMEM((max(slots, token_rows), width), BF),
        pltpu.VMEM((buffers, features, width), BF),
        pltpu.VMEM((buffers, features, width), BF),
        pltpu.VMEM((buffers, width, features), BF),
    ]
    scratch += DenseGather.semaphores(len(dense), depth, high_count)
    scratch += ExpertGather.semaphores(depth, local_count)
    scratch += [
        dma((micro_count, 2, depth)),
        dma((micro_count, depth)),
        dma((10 + micro_count,)),
        dma((owners - 1, micro_count)),
        dma((owners - 1, micro_count)),
        dma((owners - 1, micro_count)),
        dma((owners - 1, micro_count)),
        dma((loads, 3)),
        dma((buffers, 3)),
        dma((12 + 2 * local_count,)),
        dma((2, local_count, 3)),
        dma((2, local_count, 3)),
    ]
    return pl.pallas_call(
        functools.partial(forward_kernel, sizes),
        out_shape=out_shape,
        in_specs=[hbm] * 2 + [vmem] * 4 + [hbm] * 9,
        out_specs=[hbm] * len(out_shape),
        scratch_shapes=scratch,
        compiler_params=pltpu.CompilerParams(
            collective_id=0, has_side_effects=True, vmem_limit_bytes=60 * MIB
        ),
        name="gather_and_forward",
    )(tokens, cot, gates, routes, cosine, sine_part, *dense, *experts)


def add_into(target, sources, step):
    def body(here):
        value = target[here, :].astype(F32)
        for source in sources:
            value = value + source[here, :].astype(F32)
        target[here, :] = value.astype(target.dtype)

    tiles(target.shape[0], step, body)


class LineSum:
    def __init__(self, place, part, land, send_sem, recv_sem):
        self.place, self.part, self.land = place, part, land
        self.send_sem, self.recv_sem = send_sem, recv_sem

    def copy(self, z, direction):
        place = self.place
        slot = z if direction > 0 else jnp.where(z == place.z - 1, place.depth, z)
        return remote(
            self.part(z),
            self.land(slot),
            self.send_sem.at[z],
            self.recv_sem.at[slot],
            context=place.z + direction,
        )

    def upstream(self, direction):
        return self.place.z > 0 if direction > 0 else self.place.z < self.place.depth - 1

    def arrive(self, slot):
        arrived(self.land(slot), self.recv_sem.at[slot])

    def at(self, direction, step, body):
        z = self.place.z + direction * step
        pl.when(self.place.on_line(z))(lambda: body(z))

    def pass_on(self, direction, step, add):
        def body(z):
            def more():
                self.arrive(z)
                add(self.part(z), self.land(z))

            pl.when(self.upstream(direction))(more)
            self.copy(z, direction).start()

        self.at(direction, step, body)

    def end(self, add):
        for direction, slot in ((1, self.place.z), (-1, self.place.depth)):

            def body(slot=slot):
                self.arrive(slot)
                add(self.part(self.place.z), self.land(slot))

            pl.when(self.upstream(direction))(body)

    def drain(self):
        for step in range(1, self.place.depth):
            for direction in (1, -1):
                self.at(direction, step, lambda z, d=direction: self.copy(z, d).wait_send())


class DenseScatter:
    def __init__(self, place, source, low, high, line, cross, spare, out, sems):
        self.place, self.source, self.spare, self.out = place, source, spare, out
        self.low, self.high, self.cross = low, high, cross
        (
            self.l_send, self.l_recv, self.h_send, self.h_recv, z_send, z_recv,
            self.x_send, self.x_recv, self.own_sem,
        ) = sems
        self.step = min(64, low.shape[2]) if low.shape[2] % 64 == 0 else 16
        self.line = LineSum(
            place, lambda z: low.at[z, place.high], lambda slot: line.at[slot], z_send, z_recv
        )

    @staticmethod
    def semaphores(count, depth, high_count):
        dma = pltpu.SemaphoreType.DMA
        cross = dma((count, depth, high_count))
        return [
            cross, cross, dma((count, high_count)), dma((count, high_count)),
            dma((count, depth + 1)), dma((count, depth + 1)),
            dma((count,)), dma((count,)), dma((count, 2)),
        ]

    def _index(self, z, high, low):
        return (z * self.place.high_count + high) * 2 + low

    def _to_low(self, z, high):
        place = self.place
        return remote(
            self.source(self._index(z, high, 1 - place.low)),
            self.low.at[z, high],
            self.l_send.at[z, high],
            self.l_recv.at[z, high],
            experts=place.e + 1 - 2 * place.low,
        )

    def _each(self, body):
        for z in range(self.place.depth):
            for high in range(self.place.high_count):
                body(z, high)

    def start(self):
        self._each(lambda z, high: self._to_low(z, high).start())

    def add_low(self):
        place = self.place
        places = [(z, high) for z in range(place.depth) for high in range(place.high_count)]

        def load(i):
            z, high = places[i]
            return pltpu.make_async_copy(
                self.source(self._index(z, high, place.low)),
                self.spare.at[i % 2],
                self.own_sem.at[i % 2],
            )

        if self.spare is not None:
            load(0).start()
        for i, (z, high) in enumerate(places):
            self._to_low(z, high).wait_recv()
            if self.spare is None:
                own = self.source(self._index(z, high, place.low))
            else:
                if i + 1 < len(places):
                    load(i + 1).start()
                load(i).wait()
                own = self.spare.at[i % 2]
            add_into(self.low.at[z, high], [own], self.step)
        for step in range(1, place.high_count):
            self._to_high(step).start()

    def _to_high(self, step):
        place = self.place
        peer = place.peer_high(step)
        return remote(
            self.low.at[:, peer],
            self.high.at[step - 1],
            self.h_send.at[step],
            self.h_recv.at[step],
            experts=peer * 2 + place.low,
        )

    def add_high(self):
        place = self.place
        for step in range(1, place.high_count):
            self._to_high(step).wait_recv()
        for z in range(place.depth):
            add_into(
                self.low.at[z, place.high],
                [self.high.at[step - 1, z] for step in range(1, place.high_count)],
                self.step,
            )

    def _add(self, target, more):
        add_into(target, [more], self.step)

    def pass_on(self, direction, step):
        self.line.pass_on(direction, step, self._add)

    def _across(self):
        place = self.place
        return remote(
            self.low.at[place.z, place.high], self.cross, self.x_send, self.x_recv, dp=1 - place.x
        )

    def end(self):
        self.line.end(self._add)
        self._across().start()

    def _store(self):
        return pltpu.make_async_copy(self.cross, self.out, self.own_sem.at[0])

    def finish(self):
        self._across().wait_recv()
        self._add(self.cross, self.low.at[self.place.z, self.place.high])
        self._store().start()

    def drain_first(self):
        self._each(lambda z, high: self._to_low(z, high).wait_send())
        for step in range(1, self.place.high_count):
            self._to_high(step).wait_send()

    def drain(self):
        self.line.drain()
        self._across().wait_send()
        self._store().wait()


class ExpertScatter:
    def __init__(self, place, sums, cross, land, own, more, early, absorbed, outs, sems):
        self.early, self.absorbed = early, absorbed
        self.at_end = (place.z == 0) | (place.z == place.depth - 1)
        self.beside_end = (place.z == 1) | (place.z == place.depth - 2)
        self.place, self.sums, self.cross, self.land = place, sums, cross, land
        self.own, self.more, self.outs = own, more, outs
        self.x_send, self.x_recv, self.z_send, self.z_recv, self.load_sem, self.out_sem = sems
        self.local_count, self.width = cross[0].shape[1], cross[0].shape[3]

    @staticmethod
    def semaphores(depth, local_count):
        dma = pltpu.SemaphoreType.DMA
        return [
            dma((local_count, 3, depth)),
            dma((local_count, 3, depth)),
            dma((local_count, 3, depth + 1)),
            dma((local_count, 3, depth + 1)),
            dma((3, 3)),
            dma((local_count, 3)),
        ]

    def _line(self, local, kind):
        return LineSum(
            self.place,
            lambda z: self.cross[kind].at[z, local],
            lambda slot: self.land[kind].at[slot, local],
            self.z_send.at[local, kind],
            self.z_recv.at[local, kind],
        )

    def _across(self, local, kind, z):
        return remote(
            expert_slab(self.sums[kind], kind, local, self.place.other_shard(z), self.width),
            self.cross[kind].at[z, local],
            self.x_send.at[local, kind, z],
            self.x_recv.at[local, kind, z],
            dp=1 - self.place.x,
        )

    def _order(self, body):
        place = self.place
        for step in range(place.depth - 1, 0, -1):
            for direction in (1, -1):
                z = place.z + direction * step
                here = place.on_line(z)
                if step == 1:
                    here = here & jnp.logical_not(self.at_end)
                pl.when(here)(lambda z=z: body(z))

    def start(self):
        def body(z):
            for local in range(self.local_count):
                for kind in range(3):
                    self._across(local, kind, z).start()

        self._order(body)
        pl.when(jnp.logical_not(self.beside_end))(lambda: body(self.place.z))

    def absorb(self):
        z = self.place.z

        def body():
            for local in range(self.local_count):
                loads = []
                for kind in range(3):
                    source = expert_slab(
                        self.sums[kind], kind, local, self.place.other_shard(z), self.width
                    )
                    early = self.early[kind].at[1, local]
                    loads.append(
                        [
                            pltpu.make_async_copy(source, self.own[kind], self.load_sem.at[0, kind]),
                            pltpu.make_async_copy(
                                early, self.more[kind].at[0], self.load_sem.at[1, kind]
                            ),
                        ]
                    )
                stores = [
                    pltpu.make_async_copy(
                        self.own[kind], self.absorbed[kind].at[local], self.load_sem.at[0, kind]
                    )
                    for kind in range(3)
                ]
                for pair in loads:
                    for copy in pair:
                        copy.start()
                for kind in range(3):
                    for copy in loads[kind]:
                        copy.wait()
                    add_into(self.own[kind], [self.more[kind].at[0]], 64)
                    stores[kind].start()
                for kind in range(3):
                    stores[kind].wait()
                    remote(
                        self.absorbed[kind].at[local],
                        self.cross[kind].at[z, local],
                        self.x_send.at[local, kind, z],
                        self.x_recv.at[local, kind, z],
                        dp=1 - self.place.x,
                    ).start()

        pl.when(self.beside_end)(body)

    def _own_load(self, local, kind, z):
        return pltpu.make_async_copy(
            expert_slab(self.sums[kind], kind, local, self.place.shard(z), self.width),
            self.own[kind],
            self.load_sem.at[0, kind],
        )

    def _more_load(self, local, kind, slot, which):
        return pltpu.make_async_copy(
            self.land[kind].at[slot, local], self.more[kind].at[which], self.load_sem.at[1 + which, kind]
        )

    def pass_on(self, direction, step, local, kinds=(0, 1, 2)):
        def body(z):
            for kind in kinds:
                self._own_load(local, kind, z).start()
            for kind in kinds:
                line = self._line(local, kind)
                target = self.cross[kind].at[z, local]

                def come(line=line, kind=kind):
                    line.arrive(z)
                    self._more_load(local, kind, z, 0).start()

                pl.when(line.upstream(direction))(come)
                self._across(local, kind, z).wait_recv()
                self._own_load(local, kind, z).wait()

                def both(target=target, kind=kind):
                    self._more_load(local, kind, z, 0).wait()
                    add_into(target, [self.own[kind], self.more[kind].at[0]], 64)

                def single(target=target, kind=kind):
                    add_into(target, [self.own[kind]], 64)

                pl.when(line.upstream(direction))(both)
                pl.when(jnp.logical_not(line.upstream(direction)))(single)
                line.copy(z, direction).start()

        def there(z):
            if step == 1:
                pl.when(jnp.logical_not(self.at_end))(lambda: body(z))
            else:
                body(z)

        self._line(local, 0).at(direction, step, there)

    def _early_load(self, local, kind, which):
        return pltpu.make_async_copy(
            self.early[kind].at[0, local], self.more[kind].at[which], self.load_sem.at[1 + which, kind]
        )

    def end(self, local):
        place = self.place
        z = place.z
        for kind in range(3):
            self._own_load(local, kind, z).start()
        for kind in range(3):
            line = self._line(local, kind)
            target = self.cross[kind].at[z, local]
            for which, (direction, slot) in enumerate(((1, z), (-1, place.depth))):

                def come(slot=slot, which=which, line=line, kind=kind):
                    line.arrive(slot)
                    self._more_load(local, kind, slot, which).start()

                def came(which=which, kind=kind):
                    self._early_load(local, kind, which).start()

                from_end = z - direction == (0 if direction > 0 else place.depth - 1)
                pl.when(line.upstream(direction) & jnp.logical_not(from_end))(come)
                pl.when(from_end)(came)
            self._across(local, kind, z).wait_recv()
            self._own_load(local, kind, z).wait()
            add_into(target, [self.own[kind]], 64)
            for which, (direction, slot) in enumerate(((1, z), (-1, place.depth))):

                def more(slot=slot, which=which, kind=kind, target=target):
                    self._more_load(local, kind, slot, which).wait()
                    add_into(target, [self.more[kind].at[which]], 64)

                pl.when(line.upstream(direction))(more)
            self._store(local, kind).start()

    def _store(self, local, kind):
        return pltpu.make_async_copy(
            self.cross[kind].at[self.place.z, local],
            self.outs[kind].at[local],
            self.out_sem.at[local, kind],
        )

    def drain(self):
        for local in range(self.local_count):
            for kind in range(3):
                self._order(lambda z, p=(local, kind): self._across(*p, z).wait_send())
                self._across(local, kind, self.place.z).wait_send()
                line = self._line(local, kind)
                for step in range(1, self.place.depth):
                    for direction in (1, -1):

                        def sent(z, line=line, direction=direction):
                            line.copy(z, direction).wait_send()

                        def there(z, step=step, sent=sent):
                            if step == 1:
                                pl.when(jnp.logical_not(self.at_end))(lambda: sent(z))
                            else:
                                sent(z)

                        line.at(direction, step, there)
                self._store(local, kind).wait()


def backward_kernel(sizes, *refs):
    place = Place(sizes)
    depth, high_count = sizes
    owners = place.owners
    (
        tokens, cot, gates, routes, cosine, sine_part,
        qkv_w, out_w, gain_v, n1_i, k_i, v_i, q_i, att_i, hid_i, lse_i, side_i, dn2_i,
        gsg, gsu, gsd, geg, geu, ged, outs_i, dins_i, pre_g, pre_u, pre_d,
        mixed_o, input_o, gqkv_o, gout_o, gsg_o, gsu_o, gsd_o, geg_o, geu_o, ged_o, gain_o,
        eland_g, eland_u, eland_d, ret_in, ret_out, d_hidden_o, dn1_o, abs_g, abs_u, abs_d,
        *rest,
    ) = refs
    count = 5
    low, rest = rest[:count], rest[count:]
    high, rest = rest[:count], rest[count:]
    line, rest = rest[:count], rest[count:]
    cross, rest = rest[:count], rest[count:]
    (
        spare_w, spare_t, ecross_g, ecross_u, ecross_d, eown_g, eown_u, eown_d,
        emore_g, emore_u, emore_d,
        d_att, dpq, dpk, dpv, g_qkv, g_out, part, part_land,
        gain_own, gain_low, gain_high, gain_line, gain_cross, out_rows,
        *sems,
    ) = rest
    dense_sems, sems = sems[:9], sems[9:]
    expert_sems, sems = sems[:6], sems[6:]
    (
        part_send, part_recv, ri_send, ri_recv, ro_send, ro_recv,
        gain_send, gain_recv, load_sem, wq_sem, out_sem,
    ) = sems
    micro_count, rows, features = tokens.shape
    prompt = depth * PB
    length = prompt + CONT
    local_count, slots = outs_i.shape[0], outs_i.shape[1]
    total = owners * local_count
    capacity = rows * 8 // (3 * total)
    me = place.e

    def rows_of(ref, size):
        return lambda s: ref.at[pl.ds(pl.multiple_of(s * size, 16), size)]

    def columns_of(ref, size):
        return lambda s: ref.at[:, pl.ds(pl.multiple_of(s * size, 128), size)]

    sources = [
        columns_of(gsg, gsg_o.shape[1]),
        columns_of(gsu, gsu_o.shape[1]),
        rows_of(gsd, gsd_o.shape[0]),
        rows_of(g_qkv, gqkv_o.shape[0]),
        rows_of(g_out, gout_o.shape[0]),
    ]
    spares = [spare_w, spare_w, spare_t, None, None]
    dense = [
        DenseScatter(
            place, sources[i], low[i], high[i], line[i], cross[i], spares[i], out,
            [s.at[i] for s in dense_sems],
        )
        for i, out in enumerate((gsg_o, gsu_o, gsd_o, gqkv_o, gout_o))
    ]
    early, late = dense[:3], dense[3:]
    experts = ExpertScatter(
        place,
        (geg, geu, ged),
        (ecross_g, ecross_u, ecross_d),
        (eland_g, eland_u, eland_d),
        (eown_g, eown_u, eown_d),
        (emore_g, emore_u, emore_d),
        (pre_g, pre_u, pre_d),
        (abs_g, abs_u, abs_d),
        (geg_o, geu_o, ged_o),
        expert_sems,
    )
    prompts = [
        LineSum(
            place,
            lambda z, m=m: part.at[m, z],
            lambda slot, m=m: part_land.at[m, slot],
            part_send.at[m],
            part_recv.at[m],
        )
        for m in range(micro_count)
    ]

    def slot_rows(m, owner_of_rows):
        return pl.ds(pl.multiple_of((m * owners + owner_of_rows) * capacity, 16), capacity)

    def hand_back(source, land, send_sem, recv_sem, m, step):
        peer = place.peer_owner(step)
        return remote(
            source.at[:, slot_rows(m, peer)],
            land.at[m, owners - step],
            send_sem.at[step, m],
            recv_sem.at[owners - step, m],
            experts=peer,
        )

    returns = [(dins_i, ret_in, ri_send, ri_recv), (outs_i, ret_out, ro_send, ro_recv)]
    place.greet()
    for m in range(micro_count):
        for step in range(1, owners):
            hand_back(*returns[0], m, step).start()
    for d in early:
        d.start()
    experts.start()

    def fetch(pairs):
        copies = [
            pltpu.make_async_copy(source, target, load_sem.at[i])
            for i, (source, target) in enumerate(pairs)
        ]
        for copy in copies:
            copy.start()
        for copy in copies:
            copy.wait()

    def fetch_returned(source, land, recv_sem, target, m):
        for step in range(1, owners):
            arrived(land.at[m, step], recv_sem.at[step, m])
        pairs = []
        for step in range(owners):
            for local in range(local_count):
                at = pl.ds((step * local_count + local) * capacity, capacity)
                if step == 0:
                    piece = source.at[local, slot_rows(m, me)]
                else:
                    piece = land.at[m, step, local]
                pairs.append((piece, target.at[at]))
        fetch(pairs)

    for kind, d in enumerate(early):
        for direction in (1, -1):
            experts.pass_on(direction, depth - 1, 0, (kind,))
        d.add_low()
    for m in range(micro_count):
        for step in range(1, owners):
            hand_back(*returns[1], m, step).start()
    experts.absorb()
    gain_own[...] = jnp.zeros_like(gain_own)

    def mark_pairs(first, second, m):
        for i, hit, _ in one_hots(routes.at[m], gates.at[m], me, local_count, total):
            here = pl.ds(i * capacity, capacity)
            expert = lax.rem(me * local_count + i, total)
            hit_first = either(hit, routes[m, 0:1, :] == expert)
            hit_second = either(hit, routes[m, 1:2, :] == expert)
            first[here, :] = hit_first.astype(F32).astype(BF)
            second[here, :] = hit_second.astype(F32).astype(BF)

    def after_experts(hidden, extra, back, first, second, g_rows, att, d_attn, wo):
        fetch([(out_w, wo)] + [(att_i.at[m], att.at[pl.ds(m * rows, rows)]) for m in range(micro_count)])
        for m in range(micro_count):
            fetch([(hid_i.at[m], hidden), (cot.at[m], g_rows), (dn2_i.at[pl.ds(m * rows, rows)], extra)])
            mark_pairs(first, second, m)
            fetch_returned(dins_i, ret_in, ri_recv, back, m)
            gain = gain_v[1:2, :]
            for i in range(rows // PB):
                here = pl.ds(i * PB, PB)
                both = first[:, here] + second[:, here]
                d_normed = extra[here, :] + tdot(both, back[...])
                values = hidden[here, :]
                root = lax.rsqrt(jnp.mean(values * values, -1, keepdims=True) + EPSILON)
                scaled = gain * d_normed
                d_values = (
                    g_rows[here, :].astype(F32)
                    + root * scaled
                    - values * (root * root * root) * jnp.mean(values * scaled, -1, keepdims=True)
                )
                gain_own[1:2, :] += jnp.sum(d_normed * values * root, 0, keepdims=True)
                there = pl.ds(m * rows + i * PB, PB)
                extra[here, :] = d_values
                low_part = d_values.astype(BF)
                d_attn[there, :] = low_part
                d_att[there, :] = ndot(low_part, wo[...]).astype(BF)
            fetch([(extra, d_hidden_o.at[m])])
            for kind in ((0,), (1, 2))[m] if m < 2 else ():
                for direction in (1, -1):
                    experts.pass_on(direction, depth - 1, 1, (kind,))

        def out_grad(here):
            g_out[here, :] = tdot(att[:, here], d_attn[...]).astype(BF)

        tiles(features, 256, out_grad)

    pl.run_scoped(
        after_experts,
        pltpu.VMEM((rows, features), F32),
        pltpu.VMEM((rows, features), F32),
        pltpu.VMEM((total * capacity, features), BF),
        pltpu.VMEM((total * capacity, rows), BF),
        pltpu.VMEM((total * capacity, rows), BF),
        pltpu.VMEM((rows, features), BF),
        pltpu.VMEM((micro_count * rows, features), BF),
        pltpu.VMEM((micro_count * rows, features), BF),
        pltpu.VMEM((features, features), BF),
    )

    def both_ways(items, step):
        for direction in (1, -1):
            for item in items:
                item.pass_on(direction, step)

    def prompts_on(m, step):
        for direction in (1, -1):
            prompts[m].pass_on(direction, step, lambda t, s: add_into(t, [s], 64))

    def experts_on(step, local, where=True, kinds=(0, 1, 2)):
        def body():
            for direction in (1, -1):
                experts.pass_on(direction, step, local, kinds)

        pl.when(where)(body)

    inside = jnp.logical_not(experts.at_end)
    experts_on(depth - 2, 0, inside)

    def own_rows(i):
        start = place.z * PB if i == 0 else prompt + (i - 1) * PB
        return start, pl.ds(start if i else pl.multiple_of(start, PB), PB)

    def attention(k, v, q, lse, ds_s, p_s, wq, dn1):
        load_wq = pltpu.make_async_copy(qkv_w, wq, wq_sem.at[0])
        load_wq.start()
        lane = lax.broadcasted_iota(jnp.int32, (PB, 2 * HD), 1)
        wide_lane = lax.broadcasted_iota(jnp.int32, (rows, 2 * HD), 1)
        pairs = features // (2 * HD)
        ds_s[...] = jnp.zeros_like(ds_s)
        p_s[...] = jnp.zeros_like(p_s)
        for m in range(micro_count):
            fetch([(k_i.at[m], k), (v_i.at[m], v), (q_i.at[m], q), (lse_i.at[m], lse)])
            whole = pl.ds(m * rows, rows)

            def pair(index, carry):
                for kind in range(3):

                    def pass_some(kind=kind):
                        experts_on(depth - 2, m, experts.at_end, (kind,))
                        if m == 0:
                            experts_on(depth - 2, 1, inside, (kind,))

                    pl.when(index == min(2 * kind + 1, pairs - 1))(pass_some)
                lanes = pl.ds(pl.multiple_of(index * 2 * HD, 2 * HD), 2 * HD)
                for i in range(rows // PB):
                    here = pl.ds(i * PB, PB)
                    there = pl.ds(m * rows + i * PB, PB)
                    query, d_out, logs = q[here, lanes], d_att[there, lanes], lse[here, :]
                    start, table = own_rows(i)
                    seen = prompt + i * PB
                    keys, values = k[pl.ds(0, seen), lanes], v[pl.ds(0, seen), lanes]
                    column = lax.broadcasted_iota(jnp.int32, (PB, seen), 1)
                    row = lax.broadcasted_iota(jnp.int32, (PB, seen), 0)
                    allowed = column <= row + start
                    parts = []
                    for sub in range(2):
                        mine = lane // HD == sub
                        scores = ndot(jnp.where(mine, query, jnp.zeros_like(query)), keys)
                        log = jnp.sum(
                            jnp.where(lane == 2 * index + sub, logs, 0.0), -1, keepdims=True
                        )
                        probs = jnp.where(allowed, jnp.exp(scores - log), 0.0)
                        d_probs = ndot(jnp.where(mine, d_out, jnp.zeros_like(d_out)), values)
                        centre = jnp.sum(probs * d_probs, -1, keepdims=True)
                        d_scores = (probs * (d_probs - centre)).astype(BF)
                        ds_s[sub, here, pl.ds(0, seen)] = d_scores
                        p_s[sub, here, pl.ds(0, seen)] = probs.astype(BF)
                        parts.append(mdot(d_scores, keys))
                    d_query = jnp.where(lane < HD, parts[0], parts[1]) * HD**-0.5
                    d_query = rope(d_query, cosine[table, :], -sine_part[table, :])
                    dpq[there, lanes] = d_query.astype(BF)
                d_key = jnp.zeros((length, 2 * HD), F32)
                d_value = jnp.zeros((length, 2 * HD), F32)
                query, d_out = q[:, lanes], d_att[whole, lanes]
                for sub in range(2):
                    mine = wide_lane // HD == sub
                    d_key += tdot(ds_s[sub], jnp.where(mine, query, jnp.zeros_like(query)))
                    d_value += tdot(p_s[sub], jnp.where(mine, d_out, jnp.zeros_like(d_out)))
                keys_here = pl.ds(m * length, length)
                d_key = rope(d_key, cosine[...], -sine_part[...])
                dpk[keys_here, lanes] = d_key.astype(BF)
                dpv[keys_here, lanes] = d_value.astype(BF)
                return carry

            lax.fori_loop(0, pairs, pair, 0)
            if m == 0:
                load_wq.wait()
            key_w, value_w = wq[pl.ds(features, features), :], wq[pl.ds(2 * features, features), :]
            for z in range(depth):
                here = pl.ds(m * length + z * PB, PB)
                part[m, z] = (mdot(dpk[here, :], key_w) + mdot(dpv[here, :], value_w)).astype(BF)
            prompts_on(m, depth - 1)
            for i in range(rows // PB):
                _, table = own_rows(i)
                start = own_rows(i)[0] + m * length
                here = pl.ds(pl.multiple_of(start, PB), PB)
                there = pl.ds(m * rows + i * PB, PB)
                dn1[pl.ds(i * PB, PB), :] = (
                    mdot(dpq[there, :], wq[pl.ds(0, features), :])
                    + mdot(dpk[here, :], key_w)
                    + mdot(dpv[here, :], value_w)
                )
            fetch([(dn1, dn1_o.at[m])])
            if m == 0:
                for d in early:
                    d.add_high()
                both_ways(early, depth - 1)

    pl.run_scoped(
        attention,
        pltpu.VMEM((length, features), BF),
        pltpu.VMEM((length, features), BF),
        pltpu.VMEM((rows, features), BF),
        pltpu.VMEM((rows, 2 * HD), F32),
        pltpu.VMEM((2, rows, length), BF),
        pltpu.VMEM((2, rows, length), BF),
        pltpu.VMEM(qkv_w.shape, BF),
        pltpu.VMEM((rows, features), F32),
    )

    def weight_grads(n1, n1_own):
        pairs = []
        for m in range(micro_count):
            pairs.append((n1_i.at[m], n1.at[pl.ds(m * length, length)]))
            for i in range(rows // PB):
                _, here = own_rows(i)
                pairs.append((n1_i.at[m, here], n1_own.at[pl.ds(m * rows + i * PB, PB)]))
        fetch(pairs)

        def make(here):
            g_qkv[here, :] = tdot(dpq[:, here], n1_own[...]).astype(BF)

        def make_key(here):
            there = pl.ds(pl.multiple_of(here.start + features, 256), 256)
            g_qkv[there, :] = tdot(dpk[:, here], n1[...]).astype(BF)

        def make_value(here):
            there = pl.ds(pl.multiple_of(here.start + 2 * features, 256), 256)
            g_qkv[there, :] = tdot(dpv[:, here], n1[...]).astype(BF)

        tiles(features, 256, make)
        tiles(features, 256, make_key)
        tiles(features, 256, make_value)

    pl.run_scoped(
        weight_grads,
        pltpu.VMEM((micro_count * length, features), BF),
        pltpu.VMEM((micro_count * rows, features), BF),
    )
    for d in late:
        d.start()

    for d in late:
        d.add_low()

    def column_of(values):
        dims = (values.shape[1], values.shape[1])
        across = lax.broadcasted_iota(jnp.int32, dims, 1)
        diagonal = lax.broadcasted_iota(jnp.int32, dims, 0) == across
        return jnp.sum(jnp.where(diagonal, values, 0.0), -1, keepdims=True)

    def outputs(hidden, side, back, first, second):
        for m in range(micro_count):
            fetch([(hid_i.at[m], hidden), (side_i.at[pl.ds(m * rows, rows)], side)])
            mark_pairs(first, second, m)
            fetch_returned(outs_i, ret_out, ro_recv, back, m)
            for i in range(rows // PB):
                here = pl.ds(i * PB, PB)
                routed = column_of(gates[m, 0:1, here]) * tdot(first[:, here], back[...])
                routed += column_of(gates[m, 1:2, here]) * tdot(second[:, here], back[...])
                out_rows[here, :] = (hidden[here, :] + side[here, :] + routed).astype(BF)
            fetch([(out_rows, mixed_o.at[m])])
            if m == 0:
                for step in range(depth - 2, 1, -1):
                    for n in range(micro_count):
                        prompts_on(n, step)
                    both_ways(early, step)
                for step in range(depth - 3, 0, -1):
                    experts_on(step, 0)

    pl.run_scoped(
        outputs,
        pltpu.VMEM((rows, features), F32),
        pltpu.VMEM((rows, features), F32),
        pltpu.VMEM((total * capacity, features), BF),
        pltpu.VMEM((total * capacity, rows), BF),
        pltpu.VMEM((total * capacity, rows), BF),
    )

    def last_on(kind):
        for step in range(depth - 3, 0, -1):
            for local in range(1, local_count):
                for direction in (1, -1):
                    experts.pass_on(direction, step, local, (kind,))

    for d in late:
        d.add_high()
    both_ways(late, depth - 1)
    for m in range(micro_count):
        prompts_on(m, 1)
    for step in range(depth - 2, 1, -1):
        both_ways(late, step)
    both_ways(early, 1)
    last_on(0)
    last_on(1)

    def inputs(x_rows, d_hidden, dn1):
        for m in range(micro_count):
            fetch([(tokens.at[m], x_rows), (d_hidden_o.at[m], d_hidden), (dn1_o.at[m], dn1)])
            for direction, slot in ((1, place.z), (-1, depth)):

                def body(m=m, slot=slot):
                    prompts[m].arrive(slot)
                    dn1[pl.ds(0, PB), :] += part_land[m, slot].astype(F32)

                pl.when(prompts[m].upstream(direction))(body)
            gain = gain_v[0:1, :]
            for i in range(rows // PB):
                here = pl.ds(i * PB, PB)
                values, d_normed = x_rows[here, :].astype(F32), dn1[here, :]
                root = lax.rsqrt(jnp.mean(values * values, -1, keepdims=True) + EPSILON)
                scaled = gain * d_normed
                d_values = (
                    d_hidden[here, :]
                    + root * scaled
                    - values * (root * root * root) * jnp.mean(values * scaled, -1, keepdims=True)
                )
                gain_own[0:1, :] += jnp.sum(d_normed * values * root, 0, keepdims=True)
                out_rows[here, :] = d_values.astype(BF)
            fetch([(out_rows, input_o.at[m])])

    pl.run_scoped(
        inputs,
        pltpu.VMEM((rows, features), BF),
        pltpu.VMEM((rows, features), F32),
        pltpu.VMEM((rows, features), F32),
    )
    def gain_copies(first, targets, lands):
        return [
            remote(gain_own, land, gain_send.at[first + i], gain_recv.at[first + i], **target)
            for i, (target, land) in enumerate(zip(targets, lands))
        ]

    def gain_add(copies, lands):
        for copy in copies:
            copy.wait()
        total_gain = gain_own[...]
        for land in lands:
            total_gain = total_gain + land[...]
        gain_own[...] = total_gain

    peers = range(1, high_count)
    places = range(1, depth)
    stages = [
        (0, [dict(experts=place.e + 1 - 2 * place.low)], [gain_low]),
        (
            1,
            [dict(experts=place.peer_high(s) * 2 + place.low) for s in peers],
            [gain_high.at[s - 1] for s in peers],
        ),
        (
            high_count,
            [dict(context=lax.rem(place.z + s, depth)) for s in places],
            [gain_line.at[s - 1] for s in places],
        ),
        (high_count + depth - 1, [dict(dp=1 - place.x)], [gain_cross]),
    ]

    def gain_start(i):
        copies = gain_copies(*stages[i])
        for copy in copies:
            copy.start()
        return copies

    copies = gain_start(0)
    both_ways(late, 1)
    gain_add(copies, stages[0][2])
    copies = gain_start(1)
    last_on(2)
    gain_add(copies, stages[1][2])
    copies = gain_start(3)
    for d in early:
        d.end()

    experts.end(0)
    for d in dense:
        d.drain_first()
    for m in range(micro_count):
        for step in range(1, owners):
            for entry in returns:
                hand_back(*entry, m, step).wait_send()
    gain_add(copies, stages[3][2])
    copies = gain_start(2)
    for d in late:
        d.end()
    for local in range(1, local_count):
        experts.end(local)
    for d in early:
        d.finish()
    for d in late:
        d.finish()
    gain_add(copies, stages[2][2])
    fetch([(gain_own, gain_o)])
    for d in dense:
        d.drain()
    experts.drain()
    for p in prompts:
        p.drain()


def run_backward(sizes, tokens, cot, gates, routes, forward):
    depth, high_count = sizes
    micro_count, rows, features = tokens.shape
    owners = high_count * 2
    line = depth * owners
    prompt = depth * PB
    length = prompt + CONT
    cosine, sine_part = rope_tables(prompt)
    gsg, geg, outs = forward[12], forward[15], forward[18]
    local_count, slots, _ = outs.shape
    total = owners * local_count
    capacity = rows * 8 // (3 * total)
    part = gsg.shape[1] // line
    width = geg.shape[2] // (2 * depth)
    hbm, vmem = pl.BlockSpec(memory_space=pltpu.HBM), pl.BlockSpec(memory_space=pltpu.VMEM)
    shapes = [(features, part), (features, part), (part, features)]
    shapes += [(forward[0].shape[0] // line, features), (forward[1].shape[0] // line, features)]
    expert_shapes = [(features, width), (features, width), (width, features)]
    returned = (micro_count, owners, local_count, capacity, features)
    out_dims = [(micro_count, rows, features)] * 2
    out_dims += [shapes[3], shapes[4], shapes[0], shapes[1], shapes[2]]
    out_dims += [(local_count,) + s for s in expert_shapes]
    out_shape = [jax.ShapeDtypeStruct(dims, BF) for dims in out_dims]
    out_shape += [jax.ShapeDtypeStruct((8, features), F32)]
    out_shape += [jax.ShapeDtypeStruct((depth + 1, local_count) + s, BF) for s in expert_shapes]
    out_shape += [jax.ShapeDtypeStruct(returned, BF)] * 2
    out_shape += [jax.ShapeDtypeStruct((micro_count, rows, features), F32)] * 2
    out_shape += [jax.ShapeDtypeStruct((local_count,) + s, BF) for s in expert_shapes]
    scratch = [pltpu.VMEM((depth, high_count) + s, BF) for s in shapes]
    scratch += [pltpu.VMEM((high_count - 1, depth) + s, BF) for s in shapes]
    scratch += [pltpu.VMEM((depth + 1,) + s, BF) for s in shapes]
    scratch += [pltpu.VMEM(s, BF) for s in shapes]
    scratch += [pltpu.VMEM((2,) + shapes[0], BF), pltpu.VMEM((2,) + shapes[2], BF)]
    scratch += [pltpu.VMEM((depth, local_count) + s, BF) for s in expert_shapes]
    scratch += [pltpu.VMEM(s, BF) for s in expert_shapes]
    scratch += [pltpu.VMEM((2,) + s, BF) for s in expert_shapes]
    token_rows, key_rows = micro_count * rows, micro_count * length
    gain = (8, features)
    scratch += [
        pltpu.VMEM((token_rows, features), BF),
        pltpu.VMEM((token_rows, features), BF),
        pltpu.VMEM((key_rows, features), BF),
        pltpu.VMEM((key_rows, features), BF),
        pltpu.VMEM(forward[0].shape, BF),
        pltpu.VMEM(forward[1].shape, BF),
        pltpu.VMEM((micro_count, depth, PB, features), BF),
        pltpu.VMEM((micro_count, depth + 1, PB, features), BF),
        pltpu.VMEM(gain, F32),
        pltpu.VMEM(gain, F32),
        pltpu.VMEM((high_count - 1,) + gain, F32),
        pltpu.VMEM((depth - 1,) + gain, F32),
        pltpu.VMEM(gain, F32),
        pltpu.VMEM((rows, features), BF),
    ]
    dma = pltpu.SemaphoreType.DMA
    scratch += DenseScatter.semaphores(len(shapes), depth, high_count)
    scratch += ExpertScatter.semaphores(depth, local_count)
    stages = 1 + high_count + depth
    scratch += [
        dma((micro_count, depth + 1)),
        dma((micro_count, depth + 1)),
        dma((owners, micro_count)),
        dma((owners, micro_count)),
        dma((owners, micro_count)),
        dma((owners, micro_count)),
        dma((stages,)),
        dma((stages,)),
        dma((max(total, 2 + micro_count, 4 * micro_count + micro_count),)),
        dma((1,)),
        dma((1,)),
    ]
    return pl.pallas_call(
        functools.partial(backward_kernel, sizes),
        out_shape=out_shape,
        in_specs=[hbm] * 2 + [vmem] * 4 + [hbm] * 2 + [vmem] + [hbm] * 20,
        out_specs=[hbm] * len(out_shape),
        scratch_shapes=scratch,
        compiler_params=pltpu.CompilerParams(
            collective_id=1, has_side_effects=True, vmem_limit_bytes=60 * MIB
        ),
        name="backward_and_sum",
    )(tokens, cot, gates, routes, cosine, sine_part, *forward)


def finish_kernel(count, gain_width, *refs):
    low, refs = refs[:count], refs[count:]
    rows, refs = refs[:2], refs[2:]
    gain, refs = refs[0], refs[1:]
    rows_o, refs = refs[:2], refs[2:]
    wide_o, refs = refs[:count], refs[count:]
    gain_o, refs = refs[0], refs[1:]
    low_s, refs = refs[:count], refs[count:]
    wide_s, refs = refs[:count], refs[count:]
    rows_s, sem_in, sem_out = refs[:2], refs[2], refs[3]
    loads = [
        pltpu.make_async_copy(source, target, sem_in.at[i])
        for i, (source, target) in enumerate(zip(low + rows, low_s + rows_s))
    ]
    for copy in loads:
        copy.start()
    stores = [
        pltpu.make_async_copy(source, target, sem_out.at[i])
        for i, (source, target) in enumerate(zip(wide_s + rows_s, wide_o + rows_o))
    ]
    place = (lax.axis_index(CONTEXT) * lax.axis_size(EXPERTS) + lax.axis_index(EXPERTS)) * gain_width
    features = gain.shape[1]
    gain_o[...] = pltpu.roll(gain[...], lax.rem(features - place, features), 1)[:2, :gain_width]
    for i in range(count):
        loads[i].wait()
        wide_s[i][...] = low_s[i][...].astype(F32)
        stores[i].start()
    for i in range(count, count + 2):
        loads[i].wait()
        stores[i].start()
    for copy in stores:
        copy.wait()


def finish_outputs(low, rows, gain, gain_width):
    count = len(low)
    hbm, vmem = pl.BlockSpec(memory_space=pltpu.HBM), pl.BlockSpec(memory_space=pltpu.VMEM)
    wide = [item.shape for item in low]
    out_shape = [jax.ShapeDtypeStruct(item.shape, BF) for item in rows]
    out_shape += [jax.ShapeDtypeStruct(dims, F32) for dims in wide]
    out_shape += [jax.ShapeDtypeStruct((2, gain_width), F32)]
    dma = pltpu.SemaphoreType.DMA
    return pl.pallas_call(
        functools.partial(finish_kernel, count, gain_width),
        out_shape=out_shape,
        in_specs=[hbm] * (count + 2) + [vmem],
        out_specs=[hbm] * (count + 2) + [vmem],
        scratch_shapes=[pltpu.VMEM(item.shape, BF) for item in low]
        + [pltpu.VMEM(dims, F32) for dims in wide]
        + [pltpu.VMEM(item.shape, BF) for item in rows]
        + [dma((count + 2,)), dma((count + 2,))],
        compiler_params=pltpu.CompilerParams(vmem_limit_bytes=60 * MIB),
        name="finish_outputs",
    )(*low, *rows, gain)


def on_device_plain(
    tokens,
    cotangent,
    gates,
    routes,
    qkv_weight,
    out_weight,
    shared_gate,
    shared_up,
    shared_down,
    gains,
    expert_gate,
    expert_up,
    expert_down,
):
    micro_count = tokens.shape[2]
    row_count = tokens.shape[4]
    feature_count = tokens.shape[5]
    owners = lax.axis_size(EXPERTS)
    local_experts = expert_gate.shape[0]
    total_experts = owners * local_experts
    capacity = row_count * 8 // (3 * total_experts)
    blocks = lax.axis_size(CONTEXT)
    prompt = blocks * PB
    scaling = HD ** (-0.5)
    w_qkv, w_out, w_sgate, w_sup, w_sdown, w_gains = (
        lax.all_gather(qkv_weight, (CONTEXT, EXPERTS), axis=1, tiled=True),
        lax.all_gather(out_weight, (CONTEXT, EXPERTS), axis=0, tiled=True),
        lax.all_gather(shared_gate, (CONTEXT, EXPERTS), axis=1, tiled=True),
        lax.all_gather(shared_up, (CONTEXT, EXPERTS), axis=1, tiled=True),
        lax.all_gather(shared_down, (CONTEXT, EXPERTS), axis=0, tiled=True),
        lax.all_gather(gains, (CONTEXT, EXPERTS), axis=1, tiled=True),
    )
    e_gate, expert_up_weight, e_down = (
        lax.all_gather(expert_gate, (DP, CONTEXT), axis=2, tiled=True),
        lax.all_gather(expert_up, (DP, CONTEXT), axis=2, tiled=True),
        lax.all_gather(expert_down, (DP, CONTEXT), axis=1, tiled=True),
    )
    gain_one = w_gains[0].astype(jnp.float32)
    gain_two = w_gains[1].astype(jnp.float32)
    here_index = lax.axis_index(CONTEXT)
    row_ids = jnp.arange(row_count, dtype=jnp.int32)
    query_pos = jnp.where(row_ids < PB, here_index * PB + row_ids, prompt + row_ids - PB)
    key_pos = jnp.arange(prompt + CONT, dtype=jnp.int32)
    allowed = key_pos[None, None, :] <= query_pos[None, :, None]
    half_size = HD // 2
    frequency = 10000.0 ** (-2.0 * jnp.arange(half_size, dtype=jnp.float32) / HD)
    angles = query_pos.astype(jnp.float32)[:, None] * frequency
    cosine = jnp.cos(angles)[:, None, :]
    sine_part = jnp.sin(angles)[:, None, :]
    kept_list = []
    mixed_list = []
    for step_index in range(micro_count):
        inputs = tokens[0, 0, step_index, 0].astype(jnp.float32)
        root_one = lax.rsqrt(jnp.mean(inputs * inputs, -1, keepdims=True) + EPSILON)
        normed_one = (inputs * root_one * gain_one).astype(jnp.bfloat16)
        projected = mdot(normed_one, w_qkv)
        query = rotate(projected[:, :feature_count], cosine, sine_part).astype(jnp.bfloat16)
        key_rows = rotate(
            projected[:, feature_count : 2 * feature_count], cosine, sine_part
        ).astype(jnp.bfloat16)
        value_rows = projected[:, 2 * feature_count :].astype(jnp.bfloat16)
        prompt_key, prompt_value = (
            lax.all_gather(key_rows[:PB], CONTEXT, axis=0, tiled=True),
            lax.all_gather(value_rows[:PB], CONTEXT, axis=0, tiled=True),
        )
        key_heads = jnp.concatenate([prompt_key, key_rows[PB:]], 0).reshape(prompt + CONT, H, HD)
        value_heads = jnp.concatenate([prompt_value, value_rows[PB:]], 0).reshape(
            prompt + CONT, H, HD
        )
        query_heads = query.reshape(row_count, H, HD)
        scores = (
            jnp.einsum("qhd,khd->hqk", query_heads, key_heads, preferred_element_type=jnp.float32)
            * scaling
        )
        scores = jnp.where(allowed, scores, -1000000000.0)
        highest = jnp.max(scores, -1, keepdims=True)
        weights = jnp.exp(scores - highest)
        total = jnp.sum(weights, -1, keepdims=True)
        log_total = highest + jnp.log(total)
        probs = (weights / total).astype(jnp.bfloat16)
        attended = (
            jnp.einsum("hqk,khd->qhd", probs, value_heads, preferred_element_type=jnp.float32)
            .reshape(row_count, feature_count)
            .astype(jnp.bfloat16)
        )
        hidden = inputs + mdot(attended, w_out)
        root_two = lax.rsqrt(jnp.mean(hidden * hidden, -1, keepdims=True) + EPSILON)
        normed_two = (hidden * root_two * gain_two).astype(jnp.bfloat16)
        side_gate = mdot(normed_two, w_sgate)
        side_up = mdot(normed_two, w_sup)
        side_act = (jax.nn.silu(side_gate) * side_up).astype(jnp.bfloat16)
        side = mdot(side_act, w_sdown)
        route_rows = routes[0, 0, step_index, 0]
        slots = slot_table(route_rows, total_experts)
        flat_dest = (route_rows * capacity + slots).reshape(-1)
        source = (
            jnp.full((total_experts * capacity,), 2 * row_count, jnp.int32)
            .at[flat_dest]
            .set(jnp.arange(2 * row_count, dtype=jnp.int32))
        )
        padded = jnp.concatenate([normed_two, jnp.zeros((1, feature_count), jnp.bfloat16)], 0)
        send = padded[source // 2].reshape(total_experts, capacity, feature_count)
        received = lax.all_to_all(send, EXPERTS, split_axis=0, concat_axis=0, tiled=True)
        count = received.shape[1]
        expert_grouped = received.reshape(owners, local_experts, count, feature_count)
        expert_gate_act = jnp.einsum(
            "send,edf->senf", expert_grouped, e_gate, preferred_element_type=jnp.float32
        )
        expert_up_act = jnp.einsum(
            "send,edf->senf", expert_grouped, expert_up_weight, preferred_element_type=jnp.float32
        )
        expert_hidden_act = (jax.nn.silu(expert_gate_act) * expert_up_act).astype(jnp.bfloat16)
        result = jnp.einsum(
            "senf,efd->send", expert_hidden_act, e_down, preferred_element_type=jnp.float32
        ).astype(jnp.bfloat16)
        expert_out = result.reshape(owners * local_experts, count, feature_count)
        expert_in = received
        returned = lax.all_to_all(
            expert_out, EXPERTS, split_axis=0, concat_axis=0, tiled=True
        ).reshape(-1, feature_count)
        gate_rows = gates[0, 0, step_index, 0]
        picked = returned[flat_dest].reshape(row_count, 2, feature_count).astype(jnp.float32)
        routed = jnp.sum(gate_rows[:, :, None] * picked, 1)
        mixed_list.append((hidden + routed + side).astype(jnp.bfloat16))
        cached = (prompt_key, prompt_value)
        kept_list.append(
            (
                inputs,
                root_one,
                normed_one,
                query,
                key_rows,
                value_rows,
                cached,
                log_total,
                attended,
                hidden,
                root_two,
                normed_two,
                side_gate,
                side_up,
                side_act,
                flat_dest,
                source,
                expert_in,
                gate_rows,
            )
        )
    acc_qkv = jnp.zeros(w_qkv.shape, jnp.float32)
    acc_out = jnp.zeros(w_out.shape, jnp.float32)
    acc_sgate = jnp.zeros(w_sgate.shape, jnp.float32)
    acc_sup = jnp.zeros(w_sup.shape, jnp.float32)
    acc_sdown = jnp.zeros(w_sdown.shape, jnp.float32)
    acc_gain_one = jnp.zeros((feature_count,), jnp.float32)
    acc_gain_two = jnp.zeros((feature_count,), jnp.float32)
    local_egate = jnp.zeros(e_gate.shape, jnp.float32)
    local_expert_up_weight = jnp.zeros(expert_up_weight.shape, jnp.float32)
    local_edown = jnp.zeros(e_down.shape, jnp.float32)
    input_list = []
    for step_index in range(micro_count):
        (
            inputs,
            root_one,
            normed_one,
            query,
            key_rows,
            value_rows,
            cached,
            log_total,
            attended,
            hidden,
            root_two,
            normed_two,
            side_gate,
            side_up,
            side_act,
            flat_dest,
            source,
            expert_in,
            gate_rows,
        ) = kept_list[step_index]
        grad_rows = cotangent[0, 0, step_index, 0].astype(jnp.float32)
        grad_low = grad_rows.astype(jnp.bfloat16)
        acc_sdown = acc_sdown + tdot(side_act, grad_low)
        d_side_act = ndot(grad_low, w_sdown).astype(jnp.bfloat16).astype(jnp.float32)
        silu_side, slope_side = silu_parts(side_gate)
        d_side_gate = (d_side_act * side_up * slope_side).astype(jnp.bfloat16)
        d_side_up = (d_side_act * silu_side).astype(jnp.bfloat16)
        acc_sgate = acc_sgate + tdot(normed_two, d_side_gate)
        acc_sup = acc_sup + tdot(normed_two, d_side_up)
        d_normed_two = ndot(d_side_gate, w_sgate) + ndot(d_side_up, w_sup)
        d_pairs = (
            (gate_rows[:, :, None] * grad_rows[:, None, :])
            .astype(jnp.bfloat16)
            .reshape(2 * row_count, feature_count)
        )
        padded_grad = jnp.concatenate([d_pairs, jnp.zeros((1, feature_count), jnp.bfloat16)], 0)
        grad_send = padded_grad[source].reshape(total_experts, capacity, feature_count)
        grad_in = lax.all_to_all(grad_send, EXPERTS, split_axis=0, concat_axis=0, tiled=True)
        grouped_grad = grad_in.reshape(owners, local_experts, capacity, feature_count)
        grouped = expert_in.reshape(owners, local_experts, capacity, feature_count)
        gate_act = jnp.einsum("send,edf->senf", grouped, e_gate, preferred_element_type=jnp.float32)
        up_act = jnp.einsum(
            "send,edf->senf", grouped, expert_up_weight, preferred_element_type=jnp.float32
        )
        silu_gate, slope_gate = silu_parts(gate_act)
        hidden_act = (silu_gate * up_act).astype(jnp.bfloat16)
        d_hidden_act = (
            jnp.einsum("send,efd->senf", grouped_grad, e_down, preferred_element_type=jnp.float32)
            .astype(jnp.bfloat16)
            .astype(jnp.float32)
        )
        d_gate_act = (d_hidden_act * up_act * slope_gate).astype(jnp.bfloat16)
        d_up_act = (d_hidden_act * silu_gate).astype(jnp.bfloat16)
        step_edown = jnp.einsum(
            "senf,send->efd", hidden_act, grouped_grad, preferred_element_type=jnp.float32
        )
        step_egate = jnp.einsum(
            "send,senf->edf", grouped, d_gate_act, preferred_element_type=jnp.float32
        )
        stepwise_expert_up = jnp.einsum(
            "send,senf->edf", grouped, d_up_act, preferred_element_type=jnp.float32
        )
        local_egate = local_egate + step_egate
        local_expert_up_weight = local_expert_up_weight + stepwise_expert_up
        local_edown = local_edown + step_edown
        d_expert_in = jnp.einsum(
            "senf,edf->send", d_gate_act, e_gate, preferred_element_type=jnp.float32
        ) + jnp.einsum(
            "senf,edf->send", d_up_act, expert_up_weight, preferred_element_type=jnp.float32
        )
        d_expert_in = d_expert_in.astype(jnp.bfloat16).reshape(
            total_experts, capacity, feature_count
        )
        back = lax.all_to_all(
            d_expert_in, EXPERTS, split_axis=0, concat_axis=0, tiled=True
        ).reshape(-1, feature_count)
        d_normed_two = d_normed_two + jnp.sum(
            back[flat_dest].reshape(row_count, 2, feature_count).astype(jnp.float32), 1
        )
        scaled_two = gain_two * d_normed_two
        d_hidden = (
            grad_rows
            + root_two * scaled_two
            - hidden * root_two**3 * jnp.mean(hidden * scaled_two, -1, keepdims=True)
        )
        acc_gain_two = acc_gain_two + jnp.sum(d_normed_two * hidden * root_two, 0)
        d_attn = d_hidden.astype(jnp.bfloat16)
        acc_out = acc_out + tdot(attended, d_attn)
        d_attended = ndot(d_attn, w_out).astype(jnp.bfloat16)
        prompt_key, prompt_value = cached
        key_heads = jnp.concatenate([prompt_key, key_rows[PB:]], 0).reshape(prompt + CONT, H, HD)
        value_heads = jnp.concatenate([prompt_value, value_rows[PB:]], 0).reshape(
            prompt + CONT, H, HD
        )
        query_heads = query.reshape(row_count, H, HD)
        scores = (
            jnp.einsum("qhd,khd->hqk", query_heads, key_heads, preferred_element_type=jnp.float32)
            * scaling
        )
        scores = jnp.where(allowed, scores, -1000000000.0)
        probs = jnp.exp(scores - log_total)
        d_heads = d_attended.reshape(row_count, H, HD)
        d_probs = jnp.einsum(
            "qhd,khd->hqk", d_heads, value_heads, preferred_element_type=jnp.float32
        )
        centre = jnp.sum(probs * d_probs, -1, keepdims=True)
        d_scores = (probs * (d_probs - centre)).astype(jnp.bfloat16)
        d_query = (
            jnp.einsum(
                "hqk,khd->qhd", d_scores, key_heads, preferred_element_type=jnp.float32
            ).reshape(row_count, feature_count)
            * scaling
        )
        d_keys = (
            jnp.einsum(
                "hqk,qhd->khd", d_scores, query_heads, preferred_element_type=jnp.float32
            ).reshape(prompt + CONT, feature_count)
            * scaling
        )
        d_values = jnp.einsum(
            "hqk,qhd->khd", probs.astype(jnp.bfloat16), d_heads, preferred_element_type=jnp.float32
        ).reshape(prompt + CONT, feature_count)
        own_dkey, own_dvalue = (
            lax.psum_scatter(
                d_keys[:prompt].astype(jnp.bfloat16), CONTEXT, scatter_dimension=0, tiled=True
            ).astype(jnp.float32),
            lax.psum_scatter(
                d_values[:prompt].astype(jnp.bfloat16), CONTEXT, scatter_dimension=0, tiled=True
            ).astype(jnp.float32),
        )
        d_key_rows = jnp.concatenate([own_dkey, d_keys[prompt:]], 0)
        d_value_rows = jnp.concatenate([own_dvalue, d_values[prompt:]], 0)
        d_projected = jnp.concatenate(
            [
                rotate(d_query, cosine, -sine_part).astype(jnp.bfloat16),
                rotate(d_key_rows, cosine, -sine_part).astype(jnp.bfloat16),
                d_value_rows.astype(jnp.bfloat16),
            ],
            1,
        )
        acc_qkv = acc_qkv + tdot(normed_one, d_projected)
        d_normed_one = ndot(d_projected, w_qkv)
        scaled_one = gain_one * d_normed_one
        d_inputs = (
            d_hidden
            + root_one * scaled_one
            - inputs * root_one**3 * jnp.mean(inputs * scaled_one, -1, keepdims=True)
        )
        acc_gain_one = acc_gain_one + jnp.sum(d_normed_one * inputs * root_one, 0)
        input_list.append(d_inputs.astype(jnp.bfloat16))
    sharded_expert_gate, sharded_expert_up, sharded_expert_down = (
        lax.psum_scatter(
            local_egate.astype(jnp.bfloat16), (DP, CONTEXT), scatter_dimension=2, tiled=True
        ).astype(jnp.float32),
        lax.psum_scatter(
            local_expert_up_weight.astype(jnp.bfloat16),
            (DP, CONTEXT),
            scatter_dimension=2,
            tiled=True,
        ).astype(jnp.float32),
        lax.psum_scatter(
            local_edown.astype(jnp.bfloat16), (DP, CONTEXT), scatter_dimension=1, tiled=True
        ).astype(jnp.float32),
    )
    acc_gains = jnp.stack([acc_gain_one, acc_gain_two], 0)
    dense_shards = (
        lax.psum_scatter(acc_qkv, (CONTEXT, EXPERTS), scatter_dimension=1, tiled=True),
        lax.psum_scatter(acc_out, (CONTEXT, EXPERTS), scatter_dimension=0, tiled=True),
        lax.psum_scatter(acc_sgate, (CONTEXT, EXPERTS), scatter_dimension=1, tiled=True),
        lax.psum_scatter(acc_sup, (CONTEXT, EXPERTS), scatter_dimension=1, tiled=True),
        lax.psum_scatter(acc_sdown, (CONTEXT, EXPERTS), scatter_dimension=0, tiled=True),
        lax.psum_scatter(acc_gains, (CONTEXT, EXPERTS), scatter_dimension=1, tiled=True),
    )
    grad_qkv, grad_out, grad_sgate, grad_sup, grad_sdown, grad_gains = (
        lax.psum(dense_shards[0].astype(jnp.bfloat16), DP).astype(jnp.float32),
        lax.psum(dense_shards[1].astype(jnp.bfloat16), DP).astype(jnp.float32),
        lax.psum(dense_shards[2].astype(jnp.bfloat16), DP).astype(jnp.float32),
        lax.psum(dense_shards[3].astype(jnp.bfloat16), DP).astype(jnp.float32),
        lax.psum(dense_shards[4].astype(jnp.bfloat16), DP).astype(jnp.float32),
        lax.psum(dense_shards[5].astype(jnp.bfloat16), DP).astype(jnp.float32),
    )
    mixed = jnp.stack(mixed_list, 0).reshape(tokens.shape)
    input_grad = jnp.stack(input_list, 0).reshape(tokens.shape)
    return (
        mixed,
        input_grad,
        grad_qkv,
        grad_out,
        grad_sgate,
        grad_sup,
        grad_sdown,
        grad_gains,
        sharded_expert_gate,
        sharded_expert_up,
        sharded_expert_down,
    )


def on_device(
    tokens,
    cotangent,
    gates,
    routes,
    qkv_weight,
    out_weight,
    shared_gate,
    shared_up,
    shared_down,
    gains,
    expert_gate,
    expert_up,
    expert_down,
):
    owners = lax.axis_size(EXPERTS)
    sizes = (lax.axis_size(CONTEXT), owners // 2)
    own_at = lax.axis_index(CONTEXT) * owners + lax.axis_index(EXPERTS)
    gain_width, features = gains.shape[1], tokens.shape[5]
    gain_rows = lax.dynamic_update_slice(
        jnp.zeros((16, features), jnp.bfloat16), gains, (0, own_at * gain_width)
    )
    rows, cot = tokens[0, 0, :, 0], cotangent[0, 0, :, 0]
    gate_columns = gates[0, 0, :, 0].transpose(0, 2, 1)
    route_columns = routes[0, 0, :, 0].transpose(0, 2, 1)
    forward = run_forward(
        sizes,
        rows,
        cot,
        gate_columns,
        route_columns,
        (qkv_weight.T, out_weight, gain_rows, shared_gate, shared_up, shared_down),
        (expert_gate, expert_up, expert_down),
    )
    (
        mixed, input_grad, grad_qkv, grad_out, grad_sgate, grad_sup, grad_sdown,
        grad_egate, grad_eup, grad_edown, gain_sum, *_,
    ) = run_backward(
        sizes, rows, cot, gate_columns, route_columns, forward[:3] + forward[9:]
    )
    mixed, input_grad, grad_qkv, *rest = finish_outputs(
        (grad_qkv, grad_out, grad_sgate, grad_sup, grad_sdown, grad_egate, grad_eup, grad_edown),
        (mixed, input_grad),
        gain_sum,
        gain_width,
    )
    grad_out, grad_sgate, grad_sup, grad_sdown, grad_egate, grad_eup, grad_edown, grad_gains = rest
    return (
        mixed.reshape(tokens.shape),
        input_grad.reshape(tokens.shape),
        grad_qkv.T,
        grad_out,
        grad_sgate,
        grad_sup,
        grad_sdown,
        grad_gains,
        grad_egate,
        grad_eup,
        grad_edown,
    )


def kernels_fit(mesh_shape, arrays):
    qkv_weight, out_weight, shared_gate, _, shared_down = arrays[4:9]
    rows = (qkv_weight.shape[1], out_weight.shape[0], shared_gate.shape[1], shared_down.shape[0])
    return (
        mesh_shape[DP] == 2
        and mesh_shape[CONTEXT] >= 4
        and mesh_shape[EXPERTS] % 2 == 0
        and all(count % 16 == 0 for count in rows)
        and shared_gate.shape[1] % 128 == 0
        and arrays[10].shape[2] % 128 == 0
        and shared_gate.shape[1] * mesh_shape[EXPERTS] == 2 * arrays[10].shape[2]
    )


def solution(mesh):
    def device_program(*arrays):
        return (on_device if kernels_fit(mesh.shape, arrays) else on_device_plain)(*arrays)

    return jax.shard_map(
        device_program,
        mesh=mesh,
        in_specs=(
            P(DP, EXPERTS, None, CONTEXT, None, None),
            P(DP, EXPERTS, None, CONTEXT, None, None),
            P(DP, EXPERTS, None, CONTEXT, None, None),
            P(DP, EXPERTS, None, CONTEXT, None, None),
            P(None, (CONTEXT, EXPERTS)),
            P((CONTEXT, EXPERTS), None),
            P(None, (CONTEXT, EXPERTS)),
            P(None, (CONTEXT, EXPERTS)),
            P((CONTEXT, EXPERTS), None),
            P(None, (CONTEXT, EXPERTS)),
            P(EXPERTS, None, (DP, CONTEXT)),
            P(EXPERTS, None, (DP, CONTEXT)),
            P(EXPERTS, (DP, CONTEXT), None),
        ),
        out_specs=(
            P(DP, EXPERTS, None, CONTEXT, None, None),
            P(DP, EXPERTS, None, CONTEXT, None, None),
            P(None, (CONTEXT, EXPERTS)),
            P((CONTEXT, EXPERTS), None),
            P(None, (CONTEXT, EXPERTS)),
            P(None, (CONTEXT, EXPERTS)),
            P((CONTEXT, EXPERTS), None),
            P(None, (CONTEXT, EXPERTS)),
            P(EXPERTS, None, (DP, CONTEXT)),
            P(EXPERTS, None, (DP, CONTEXT)),
            P(EXPERTS, (DP, CONTEXT), None),
        ),
        check_vma=False,
    )
```

```python
import functools

import jax
import jax.numpy as jnp
import numpy as np
from jax import lax
from jax.experimental import pallas as pl
from jax.experimental.pallas import tpu as pltpu
from jax.sharding import PartitionSpec as P

DP, CONTEXT, EXPERTS = "dp", "context", "experts"

H = 12
HD = 64
PB = 128
CONT = 256


EPSILON = 1e-06


def mdot(former, latter):
    return jnp.dot(former, latter, preferred_element_type=jnp.float32)


def tdot(former, latter):
    return lax.dot_general(
        former, latter, (((0,), (0,)), ((), ())), preferred_element_type=jnp.float32
    )


def ndot(former, latter):
    return lax.dot_general(
        former, latter, (((1,), (1,)), ((), ())), preferred_element_type=jnp.float32
    )


def rotate(values, cosine, sine_part):
    half_size = HD // 2
    shaped = values.reshape(values.shape[0], H, HD)
    former = shaped[..., :half_size]
    latter = shaped[..., half_size:]
    turned = jnp.concatenate(
        [former * cosine - latter * sine_part, latter * cosine + former * sine_part], -1
    )
    return turned.reshape(values.shape)


def slot_table(routes_block, expert_count):
    flat_routes = routes_block.reshape(-1)
    onehot = (flat_routes[:, None] == jnp.arange(expert_count, dtype=jnp.int32)[None, :]).astype(
        jnp.int32
    )
    before = jnp.cumsum(onehot, 0) - onehot
    return jnp.sum(before * onehot, 1).reshape(routes_block.shape)


def silu_parts(values):
    sigma = jax.nn.sigmoid(values)
    return (values * sigma, sigma * (1.0 + values * (1.0 - sigma)))


MESH = pl.DeviceIdType.MESH
MIB = 1024 * 1024
BF = jnp.bfloat16
F32 = jnp.float32


def remote(source, target, send_sem, recv_sem, **device):
    return pltpu.make_async_remote_copy(
        src_ref=source,
        dst_ref=target,
        send_sem=send_sem,
        recv_sem=recv_sem,
        device_id=device,
        device_id_type=MESH,
    )


def arrived(slot, recv_sem):
    remote(slot, slot, recv_sem, recv_sem, context=0).wait_recv()


def either(first, second):
    return jnp.logical_and(first, second)


class Place:
    def __init__(self, sizes):
        self.depth, self.high_count = sizes
        self.owners = self.high_count * 2
        self.x = lax.axis_index(DP)
        self.z = lax.axis_index(CONTEXT)
        self.e = lax.axis_index(EXPERTS)
        self.high = self.e // 2
        self.low = self.e % 2

    def shard(self, z):
        return self.x * self.depth + z

    def other_shard(self, z):
        return (1 - self.x) * self.depth + z

    def peer_high(self, step):
        return lax.rem(self.high + step, self.high_count)

    def peer_owner(self, step):
        return lax.rem(self.e + step, self.owners)

    def on_line(self, z):
        return (z >= 0) & (z < self.depth)

    def greet(self):
        barrier = pltpu.get_barrier_semaphore()

        def signal(**device):
            pl.semaphore_signal(barrier, inc=1, device_id=device, device_id_type=MESH)

        signal(dp=1 - self.x)
        for step in range(1, self.owners):
            signal(experts=self.peer_owner(step))
        for step in range(1, self.depth):
            signal(context=lax.rem(self.z + step, self.depth))
        count = self.owners + self.depth - 1
        pl.semaphore_wait(barrier, count)


class Line:
    def __init__(self, place, own, slot, send_sem, recv_sem):
        self.place, self.own, self.slot = place, own, slot
        self.send_sem, self.recv_sem = send_sem, recv_sem

    def _copy(self, direction, step):
        place = self.place
        z = place.z - direction * step
        source = self.own if step == 0 else self.slot(z)
        return remote(
            source,
            self.slot(z),
            self.send_sem.at[(direction + 1) // 2, step],
            self.recv_sem.at[z],
            context=place.z + direction,
        )

    def _valid(self, direction, step):
        place = self.place
        return place.on_line(place.z - direction * step) & place.on_line(place.z + direction)

    def send(self, direction, step):
        if step < self.place.depth - 1:
            pl.when(self._valid(direction, step))(lambda: self._copy(direction, step).start())

    def start(self):
        self.send(1, 0)
        self.send(-1, 0)

    def hop(self, step, then=None):
        for direction in (1, -1):
            z = self.place.z - direction * (step + 1)

            def body(direction=direction, z=z):
                arrived(self.slot(z), self.recv_sem.at[z])
                self.send(direction, step + 1)
                if then is not None:
                    then(z)

            pl.when(self.place.on_line(z))(body)

    def drain(self):
        for direction in (1, -1):
            for step in range(self.place.depth - 1):
                pl.when(self._valid(direction, step))(
                    lambda d=direction, s=step: self._copy(d, s).wait_send()
                )


class DenseGather:
    def __init__(self, place, own, slot, sems):
        self.place, self.own, self.slot_of = place, own, slot
        zs, zr, self.h_send, self.h_recv, self.l_send, self.l_recv = sems
        self.line = Line(place, own, lambda z: self.slot(z, place.high, place.low), zs, zr)

    @staticmethod
    def semaphores(count, depth, high_count):
        dma = pltpu.SemaphoreType.DMA
        cross = dma((count, high_count, depth))
        return [dma((count, 2, depth)), dma((count, depth)), cross, cross, cross, cross]

    def slot(self, z, high, low):
        return self.slot_of((z * self.place.high_count + high) * 2 + low)

    def _to_high(self, z, step, own):
        place = self.place
        target = self.slot(z, place.high, place.low)
        return remote(
            self.own if own else target,
            target,
            self.h_send.at[step, z],
            self.h_recv.at[place.high, z],
            experts=place.peer_high(step) * 2 + place.low,
        )

    def _to_low(self, z, high, own):
        place = self.place
        target = self.slot(z, high, place.low)
        return remote(
            self.own if own else target,
            target,
            self.l_send.at[high, z],
            self.l_recv.at[high, z],
            experts=place.e + 1 - 2 * place.low,
        )

    def _spread(self, z, own=False):
        for step in range(1, self.place.high_count):
            self._to_high(z, step, own).start()
        self._to_low(z, self.place.high, own).start()

    def start(self):
        self.line.start()
        self._spread(self.place.z, True)

    def hop(self, step):
        self.line.hop(step, self._spread)

    def cross(self, z):
        place = self.place
        for step in range(1, place.high_count):
            high = place.peer_high(step)
            arrived(self.slot(z, high, place.low), self.h_recv.at[high, z])
            self._to_low(z, high, False).start()

    def finish(self, z):
        place = self.place
        for high in range(place.high_count):
            arrived(self.slot(z, high, 1 - place.low), self.l_recv.at[high, z])

    def drain(self):
        place = self.place
        self.line.drain()
        for z in range(place.depth):
            for step in range(1, place.high_count):
                self._to_high(z, step, False).wait_send()
            for high in range(place.high_count):
                self._to_low(z, high, False).wait_send()


def expert_slab(ref, kind, local, shard, width):
    start = pl.multiple_of(shard * width, 128)
    if kind == 2:
        return ref.at[local, pl.ds(start, width)]
    return ref.at[local, :, pl.ds(start, width)]


class ExpertGather:
    def __init__(self, place, own, out, sems):
        self.place, self.own, self.out = place, own, out
        self.z_send, self.z_recv, self.x_send, self.x_recv = sems
        self.local_count, self.width = own[0].shape[0], own[0].shape[2]

    @staticmethod
    def semaphores(depth, local_count):
        dma = pltpu.SemaphoreType.DMA
        return [
            dma((local_count, 3, 2, depth)),
            dma((local_count, 3, depth)),
            dma((local_count, 3, depth)),
            dma((local_count, 3, depth)),
        ]

    def slot(self, local, kind, shard):
        return expert_slab(self.out[kind], kind, local, shard, self.width)

    def _line(self, local, kind):
        return Line(
            self.place,
            self.own[kind].at[local],
            lambda z: self.slot(local, kind, self.place.shard(z)),
            self.z_send.at[local, kind],
            self.z_recv.at[local, kind],
        )

    def _across(self, local, kind, z, own=False):
        target = self.slot(local, kind, self.place.shard(z))
        return remote(
            self.own[kind].at[local] if own else target,
            target,
            self.x_send.at[local, kind, z],
            self.x_recv.at[local, kind, z],
            dp=1 - self.place.x,
        )

    def start_x(self):
        for local in range(self.local_count):
            for kind in range(3):
                self._across(local, kind, self.place.z, True).start()

    def start_z(self):
        for local in range(self.local_count):
            for kind in range(3):
                self._line(local, kind).start()

    def hop(self, local, step, kinds=(0, 1, 2)):
        for kind in kinds:
            self._line(local, kind).hop(
                step, lambda z, kind=kind: self._across(local, kind, z).start()
            )

    def wait_x(self, local, z):
        for kind in range(3):
            arrived(
                self.slot(local, kind, self.place.other_shard(z)), self.x_recv.at[local, kind, z]
            )

    def drain(self):
        for local in range(self.local_count):
            for kind in range(3):
                self._line(local, kind).drain()
                for z in range(self.place.depth):
                    self._across(local, kind, z).wait_send()


def rope(values, cosine, sine_part):
    lane = lax.broadcasted_iota(jnp.int32, cosine.shape, 1)
    first = lax.rem(lane, HD) < HD // 2
    turned = []
    for start in range(0, values.shape[1], 2 * HD):
        part = values[:, start : start + 2 * HD]
        partner = jnp.where(
            first, pltpu.roll(part, 2 * HD - HD // 2, 1), pltpu.roll(part, HD // 2, 1)
        )
        turned.append(part * cosine + partner * sine_part)
    return jnp.concatenate(turned, 1)


def norm_rows(values, gain):
    root = lax.rsqrt(jnp.mean(values * values, -1, keepdims=True) + EPSILON)
    return (values * root * gain).astype(BF)


def tiles(total, size, body):
    def run(i, carry):
        body(pl.ds(pl.multiple_of(i * size, size), size))
        return carry

    lax.fori_loop(0, total // size, run, 0)


def one_hots(routes, gates, me, local_count, total):
    rows = routes.shape[1]
    capacity = rows * 8 // (3 * total)
    first, second = routes[0:1, :], routes[1:2, :]
    ids = lax.rem(
        lax.broadcasted_iota(jnp.int32, (total, rows), 0) + me * local_count, total
    )
    named = (first == ids) | (second == ids)
    earlier = (
        lax.broadcasted_iota(jnp.int32, (rows, rows), 0)
        < lax.broadcasted_iota(jnp.int32, (rows, rows), 1)
    ).astype(F32).astype(BF)
    counts = mdot(named.astype(F32).astype(BF), earlier).astype(jnp.int32)
    places = jnp.where(named, counts, -1)
    weights = jnp.where(first == ids, gates[0:1, :], 0.0) + jnp.where(
        second == ids, gates[1:2, :], 0.0
    )
    slot = lax.broadcasted_iota(jnp.int32, (capacity, rows), 0)
    for i in range(total):
        yield i, slot == places[i : i + 1, :], weights[i : i + 1, :]


def ffn_chunk(x, g, weights, saved, sums, grads, tile):
    gate_w, up_w, down_w = weights
    act_s, d_gate_s, d_up_s = saved
    out_sum, in_sum = sums

    def forward(here):
        x_rows, g_rows = x[here, :], g[here, :]
        gate = mdot(x_rows, gate_w[...])
        up = mdot(x_rows, up_w[...])
        d_act = ndot(g_rows, down_w[...]).astype(BF).astype(F32)
        sigma = jax.nn.sigmoid(gate)
        silu = gate * sigma
        act = (silu * up).astype(BF)
        d_gate = (d_act * up * (sigma * (1.0 + gate * (1.0 - sigma)))).astype(BF)
        d_up = (d_act * silu).astype(BF)
        act_s[here, :] = act
        d_gate_s[here, :] = d_gate
        d_up_s[here, :] = d_up
        out_sum[here, :] += mdot(act, down_w[...])
        in_sum[here, :] += ndot(d_gate, gate_w[...]) + ndot(d_up, up_w[...])

    rows = x.shape[0]
    tiles(rows, tile, forward)
    used = pl.ds(0, rows)

    def weight_grads(here):
        grads[0][here, :] = tdot(x[:, here], d_gate_s[used, :]).astype(BF)
        grads[1][here, :] = tdot(x[:, here], d_up_s[used, :]).astype(BF)
        grads[2][:, here] = tdot(act_s[used, :], g[:, here]).astype(BF)

    tiles(x.shape[1], 256, weight_grads)


def forward_kernel(sizes, *refs):
    place = Place(sizes)
    depth, high_count = sizes
    owners = place.owners
    (
        tokens, cot, gates, routes, cosine, sine_part,
        qkv_in, out_in, gain_in, sg_in, su_in, sd_in, eg_in, eu_in, ed_in,
        qkv_o, out_o, gain_o, sg_o, su_o, sd_o, eg_o, eu_o, ed_o,
        n1_o, k_o, v_o, q_o, att_o, hid_o, lse_o, side_o, dn2_o,
        gsg_o, gsu_o, gsd_o, geg_o, geu_o, ged_o, outs_o, dins_o, pre_g, pre_u, pre_d,
        xk, wq, wo, gain_land, gain_v, g_all, n2, in_s, do_s, send_in, send_do,
        wg, wu, wd, act_s, dg_s, du_s, stage_g, stage_u, stage_d,
        *sems,
    ) = refs
    dense_sems, sems = sems[:6], sems[6:]
    expert_sems, sems = sems[:4], sems[4:]
    (
        line_send, line_recv, load_sem, ai_send, ai_recv, ad_send, ad_recv,
        chunk_sem, store_sem, out_sem, pre_send, pre_recv,
    ) = sems
    micro_count, rows, features = tokens.shape
    prompt = depth * PB
    length = prompt + CONT
    local_count, _, width = eg_in.shape
    total = owners * local_count
    capacity = rows * 8 // (3 * total)
    slots = in_s.shape[1]
    me = place.e

    def dense(i, own, slot):
        return DenseGather(place, own, slot, [s.at[i] for s in dense_sems])

    def rows_of(ref, count):
        return lambda s: ref.at[pl.ds(pl.multiple_of(s * count, 16), count)]

    def columns_of(ref, count):
        return lambda s: ref.at[:, pl.ds(pl.multiple_of(s * count, 128), count)]

    early = [
        dense(0, qkv_in, rows_of(wq, qkv_in.shape[0])),
        dense(1, out_in, rows_of(wo, out_in.shape[0])),
        dense(2, gain_in, rows_of(gain_land, gain_in.shape[0])),
    ]
    late = [
        dense(3, sg_in, columns_of(sg_o, sg_in.shape[1])),
        dense(4, su_in, columns_of(su_o, su_in.shape[1])),
        dense(5, sd_in, rows_of(sd_o, sd_in.shape[0])),
    ]
    experts = ExpertGather(place, (eg_in, eu_in, ed_in), (eg_o, eu_o, ed_o), expert_sems)
    own_prompt = pl.ds(pl.multiple_of(place.z * PB, PB), PB)
    prompts = [
        Line(
            place,
            tokens.at[m, pl.ds(0, PB)],
            lambda z, m=m: xk.at[m, pl.ds(pl.multiple_of(z * PB, PB), PB)],
            line_send.at[m],
            line_recv.at[m],
        )
        for m in range(micro_count)
    ]
    own_at = (place.z * high_count + place.high) * 2 + place.low
    loads = [
        (tokens.at[:, pl.ds(0, PB)], xk.at[:, own_prompt]),
        (tokens.at[:, pl.ds(PB, CONT)], xk.at[:, pl.ds(prompt, CONT)]),
    ]
    loads += [(cot.at[m], g_all.at[pl.ds(m * rows, rows)]) for m in range(micro_count)]
    loads += [(d.own, d.slot_of(own_at)) for d in early]
    bounce = [
        (sg_in, wg.at[0, :, pl.ds(0, sg_in.shape[1])], late[0].slot_of(own_at)),
        (su_in, wu.at[0, :, pl.ds(0, su_in.shape[1])], late[1].slot_of(own_at)),
        (sd_in, wd.at[0, pl.ds(0, sd_in.shape[0])], late[2].slot_of(own_at)),
    ]
    loads += [(source, middle) for source, middle, _ in bounce]
    load_copies = [
        pltpu.make_async_copy(source, target, load_sem.at[i])
        for i, (source, target) in enumerate(loads)
    ]
    bounce_copies = [
        pltpu.make_async_copy(middle, target, load_sem.at[i])
        for i, (_, middle, target) in enumerate(bounce)
    ]
    for copy in load_copies:
        copy.start()
    place.greet()
    for d in early:
        d.start()
    experts.start_x()
    for copy in load_copies:
        copy.wait()
    for copy in bounce_copies:
        copy.start()
    stores = []

    def store(source, target):
        copy = pltpu.make_async_copy(source, target, out_sem.at[len(stores)])
        copy.start()
        stores.append(copy)

    def slot_rows(m, sender):
        return pl.ds(pl.multiple_of((m * owners + sender) * capacity, 16), capacity)

    def exchange(buffer, land, send_sem, recv_sem, m, step):
        return remote(
            buffer.at[step - 1, m],
            land.at[:, slot_rows(m, me)],
            send_sem.at[step - 1, m],
            recv_sem.at[step - 1, m],
            experts=place.peer_owner(step),
        )

    def exchanged(land, recv_sem, m, step):
        sender = lax.rem(me - step + owners, owners)
        arrived(land.at[:, slot_rows(m, sender)], recv_sem.at[step - 1, m])

    def put(buffer, land, m, i, value):
        if i < local_count:
            land[i, slot_rows(m, me), :] = value
        else:
            buffer[i // local_count - 1, m, i % local_count] = value

    def expert_gradients(m):
        g_rows = g_all[pl.ds(m * rows, rows), :]
        for i, hit, weight in one_hots(routes.at[m], gates.at[m], me, local_count, total):
            gate = jnp.sum(jnp.where(hit, weight, 0.0), -1, keepdims=True)
            value = mdot(hit.astype(F32).astype(BF), g_rows)
            put(send_do, do_s, m, i, (gate * value).astype(BF))

    def early_hop(step):
        for d in early:
            d.hop(step)

    for step in range(depth - 2):
        if step < micro_count:
            expert_gradients(step)
        early_hop(step)
    for m in range(max(depth - 2, 0), micro_count):
        expert_gradients(m)
    prompts[0].start()
    early_hop(depth - 2)
    for m in range(micro_count):
        for step in range(1, owners):
            exchange(send_do, do_s, ad_send, ad_recv, m, step).start()
    prompts[0].hop(0)
    for z in range(depth):
        for d in early:
            d.cross(z)
    for step in range(1, depth - 1):
        prompts[0].hop(step)
        if step == 1:
            for prompt_line in prompts[1:]:
                prompt_line.start()
    for z in range(depth):
        for d in early:
            d.finish(z)
    store(wq, qkv_o)
    store(wo, out_o)
    shards = depth * owners
    gain_rows = gain_in.shape[0]
    gain_sum = jnp.zeros((8, features), F32)
    for s in range(shards):
        gain_sum += gain_land[pl.ds(s * gain_rows, gain_rows), :].astype(F32)[:8]
    gain_v[...] = gain_sum
    store(gain_v, gain_o)

    def own_rows(i):
        start = place.z * PB if i == 0 else prompt + (i - 1) * PB
        return start, pl.ds(start if i else pl.multiple_of(start, PB), PB)

    def front(n1, k, v, q, att, hid, lse):
        lse[...] = jnp.zeros_like(lse)
        pairs = features // (2 * HD)

        def prompt_hop(step):
            for prompt_line in prompts[1:]:
                prompt_line.hop(step)
            if step == depth - 2:
                experts.start_z()

        def project_all(m):
            def project(here):
                normed = norm_rows(xk[m, here, :].astype(F32), gain_v[0:1, :])
                n1[m, here, :] = normed
                key = ndot(normed, wq[pl.ds(features, features), :])
                k[m, here, :] = rope(key, cosine[here, :], sine_part[here, :]).astype(BF)
                v[m, here, :] = ndot(normed, wq[pl.ds(2 * features, features), :]).astype(BF)

            tiles(length, 256, project)
            for i in range(rows // PB):
                _, here = own_rows(i)
                query = ndot(n1[m, here, :], wq[pl.ds(0, features), :])
                query = rope(query, cosine[here, :], sine_part[here, :]).astype(BF)
                q[m, pl.ds(i * PB, PB), :] = query * jnp.asarray(HD**-0.5, BF)
        lane = lax.broadcasted_iota(jnp.int32, (PB, 2 * HD), 1)
        for m in range(micro_count):
            project_all(m)

            def pair(index, carry):
                if m == 0:
                    for step in range(depth - 1):
                        pl.when(index == min(step, pairs - 1))(lambda step=step: prompt_hop(step))
                lanes = pl.ds(pl.multiple_of(index * 2 * HD, 2 * HD), 2 * HD)
                for i in range(rows // PB):
                    here = pl.ds(i * PB, PB)
                    query = q[m, here, lanes]
                    seen = prompt + i * PB
                    keys, values = k[m, pl.ds(0, seen), lanes], v[m, pl.ds(0, seen), lanes]
                    column = lax.broadcasted_iota(jnp.int32, (PB, seen), 1)
                    row = lax.broadcasted_iota(jnp.int32, (PB, seen), 0)
                    allowed = column <= row + own_rows(i)[0]
                    parts = []
                    logs = lse[m, here, :]
                    for sub in range(2):
                        only = jnp.where(lane // HD == sub, query, jnp.zeros_like(query))
                        scores = jnp.where(allowed, ndot(only, keys), -1000000000.0)
                        highest = jnp.max(scores, -1, keepdims=True)
                        weights = jnp.exp(scores - highest)
                        sums = jnp.sum(weights, -1, keepdims=True)
                        parts.append(mdot((weights * (1.0 / sums)).astype(BF), values))
                        logs = jnp.where(lane == 2 * index + sub, highest + jnp.log(sums), logs)
                    lse[m, here, :] = logs
                    att[m, here, lanes] = jnp.where(lane < HD, parts[0], parts[1]).astype(BF)
                return carry

            lax.fori_loop(0, pairs, pair, 0)
            if m == 0:
                for copy in bounce_copies:
                    copy.wait()
                for d in late:
                    d.start()
            if m == micro_count - 1:
                experts.hop(0, 0)
                for d in late:
                    d.cross(place.z)
            for i in range(rows // PB):
                here = pl.ds(i * PB, PB)
                hidden = xk[m, own_rows(i)[1], :].astype(F32) + mdot(att[m, here, :], wo[...])
                hid[m, here, :] = hidden
                n2[pl.ds(m * rows + i * PB, PB), :] = norm_rows(hidden, gain_v[1:2, :])
            normed = n2[pl.ds(m * rows, rows), :]
            for i, hit, _ in one_hots(routes.at[m], gates.at[m], me, local_count, total):
                value = mdot(hit.astype(F32).astype(BF), normed)
                put(send_in, in_s, m, i, value.astype(BF))
            for step in range(1, owners):
                exchange(send_in, in_s, ai_send, ai_recv, m, step).start()
        store(n1, n1_o)
        store(k, k_o)
        store(v, v_o)
        store(q, q_o)
        store(att, att_o)
        store(hid, hid_o)
        store(lse, lse_o)
        for copy in stores:
            copy.wait()

    pl.run_scoped(
        front,
        pltpu.VMEM((micro_count, length, features), BF),
        pltpu.VMEM((micro_count, length, features), BF),
        pltpu.VMEM((micro_count, length, features), BF),
        pltpu.VMEM((micro_count, rows, features), BF),
        pltpu.VMEM((micro_count, rows, features), BF),
        pltpu.VMEM((micro_count, rows, features), F32),
        pltpu.VMEM((micro_count, rows, 2 * HD), F32),
    )
    saved = (act_s, dg_s, du_s)
    staged = (stage_g, stage_u, stage_d)

    def chunk_loads(sources, slot):
        return [
            pltpu.make_async_copy(source, buffer.at[slot], chunk_sem.at[slot, kind])
            for kind, (source, buffer) in enumerate(zip(sources, (wg, wu, wd)))
        ]

    def chunk_stores(targets, slot):
        return [
            pltpu.make_async_copy(buffer.at[slot], target, store_sem.at[slot, kind])
            for kind, (target, buffer) in enumerate(zip(targets, staged))
        ]

    def wait_rows():
        for m in range(micro_count):
            for step in range(1, owners):
                exchanged(in_s, ai_recv, m, step)
                exchanged(do_s, ad_recv, m, step)

    at_end = (place.z == 0) | (place.z == depth - 1)
    beside_end = (place.z == 1) | (place.z == depth - 2)

    def sums_to_neighbour(which):
        z = jnp.where(place.z == 0, 1, depth - 2)
        return [
            remote(
                expert_slab(
                    ref, kind, local, (place.other_shard if crossed else place.shard)(z), width
                ),
                land.at[crossed, local],
                pre_send.at[crossed, local, kind],
                pre_recv.at[crossed, local, kind],
                context=z,
            )
            for crossed in which
            for local in range(local_count)
            for kind, (ref, land) in enumerate(
                ((geg_o, pre_g), (geu_o, pre_u), (ged_o, pre_d))
            )
        ]

    def send_sums(crossed):
        def body():
            for copy in sums_to_neighbour((crossed,)):
                copy.start()

        pl.when(at_end)(body)

    def sums_sent():
        for copy in sums_to_neighbour((0, 1)):
            copy.wait_send()

    def sums_arrived():
        for crossed in (1, 0):
            for local in range(local_count):
                for kind, land in enumerate((pre_g, pre_u, pre_d)):
                    arrived(land.at[crossed, local], pre_recv.at[crossed, local, kind])

    def returns(local):
        return [
            pltpu.make_async_copy(source.at[local], target.at[local], out_sem.at[2 + 2 * local + i])
            for i, (source, target) in enumerate(((in_s, outs_o), (do_s, dins_o)))
        ]

    def both(out_sum, in_sum, side_sum, normed_sum):
        out_sum[...] = jnp.zeros_like(out_sum)
        in_sum[...] = jnp.zeros_like(in_sum)
        side_sum[...] = jnp.zeros_like(side_sum)
        normed_sum[...] = jnp.zeros_like(normed_sum)
        group = late[0].own.shape[1] * owners // width

        def store_grads(targets, slot, stored):
            def previous():
                for copy in chunk_stores(targets, slot):
                    copy.wait()

            pl.when(stored)(previous)
            return lambda: [copy.start() for copy in chunk_stores(targets, slot)]

        def shared_part(refs, c):
            here = pl.ds(pl.multiple_of(c * width, 128), width)
            return [refs[0].at[:, here], refs[1].at[:, here], refs[2].at[here]]

        def shared_item(w, z):
            for d in late:
                d.finish(z)

            def one(i, carry):
                c = z * group + i
                loads = chunk_loads(shared_part((sg_o, su_o, sd_o), c), 2 * local_count + i)
                for copy in loads:
                    copy.wait()
                send = store_grads(shared_part((gsg_o, gsu_o, gsd_o), c), i, w > 0)
                ffn_chunk(
                    n2,
                    g_all,
                    [buffer.at[2 * local_count + i] for buffer in (wg, wu, wd)],
                    saved,
                    (side_sum, normed_sum),
                    [buffer.at[i] for buffer in staged],
                    micro_count * rows,
                )
                send()
                return carry

            for i in range(group):
                for copy in chunk_loads(
                    shared_part((sg_o, su_o, sd_o), z * group + i), 2 * local_count + i
                ):
                    copy.start()
            lax.fori_loop(0, group, one, 0)

        def expert_item(w, z, crossed, local, side, ahead):
            shard = jnp.where(crossed, place.other_shard(z), place.shard(z))

            def load(n):
                sources = [
                    expert_slab(ref, k, n, shard, width) for k, ref in enumerate((eg_o, eu_o, ed_o))
                ]
                return chunk_loads(sources, side * local_count + n)

            def begin(n):
                def own():
                    mine = [ref.at[n] for ref in (eg_in, eu_in, ed_in)]
                    for copy in chunk_loads(mine, side * local_count + n):
                        copy.start()

                def landed():
                    pl.when(crossed)(lambda: experts.wait_x(n, z))
                    for copy in load(n):
                        copy.start()

                pl.when(w == 1)(own)
                pl.when(w > 1)(landed)

            def begin_rest():
                for n in range(1, local_count):
                    begin(n)

            pl.when(w == 1)(wait_rows)
            pl.when(local == 0)(lambda: begin(0))
            pl.when(ahead & (local == 0))(begin_rest)
            pl.when(jnp.logical_not(ahead) & (local > 0))(lambda: begin(local))
            for copy in load(local):
                copy.wait()
            targets = [
                expert_slab(ref, k, local, shard, width) for k, ref in enumerate((geg_o, geu_o, ged_o))
            ]
            send = store_grads(targets, local, True)
            ffn_chunk(
                in_s.at[local],
                do_s.at[local],
                [buffer.at[side * local_count + local] for buffer in (wg, wu, wd)],
                saved,
                (out_sum.at[local], in_sum.at[local]),
                [buffer.at[local] for buffer in staged],
                slots,
            )
            send()

        def crossing(step):
            for d in late:
                for z in (place.z - 1 - step, place.z + 1 + step):
                    pl.when(place.on_line(z))(lambda d=d, z=z: d.cross(z))

        def late_hop(step, which=late):
            for d in which:
                d.hop(step)

        heads = 2 * local_count + 1
        in_step = 2 * heads
        after_item = [(local, lambda local=local: experts.hop(local, 0)) for local in range(1, local_count)]
        after_item = [(local - 1, run) for local, run in after_item]
        after_item += [(local_count, lambda: late_hop(0)), (heads - 1, lambda: crossing(0))]
        for step in range(1, depth - 1):
            here = heads + in_step * step
            late_spot, cross_spot = here + 3, here + 5
            if step == depth - 2:
                before = here - in_step
                spots = [(0, before + 3), (0, before + 5), (0, before + 7)]
                spots += [(local, here - 1) for local in range(1, local_count)]
                spots += [(local, here + 1) for local in range(1, local_count)] * 2
                late_spot, cross_spot = here + 5, here + 7
                after_item.append((here + 3, lambda step=step: late_hop(step, late[:1])))
                kinds = {}
                for local, at in spots:
                    kind = kinds.get(local, 0)
                    kinds[local] = kind + 1
                    after_item.append(
                        (at, lambda p=(local, step, (kind,)): experts.hop(*p))
                    )
            else:
                if step == 1:
                    spots = [heads + 3, jnp.where(at_end, here - 1, heads + 5)]
                    late_spot = jnp.where(at_end, here + 3, heads + 7)
                else:
                    spots = [here - 3, here - 1]
                for local in range(local_count):
                    at = spots[min(local, 1)]
                    after_item.append((at, lambda p=(local, step): experts.hop(*p)))
            rest = late[1:] if step == depth - 2 else late
            after_item.append((late_spot, lambda p=(step, rest): late_hop(*p)))
            after_item.append((cross_spot, lambda step=step: crossing(step)))
        after_item.append((heads + in_step - 3, lambda: send_sums(0)))
        after_item.append((heads + in_step - 1, lambda: send_sums(1)))
        count = heads + in_step * (depth - 1)

        def finish(local):
            def convert(here):
                in_s[local, here, :] = out_sum[local, here, :].astype(BF)
                do_s[local, here, :] = in_sum[local, here, :].astype(BF)

            tiles(slots, 256, convert)
            for copy in returns(local):
                copy.start()

        def side_sums():
            return [
                pltpu.make_async_copy(side_sum, side_o, out_sem.at[0]),
                pltpu.make_async_copy(normed_sum, dn2_o, out_sem.at[1]),
            ]

        def finish_routed():
            for local in range(local_count):
                finish(local)

        def early_drain():
            for line in prompts:
                line.drain()
            for d in early:
                d.drain()
            for m in range(micro_count):
                for step in range(1, owners):
                    exchange(send_do, do_s, ad_send, ad_recv, m, step).wait_send()
                    exchange(send_in, in_s, ai_send, ai_recv, m, step).wait_send()

        after_item.append((count - in_step, early_drain))
        after_item.append((count - 3, finish_routed))

        def item(w, carry):
            head = w < heads
            after = jnp.maximum(w - heads, 0)
            step, spot = after // in_step, lax.rem(after, in_step)
            kind = jnp.where(head, w - 1, spot // 2)
            is_shared = kind == jnp.where(head, -1, 2 * local_count)
            crossed = kind >= local_count
            local = jnp.clip(jnp.where(crossed, kind - local_count, kind), 0, local_count - 1)
            z = jnp.where(head, place.z, place.z + (2 * lax.rem(spot, 2) - 1) * (1 + step))
            valid = place.on_line(z)
            pl.when(valid & is_shared)(lambda: shared_item(w, z))
            ahead = head | (step < depth - 2)
            side = jnp.where(head, 0, lax.rem(spot, 2))
            pl.when(valid & jnp.logical_not(is_shared))(
                lambda: expert_item(w, z, crossed, local, side, ahead)
            )
            for at, run in after_item:
                pl.when(w == at)(run)
            return carry

        lax.fori_loop(0, count, item, 0)
        for copy in side_sums():
            copy.start()
        for d in late:
            d.drain()
        experts.drain()
        for local in range(local_count):
            targets = [expert_slab(ref, k, local, 0, width) for k, ref in enumerate((geg_o, geu_o, ged_o))]
            for copy in chunk_stores(targets, local):
                copy.wait()
        for copy in side_sums():
            copy.wait()

    pl.run_scoped(
        both,
        pltpu.VMEM((local_count, slots, features), F32),
        pltpu.VMEM((local_count, slots, features), F32),
        pltpu.VMEM((micro_count * rows, features), F32),
        pltpu.VMEM((micro_count * rows, features), F32),
    )
    for local in range(local_count):
        for copy in returns(local):
            copy.wait()
    pl.when(beside_end)(sums_arrived)
    pl.when(at_end)(sums_sent)


def rope_tables(prompt):
    positions = np.arange(prompt + CONT, dtype=np.float64)
    frequency = 10000.0 ** (-2.0 * np.arange(HD // 2) / HD)
    angles = positions[:, None] * frequency
    cosine, sine_part = np.cos(angles), np.sin(angles)
    return (
        np.concatenate([cosine] * 4, 1).astype(np.float32),
        np.concatenate([-sine_part, sine_part] * 2, 1).astype(np.float32),
    )


def run_forward(sizes, tokens, cot, gates, routes, dense, experts):
    depth, high_count = sizes
    micro_count, rows, features = tokens.shape
    owners = high_count * 2
    line = depth * owners
    prompt = depth * PB
    length = prompt + CONT
    local_count, _, width = experts[0].shape
    hidden_units = dense[3].shape[1] * line
    capacity = rows * 8 // (3 * owners * local_count)
    slots = micro_count * owners * capacity
    cosine, sine_part = rope_tables(prompt)
    hbm, vmem = pl.BlockSpec(memory_space=pltpu.HBM), pl.BlockSpec(memory_space=pltpu.VMEM)

    def shape(dtype, *dims):
        return jax.ShapeDtypeStruct(dims, dtype)

    token_rows = micro_count * rows
    wide, tall = (features, hidden_units), (hidden_units, features)
    out_shape = [
        shape(BF, dense[0].shape[0] * line, features),
        shape(BF, dense[1].shape[0] * line, features),
        shape(F32, 8, features),
        shape(BF, *wide), shape(BF, *wide), shape(BF, *tall),
        shape(BF, local_count, *wide), shape(BF, local_count, *wide), shape(BF, local_count, *tall),
        shape(BF, micro_count, length, features),
        shape(BF, micro_count, length, features),
        shape(BF, micro_count, length, features),
        shape(BF, micro_count, rows, features),
        shape(BF, micro_count, rows, features),
        shape(F32, micro_count, rows, features),
        shape(F32, micro_count, rows, 2 * HD),
        shape(F32, token_rows, features),
        shape(F32, token_rows, features),
        shape(BF, *wide), shape(BF, *wide), shape(BF, *tall),
        shape(BF, local_count, *wide), shape(BF, local_count, *wide), shape(BF, local_count, *tall),
        shape(BF, local_count, slots, features),
        shape(BF, local_count, slots, features),
        shape(BF, 2, local_count, features, width),
        shape(BF, 2, local_count, features, width),
        shape(BF, 2, local_count, width, features),
    ]
    dma = pltpu.SemaphoreType.DMA
    buffers = max(2, local_count)
    loads = 2 * local_count + 2
    send = pltpu.VMEM((owners - 1, micro_count, local_count, capacity, features), BF)
    scratch = [
        pltpu.VMEM((micro_count, length, features), BF),
        pltpu.VMEM(out_shape[0].shape, BF),
        pltpu.VMEM(out_shape[1].shape, BF),
        pltpu.VMEM((dense[2].shape[0] * line, features), BF),
        pltpu.VMEM((8, features), F32),
        pltpu.VMEM((token_rows, features), BF),
        pltpu.VMEM((token_rows, features), BF),
        pltpu.VMEM((local_count, slots, features), BF),
        pltpu.VMEM((local_count, slots, features), BF),
        send,
        send,
        pltpu.VMEM((loads, features, width), BF),
        pltpu.VMEM((loads, features, width), BF),
        pltpu.VMEM((loads, width, features), BF),
        pltpu.VMEM((max(slots, token_rows), width), BF),
        pltpu.VMEM((max(slots, token_rows), width), BF),
        pltpu.VMEM((max(slots, token_rows), width), BF),
        pltpu.VMEM((buffers, features, width), BF),
        pltpu.VMEM((buffers, features, width), BF),
        pltpu.VMEM((buffers, width, features), BF),
    ]
    scratch += DenseGather.semaphores(len(dense), depth, high_count)
    scratch += ExpertGather.semaphores(depth, local_count)
    scratch += [
        dma((micro_count, 2, depth)),
        dma((micro_count, depth)),
        dma((10 + micro_count,)),
        dma((owners - 1, micro_count)),
        dma((owners - 1, micro_count)),
        dma((owners - 1, micro_count)),
        dma((owners - 1, micro_count)),
        dma((loads, 3)),
        dma((buffers, 3)),
        dma((12 + 2 * local_count,)),
        dma((2, local_count, 3)),
        dma((2, local_count, 3)),
    ]
    return pl.pallas_call(
        functools.partial(forward_kernel, sizes),
        out_shape=out_shape,
        in_specs=[hbm] * 2 + [vmem] * 4 + [hbm] * 9,
        out_specs=[hbm] * len(out_shape),
        scratch_shapes=scratch,
        compiler_params=pltpu.CompilerParams(
            collective_id=0, has_side_effects=True, vmem_limit_bytes=60 * MIB
        ),
        name="gather_and_forward",
    )(tokens, cot, gates, routes, cosine, sine_part, *dense, *experts)


def add_into(target, sources, step):
    def body(here):
        value = target[here, :].astype(F32)
        for source in sources:
            value = value + source[here, :].astype(F32)
        target[here, :] = value.astype(target.dtype)

    tiles(target.shape[0], step, body)


class LineSum:
    def __init__(self, place, part, land, send_sem, recv_sem):
        self.place, self.part, self.land = place, part, land
        self.send_sem, self.recv_sem = send_sem, recv_sem

    def copy(self, z, direction):
        place = self.place
        slot = z if direction > 0 else jnp.where(z == place.z - 1, place.depth, z)
        return remote(
            self.part(z),
            self.land(slot),
            self.send_sem.at[z],
            self.recv_sem.at[slot],
            context=place.z + direction,
        )

    def upstream(self, direction):
        return self.place.z > 0 if direction > 0 else self.place.z < self.place.depth - 1

    def arrive(self, slot):
        arrived(self.land(slot), self.recv_sem.at[slot])

    def at(self, direction, step, body):
        z = self.place.z + direction * step
        pl.when(self.place.on_line(z))(lambda: body(z))

    def pass_on(self, direction, step, add):
        def body(z):
            def more():
                self.arrive(z)
                add(self.part(z), self.land(z))

            pl.when(self.upstream(direction))(more)
            self.copy(z, direction).start()

        self.at(direction, step, body)

    def end(self, add):
        for direction, slot in ((1, self.place.z), (-1, self.place.depth)):

            def body(slot=slot):
                self.arrive(slot)
                add(self.part(self.place.z), self.land(slot))

            pl.when(self.upstream(direction))(body)

    def drain(self):
        for step in range(1, self.place.depth):
            for direction in (1, -1):
                self.at(direction, step, lambda z, d=direction: self.copy(z, d).wait_send())


class DenseScatter:
    def __init__(self, place, source, low, high, line, cross, spare, out, sems):
        self.place, self.source, self.spare, self.out = place, source, spare, out
        self.low, self.high, self.cross = low, high, cross
        (
            self.l_send, self.l_recv, self.h_send, self.h_recv, z_send, z_recv,
            self.x_send, self.x_recv, self.own_sem,
        ) = sems
        self.step = min(64, low.shape[2]) if low.shape[2] % 64 == 0 else 16
        self.line = LineSum(
            place, lambda z: low.at[z, place.high], lambda slot: line.at[slot], z_send, z_recv
        )

    @staticmethod
    def semaphores(count, depth, high_count):
        dma = pltpu.SemaphoreType.DMA
        cross = dma((count, depth, high_count))
        return [
            cross, cross, dma((count, high_count)), dma((count, high_count)),
            dma((count, depth + 1)), dma((count, depth + 1)),
            dma((count,)), dma((count,)), dma((count, 2)),
        ]

    def _index(self, z, high, low):
        return (z * self.place.high_count + high) * 2 + low

    def _to_low(self, z, high):
        place = self.place
        return remote(
            self.source(self._index(z, high, 1 - place.low)),
            self.low.at[z, high],
            self.l_send.at[z, high],
            self.l_recv.at[z, high],
            experts=place.e + 1 - 2 * place.low,
        )

    def _each(self, body):
        for z in range(self.place.depth):
            for high in range(self.place.high_count):
                body(z, high)

    def start(self):
        self._each(lambda z, high: self._to_low(z, high).start())

    def add_low(self):
        place = self.place
        places = [(z, high) for z in range(place.depth) for high in range(place.high_count)]

        def load(i):
            z, high = places[i]
            return pltpu.make_async_copy(
                self.source(self._index(z, high, place.low)),
                self.spare.at[i % 2],
                self.own_sem.at[i % 2],
            )

        if self.spare is not None:
            load(0).start()
        for i, (z, high) in enumerate(places):
            self._to_low(z, high).wait_recv()
            if self.spare is None:
                own = self.source(self._index(z, high, place.low))
            else:
                if i + 1 < len(places):
                    load(i + 1).start()
                load(i).wait()
                own = self.spare.at[i % 2]
            add_into(self.low.at[z, high], [own], self.step)
        for step in range(1, place.high_count):
            self._to_high(step).start()

    def _to_high(self, step):
        place = self.place
        peer = place.peer_high(step)
        return remote(
            self.low.at[:, peer],
            self.high.at[step - 1],
            self.h_send.at[step],
            self.h_recv.at[step],
            experts=peer * 2 + place.low,
        )

    def add_high(self):
        place = self.place
        for step in range(1, place.high_count):
            self._to_high(step).wait_recv()
        for z in range(place.depth):
            add_into(
                self.low.at[z, place.high],
                [self.high.at[step - 1, z] for step in range(1, place.high_count)],
                self.step,
            )

    def _add(self, target, more):
        add_into(target, [more], self.step)

    def pass_on(self, direction, step):
        self.line.pass_on(direction, step, self._add)

    def _across(self):
        place = self.place
        return remote(
            self.low.at[place.z, place.high], self.cross, self.x_send, self.x_recv, dp=1 - place.x
        )

    def end(self):
        self.line.end(self._add)
        self._across().start()

    def _store(self):
        return pltpu.make_async_copy(self.cross, self.out, self.own_sem.at[0])

    def finish(self):
        self._across().wait_recv()
        self._add(self.cross, self.low.at[self.place.z, self.place.high])
        self._store().start()

    def drain_first(self):
        self._each(lambda z, high: self._to_low(z, high).wait_send())
        for step in range(1, self.place.high_count):
            self._to_high(step).wait_send()

    def drain(self):
        self.line.drain()
        self._across().wait_send()
        self._store().wait()


class ExpertScatter:
    def __init__(self, place, sums, cross, land, own, more, early, absorbed, outs, sems):
        self.early, self.absorbed = early, absorbed
        self.at_end = (place.z == 0) | (place.z == place.depth - 1)
        self.beside_end = (place.z == 1) | (place.z == place.depth - 2)
        self.place, self.sums, self.cross, self.land = place, sums, cross, land
        self.own, self.more, self.outs = own, more, outs
        self.x_send, self.x_recv, self.z_send, self.z_recv, self.load_sem, self.out_sem = sems
        self.local_count, self.width = cross[0].shape[1], cross[0].shape[3]

    @staticmethod
    def semaphores(depth, local_count):
        dma = pltpu.SemaphoreType.DMA
        return [
            dma((local_count, 3, depth)),
            dma((local_count, 3, depth)),
            dma((local_count, 3, depth + 1)),
            dma((local_count, 3, depth + 1)),
            dma((3, 3)),
            dma((local_count, 3)),
        ]

    def _line(self, local, kind):
        return LineSum(
            self.place,
            lambda z: self.cross[kind].at[z, local],
            lambda slot: self.land[kind].at[slot, local],
            self.z_send.at[local, kind],
            self.z_recv.at[local, kind],
        )

    def _across(self, local, kind, z):
        return remote(
            expert_slab(self.sums[kind], kind, local, self.place.other_shard(z), self.width),
            self.cross[kind].at[z, local],
            self.x_send.at[local, kind, z],
            self.x_recv.at[local, kind, z],
            dp=1 - self.place.x,
        )

    def _order(self, body):
        place = self.place
        for step in range(place.depth - 1, 0, -1):
            for direction in (1, -1):
                z = place.z + direction * step
                here = place.on_line(z)
                if step == 1:
                    here = here & jnp.logical_not(self.at_end)
                pl.when(here)(lambda z=z: body(z))

    def start(self):
        def body(z):
            for local in range(self.local_count):
                for kind in range(3):
                    self._across(local, kind, z).start()

        self._order(body)
        pl.when(jnp.logical_not(self.beside_end))(lambda: body(self.place.z))

    def absorb(self):
        z = self.place.z

        def body():
            for local in range(self.local_count):
                loads = []
                for kind in range(3):
                    source = expert_slab(
                        self.sums[kind], kind, local, self.place.other_shard(z), self.width
                    )
                    early = self.early[kind].at[1, local]
                    loads.append(
                        [
                            pltpu.make_async_copy(source, self.own[kind], self.load_sem.at[0, kind]),
                            pltpu.make_async_copy(
                                early, self.more[kind].at[0], self.load_sem.at[1, kind]
                            ),
                        ]
                    )
                stores = [
                    pltpu.make_async_copy(
                        self.own[kind], self.absorbed[kind].at[local], self.load_sem.at[0, kind]
                    )
                    for kind in range(3)
                ]
                for pair in loads:
                    for copy in pair:
                        copy.start()
                for kind in range(3):
                    for copy in loads[kind]:
                        copy.wait()
                    add_into(self.own[kind], [self.more[kind].at[0]], 64)
                    stores[kind].start()
                for kind in range(3):
                    stores[kind].wait()
                    remote(
                        self.absorbed[kind].at[local],
                        self.cross[kind].at[z, local],
                        self.x_send.at[local, kind, z],
                        self.x_recv.at[local, kind, z],
                        dp=1 - self.place.x,
                    ).start()

        pl.when(self.beside_end)(body)

    def _own_load(self, local, kind, z):
        return pltpu.make_async_copy(
            expert_slab(self.sums[kind], kind, local, self.place.shard(z), self.width),
            self.own[kind],
            self.load_sem.at[0, kind],
        )

    def _more_load(self, local, kind, slot, which):
        return pltpu.make_async_copy(
            self.land[kind].at[slot, local], self.more[kind].at[which], self.load_sem.at[1 + which, kind]
        )

    def pass_on(self, direction, step, local, kinds=(0, 1, 2)):
        def body(z):
            for kind in kinds:
                self._own_load(local, kind, z).start()
            for kind in kinds:
                line = self._line(local, kind)
                target = self.cross[kind].at[z, local]

                def come(line=line, kind=kind):
                    line.arrive(z)
                    self._more_load(local, kind, z, 0).start()

                pl.when(line.upstream(direction))(come)
                self._across(local, kind, z).wait_recv()
                self._own_load(local, kind, z).wait()

                def both(target=target, kind=kind):
                    self._more_load(local, kind, z, 0).wait()
                    add_into(target, [self.own[kind], self.more[kind].at[0]], 64)

                def single(target=target, kind=kind):
                    add_into(target, [self.own[kind]], 64)

                pl.when(line.upstream(direction))(both)
                pl.when(jnp.logical_not(line.upstream(direction)))(single)
                line.copy(z, direction).start()

        def there(z):
            if step == 1:
                pl.when(jnp.logical_not(self.at_end))(lambda: body(z))
            else:
                body(z)

        self._line(local, 0).at(direction, step, there)

    def _early_load(self, local, kind, which):
        return pltpu.make_async_copy(
            self.early[kind].at[0, local], self.more[kind].at[which], self.load_sem.at[1 + which, kind]
        )

    def end(self, local):
        place = self.place
        z = place.z
        for kind in range(3):
            self._own_load(local, kind, z).start()
        for kind in range(3):
            line = self._line(local, kind)
            target = self.cross[kind].at[z, local]
            for which, (direction, slot) in enumerate(((1, z), (-1, place.depth))):

                def come(slot=slot, which=which, line=line, kind=kind):
                    line.arrive(slot)
                    self._more_load(local, kind, slot, which).start()

                def came(which=which, kind=kind):
                    self._early_load(local, kind, which).start()

                from_end = z - direction == (0 if direction > 0 else place.depth - 1)
                pl.when(line.upstream(direction) & jnp.logical_not(from_end))(come)
                pl.when(from_end)(came)
            self._across(local, kind, z).wait_recv()
            self._own_load(local, kind, z).wait()
            add_into(target, [self.own[kind]], 64)
            for which, (direction, slot) in enumerate(((1, z), (-1, place.depth))):

                def more(slot=slot, which=which, kind=kind, target=target):
                    self._more_load(local, kind, slot, which).wait()
                    add_into(target, [self.more[kind].at[which]], 64)

                pl.when(line.upstream(direction))(more)
            self._store(local, kind).start()

    def _store(self, local, kind):
        return pltpu.make_async_copy(
            self.cross[kind].at[self.place.z, local],
            self.outs[kind].at[local],
            self.out_sem.at[local, kind],
        )

    def drain(self):
        for local in range(self.local_count):
            for kind in range(3):
                self._order(lambda z, p=(local, kind): self._across(*p, z).wait_send())
                self._across(local, kind, self.place.z).wait_send()
                line = self._line(local, kind)
                for step in range(1, self.place.depth):
                    for direction in (1, -1):

                        def sent(z, line=line, direction=direction):
                            line.copy(z, direction).wait_send()

                        def there(z, step=step, sent=sent):
                            if step == 1:
                                pl.when(jnp.logical_not(self.at_end))(lambda: sent(z))
                            else:
                                sent(z)

                        line.at(direction, step, there)
                self._store(local, kind).wait()


def backward_kernel(sizes, *refs):
    place = Place(sizes)
    depth, high_count = sizes
    owners = place.owners
    (
        tokens, cot, gates, routes, cosine, sine_part,
        qkv_w, out_w, gain_v, n1_i, k_i, v_i, q_i, att_i, hid_i, lse_i, side_i, dn2_i,
        gsg, gsu, gsd, geg, geu, ged, outs_i, dins_i, pre_g, pre_u, pre_d,
        mixed_o, input_o, gqkv_o, gout_o, gsg_o, gsu_o, gsd_o, geg_o, geu_o, ged_o, gain_o,
        eland_g, eland_u, eland_d, ret_in, ret_out, d_hidden_o, dn1_o, abs_g, abs_u, abs_d,
        *rest,
    ) = refs
    count = 5
    low, rest = rest[:count], rest[count:]
    high, rest = rest[:count], rest[count:]
    line, rest = rest[:count], rest[count:]
    cross, rest = rest[:count], rest[count:]
    (
        spare_w, spare_t, ecross_g, ecross_u, ecross_d, eown_g, eown_u, eown_d,
        emore_g, emore_u, emore_d,
        d_att, dpq, dpk, dpv, g_qkv, g_out, part, part_land,
        gain_own, gain_low, gain_high, gain_line, gain_cross, out_rows,
        *sems,
    ) = rest
    dense_sems, sems = sems[:9], sems[9:]
    expert_sems, sems = sems[:6], sems[6:]
    (
        part_send, part_recv, ri_send, ri_recv, ro_send, ro_recv,
        gain_send, gain_recv, load_sem, wq_sem, out_sem,
    ) = sems
    micro_count, rows, features = tokens.shape
    prompt = depth * PB
    length = prompt + CONT
    local_count, slots = outs_i.shape[0], outs_i.shape[1]
    total = owners * local_count
    capacity = rows * 8 // (3 * total)
    me = place.e

    def rows_of(ref, size):
        return lambda s: ref.at[pl.ds(pl.multiple_of(s * size, 16), size)]

    def columns_of(ref, size):
        return lambda s: ref.at[:, pl.ds(pl.multiple_of(s * size, 128), size)]

    sources = [
        columns_of(gsg, gsg_o.shape[1]),
        columns_of(gsu, gsu_o.shape[1]),
        rows_of(gsd, gsd_o.shape[0]),
        rows_of(g_qkv, gqkv_o.shape[0]),
        rows_of(g_out, gout_o.shape[0]),
    ]
    spares = [spare_w, spare_w, spare_t, None, None]
    dense = [
        DenseScatter(
            place, sources[i], low[i], high[i], line[i], cross[i], spares[i], out,
            [s.at[i] for s in dense_sems],
        )
        for i, out in enumerate((gsg_o, gsu_o, gsd_o, gqkv_o, gout_o))
    ]
    early, late = dense[:3], dense[3:]
    experts = ExpertScatter(
        place,
        (geg, geu, ged),
        (ecross_g, ecross_u, ecross_d),
        (eland_g, eland_u, eland_d),
        (eown_g, eown_u, eown_d),
        (emore_g, emore_u, emore_d),
        (pre_g, pre_u, pre_d),
        (abs_g, abs_u, abs_d),
        (geg_o, geu_o, ged_o),
        expert_sems,
    )
    prompts = [
        LineSum(
            place,
            lambda z, m=m: part.at[m, z],
            lambda slot, m=m: part_land.at[m, slot],
            part_send.at[m],
            part_recv.at[m],
        )
        for m in range(micro_count)
    ]

    def slot_rows(m, owner_of_rows):
        return pl.ds(pl.multiple_of((m * owners + owner_of_rows) * capacity, 16), capacity)

    def hand_back(source, land, send_sem, recv_sem, m, step):
        peer = place.peer_owner(step)
        return remote(
            source.at[:, slot_rows(m, peer)],
            land.at[m, owners - step],
            send_sem.at[step, m],
            recv_sem.at[owners - step, m],
            experts=peer,
        )

    returns = [(dins_i, ret_in, ri_send, ri_recv), (outs_i, ret_out, ro_send, ro_recv)]
    place.greet()
    for m in range(micro_count):
        for step in range(1, owners):
            hand_back(*returns[0], m, step).start()
    for d in early:
        d.start()
    experts.start()

    def fetch(pairs):
        copies = [
            pltpu.make_async_copy(source, target, load_sem.at[i])
            for i, (source, target) in enumerate(pairs)
        ]
        for copy in copies:
            copy.start()
        for copy in copies:
            copy.wait()

    def fetch_returned(source, land, recv_sem, target, m):
        for step in range(1, owners):
            arrived(land.at[m, step], recv_sem.at[step, m])
        pairs = []
        for step in range(owners):
            for local in range(local_count):
                at = pl.ds((step * local_count + local) * capacity, capacity)
                if step == 0:
                    piece = source.at[local, slot_rows(m, me)]
                else:
                    piece = land.at[m, step, local]
                pairs.append((piece, target.at[at]))
        fetch(pairs)

    for kind, d in enumerate(early):
        for direction in (1, -1):
            experts.pass_on(direction, depth - 1, 0, (kind,))
        d.add_low()
    for m in range(micro_count):
        for step in range(1, owners):
            hand_back(*returns[1], m, step).start()
    experts.absorb()
    gain_own[...] = jnp.zeros_like(gain_own)

    def mark_pairs(first, second, m):
        for i, hit, _ in one_hots(routes.at[m], gates.at[m], me, local_count, total):
            here = pl.ds(i * capacity, capacity)
            expert = lax.rem(me * local_count + i, total)
            hit_first = either(hit, routes[m, 0:1, :] == expert)
            hit_second = either(hit, routes[m, 1:2, :] == expert)
            first[here, :] = hit_first.astype(F32).astype(BF)
            second[here, :] = hit_second.astype(F32).astype(BF)

    def after_experts(hidden, extra, back, first, second, g_rows, att, d_attn, wo):
        fetch([(out_w, wo)] + [(att_i.at[m], att.at[pl.ds(m * rows, rows)]) for m in range(micro_count)])
        for m in range(micro_count):
            fetch([(hid_i.at[m], hidden), (cot.at[m], g_rows), (dn2_i.at[pl.ds(m * rows, rows)], extra)])
            mark_pairs(first, second, m)
            fetch_returned(dins_i, ret_in, ri_recv, back, m)
            gain = gain_v[1:2, :]
            for i in range(rows // PB):
                here = pl.ds(i * PB, PB)
                both = first[:, here] + second[:, here]
                d_normed = extra[here, :] + tdot(both, back[...])
                values = hidden[here, :]
                root = lax.rsqrt(jnp.mean(values * values, -1, keepdims=True) + EPSILON)
                scaled = gain * d_normed
                d_values = (
                    g_rows[here, :].astype(F32)
                    + root * scaled
                    - values * (root * root * root) * jnp.mean(values * scaled, -1, keepdims=True)
                )
                gain_own[1:2, :] += jnp.sum(d_normed * values * root, 0, keepdims=True)
                there = pl.ds(m * rows + i * PB, PB)
                extra[here, :] = d_values
                low_part = d_values.astype(BF)
                d_attn[there, :] = low_part
                d_att[there, :] = ndot(low_part, wo[...]).astype(BF)
            fetch([(extra, d_hidden_o.at[m])])
            for kind in ((0,), (1, 2))[m] if m < 2 else ():
                for direction in (1, -1):
                    experts.pass_on(direction, depth - 1, 1, (kind,))

        def out_grad(here):
            g_out[here, :] = tdot(att[:, here], d_attn[...]).astype(BF)

        tiles(features, 256, out_grad)

    pl.run_scoped(
        after_experts,
        pltpu.VMEM((rows, features), F32),
        pltpu.VMEM((rows, features), F32),
        pltpu.VMEM((total * capacity, features), BF),
        pltpu.VMEM((total * capacity, rows), BF),
        pltpu.VMEM((total * capacity, rows), BF),
        pltpu.VMEM((rows, features), BF),
        pltpu.VMEM((micro_count * rows, features), BF),
        pltpu.VMEM((micro_count * rows, features), BF),
        pltpu.VMEM((features, features), BF),
    )

    def both_ways(items, step):
        for direction in (1, -1):
            for item in items:
                item.pass_on(direction, step)

    def prompts_on(m, step):
        for direction in (1, -1):
            prompts[m].pass_on(direction, step, lambda t, s: add_into(t, [s], 64))

    def experts_on(step, local, where=True, kinds=(0, 1, 2)):
        def body():
            for direction in (1, -1):
                experts.pass_on(direction, step, local, kinds)

        pl.when(where)(body)

    inside = jnp.logical_not(experts.at_end)
    experts_on(depth - 2, 0, inside)

    def own_rows(i):
        start = place.z * PB if i == 0 else prompt + (i - 1) * PB
        return start, pl.ds(start if i else pl.multiple_of(start, PB), PB)

    def attention(k, v, q, lse, ds_s, p_s, wq, dn1):
        load_wq = pltpu.make_async_copy(qkv_w, wq, wq_sem.at[0])
        load_wq.start()
        lane = lax.broadcasted_iota(jnp.int32, (PB, 2 * HD), 1)
        wide_lane = lax.broadcasted_iota(jnp.int32, (rows, 2 * HD), 1)
        pairs = features // (2 * HD)
        ds_s[...] = jnp.zeros_like(ds_s)
        p_s[...] = jnp.zeros_like(p_s)
        for m in range(micro_count):
            fetch([(k_i.at[m], k), (v_i.at[m], v), (q_i.at[m], q), (lse_i.at[m], lse)])
            whole = pl.ds(m * rows, rows)

            def pair(index, carry):
                for kind in range(3):

                    def pass_some(kind=kind):
                        experts_on(depth - 2, m, experts.at_end, (kind,))
                        if m == 0:
                            experts_on(depth - 2, 1, inside, (kind,))

                    pl.when(index == min(2 * kind + 1, pairs - 1))(pass_some)
                lanes = pl.ds(pl.multiple_of(index * 2 * HD, 2 * HD), 2 * HD)
                for i in range(rows // PB):
                    here = pl.ds(i * PB, PB)
                    there = pl.ds(m * rows + i * PB, PB)
                    query, d_out, logs = q[here, lanes], d_att[there, lanes], lse[here, :]
                    start, table = own_rows(i)
                    seen = prompt + i * PB
                    keys, values = k[pl.ds(0, seen), lanes], v[pl.ds(0, seen), lanes]
                    column = lax.broadcasted_iota(jnp.int32, (PB, seen), 1)
                    row = lax.broadcasted_iota(jnp.int32, (PB, seen), 0)
                    allowed = column <= row + start
                    parts = []
                    for sub in range(2):
                        mine = lane // HD == sub
                        scores = ndot(jnp.where(mine, query, jnp.zeros_like(query)), keys)
                        log = jnp.sum(
                            jnp.where(lane == 2 * index + sub, logs, 0.0), -1, keepdims=True
                        )
                        probs = jnp.where(allowed, jnp.exp(scores - log), 0.0)
                        d_probs = ndot(jnp.where(mine, d_out, jnp.zeros_like(d_out)), values)
                        centre = jnp.sum(probs * d_probs, -1, keepdims=True)
                        d_scores = (probs * (d_probs - centre)).astype(BF)
                        ds_s[sub, here, pl.ds(0, seen)] = d_scores
                        p_s[sub, here, pl.ds(0, seen)] = probs.astype(BF)
                        parts.append(mdot(d_scores, keys))
                    d_query = jnp.where(lane < HD, parts[0], parts[1]) * HD**-0.5
                    d_query = rope(d_query, cosine[table, :], -sine_part[table, :])
                    dpq[there, lanes] = d_query.astype(BF)
                d_key = jnp.zeros((length, 2 * HD), F32)
                d_value = jnp.zeros((length, 2 * HD), F32)
                query, d_out = q[:, lanes], d_att[whole, lanes]
                for sub in range(2):
                    mine = wide_lane // HD == sub
                    d_key += tdot(ds_s[sub], jnp.where(mine, query, jnp.zeros_like(query)))
                    d_value += tdot(p_s[sub], jnp.where(mine, d_out, jnp.zeros_like(d_out)))
                keys_here = pl.ds(m * length, length)
                d_key = rope(d_key, cosine[...], -sine_part[...])
                dpk[keys_here, lanes] = d_key.astype(BF)
                dpv[keys_here, lanes] = d_value.astype(BF)
                return carry

            lax.fori_loop(0, pairs, pair, 0)
            if m == 0:
                load_wq.wait()
            key_w, value_w = wq[pl.ds(features, features), :], wq[pl.ds(2 * features, features), :]
            for z in range(depth):
                here = pl.ds(m * length + z * PB, PB)
                part[m, z] = (mdot(dpk[here, :], key_w) + mdot(dpv[here, :], value_w)).astype(BF)
            prompts_on(m, depth - 1)
            for i in range(rows // PB):
                _, table = own_rows(i)
                start = own_rows(i)[0] + m * length
                here = pl.ds(pl.multiple_of(start, PB), PB)
                there = pl.ds(m * rows + i * PB, PB)
                dn1[pl.ds(i * PB, PB), :] = (
                    mdot(dpq[there, :], wq[pl.ds(0, features), :])
                    + mdot(dpk[here, :], key_w)
                    + mdot(dpv[here, :], value_w)
                )
            fetch([(dn1, dn1_o.at[m])])
            if m == 0:
                for d in early:
                    d.add_high()
                both_ways(early, depth - 1)

    pl.run_scoped(
        attention,
        pltpu.VMEM((length, features), BF),
        pltpu.VMEM((length, features), BF),
        pltpu.VMEM((rows, features), BF),
        pltpu.VMEM((rows, 2 * HD), F32),
        pltpu.VMEM((2, rows, length), BF),
        pltpu.VMEM((2, rows, length), BF),
        pltpu.VMEM(qkv_w.shape, BF),
        pltpu.VMEM((rows, features), F32),
    )

    def weight_grads(n1, n1_own):
        pairs = []
        for m in range(micro_count):
            pairs.append((n1_i.at[m], n1.at[pl.ds(m * length, length)]))
            for i in range(rows // PB):
                _, here = own_rows(i)
                pairs.append((n1_i.at[m, here], n1_own.at[pl.ds(m * rows + i * PB, PB)]))
        fetch(pairs)

        def make(here):
            g_qkv[here, :] = tdot(dpq[:, here], n1_own[...]).astype(BF)

        def make_key(here):
            there = pl.ds(pl.multiple_of(here.start + features, 256), 256)
            g_qkv[there, :] = tdot(dpk[:, here], n1[...]).astype(BF)

        def make_value(here):
            there = pl.ds(pl.multiple_of(here.start + 2 * features, 256), 256)
            g_qkv[there, :] = tdot(dpv[:, here], n1[...]).astype(BF)

        tiles(features, 256, make)
        tiles(features, 256, make_key)
        tiles(features, 256, make_value)

    pl.run_scoped(
        weight_grads,
        pltpu.VMEM((micro_count * length, features), BF),
        pltpu.VMEM((micro_count * rows, features), BF),
    )
    for d in late:
        d.start()

    for d in late:
        d.add_low()

    def column_of(values):
        dims = (values.shape[1], values.shape[1])
        across = lax.broadcasted_iota(jnp.int32, dims, 1)
        diagonal = lax.broadcasted_iota(jnp.int32, dims, 0) == across
        return jnp.sum(jnp.where(diagonal, values, 0.0), -1, keepdims=True)

    def outputs(hidden, side, back, first, second):
        for m in range(micro_count):
            fetch([(hid_i.at[m], hidden), (side_i.at[pl.ds(m * rows, rows)], side)])
            mark_pairs(first, second, m)
            fetch_returned(outs_i, ret_out, ro_recv, back, m)
            for i in range(rows // PB):
                here = pl.ds(i * PB, PB)
                routed = column_of(gates[m, 0:1, here]) * tdot(first[:, here], back[...])
                routed += column_of(gates[m, 1:2, here]) * tdot(second[:, here], back[...])
                out_rows[here, :] = (hidden[here, :] + side[here, :] + routed).astype(BF)
            fetch([(out_rows, mixed_o.at[m])])
            if m == 0:
                for step in range(depth - 2, 1, -1):
                    for n in range(micro_count):
                        prompts_on(n, step)
                    both_ways(early, step)
                for step in range(depth - 3, 0, -1):
                    experts_on(step, 0)

    pl.run_scoped(
        outputs,
        pltpu.VMEM((rows, features), F32),
        pltpu.VMEM((rows, features), F32),
        pltpu.VMEM((total * capacity, features), BF),
        pltpu.VMEM((total * capacity, rows), BF),
        pltpu.VMEM((total * capacity, rows), BF),
    )

    def last_on(kind):
        for step in range(depth - 3, 0, -1):
            for local in range(1, local_count):
                for direction in (1, -1):
                    experts.pass_on(direction, step, local, (kind,))

    for d in late:
        d.add_high()
    both_ways(late, depth - 1)
    for m in range(micro_count):
        prompts_on(m, 1)
    for step in range(depth - 2, 1, -1):
        both_ways(late, step)
    both_ways(early, 1)
    last_on(0)
    last_on(1)

    def inputs(x_rows, d_hidden, dn1):
        for m in range(micro_count):
            fetch([(tokens.at[m], x_rows), (d_hidden_o.at[m], d_hidden), (dn1_o.at[m], dn1)])
            for direction, slot in ((1, place.z), (-1, depth)):

                def body(m=m, slot=slot):
                    prompts[m].arrive(slot)
                    dn1[pl.ds(0, PB), :] += part_land[m, slot].astype(F32)

                pl.when(prompts[m].upstream(direction))(body)
            gain = gain_v[0:1, :]
            for i in range(rows // PB):
                here = pl.ds(i * PB, PB)
                values, d_normed = x_rows[here, :].astype(F32), dn1[here, :]
                root = lax.rsqrt(jnp.mean(values * values, -1, keepdims=True) + EPSILON)
                scaled = gain * d_normed
                d_values = (
                    d_hidden[here, :]
                    + root * scaled
                    - values * (root * root * root) * jnp.mean(values * scaled, -1, keepdims=True)
                )
                gain_own[0:1, :] += jnp.sum(d_normed * values * root, 0, keepdims=True)
                out_rows[here, :] = d_values.astype(BF)
            fetch([(out_rows, input_o.at[m])])

    pl.run_scoped(
        inputs,
        pltpu.VMEM((rows, features), BF),
        pltpu.VMEM((rows, features), F32),
        pltpu.VMEM((rows, features), F32),
    )
    def gain_copies(first, targets, lands):
        return [
            remote(gain_own, land, gain_send.at[first + i], gain_recv.at[first + i], **target)
            for i, (target, land) in enumerate(zip(targets, lands))
        ]

    def gain_add(copies, lands):
        for copy in copies:
            copy.wait()
        total_gain = gain_own[...]
        for land in lands:
            total_gain = total_gain + land[...]
        gain_own[...] = total_gain

    peers = range(1, high_count)
    places = range(1, depth)
    stages = [
        (0, [dict(experts=place.e + 1 - 2 * place.low)], [gain_low]),
        (
            1,
            [dict(experts=place.peer_high(s) * 2 + place.low) for s in peers],
            [gain_high.at[s - 1] for s in peers],
        ),
        (
            high_count,
            [dict(context=lax.rem(place.z + s, depth)) for s in places],
            [gain_line.at[s - 1] for s in places],
        ),
        (high_count + depth - 1, [dict(dp=1 - place.x)], [gain_cross]),
    ]

    def gain_start(i):
        copies = gain_copies(*stages[i])
        for copy in copies:
            copy.start()
        return copies

    copies = gain_start(0)
    both_ways(late, 1)
    gain_add(copies, stages[0][2])
    copies = gain_start(1)
    last_on(2)
    gain_add(copies, stages[1][2])
    copies = gain_start(3)
    for d in early:
        d.end()

    experts.end(0)
    for d in dense:
        d.drain_first()
    for m in range(micro_count):
        for step in range(1, owners):
            for entry in returns:
                hand_back(*entry, m, step).wait_send()
    gain_add(copies, stages[3][2])
    copies = gain_start(2)
    for local in range(1, local_count):
        experts.end(local)
    for d in late:
        d.end()
    for d in early:
        d.finish()
    for d in late:
        d.finish()
    gain_add(copies, stages[2][2])
    fetch([(gain_own, gain_o)])
    for d in dense:
        d.drain()
    experts.drain()
    for p in prompts:
        p.drain()


def run_backward(sizes, tokens, cot, gates, routes, forward):
    depth, high_count = sizes
    micro_count, rows, features = tokens.shape
    owners = high_count * 2
    line = depth * owners
    prompt = depth * PB
    length = prompt + CONT
    cosine, sine_part = rope_tables(prompt)
    gsg, geg, outs = forward[12], forward[15], forward[18]
    local_count, slots, _ = outs.shape
    total = owners * local_count
    capacity = rows * 8 // (3 * total)
    part = gsg.shape[1] // line
    width = geg.shape[2] // (2 * depth)
    hbm, vmem = pl.BlockSpec(memory_space=pltpu.HBM), pl.BlockSpec(memory_space=pltpu.VMEM)
    shapes = [(features, part), (features, part), (part, features)]
    shapes += [(forward[0].shape[0] // line, features), (forward[1].shape[0] // line, features)]
    expert_shapes = [(features, width), (features, width), (width, features)]
    returned = (micro_count, owners, local_count, capacity, features)
    out_dims = [(micro_count, rows, features)] * 2
    out_dims += [shapes[3], shapes[4], shapes[0], shapes[1], shapes[2]]
    out_dims += [(local_count,) + s for s in expert_shapes]
    out_shape = [jax.ShapeDtypeStruct(dims, BF) for dims in out_dims]
    out_shape += [jax.ShapeDtypeStruct((8, features), F32)]
    out_shape += [jax.ShapeDtypeStruct((depth + 1, local_count) + s, BF) for s in expert_shapes]
    out_shape += [jax.ShapeDtypeStruct(returned, BF)] * 2
    out_shape += [jax.ShapeDtypeStruct((micro_count, rows, features), F32)] * 2
    out_shape += [jax.ShapeDtypeStruct((local_count,) + s, BF) for s in expert_shapes]
    scratch = [pltpu.VMEM((depth, high_count) + s, BF) for s in shapes]
    scratch += [pltpu.VMEM((high_count - 1, depth) + s, BF) for s in shapes]
    scratch += [pltpu.VMEM((depth + 1,) + s, BF) for s in shapes]
    scratch += [pltpu.VMEM(s, BF) for s in shapes]
    scratch += [pltpu.VMEM((2,) + shapes[0], BF), pltpu.VMEM((2,) + shapes[2], BF)]
    scratch += [pltpu.VMEM((depth, local_count) + s, BF) for s in expert_shapes]
    scratch += [pltpu.VMEM(s, BF) for s in expert_shapes]
    scratch += [pltpu.VMEM((2,) + s, BF) for s in expert_shapes]
    token_rows, key_rows = micro_count * rows, micro_count * length
    gain = (8, features)
    scratch += [
        pltpu.VMEM((token_rows, features), BF),
        pltpu.VMEM((token_rows, features), BF),
        pltpu.VMEM((key_rows, features), BF),
        pltpu.VMEM((key_rows, features), BF),
        pltpu.VMEM(forward[0].shape, BF),
        pltpu.VMEM(forward[1].shape, BF),
        pltpu.VMEM((micro_count, depth, PB, features), BF),
        pltpu.VMEM((micro_count, depth + 1, PB, features), BF),
        pltpu.VMEM(gain, F32),
        pltpu.VMEM(gain, F32),
        pltpu.VMEM((high_count - 1,) + gain, F32),
        pltpu.VMEM((depth - 1,) + gain, F32),
        pltpu.VMEM(gain, F32),
        pltpu.VMEM((rows, features), BF),
    ]
    dma = pltpu.SemaphoreType.DMA
    scratch += DenseScatter.semaphores(len(shapes), depth, high_count)
    scratch += ExpertScatter.semaphores(depth, local_count)
    stages = 1 + high_count + depth
    scratch += [
        dma((micro_count, depth + 1)),
        dma((micro_count, depth + 1)),
        dma((owners, micro_count)),
        dma((owners, micro_count)),
        dma((owners, micro_count)),
        dma((owners, micro_count)),
        dma((stages,)),
        dma((stages,)),
        dma((max(total, 2 + micro_count, 4 * micro_count + micro_count),)),
        dma((1,)),
        dma((1,)),
    ]
    return pl.pallas_call(
        functools.partial(backward_kernel, sizes),
        out_shape=out_shape,
        in_specs=[hbm] * 2 + [vmem] * 4 + [hbm] * 2 + [vmem] + [hbm] * 20,
        out_specs=[hbm] * len(out_shape),
        scratch_shapes=scratch,
        compiler_params=pltpu.CompilerParams(
            collective_id=1, has_side_effects=True, vmem_limit_bytes=60 * MIB
        ),
        name="backward_and_sum",
    )(tokens, cot, gates, routes, cosine, sine_part, *forward)


def finish_kernel(count, gain_width, *refs):
    low, refs = refs[:count], refs[count:]
    rows, refs = refs[:2], refs[2:]
    gain, refs = refs[0], refs[1:]
    rows_o, refs = refs[:2], refs[2:]
    wide_o, refs = refs[:count], refs[count:]
    gain_o, refs = refs[0], refs[1:]
    low_s, refs = refs[:count], refs[count:]
    wide_s, refs = refs[:count], refs[count:]
    rows_s, sem_in, sem_out = refs[:2], refs[2], refs[3]
    loads = [
        pltpu.make_async_copy(source, target, sem_in.at[i])
        for i, (source, target) in enumerate(zip(low + rows, low_s + rows_s))
    ]
    for copy in loads:
        copy.start()
    stores = [
        pltpu.make_async_copy(source, target, sem_out.at[i])
        for i, (source, target) in enumerate(zip(wide_s + rows_s, wide_o + rows_o))
    ]
    place = (lax.axis_index(CONTEXT) * lax.axis_size(EXPERTS) + lax.axis_index(EXPERTS)) * gain_width
    features = gain.shape[1]
    gain_o[...] = pltpu.roll(gain[...], lax.rem(features - place, features), 1)[:2, :gain_width]
    for i in range(count):
        loads[i].wait()
        wide_s[i][...] = low_s[i][...].astype(F32)
        stores[i].start()
    for i in range(count, count + 2):
        loads[i].wait()
        stores[i].start()
    for copy in stores:
        copy.wait()


def finish_outputs(low, rows, gain, gain_width):
    count = len(low)
    hbm, vmem = pl.BlockSpec(memory_space=pltpu.HBM), pl.BlockSpec(memory_space=pltpu.VMEM)
    wide = [item.shape for item in low]
    out_shape = [jax.ShapeDtypeStruct(item.shape, BF) for item in rows]
    out_shape += [jax.ShapeDtypeStruct(dims, F32) for dims in wide]
    out_shape += [jax.ShapeDtypeStruct((2, gain_width), F32)]
    dma = pltpu.SemaphoreType.DMA
    return pl.pallas_call(
        functools.partial(finish_kernel, count, gain_width),
        out_shape=out_shape,
        in_specs=[hbm] * (count + 2) + [vmem],
        out_specs=[hbm] * (count + 2) + [vmem],
        scratch_shapes=[pltpu.VMEM(item.shape, BF) for item in low]
        + [pltpu.VMEM(dims, F32) for dims in wide]
        + [pltpu.VMEM(item.shape, BF) for item in rows]
        + [dma((count + 2,)), dma((count + 2,))],
        compiler_params=pltpu.CompilerParams(vmem_limit_bytes=60 * MIB),
        name="finish_outputs",
    )(*low, *rows, gain)


def on_device_plain(
    tokens,
    cotangent,
    gates,
    routes,
    qkv_weight,
    out_weight,
    shared_gate,
    shared_up,
    shared_down,
    gains,
    expert_gate,
    expert_up,
    expert_down,
):
    micro_count = tokens.shape[2]
    row_count = tokens.shape[4]
    feature_count = tokens.shape[5]
    owners = lax.axis_size(EXPERTS)
    local_experts = expert_gate.shape[0]
    total_experts = owners * local_experts
    capacity = row_count * 8 // (3 * total_experts)
    blocks = lax.axis_size(CONTEXT)
    prompt = blocks * PB
    scaling = HD ** (-0.5)
    w_qkv, w_out, w_sgate, w_sup, w_sdown, w_gains = (
        lax.all_gather(qkv_weight, (CONTEXT, EXPERTS), axis=1, tiled=True),
        lax.all_gather(out_weight, (CONTEXT, EXPERTS), axis=0, tiled=True),
        lax.all_gather(shared_gate, (CONTEXT, EXPERTS), axis=1, tiled=True),
        lax.all_gather(shared_up, (CONTEXT, EXPERTS), axis=1, tiled=True),
        lax.all_gather(shared_down, (CONTEXT, EXPERTS), axis=0, tiled=True),
        lax.all_gather(gains, (CONTEXT, EXPERTS), axis=1, tiled=True),
    )
    e_gate, expert_up_weight, e_down = (
        lax.all_gather(expert_gate, (DP, CONTEXT), axis=2, tiled=True),
        lax.all_gather(expert_up, (DP, CONTEXT), axis=2, tiled=True),
        lax.all_gather(expert_down, (DP, CONTEXT), axis=1, tiled=True),
    )
    gain_one = w_gains[0].astype(jnp.float32)
    gain_two = w_gains[1].astype(jnp.float32)
    here_index = lax.axis_index(CONTEXT)
    row_ids = jnp.arange(row_count, dtype=jnp.int32)
    query_pos = jnp.where(row_ids < PB, here_index * PB + row_ids, prompt + row_ids - PB)
    key_pos = jnp.arange(prompt + CONT, dtype=jnp.int32)
    allowed = key_pos[None, None, :] <= query_pos[None, :, None]
    half_size = HD // 2
    frequency = 10000.0 ** (-2.0 * jnp.arange(half_size, dtype=jnp.float32) / HD)
    angles = query_pos.astype(jnp.float32)[:, None] * frequency
    cosine = jnp.cos(angles)[:, None, :]
    sine_part = jnp.sin(angles)[:, None, :]
    kept_list = []
    mixed_list = []
    for step_index in range(micro_count):
        inputs = tokens[0, 0, step_index, 0].astype(jnp.float32)
        root_one = lax.rsqrt(jnp.mean(inputs * inputs, -1, keepdims=True) + EPSILON)
        normed_one = (inputs * root_one * gain_one).astype(jnp.bfloat16)
        projected = mdot(normed_one, w_qkv)
        query = rotate(projected[:, :feature_count], cosine, sine_part).astype(jnp.bfloat16)
        key_rows = rotate(
            projected[:, feature_count : 2 * feature_count], cosine, sine_part
        ).astype(jnp.bfloat16)
        value_rows = projected[:, 2 * feature_count :].astype(jnp.bfloat16)
        prompt_key, prompt_value = (
            lax.all_gather(key_rows[:PB], CONTEXT, axis=0, tiled=True),
            lax.all_gather(value_rows[:PB], CONTEXT, axis=0, tiled=True),
        )
        key_heads = jnp.concatenate([prompt_key, key_rows[PB:]], 0).reshape(prompt + CONT, H, HD)
        value_heads = jnp.concatenate([prompt_value, value_rows[PB:]], 0).reshape(
            prompt + CONT, H, HD
        )
        query_heads = query.reshape(row_count, H, HD)
        scores = (
            jnp.einsum("qhd,khd->hqk", query_heads, key_heads, preferred_element_type=jnp.float32)
            * scaling
        )
        scores = jnp.where(allowed, scores, -1000000000.0)
        highest = jnp.max(scores, -1, keepdims=True)
        weights = jnp.exp(scores - highest)
        total = jnp.sum(weights, -1, keepdims=True)
        log_total = highest + jnp.log(total)
        probs = (weights / total).astype(jnp.bfloat16)
        attended = (
            jnp.einsum("hqk,khd->qhd", probs, value_heads, preferred_element_type=jnp.float32)
            .reshape(row_count, feature_count)
            .astype(jnp.bfloat16)
        )
        hidden = inputs + mdot(attended, w_out)
        root_two = lax.rsqrt(jnp.mean(hidden * hidden, -1, keepdims=True) + EPSILON)
        normed_two = (hidden * root_two * gain_two).astype(jnp.bfloat16)
        side_gate = mdot(normed_two, w_sgate)
        side_up = mdot(normed_two, w_sup)
        side_act = (jax.nn.silu(side_gate) * side_up).astype(jnp.bfloat16)
        side = mdot(side_act, w_sdown)
        route_rows = routes[0, 0, step_index, 0]
        slots = slot_table(route_rows, total_experts)
        flat_dest = (route_rows * capacity + slots).reshape(-1)
        source = (
            jnp.full((total_experts * capacity,), 2 * row_count, jnp.int32)
            .at[flat_dest]
            .set(jnp.arange(2 * row_count, dtype=jnp.int32))
        )
        padded = jnp.concatenate([normed_two, jnp.zeros((1, feature_count), jnp.bfloat16)], 0)
        send = padded[source // 2].reshape(total_experts, capacity, feature_count)
        received = lax.all_to_all(send, EXPERTS, split_axis=0, concat_axis=0, tiled=True)
        count = received.shape[1]
        expert_grouped = received.reshape(owners, local_experts, count, feature_count)
        expert_gate_act = jnp.einsum(
            "send,edf->senf", expert_grouped, e_gate, preferred_element_type=jnp.float32
        )
        expert_up_act = jnp.einsum(
            "send,edf->senf", expert_grouped, expert_up_weight, preferred_element_type=jnp.float32
        )
        expert_hidden_act = (jax.nn.silu(expert_gate_act) * expert_up_act).astype(jnp.bfloat16)
        result = jnp.einsum(
            "senf,efd->send", expert_hidden_act, e_down, preferred_element_type=jnp.float32
        ).astype(jnp.bfloat16)
        expert_out = result.reshape(owners * local_experts, count, feature_count)
        expert_in = received
        returned = lax.all_to_all(
            expert_out, EXPERTS, split_axis=0, concat_axis=0, tiled=True
        ).reshape(-1, feature_count)
        gate_rows = gates[0, 0, step_index, 0]
        picked = returned[flat_dest].reshape(row_count, 2, feature_count).astype(jnp.float32)
        routed = jnp.sum(gate_rows[:, :, None] * picked, 1)
        mixed_list.append((hidden + routed + side).astype(jnp.bfloat16))
        cached = (prompt_key, prompt_value)
        kept_list.append(
            (
                inputs,
                root_one,
                normed_one,
                query,
                key_rows,
                value_rows,
                cached,
                log_total,
                attended,
                hidden,
                root_two,
                normed_two,
                side_gate,
                side_up,
                side_act,
                flat_dest,
                source,
                expert_in,
                gate_rows,
            )
        )
    acc_qkv = jnp.zeros(w_qkv.shape, jnp.float32)
    acc_out = jnp.zeros(w_out.shape, jnp.float32)
    acc_sgate = jnp.zeros(w_sgate.shape, jnp.float32)
    acc_sup = jnp.zeros(w_sup.shape, jnp.float32)
    acc_sdown = jnp.zeros(w_sdown.shape, jnp.float32)
    acc_gain_one = jnp.zeros((feature_count,), jnp.float32)
    acc_gain_two = jnp.zeros((feature_count,), jnp.float32)
    local_egate = jnp.zeros(e_gate.shape, jnp.float32)
    local_expert_up_weight = jnp.zeros(expert_up_weight.shape, jnp.float32)
    local_edown = jnp.zeros(e_down.shape, jnp.float32)
    input_list = []
    for step_index in range(micro_count):
        (
            inputs,
            root_one,
            normed_one,
            query,
            key_rows,
            value_rows,
            cached,
            log_total,
            attended,
            hidden,
            root_two,
            normed_two,
            side_gate,
            side_up,
            side_act,
            flat_dest,
            source,
            expert_in,
            gate_rows,
        ) = kept_list[step_index]
        grad_rows = cotangent[0, 0, step_index, 0].astype(jnp.float32)
        grad_low = grad_rows.astype(jnp.bfloat16)
        acc_sdown = acc_sdown + tdot(side_act, grad_low)
        d_side_act = ndot(grad_low, w_sdown).astype(jnp.bfloat16).astype(jnp.float32)
        silu_side, slope_side = silu_parts(side_gate)
        d_side_gate = (d_side_act * side_up * slope_side).astype(jnp.bfloat16)
        d_side_up = (d_side_act * silu_side).astype(jnp.bfloat16)
        acc_sgate = acc_sgate + tdot(normed_two, d_side_gate)
        acc_sup = acc_sup + tdot(normed_two, d_side_up)
        d_normed_two = ndot(d_side_gate, w_sgate) + ndot(d_side_up, w_sup)
        d_pairs = (
            (gate_rows[:, :, None] * grad_rows[:, None, :])
            .astype(jnp.bfloat16)
            .reshape(2 * row_count, feature_count)
        )
        padded_grad = jnp.concatenate([d_pairs, jnp.zeros((1, feature_count), jnp.bfloat16)], 0)
        grad_send = padded_grad[source].reshape(total_experts, capacity, feature_count)
        grad_in = lax.all_to_all(grad_send, EXPERTS, split_axis=0, concat_axis=0, tiled=True)
        grouped_grad = grad_in.reshape(owners, local_experts, capacity, feature_count)
        grouped = expert_in.reshape(owners, local_experts, capacity, feature_count)
        gate_act = jnp.einsum("send,edf->senf", grouped, e_gate, preferred_element_type=jnp.float32)
        up_act = jnp.einsum(
            "send,edf->senf", grouped, expert_up_weight, preferred_element_type=jnp.float32
        )
        silu_gate, slope_gate = silu_parts(gate_act)
        hidden_act = (silu_gate * up_act).astype(jnp.bfloat16)
        d_hidden_act = (
            jnp.einsum("send,efd->senf", grouped_grad, e_down, preferred_element_type=jnp.float32)
            .astype(jnp.bfloat16)
            .astype(jnp.float32)
        )
        d_gate_act = (d_hidden_act * up_act * slope_gate).astype(jnp.bfloat16)
        d_up_act = (d_hidden_act * silu_gate).astype(jnp.bfloat16)
        step_edown = jnp.einsum(
            "senf,send->efd", hidden_act, grouped_grad, preferred_element_type=jnp.float32
        )
        step_egate = jnp.einsum(
            "send,senf->edf", grouped, d_gate_act, preferred_element_type=jnp.float32
        )
        stepwise_expert_up = jnp.einsum(
            "send,senf->edf", grouped, d_up_act, preferred_element_type=jnp.float32
        )
        local_egate = local_egate + step_egate
        local_expert_up_weight = local_expert_up_weight + stepwise_expert_up
        local_edown = local_edown + step_edown
        d_expert_in = jnp.einsum(
            "senf,edf->send", d_gate_act, e_gate, preferred_element_type=jnp.float32
        ) + jnp.einsum(
            "senf,edf->send", d_up_act, expert_up_weight, preferred_element_type=jnp.float32
        )
        d_expert_in = d_expert_in.astype(jnp.bfloat16).reshape(
            total_experts, capacity, feature_count
        )
        back = lax.all_to_all(
            d_expert_in, EXPERTS, split_axis=0, concat_axis=0, tiled=True
        ).reshape(-1, feature_count)
        d_normed_two = d_normed_two + jnp.sum(
            back[flat_dest].reshape(row_count, 2, feature_count).astype(jnp.float32), 1
        )
        scaled_two = gain_two * d_normed_two
        d_hidden = (
            grad_rows
            + root_two * scaled_two
            - hidden * root_two**3 * jnp.mean(hidden * scaled_two, -1, keepdims=True)
        )
        acc_gain_two = acc_gain_two + jnp.sum(d_normed_two * hidden * root_two, 0)
        d_attn = d_hidden.astype(jnp.bfloat16)
        acc_out = acc_out + tdot(attended, d_attn)
        d_attended = ndot(d_attn, w_out).astype(jnp.bfloat16)
        prompt_key, prompt_value = cached
        key_heads = jnp.concatenate([prompt_key, key_rows[PB:]], 0).reshape(prompt + CONT, H, HD)
        value_heads = jnp.concatenate([prompt_value, value_rows[PB:]], 0).reshape(
            prompt + CONT, H, HD
        )
        query_heads = query.reshape(row_count, H, HD)
        scores = (
            jnp.einsum("qhd,khd->hqk", query_heads, key_heads, preferred_element_type=jnp.float32)
            * scaling
        )
        scores = jnp.where(allowed, scores, -1000000000.0)
        probs = jnp.exp(scores - log_total)
        d_heads = d_attended.reshape(row_count, H, HD)
        d_probs = jnp.einsum(
            "qhd,khd->hqk", d_heads, value_heads, preferred_element_type=jnp.float32
        )
        centre = jnp.sum(probs * d_probs, -1, keepdims=True)
        d_scores = (probs * (d_probs - centre)).astype(jnp.bfloat16)
        d_query = (
            jnp.einsum(
                "hqk,khd->qhd", d_scores, key_heads, preferred_element_type=jnp.float32
            ).reshape(row_count, feature_count)
            * scaling
        )
        d_keys = (
            jnp.einsum(
                "hqk,qhd->khd", d_scores, query_heads, preferred_element_type=jnp.float32
            ).reshape(prompt + CONT, feature_count)
            * scaling
        )
        d_values = jnp.einsum(
            "hqk,qhd->khd", probs.astype(jnp.bfloat16), d_heads, preferred_element_type=jnp.float32
        ).reshape(prompt + CONT, feature_count)
        own_dkey, own_dvalue = (
            lax.psum_scatter(
                d_keys[:prompt].astype(jnp.bfloat16), CONTEXT, scatter_dimension=0, tiled=True
            ).astype(jnp.float32),
            lax.psum_scatter(
                d_values[:prompt].astype(jnp.bfloat16), CONTEXT, scatter_dimension=0, tiled=True
            ).astype(jnp.float32),
        )
        d_key_rows = jnp.concatenate([own_dkey, d_keys[prompt:]], 0)
        d_value_rows = jnp.concatenate([own_dvalue, d_values[prompt:]], 0)
        d_projected = jnp.concatenate(
            [
                rotate(d_query, cosine, -sine_part).astype(jnp.bfloat16),
                rotate(d_key_rows, cosine, -sine_part).astype(jnp.bfloat16),
                d_value_rows.astype(jnp.bfloat16),
            ],
            1,
        )
        acc_qkv = acc_qkv + tdot(normed_one, d_projected)
        d_normed_one = ndot(d_projected, w_qkv)
        scaled_one = gain_one * d_normed_one
        d_inputs = (
            d_hidden
            + root_one * scaled_one
            - inputs * root_one**3 * jnp.mean(inputs * scaled_one, -1, keepdims=True)
        )
        acc_gain_one = acc_gain_one + jnp.sum(d_normed_one * inputs * root_one, 0)
        input_list.append(d_inputs.astype(jnp.bfloat16))
    sharded_expert_gate, sharded_expert_up, sharded_expert_down = (
        lax.psum_scatter(
            local_egate.astype(jnp.bfloat16), (DP, CONTEXT), scatter_dimension=2, tiled=True
        ).astype(jnp.float32),
        lax.psum_scatter(
            local_expert_up_weight.astype(jnp.bfloat16),
            (DP, CONTEXT),
            scatter_dimension=2,
            tiled=True,
        ).astype(jnp.float32),
        lax.psum_scatter(
            local_edown.astype(jnp.bfloat16), (DP, CONTEXT), scatter_dimension=1, tiled=True
        ).astype(jnp.float32),
    )
    acc_gains = jnp.stack([acc_gain_one, acc_gain_two], 0)
    dense_shards = (
        lax.psum_scatter(acc_qkv, (CONTEXT, EXPERTS), scatter_dimension=1, tiled=True),
        lax.psum_scatter(acc_out, (CONTEXT, EXPERTS), scatter_dimension=0, tiled=True),
        lax.psum_scatter(acc_sgate, (CONTEXT, EXPERTS), scatter_dimension=1, tiled=True),
        lax.psum_scatter(acc_sup, (CONTEXT, EXPERTS), scatter_dimension=1, tiled=True),
        lax.psum_scatter(acc_sdown, (CONTEXT, EXPERTS), scatter_dimension=0, tiled=True),
        lax.psum_scatter(acc_gains, (CONTEXT, EXPERTS), scatter_dimension=1, tiled=True),
    )
    grad_qkv, grad_out, grad_sgate, grad_sup, grad_sdown, grad_gains = (
        lax.psum(dense_shards[0].astype(jnp.bfloat16), DP).astype(jnp.float32),
        lax.psum(dense_shards[1].astype(jnp.bfloat16), DP).astype(jnp.float32),
        lax.psum(dense_shards[2].astype(jnp.bfloat16), DP).astype(jnp.float32),
        lax.psum(dense_shards[3].astype(jnp.bfloat16), DP).astype(jnp.float32),
        lax.psum(dense_shards[4].astype(jnp.bfloat16), DP).astype(jnp.float32),
        lax.psum(dense_shards[5].astype(jnp.bfloat16), DP).astype(jnp.float32),
    )
    mixed = jnp.stack(mixed_list, 0).reshape(tokens.shape)
    input_grad = jnp.stack(input_list, 0).reshape(tokens.shape)
    return (
        mixed,
        input_grad,
        grad_qkv,
        grad_out,
        grad_sgate,
        grad_sup,
        grad_sdown,
        grad_gains,
        sharded_expert_gate,
        sharded_expert_up,
        sharded_expert_down,
    )


def on_device(
    tokens,
    cotangent,
    gates,
    routes,
    qkv_weight,
    out_weight,
    shared_gate,
    shared_up,
    shared_down,
    gains,
    expert_gate,
    expert_up,
    expert_down,
):
    owners = lax.axis_size(EXPERTS)
    sizes = (lax.axis_size(CONTEXT), owners // 2)
    own_at = lax.axis_index(CONTEXT) * owners + lax.axis_index(EXPERTS)
    gain_width, features = gains.shape[1], tokens.shape[5]
    gain_rows = lax.dynamic_update_slice(
        jnp.zeros((16, features), jnp.bfloat16), gains, (0, own_at * gain_width)
    )
    rows, cot = tokens[0, 0, :, 0], cotangent[0, 0, :, 0]
    gate_columns = gates[0, 0, :, 0].transpose(0, 2, 1)
    route_columns = routes[0, 0, :, 0].transpose(0, 2, 1)
    forward = run_forward(
        sizes,
        rows,
        cot,
        gate_columns,
        route_columns,
        (qkv_weight.T, out_weight, gain_rows, shared_gate, shared_up, shared_down),
        (expert_gate, expert_up, expert_down),
    )
    (
        mixed, input_grad, grad_qkv, grad_out, grad_sgate, grad_sup, grad_sdown,
        grad_egate, grad_eup, grad_edown, gain_sum, *_,
    ) = run_backward(
        sizes, rows, cot, gate_columns, route_columns, forward[:3] + forward[9:]
    )
    mixed, input_grad, grad_qkv, *rest = finish_outputs(
        (grad_qkv, grad_out, grad_sgate, grad_sup, grad_sdown, grad_egate, grad_eup, grad_edown),
        (mixed, input_grad),
        gain_sum,
        gain_width,
    )
    grad_out, grad_sgate, grad_sup, grad_sdown, grad_egate, grad_eup, grad_edown, grad_gains = rest
    return (
        mixed.reshape(tokens.shape),
        input_grad.reshape(tokens.shape),
        grad_qkv.T,
        grad_out,
        grad_sgate,
        grad_sup,
        grad_sdown,
        grad_gains,
        grad_egate,
        grad_eup,
        grad_edown,
    )


def kernels_fit(mesh_shape, arrays):
    qkv_weight, out_weight, shared_gate, _, shared_down = arrays[4:9]
    rows = (qkv_weight.shape[1], out_weight.shape[0], shared_gate.shape[1], shared_down.shape[0])
    return (
        mesh_shape[DP] == 2
        and mesh_shape[CONTEXT] >= 4
        and mesh_shape[EXPERTS] % 2 == 0
        and all(count % 16 == 0 for count in rows)
        and shared_gate.shape[1] % 128 == 0
        and arrays[10].shape[2] % 128 == 0
        and shared_gate.shape[1] * mesh_shape[EXPERTS] == 2 * arrays[10].shape[2]
    )


def solution(mesh):
    def device_program(*arrays):
        return (on_device if kernels_fit(mesh.shape, arrays) else on_device_plain)(*arrays)

    return jax.shard_map(
        device_program,
        mesh=mesh,
        in_specs=(
            P(DP, EXPERTS, None, CONTEXT, None, None),
            P(DP, EXPERTS, None, CONTEXT, None, None),
            P(DP, EXPERTS, None, CONTEXT, None, None),
            P(DP, EXPERTS, None, CONTEXT, None, None),
            P(None, (CONTEXT, EXPERTS)),
            P((CONTEXT, EXPERTS), None),
            P(None, (CONTEXT, EXPERTS)),
            P(None, (CONTEXT, EXPERTS)),
            P((CONTEXT, EXPERTS), None),
            P(None, (CONTEXT, EXPERTS)),
            P(EXPERTS, None, (DP, CONTEXT)),
            P(EXPERTS, None, (DP, CONTEXT)),
            P(EXPERTS, (DP, CONTEXT), None),
        ),
        out_specs=(
            P(DP, EXPERTS, None, CONTEXT, None, None),
            P(DP, EXPERTS, None, CONTEXT, None, None),
            P(None, (CONTEXT, EXPERTS)),
            P((CONTEXT, EXPERTS), None),
            P(None, (CONTEXT, EXPERTS)),
            P(None, (CONTEXT, EXPERTS)),
            P((CONTEXT, EXPERTS), None),
            P(None, (CONTEXT, EXPERTS)),
            P(EXPERTS, None, (DP, CONTEXT)),
            P(EXPERTS, None, (DP, CONTEXT)),
            P(EXPERTS, (DP, CONTEXT), None),
        ),
        check_vma=False,
    )
```
